128 devices in a mesh: dp: 16 (over x, y), row: 2 (over z_hi), col: 4 (over z_lo, core).
Axes of the slice: x: 4, y: 4, z: 4 (z_hi: 2, z_lo: 2; z = z_hi * 2 + z_lo), core: 2. Of those that a mesh axis runs over, the one named last changes fastest.
Arguments:
- tokens: bfloat16 [16384, 2048], P(('dp', 'row'), 'col'), may hold values from -6 to 6
- norm1_gain: float32 [2048], P('col'), may hold values from 0.5 to 1.5
- w_qkv: bfloat16 [2048, 8, 512], P('col', 'row'), may hold values from -0.125 to 0.125
- q_gain: float32 [128], replicated, may hold values from 0.1 to 1.9
- k_gain: float32 [128], replicated, may hold values from 0.1 to 1.9
- w_out: bfloat16 [2048, 2048], P('row', 'col'), may hold values from -0.5 to 0.5
- norm2_gain: float32 [2048], P('col'), may hold values from 0.5 to 1.5
- w_gate_up: bfloat16 [2048, 2, 6144], P('col', None, 'row'), may hold values from -0.125 to 0.125
- w_down: bfloat16 [6144, 2048], P('row', 'col'), may hold values from -0.078125 to 0.078125
- out_grad: bfloat16 [16384, 2048], P(('dp', 'row'), 'col'), may hold values from -6 to 6
- seq_lengths: int32 [64], replicated, may hold values from 1 to 1021, as said below
- seq_group: int32 [64], replicated, may hold values from 0 to 15, as said below
- seq_start: int32 [64], replicated, may hold values from 0 to 1023, as said below
Outputs:
- layer_out: bfloat16 [16384, 2048], P(('dp', 'row'), 'col')
- grad_tokens: float32 [16384, 2048], P(('dp', 'row'), 'col')
- grad_norm1_gain: float32 [2048], replicated
- grad_w_qkv: float32 [2048, 8, 512], P('col', 'row')
- grad_q_gain: float32 [128], replicated
- grad_k_gain: float32 [128], replicated
- grad_w_out: float32 [2048, 2048], P('row', 'col')
- grad_norm2_gain: float32 [2048], replicated
- grad_w_gate_up: float32 [2048, 2, 6144], P('col', None, 'row')
- grad_w_down: float32 [6144, 2048], P('row', 'col')
The draws below stay inside these ranges and needn't reach their ends.
Inputs may be any that keep to these rules, and one draw needn't show every extreme that they name: `seq_lengths`: the lengths of the 4 sequences of one group sum to 1024. `seq_group`: each group holds 4 sequences. `seq_start`: the sequences of one group lie end to end over its slots 0 to 1023 without gaps, in some order.
All inputs are finite; a program needn't handle non-finite values.
Results may differ from the reference program's by a relative error of at most 0.02.
Values may be sent and summed in bfloat16 or wider, within the bound.
A program may use at most 192 MiB of HBM per device.

```python
import math
import jax
import jax.numpy as jnp
from jax import lax

D = 2048
HEADS = 16
KV = 8
HD = 128
FF = 6144
SEQS_GROUP = 4
GROUP = 1024
TOKENS = 16384
QBLOCK = 512
N_DP = 16


def sequence_table(key):
    key_short = jax.random.fold_in(key, 11)
    key_order = jax.random.fold_in(key, 12)
    key_shuffle = jax.random.fold_in(key, 13)
    key_pick = jax.random.fold_in(key, 14)
    chosen = jax.random.randint(key_pick, (), 0, N_DP, dtype=jnp.int32)
    group_ids = jnp.arange(N_DP, dtype=jnp.int32)[:, None]
    shorts = jax.random.randint(key_short, (N_DP, SEQS_GROUP - 1), 1, GROUP // 64 + 4, dtype=jnp.int32)
    shorts = jnp.where(group_ids == chosen, 1, shorts).astype(jnp.int32)
    longest = GROUP - jnp.sum(shorts, axis=1)
    lengths = jnp.concatenate([longest[:, None], shorts], axis=1).astype(jnp.int32)
    order = jax.vmap(lambda one_key: jax.random.permutation(one_key, SEQS_GROUP))(jax.random.split(key_order, N_DP)).astype(jnp.int32)
    order = jnp.where(group_ids == chosen, jnp.arange(SEQS_GROUP, dtype=jnp.int32)[None, :], order).astype(jnp.int32)
    placed = jnp.take_along_axis(lengths, order, axis=1)
    begins = (jnp.cumsum(placed, axis=1) - placed).astype(jnp.int32)
    inverse = jnp.argsort(order, axis=1).astype(jnp.int32)
    starts = jnp.take_along_axis(begins, inverse, axis=1).astype(jnp.int32)
    owners = jnp.broadcast_to(jnp.arange(N_DP, dtype=jnp.int32)[:, None], (N_DP, SEQS_GROUP))
    shuffle = jax.random.permutation(key_shuffle, N_DP * SEQS_GROUP)
    return (lengths.reshape(-1)[shuffle], owners.reshape(-1)[shuffle], starts.reshape(-1)[shuffle])


def draw_seq_lengths(key, part):
    return sequence_table(key)[0]


def draw_seq_group(key, part):
    return sequence_table(key)[1]


def draw_seq_start(key, part):
    return sequence_table(key)[2]


def block_levels(key, extent, cuts, least, high):
    def one(dim, shards_of):
        steps = jax.random.uniform(jax.random.fold_in(jax.random.fold_in(key, 6), dim), (shards_of,), jnp.float32, least / len(cuts), high / len(cuts))
        return jnp.repeat(jnp.exp(steps), extent[dim] // shards_of).reshape((-1,) + (1,) * (len(extent) - dim - 1))

    level = one(*cuts[0])
    for cut in cuts[1:]:
        level = level * one(*cut)
    return level


def gaussian(key, shape, deviation, most, pieces=(), held_as=jnp.bfloat16):
    entries = deviation * jax.random.normal(key, shape, jnp.float32)
    if pieces:
        entries = entries * block_levels(key, shape, pieces, -0.22, 0.18)
    return jnp.clip(entries, -most, most).astype(held_as)


def setup_inputs(seed: int = 0) -> dict:
    streams_of = jax.random.split(jax.random.key(seed), 14)
    tokens = gaussian(streams_of[0], (TOKENS, D), 1.0, 6.0, ((0, 32), (1, 4)))
    norm1_gain = jnp.clip(1.0 + 0.1 * jax.random.normal(streams_of[1], (D,), jnp.float32), 0.5, 1.5)
    w_qkv = gaussian(streams_of[2], (D, KV, 4 * HD), D ** -0.5, 0.125, ((0, 4), (1, 2)))
    q_gain = jnp.clip(1.0 + 0.18 * jax.random.normal(streams_of[3], (HD,), jnp.float32), 0.1, 1.9)
    k_gain = jnp.clip(1.0 + 0.18 * jax.random.normal(streams_of[4], (HD,), jnp.float32), 0.1, 1.9)
    w_out = gaussian(streams_of[5], (HEADS * HD, D), (HEADS * HD // 16) ** -0.5, 0.5, ((0, 2), (1, 4)))
    norm2_gain = jnp.clip(1.0 + 0.1 * jax.random.normal(streams_of[6], (D,), jnp.float32), 0.5, 1.5)
    w_gate_up = gaussian(streams_of[7], (D, 2, FF), D ** -0.5, 0.125, ((0, 4), (2, 2)))
    w_down = gaussian(streams_of[8], (FF, D), FF ** -0.5, 0.078125, ((0, 2), (1, 4)))
    out_grad = gaussian(streams_of[9], (TOKENS, D), 1.0, 6.0, ((0, 32), (1, 4)))
    seq_lengths = draw_seq_lengths(jax.random.fold_in(streams_of[13], 71), 0)
    seq_group = draw_seq_group(jax.random.fold_in(streams_of[13], 71), 0)
    seq_start = draw_seq_start(jax.random.fold_in(streams_of[13], 71), 0)
    return dict(tokens=tokens, norm1_gain=norm1_gain, w_qkv=w_qkv, q_gain=q_gain, k_gain=k_gain, w_out=w_out, norm2_gain=norm2_gain, w_gate_up=w_gate_up, w_down=w_down, out_grad=out_grad, seq_lengths=seq_lengths, seq_group=seq_group, seq_start=seq_start)


EPS = 1e-06
THETA = 1000000.0
HIGH = lax.Precision.HIGHEST

@jax.custom_vjp
def low(v):
    return lax.optimization_barrier(v.astype(jnp.bfloat16)).astype(jnp.float32)

@jax.custom_vjp
def low_back(v):
    return v

def low_keep(v):
    return (low(v), None)

def low_pass(kept, grad):
    return (grad,)

def back_keep(v):
    return (v, None)

def back_low(kept, grad):
    return (low(grad),)
low.defvjp(low_keep, low_pass)
low_back.defvjp(back_keep, back_low)

def rms_norm(value, gain):
    return value * lax.rsqrt(lax.optimization_barrier(jnp.mean(value * value, axis=-1, keepdims=True)) + EPS) * gain

def rotate(value, cosine, sine):
    half = value.shape[-1] // 2
    first = value[..., :half]
    second = value[..., half:]
    return jnp.concatenate([first * cosine - second * sine, second * cosine + first * sine], axis=-1)

def layout(seq_lengths, seq_group, seq_start, group_index, slots_count):
    slots = jnp.arange(slots_count, dtype=jnp.int32)
    inside = (seq_group[None, :] == group_index) & (seq_start[None, :] <= slots[:, None]) & (slots[:, None] < (seq_start + seq_lengths)[None, :])
    labels = jnp.arange(1, seq_lengths.shape[0] + 1, dtype=jnp.int32)
    segment = lax.optimization_barrier(jnp.sum(jnp.where(inside, labels[None, :], 0), axis=1)).astype(jnp.int32)
    offset = lax.optimization_barrier(jnp.sum(jnp.where(inside, seq_start[None, :], 0), axis=1)).astype(jnp.int32)
    return (segment, slots, (slots - offset).astype(jnp.int32))

def angles(position, head):
    half = head // 2
    freq = THETA ** (-(jnp.arange(half, dtype=jnp.float32) * 2.0 / head))
    angle = position.astype(jnp.float32)[:, None] * freq[None, :]
    return (jnp.cos(angle), jnp.sin(angle))

def attend_block(query, keys, values, seg_q, seg_k, slot_q, slot_k):
    scale = 1.0 / math.sqrt(query.shape[-1])
    score = low_back(jnp.einsum('bgjd,kgd->bgjk', query, keys, precision=HIGH) * scale)
    allowed = (seg_q[:, None] == seg_k[None, :]) & (slot_k[None, :] <= slot_q[:, None])
    score = jnp.where(allowed[:, None, None, :], score, -1e+30)
    peak = lax.optimization_barrier(jnp.max(score, axis=-1, keepdims=True))
    weight = jnp.exp(score - peak)
    prob = weight / lax.optimization_barrier(jnp.sum(weight, axis=-1, keepdims=True))
    return jnp.einsum('bgjk,kgd->bgjd', low(prob), values, precision=HIGH)

def group_attention(query, keys, values, segment, slots):
    count = query.shape[0] // QBLOCK
    blocks = query.reshape(count, QBLOCK, query.shape[1], query.shape[2], query.shape[3])
    step = jax.checkpoint(attend_block)

    def one_block(item):
        return step(item[0], keys, values, item[1], segment, item[2], slots)
    result = lax.map(one_block, (blocks, segment.reshape(count, QBLOCK), slots.reshape(count, QBLOCK)))
    return result.reshape(query.shape)

def forward(stream, norm1_gain, w_qkv, q_gain, k_gain, w_out, norm2_gain, w_gate_up, w_down, cosine, sine, segment, slots):
    count = stream.shape[0]
    normed = low(rms_norm(stream, norm1_gain))
    mixed = jnp.dot(normed, w_qkv.reshape(D, KV * 4 * HD), precision=HIGH)
    heads = low_back(low(mixed)).reshape(count, KV, 4, HD)
    query = low(rotate(rms_norm(heads[:, :, 0:2], q_gain), cosine[:, None, None], sine[:, None, None]))
    keys = low(rotate(rms_norm(heads[:, :, 2], k_gain), cosine[:, None], sine[:, None]))
    values = heads[:, :, 3]
    groups = count // GROUP

    def per_group(item):
        return group_attention(item[0], item[1], item[2], item[3], item[4])
    attended = lax.map(per_group, (query.reshape(groups, GROUP, KV, 2, HD), keys.reshape(groups, GROUP, KV, HD), values.reshape(groups, GROUP, KV, HD), segment.reshape(groups, GROUP), slots.reshape(groups, GROUP)))
    attended = low_back(low(attended.reshape(count, HEADS * HD)))
    branch = low_back(jnp.dot(attended, w_out, precision=HIGH))
    middle = stream + branch
    normed_two = low(rms_norm(middle, norm2_gain))
    gate_up = low_back(jnp.dot(normed_two, w_gate_up.reshape(D, 2 * FF), precision=HIGH))
    hidden = low(jax.nn.silu(gate_up[:, :FF]) * gate_up[:, FF:])
    return middle + low_back(jnp.dot(hidden, w_down, precision=HIGH))

def reference(tokens, norm1_gain, w_qkv, q_gain, k_gain, w_out, norm2_gain, w_gate_up, w_down, out_grad, seq_lengths, seq_group, seq_start):

    def one_layout(group_index):
        return layout(seq_lengths, seq_group, seq_start, group_index, GROUP)
    segment, slots, position = jax.vmap(one_layout)(jnp.arange(N_DP, dtype=jnp.int32))
    cosine, sine = angles(position.reshape(-1), HD)
    segment = segment.reshape(-1)
    slots = slots.reshape(-1)
    inputs = [item.astype(jnp.float32) for item in (tokens, norm1_gain, w_qkv, q_gain, k_gain, w_out, norm2_gain, w_gate_up, w_down)]

    def closed(stream, gain_one, weight_qkv, gain_q, gain_k, weight_out, gain_two, weight_gate_up, weight_down):
        return forward(stream, gain_one, weight_qkv, gain_q, gain_k, weight_out, gain_two, weight_gate_up, weight_down, cosine, sine, segment, slots)
    result, backward = jax.vjp(closed, *inputs)
    grads = backward(out_grad.astype(jnp.float32))
    return (result.astype(jnp.bfloat16), grads[0], grads[1], grads[2], grads[3], grads[4], grads[5], grads[6], grads[7], grads[8])
```

```python
import math

import jax
import jax.numpy as jnp
from jax import lax
from jax.experimental import pallas as pl
from jax.experimental.pallas import tpu as pltpu
from jax.sharding import PartitionSpec as P

EPS = 1e-06
THETA = 1000000.0
BF = jnp.bfloat16
F32 = jnp.float32
Z = ("row", "col")
MESH = pl.DeviceIdType.MESH
VMEM_LIMIT = 60 * 1024 * 1024

GROUP, WIDTH, TILE, UNITS, HEAD = 1024, 2048, 512, 768, 128
OWN = GROUP // 8
DP = 16


def dot(left, right, dims):
    return lax.dot_general(left, right, (dims, ((), ())), preferred_element_type=F32)


def mm(left, right):
    return dot(left, right, ((1,), (0,)))


def mm_t(left, right):
    return dot(left, right, ((1,), (1,)))


def t_mm(left, right):
    return dot(left, right, ((0,), (0,)))


def place():
    row, col = lax.axis_index("row"), lax.axis_index("col")
    j = 4 * row + col
    return lax.axis_index("dp"), row, col, j // 2, j % 2


def on_ring(z, k):
    j = 2 * z + k
    return {"row": j // 4, "col": j % 4}


def remote(src, dst, send, recv, device):
    return pltpu.make_async_remote_copy(
        src_ref=src, dst_ref=dst, send_sem=send, recv_sem=recv, device_id=device, device_id_type=MESH
    )


def meet(devices):
    barrier = pltpu.get_barrier_semaphore()
    for device in devices:
        pl.semaphore_signal(barrier, inc=1, device_id=device, device_id_type=MESH)
    pl.semaphore_wait(barrier, len(devices))


def ring_friends():
    _, _, _, z, k = place()
    other = z + 1 - 2 * (z % 2)
    return [
        on_ring((z + 1) % 4, k),
        on_ring((z + 3) % 4, k),
        on_ring(z, 1 - k),
        on_ring(other, 1 - k),
    ]


def dp_friends():
    p = lax.axis_index("dp")
    return [{"dp": (p + o) % DP} for o in range(1, DP)]


def tile_at(buf):
    def loc(j, half=None):
        row, col = j // 4, j % 4
        first = pl.multiple_of(row * TILE, TILE)
        rows = pl.ds(first, TILE)
        if half is not None:
            rows = pl.ds(first + half * (TILE // 2), TILE // 2)
        return buf.at[rows, pl.ds(pl.multiple_of(col * TILE, TILE), TILE)]

    return loc


def rows_at(buf):
    def loc(j, half=None):
        first = pl.multiple_of(j * OWN, OWN)
        rows = pl.ds(first, OWN)
        if half is not None:
            rows = pl.ds(first + half * (OWN // 2), OWN // 2)
        return buf.at[rows]

    return loc


class Gather:
    def __init__(self, loc, send, recv, own=None):
        _, _, _, z, k = place()
        up, down, far = (z + 1) % 4, (z + 3) % 4, (z + 2) % 4
        to_up, to_down, peer = on_ring(up, k), on_ring(down, k), on_ring(z, 1 - k)

        def out(slot, src, dst, device):
            return remote(src, dst, send.at[slot], recv.at[slot], device)

        def into(slot, dst):
            return remote(dst, dst, send.at[slot], recv.at[slot], peer)

        mine = loc(2 * z + k)
        own = mine if own is None else own
        left, right, across = 2 * down + k, 2 * up + k, 2 * far + k
        self.first = [out(0, own, mine, to_up), out(1, own, mine, to_down), out(4, own, mine, peer)]
        self.from_left = [
            out(2, loc(left, 0), loc(left, 0), to_up),
            out(5, loc(left), loc(left), peer),
        ]
        self.from_right = [
            out(3, loc(right, 1), loc(right, 1), to_down),
            out(6, loc(right), loc(right), peer),
        ]
        self.from_far = [
            out(7, loc(across, 0), loc(across, 0), peer),
            out(8, loc(across, 1), loc(across, 1), peer),
        ]
        theirs = [2 * z + 1 - k, 2 * down + 1 - k, 2 * up + 1 - k, 2 * far + 1 - k]
        self.arrivals = {
            0: into(0, loc(left)),
            1: into(1, loc(right)),
            2: into(2, loc(across, 0)),
            3: into(3, loc(across, 1)),
            4: into(4, loc(theirs[0])),
            5: into(5, loc(theirs[1])),
            6: into(6, loc(theirs[2])),
            7: into(7, loc(theirs[3], 0)),
            8: into(8, loc(theirs[3], 1)),
        }

    def start(self):
        for copy in self.first:
            copy.start()

    def forward(self):
        self.arrivals[0].wait_recv()
        for copy in self.from_left:
            copy.start()
        self.arrivals[1].wait_recv()
        for copy in self.from_right:
            copy.start()

    def share(self):
        for half in range(2):
            self.arrivals[2 + half].wait_recv()
            self.from_far[half].start()

    def finish(self):
        for slot in range(4, 9):
            self.arrivals[slot].wait_recv()

    def drain(self):
        for copy in self.first + self.from_left + self.from_right + self.from_far:
            copy.wait_send()


GATHER_SEMS = [pltpu.SemaphoreType.DMA((9,)), pltpu.SemaphoreType.DMA((9,))]


class Scatter:
    def __init__(self, parts, theirs, sums, near, full, send, recv):
        _, _, _, z, k = place()
        self.parts, self.theirs, self.sums, self.near, self.full = parts, theirs, sums, near, full
        self.k = k
        to_up, to_down = on_ring((z + 1) % 4, k), on_ring((z + 3) % 4, k)
        peer = on_ring(z, 1 - k)
        half = OWN // 2
        other = pl.ds(pl.multiple_of((1 - k) * OWN, OWN), OWN)

        def copy(slot, src, dst, device):
            return remote(src, dst, send.at[slot], recv.at[slot], device)

        self.copies = [copy(d, parts.at[d, other], theirs.at[d], peer) for d in range(4)] + [
            copy(4, sums.at[0, pl.ds(0, half)], near.at[0], to_up),
            copy(5, sums.at[0, pl.ds(half, half)], near.at[1], to_down),
            copy(6, sums.at[1], full.at[0], to_up),
            copy(7, sums.at[2], full.at[1], to_down),
        ]

    def put(self, d):
        self.copies[d].start()

    def own(self, d, rows, count):
        first = pl.multiple_of(self.k * OWN + rows, count)
        return self.parts[d, pl.ds(first, count)].astype(F32) + self.theirs[
            d, pl.ds(rows, count)
        ].astype(F32)

    def across(self):
        self.copies[2].wait_recv()

        @pl.loop(0, OWN // 16)
        def _(i):
            rows = pl.multiple_of(i * 16, 16)
            self.sums[0, pl.ds(rows, 16)] = self.own(2, rows, 16).astype(BF)

        self.copies[4].start()
        self.copies[5].start()

    def beside(self, side):
        d, half = (1, 3)[side], OWN // 2
        self.copies[d].wait_recv()
        self.copies[4 + side].wait_recv()

        @pl.loop(0, half // 16)
        def _(i):
            rows = pl.multiple_of(i * 16, 16)
            here = pl.multiple_of(rows + side * half, 16)
            there = pl.multiple_of(rows + (1 - side) * half, 16)
            added = self.own(d, here, 16) + self.near[side, pl.ds(rows, 16)].astype(F32)
            self.sums[1 + side, pl.ds(here, 16)] = added.astype(BF)
            self.sums[1 + side, pl.ds(there, 16)] = self.own(d, there, 16).astype(BF)

        self.copies[6 + side].start()

    def arrive(self):
        self.copies[0].wait_recv()
        self.copies[6].wait_recv()
        self.copies[7].wait_recv()

    def total(self, rows, count):
        return (
            self.own(0, rows, count)
            + self.full[0, pl.ds(rows, count)].astype(F32)
            + self.full[1, pl.ds(rows, count)].astype(F32)
        )

    def drain(self):
        for copy in self.copies:
            copy.wait_send()


def scatter_scratch():
    return [
        pltpu.VMEM((4, 2 * OWN, WIDTH), BF),
        pltpu.VMEM((4, OWN, WIDTH), BF),
        pltpu.VMEM((3, OWN, WIDTH), BF),
        pltpu.VMEM((2, OWN // 2, WIDTH), BF),
        pltpu.VMEM((2, OWN, WIDTH), BF),
        pltpu.SemaphoreType.DMA((8,)),
        pltpu.SemaphoreType.DMA((8,)),
    ]


def head_norm(value):
    return lax.rsqrt(jnp.mean(value * value, axis=1, keepdims=True) + EPS)


def turn(value, cosine, sine):
    return value * cosine + pltpu.roll(value, HEAD // 2, 1) * sine


def turn_back(value, cosine, sine):
    return value * cosine - pltpu.roll(value, HEAD // 2, 1) * sine


LOG2 = math.log2(math.e)
SCALE = 1.0 / math.sqrt(HEAD)
QROWS = 256


def allowed_keys(start, first, keys):
    slots = lax.broadcasted_iota(jnp.int32, (QROWS, keys), 1)
    query = lax.broadcasted_iota(jnp.int32, (QROWS, keys), 0) + first
    return (slots >= start) & (slots <= query)


def forward_kernel(
    tok, og, gains, q_gain, k_gain, start, cosine, sine, wq_pair, wq_part, wg_pair, wg_part, w_out, w_down,
    h2_o, g_o, wq_o, wo_o, wg_o, wd_o, h1_o, raw_o, q_o, k_o, att_o, lse_o, mid_o, gain_o, x_o,
    x, h1, h2, g, wq, wo, raw, qs, ks, att, lse, mid, gain,
    xs, xr, gs, gr, hs, hr,
    parts, theirs, sums, near, full, rs_s, rs_r,
    zs, zr, ps, pr, ys, yr, ns, nr, loc_s, out_s,
):
    p, row, col, z, k = place()
    me = 2 * z + k
    lo = z % 2
    other = z + 1 - 2 * lo
    peer = on_ring(z, 1 - k)
    meet(ring_friends() + dp_friends())

    gain[col] = gains[...]
    gain_copies = [
        remote(gains, gain.at[col], ns.at[i], nr.at[col], device)
        for i, device in enumerate([peer, on_ring(other, k), on_ring(other, 1 - k)])
    ]
    for copy in gain_copies:
        copy.start()

    def part(weight, rows, index):
        return weight.at[:, pl.ds(pl.multiple_of(index * rows, 16), rows)]

    rows_of = [32, 16, 32, 48]
    weights = [wq, wo, wg_o, wd_o]

    def crossing(a, kk):
        target = 2 * (1 - lo) + kk
        src = [
            wq_part.at[kk],
            w_out.at[pl.ds(pl.multiple_of(target * 256 + p * 16, 16), 16)],
            wg_part.at[kk],
            w_down.at[pl.ds(pl.multiple_of(target * UNITS + p * 48, 16), 48)],
        ][a]
        dst = weights[a].at[col, pl.ds(pl.multiple_of(p * rows_of[a], 16), rows_of[a])]
        return remote(src, dst, zs.at[a, kk], zr.at[a, k], on_ring(other, kk))

    def crossed(a, kk):
        source = 2 * (1 - lo) + kk
        dst = weights[a].at[source, pl.ds(pl.multiple_of(p * rows_of[a], 16), rows_of[a])]
        return remote(dst, dst, zs.at[a, kk], zr.at[a, kk], peer)

    def beside(a):
        src = [
            lambda c, kk: wq_pair.at[kk],
            lambda c, kk: w_out.at[pl.ds(pl.multiple_of(c * 256, 256), 256)],
            lambda c, kk: wg_pair.at[kk],
            lambda c, kk: w_down.at[pl.ds(pl.multiple_of(c * UNITS, 256), UNITS)],
        ][a]
        there = 2 * lo + 1 - k
        keep = pltpu.make_async_copy(src(col, k), weights[a].at[col], loc_s.at[a])
        give = remote(src(there, 1 - k), weights[a].at[col], ps.at[a], pr.at[a], peer)
        take = remote(weights[a].at[there], weights[a].at[there], ps.at[a], pr.at[a], peer)
        return keep, give, take

    def spread(a, o):
        q = (p + o) % DP
        pair = pl.ds(2 * (1 - lo), 2)
        rows = rows_of[a]
        mine = weights[a].at[pair, pl.ds(pl.multiple_of(p * rows, 16), rows)]
        arriving = weights[a].at[pair, pl.ds(pl.multiple_of(q * rows, 16), rows)]
        send = remote(mine, mine, ys.at[a, q], yr.at[a, p], {"dp": q})
        take = remote(arriving, arriving, ys.at[a, q], yr.at[a, q], {"dp": q})
        return send, take

    def spread_start(a):
        @pl.loop(1, DP)
        def _(o):
            spread(a, o)[0].start()

    def spread_wait(a):
        @pl.loop(1, DP)
        def _(o):
            send, take = spread(a, o)
            take.wait_recv()
            send.wait_send()

    for a in (0, 1):
        for kk in range(2):
            crossing(a, kk).start()
    x_gather = Gather(tile_at(x), xs, xr, tok)
    x_gather.start()
    for a in range(2):
        beside(a)[0].start()
        beside(a)[1].start()
    keep_x = pltpu.make_async_copy(tok, tile_at(x)(me), loc_s.at[4])
    keep_x.start()
    keep_g = pltpu.make_async_copy(og, tile_at(g)(me), loc_s.at[5])
    keep_g.start()
    for a in (0, 1):
        for kk in range(2):
            crossed(a, kk).wait_recv()
        spread_start(a)
    for a in (2, 3):
        beside(a)[0].start()
        beside(a)[1].start()
    x_gather.forward()
    for a in (2, 3):
        for kk in range(2):
            crossing(a, kk).start()
    x_gather.share()
    g_gather = Gather(tile_at(g), gs, gr, og)
    g_gather.start()
    for c in range(4):

        @pl.when(c != col)
        def _():
            remote(gain.at[c], gain.at[c], ns.at[0], nr.at[c], peer).wait_recv()

    keep_x.wait()
    x_gather.finish()
    for a in (2, 3):
        for kk in range(2):
            crossed(a, kk).wait_recv()
        spread_start(a)

    def gain_row(which):
        return jnp.concatenate([gain[c, which : which + 1] for c in range(4)], axis=1)

    gain_one = gain_row(0)

    @pl.loop(0, GROUP // 64)
    def _(i):
        rows = pl.ds(pl.multiple_of(i * 64, 64), 64)
        value = x[rows].astype(F32)
        h1[rows] = (value * head_norm(value) * gain_one).astype(BF)

    for a in range(2):
        keep, _, take = beside(a)
        keep.wait()
        take.wait_recv()
        spread_wait(a)

    @pl.loop(0, GROUP // 256)
    def _(i):
        rows = pl.ds(pl.multiple_of(i * 256, 256), 256)
        mixed = mm(h1[rows], wq[...].reshape(WIDTH, 4 * HEAD)).astype(BF)
        raw[rows] = mixed
        cos_rows, sin_rows = cosine[rows], sine[rows]
        for piece in range(3):
            value = mixed[:, piece * HEAD : (piece + 1) * HEAD].astype(F32)
            by = q_gain[...] if piece < 2 else k_gain[...]
            turned = turn(value * head_norm(value) * by, cos_rows, sin_rows).astype(BF)
            if piece < 2:
                qs[piece, rows] = turned
            else:
                ks[rows] = turned

    g_gather.forward()
    saves = [
        pltpu.make_async_copy(src, dst, out_s.at[i])
        for i, (src, dst) in enumerate(
            [
                (h1, h1_o), (wq, wq_o), (raw, raw_o), (qs, q_o), (ks, k_o), (gain, gain_o),
                (x.at[pl.ds(pl.multiple_of(me * OWN, OWN), OWN)], x_o), (wo, wo_o),
                (att, att_o), (lse, lse_o), (g, g_o), (mid, mid_o), (h2, h2_o),
            ]
        )
    ]
    for i in range(8):
        saves[i].start()

    for block in range(GROUP // QROWS):
        first, keys = block * QROWS, (block + 1) * QROWS
        rows = pl.ds(first, QROWS)
        allowed = allowed_keys(start[rows], first, keys)

        @pl.loop(0, 2)
        def _(h):
            score = mm_t(qs[h, rows], ks[:keys]) * (SCALE * LOG2)
            score = jnp.where(allowed, score, -1e30)
            peak = jnp.max(score, axis=1, keepdims=True)
            weight = jnp.exp2(score - peak)
            total = jnp.sum(weight, axis=1, keepdims=True)
            out = mm(weight.astype(BF), raw[:keys, 3 * HEAD :]) / total
            att[h, rows] = out.astype(BF)
            lse[h, rows] = jnp.broadcast_to(peak + jnp.log2(total), (QROWS, HEAD))

    saves[8].start()
    saves[9].start()
    g_gather.share()

    scatter = Scatter(parts, theirs, sums, near, full, rs_s, rs_r)

    def project(d):
        rows = pl.ds(pl.multiple_of((z + d) % 4 * 256, 256), 256)
        left = jnp.concatenate([att[0, rows], att[1, rows]], axis=1)
        for c in range(4):
            parts[d, :, c * TILE : (c + 1) * TILE] = mm(left, wo[c]).astype(BF)
        scatter.put(d)

    project(2)
    project(1)
    scatter.across()
    project(3)
    project(0)
    scatter.beside(0)
    scatter.beside(1)
    g_gather.finish()
    keep_g.wait()
    saves[10].start()
    scatter.arrive()
    gain_two = gain_row(1)

    @pl.loop(0, OWN // 16)
    def _(i):
        first = pl.multiple_of(i * 16, 16)
        there = pl.ds(pl.multiple_of(me * OWN + first, 16), 16)
        value = x[there].astype(F32) + scatter.total(first, 16)
        mid[pl.ds(first, 16)] = value
        h2[there] = (value * head_norm(value) * gain_two).astype(BF)

    saves[11].start()
    h2_gather = Gather(rows_at(h2), hs, hr)
    h2_gather.start()
    h2_gather.forward()
    for a in (2, 3):
        keep, _, take = beside(a)
        keep.wait()
        take.wait_recv()
        spread_wait(a)
    h2_gather.share()
    h2_gather.finish()
    saves[12].start()
    for copy in gain_copies:
        copy.wait_send()
    for a in range(4):
        beside(a)[1].wait_send()
        for kk in range(2):
            crossing(a, kk).wait_send()
    x_gather.drain()
    g_gather.drain()
    h2_gather.drain()
    scatter.drain()
    for copy in saves:
        copy.wait()


def forward_call(tok, og, gains, q_gain, k_gain, start, cosine, sine, wq_pair, wq_part, wg_pair, wg_part, w_out, w_down):
    hbm = pl.BlockSpec(memory_space=pl.ANY)
    vmem = pl.BlockSpec(memory_space=pltpu.VMEM)
    dma = pltpu.SemaphoreType.DMA

    def out(shape, dtype=BF):
        return jax.ShapeDtypeStruct(shape, dtype)

    wide = (GROUP, WIDTH)
    return pl.pallas_call(
        forward_kernel,
        out_shape=[
            out(wide), out(wide), out((4, TILE, 512)), out((4, 256, TILE)), out((4, TILE, 2 * UNITS)),
            out((4, UNITS, TILE)), out(wide), out((GROUP, 512)), out((2, GROUP, HEAD)), out((GROUP, HEAD)),
            out((2, GROUP, HEAD)), out((2, GROUP, HEAD), F32), out((OWN, WIDTH), F32), out((4, 8, TILE), F32),
            out((OWN, WIDTH)),
        ],
        in_specs=[vmem] * 8 + [hbm] * 6,
        out_specs=[hbm] * 15,
        scratch_shapes=[
            pltpu.VMEM(wide, BF), pltpu.VMEM(wide, BF), pltpu.VMEM(wide, BF), pltpu.VMEM(wide, BF),
            pltpu.VMEM((4, TILE, 512), BF), pltpu.VMEM((4, 256, TILE), BF), pltpu.VMEM((GROUP, 512), BF),
            pltpu.VMEM((2, GROUP, HEAD), BF), pltpu.VMEM((GROUP, HEAD), BF), pltpu.VMEM((2, GROUP, HEAD), BF),
            pltpu.VMEM((2, GROUP, HEAD), F32), pltpu.VMEM((OWN, WIDTH), F32), pltpu.VMEM((4, 8, TILE), F32),
        ]
        + GATHER_SEMS * 3
        + scatter_scratch()
        + [dma((4, 2)), dma((4, 2)), dma((4,)), dma((4,)), dma((4, DP)), dma((4, DP)), dma((3,)), dma((4,)), dma((6,)), dma((13,))],
        compiler_params=pltpu.CompilerParams(
            collective_id=1, has_side_effects=True, vmem_limit_bytes=VMEM_LIMIT
        ),
        cost_estimate=pl.CostEstimate(flops=4_000_000_000, bytes_accessed=60_000_000, transcendentals=2_000_000),
        name="forward",
    )(tok, og, gains, q_gain, k_gain, start, cosine, sine, wq_pair, wq_part, wg_pair, wg_part, w_out, w_down)


def middle_kernel(h2, g, wg, wd, grads, ggu, hid, h2_t):
    @pl.when(pl.program_id(0) == 0)
    def _():
        @pl.loop(0, 8)
        def _(i):
            cols = pl.ds(pl.multiple_of(i * 256, 256), 256)
            h2_t[cols] = h2[:, cols].T

    @pl.loop(0, GROUP // 256)
    def _(i):
        rows = pl.ds(pl.multiple_of(i * 256, 256), 256)
        pair = mm(h2[rows], wg[...].reshape(WIDTH, 512))
        back = mm_t(g[rows, :TILE], wd[0])
        for c in range(1, 4):
            back += mm_t(g[rows, c * TILE : (c + 1) * TILE], wd[c])
        gate, up = pair[:, :256], pair[:, 256:]
        sig = 1.0 / (1.0 + jnp.exp(-gate))
        silu = gate * sig
        hid[rows] = (silu * up).astype(BF)
        ggu[rows, :256] = (back * up * sig * (1.0 + gate * (1.0 - sig))).astype(BF)
        ggu[rows, 256:] = (back * silu).astype(BF)

    hid_t = hid[...].T

    @pl.loop(0, 4)
    def _(c):
        cols = pl.ds(pl.multiple_of(c * TILE, TILE), TILE)
        up_grad = mm(h2_t[cols], ggu[...]).astype(BF).reshape(DP, 1, 32, 512)
        down_grad = mm(hid_t, g[:, cols]).astype(BF).reshape(DP, 1, 16, 512)
        grads[:, 0, pl.ds(c, 1), :32] = up_grad
        grads[:, 0, pl.ds(c, 1), 32:] = down_grad


def middle_call(h2, g, wg, wd):
    once = pl.Buffered(1)
    wide = pl.BlockSpec((GROUP, WIDTH), lambda u: (0, 0), pipeline_mode=once)
    return pl.pallas_call(
        middle_kernel,
        grid=(3,),
        out_shape=[
            jax.ShapeDtypeStruct((DP, 3, 4, 48, 512), BF),
            jax.ShapeDtypeStruct((GROUP, 2 * UNITS), BF),
            jax.ShapeDtypeStruct((GROUP, UNITS), BF),
        ],
        in_specs=[
            wide,
            wide,
            pl.BlockSpec((4, TILE, 512), lambda u: (0, 0, u)),
            pl.BlockSpec((4, 256, TILE), lambda u: (0, u, 0)),
        ],
        out_specs=[
            pl.BlockSpec((DP, 1, 4, 48, 512), lambda u: (0, u, 0, 0, 0)),
            pl.BlockSpec((GROUP, 512), lambda u: (0, u)),
            pl.BlockSpec((GROUP, 256), lambda u: (0, u)),
        ],
        scratch_shapes=[pltpu.VMEM((WIDTH, GROUP), BF)],
        compiler_params=pltpu.CompilerParams(vmem_limit_bytes=VMEM_LIMIT),
        cost_estimate=pl.CostEstimate(flops=19_000_000_000, bytes_accessed=32_000_000, transcendentals=800_000),
        name="feed_forward",
    )(h2, g, wg, wd)


def starts_of(seq_lengths, seq_group, seq_start, group_index):
    slots = jnp.arange(GROUP, dtype=jnp.int32)
    inside = (
        (seq_group[None, :] == group_index)
        & (seq_start[None, :] <= slots[:, None])
        & (slots[:, None] < (seq_start + seq_lengths)[None, :])
    )
    return (jnp.sum(jnp.where(inside, seq_start[None, :], 0), axis=1), slots)


def angles(position):
    half = HEAD // 2
    freq = THETA ** (-(jnp.arange(half, dtype=F32) * 2.0 / HEAD))
    angle = position.astype(F32)[:, None] * freq[None, :]
    return (jnp.cos(angle), jnp.sin(angle))


def exchange(piece):
    return lax.all_to_all(piece, "col", split_axis=0, concat_axis=0, tiled=True)


def scatter_rows(partial):
    return lax.psum_scatter(partial.astype(BF), Z, scatter_dimension=0, tiled=True).astype(F32)


def gather_rows(block):
    return lax.all_gather(block, Z, axis=0, tiled=True)


def rows_to_tile(block):
    return lax.all_to_all(block, "col", split_axis=1, concat_axis=0, tiled=True)


def norm_backward(grad, value, scale, gain):
    inner = jnp.sum(grad * gain * value, axis=1, keepdims=True)
    gain_grad = jnp.sum(grad * value * scale, axis=0)
    back = scale * gain * grad - value * (scale * scale * scale * inner / value.shape[1])
    return (back, gain_grad)


def head_backward(grad, value, gain, cosine, sine):
    half = HEAD // 2
    first, second = grad[:, :half], grad[:, half:]
    grad = jnp.concatenate([first * cosine + second * sine, second * cosine - first * sine], axis=1)
    scale = lax.rsqrt(jnp.mean(value * value, axis=1, keepdims=True) + EPS)
    return norm_backward(grad, value, scale, gain)


def body(
    tokens, norm1_gain, w_qkv, q_gain, k_gain, w_out, norm2_gain, w_gate_up, w_down, out_grad,
    seq_lengths, seq_group, seq_start,
):
    me = lax.axis_index("row") * 4 + lax.axis_index("col")
    p = lax.axis_index("dp")
    lo = lax.axis_index("col") // 2
    start, slots = starts_of(seq_lengths, seq_group, seq_start, p)
    cosine, sine = angles(slots - start)
    cos_wide = jnp.concatenate([cosine, cosine], axis=1)
    sin_wide = jnp.concatenate([-sine, sine], axis=1)
    gains = jnp.concatenate([norm1_gain[None], norm2_gain[None], jnp.zeros((6, TILE), F32)])

    def pair(weight, index, cut):
        return lax.dynamic_index_in_dim(weight, index, cut, keepdims=False)

    wq5 = w_qkv.reshape(TILE, 2, 2, 512)
    wq_pair = pair(wq5, lo, 1).transpose(1, 0, 2)
    wq_part = pair(lax.dynamic_slice_in_dim(wq5, p * 32, 32, 0), 1 - lo, 1).transpose(1, 0, 2)
    wg7 = w_gate_up.reshape(TILE, 2, 2, 2, 3, 256)

    def order(block):
        return block.transpose(2, 0, 3, 1, 4).reshape(2, -1, 2 * UNITS)

    wg_pair = order(pair(wg7, lo, 2))
    wg_part = order(pair(lax.dynamic_slice_in_dim(wg7, p * 32, 32, 0), 1 - lo, 2))

    (h2, g, wq, wo, wg, wd, h1, raw, qs, ks, att, lse, middle, gain, x_own) = forward_call(
        tokens, out_grad, gains, q_gain[None], k_gain[None], start[:, None], cos_wide, sin_wide,
        wq_pair, wq_part, wg_pair, wg_part, w_out, w_down,
    )
    gain_one = gain[:, 0].reshape(1, WIDTH)
    gain_two = gain[:, 1].reshape(1, WIDTH)
    big, ggu, hid = middle_call(h2, g, wg, wd)
    big = lax.psum_scatter(big, "dp", scatter_dimension=0, tiled=False)

    wd2 = wd.transpose(1, 0, 2).reshape(UNITS, WIDTH)
    wo2 = wo.transpose(1, 0, 2).reshape(256, WIDTH)
    result = rows_to_tile((middle + scatter_rows(mm(hid, wd2))).astype(BF))
    scale_two = lax.rsqrt(jnp.mean(middle * middle, axis=1, keepdims=True) + EPS)
    back, gain_two_grad = norm_backward(
        scatter_rows(mm_t(ggu, wg.reshape(WIDTH, 2 * UNITS))), middle, scale_two, gain_two
    )
    middle_grad = lax.dynamic_slice_in_dim(g, me * OWN, OWN, 0).astype(F32) + back
    middle_all = gather_rows(middle_grad.astype(BF))
    att2 = jnp.concatenate([att[0], att[1]], axis=1)
    g_out = t_mm(att2, middle_all).astype(BF)
    head_grad = mm_t(middle_all, wo2).astype(BF).reshape(GROUP, 2, HEAD).transpose(1, 0, 2)
    value_low = raw[:, 3 * HEAD :]
    allowed = (slots[None, :] >= start[:, None]) & (slots[None, :] <= slots[:, None])
    key_grad, value_grad, pieces, gain_q_grad = 0.0, 0.0, [], 0.0
    for h in range(2):
        score = jnp.where(allowed, mm_t(qs[h], ks) * (SCALE * LOG2), -1e30)
        prob = jnp.exp2(score - lse[h, :, :1])
        prob_grad = mm_t(head_grad[h], value_low)
        delta = jnp.sum(prob_grad * prob, axis=-1, keepdims=True)
        score_grad = (prob * (prob_grad - delta)).astype(BF)
        key_grad += t_mm(score_grad, qs[h]) * SCALE
        value_grad += t_mm(prob.astype(BF), head_grad[h])
        piece, gain_grad = head_backward(
            mm(score_grad, ks) * SCALE, raw[:, h * HEAD : (h + 1) * HEAD].astype(F32), q_gain, cosine, sine
        )
        gain_q_grad += gain_grad
        pieces.append(piece)
    piece, gain_k_grad = head_backward(
        key_grad, raw[:, 2 * HEAD : 3 * HEAD].astype(F32), k_gain, cosine, sine
    )
    heads_grad = jnp.concatenate(pieces + [piece, value_grad], axis=1).astype(BF)
    g_qkv = t_mm(h1, heads_grad).astype(BF)
    small = jnp.concatenate(
        [
            g_qkv.reshape(4, DP, 32, 512).transpose(1, 0, 2, 3),
            g_out.reshape(DP, 16, 4, 512).transpose(0, 2, 1, 3),
        ],
        axis=2,
    )
    small = lax.psum_scatter(small, "dp", scatter_dimension=0, tiled=False)
    x_float = x_own.astype(F32)
    scale_one = lax.rsqrt(jnp.mean(x_float * x_float, axis=1, keepdims=True) + EPS)
    back, gain_one_grad = norm_backward(
        scatter_rows(mm_t(heads_grad, wq.reshape(WIDTH, 512))), x_float, scale_one, gain_one
    )
    stream_grad = rows_to_tile(middle_grad + back)
    totals = lax.psum(
        jnp.concatenate([gain_one_grad, gain_two_grad, gain_q_grad, gain_k_grad]),
        ("dp", "row", "col"),
    )
    big = lax.all_gather(exchange(big.transpose(1, 0, 2, 3)), "dp", axis=0)
    small = lax.all_gather(exchange(small), "dp", axis=0)
    g_gate_up = big[:, :, :, :32].reshape(DP, 4, 3, 32, 2, 256).transpose(0, 3, 4, 1, 2, 5)
    g_down = big[:, :, :, 32:].transpose(1, 2, 0, 3, 4)
    g_qkv = small[:, :, :32].transpose(0, 2, 1, 3)
    g_out = small[:, :, 32:].transpose(1, 0, 2, 3)
    return (
        result,
        stream_grad,
        totals[:WIDTH],
        g_qkv.reshape(w_qkv.shape).astype(F32),
        totals[2 * WIDTH : 2 * WIDTH + HEAD],
        totals[2 * WIDTH + HEAD :],
        g_out.reshape(w_out.shape).astype(F32),
        totals[WIDTH : 2 * WIDTH],
        g_gate_up.reshape(w_gate_up.shape).astype(F32),
        g_down.reshape(w_down.shape).astype(F32),
    )


def solution(mesh):
    in_specs = (
        P(("dp", "row"), "col"),
        P("col"),
        P("col", "row", None),
        P(),
        P(),
        P("row", "col"),
        P("col"),
        P("col", None, "row"),
        P("row", "col"),
        P(("dp", "row"), "col"),
        P(),
        P(),
        P(),
    )
    out_specs = (
        P(("dp", "row"), "col"),
        P(("dp", "row"), "col"),
        P(),
        P("col", "row", None),
        P(),
        P(),
        P("row", "col"),
        P(),
        P("col", None, "row"),
        P("row", "col"),
    )
    return jax.shard_map(body, mesh=mesh, in_specs=in_specs, out_specs=out_specs, check_vma=False)
```

```python
import math

import jax
import jax.numpy as jnp
from jax import lax
from jax.experimental import pallas as pl
from jax.experimental.pallas import tpu as pltpu
from jax.sharding import PartitionSpec as P

EPS = 1e-06
THETA = 1000000.0
BF = jnp.bfloat16
F32 = jnp.float32
Z = ("row", "col")
MESH = pl.DeviceIdType.MESH
VMEM_LIMIT = 60 * 1024 * 1024

GROUP, WIDTH, TILE, UNITS, HEAD = 1024, 2048, 512, 768, 128
OWN = GROUP // 8
DP = 16


def dot(left, right, dims):
    return lax.dot_general(left, right, (dims, ((), ())), preferred_element_type=F32)


def mm(left, right):
    return dot(left, right, ((1,), (0,)))


def mm_t(left, right):
    return dot(left, right, ((1,), (1,)))


def t_mm(left, right):
    return dot(left, right, ((0,), (0,)))


def place():
    row, col = lax.axis_index("row"), lax.axis_index("col")
    j = 4 * row + col
    return lax.axis_index("dp"), row, col, j // 2, j % 2


def on_ring(z, k):
    j = 2 * z + k
    return {"row": j // 4, "col": j % 4}


def remote(src, dst, send, recv, device):
    return pltpu.make_async_remote_copy(
        src_ref=src, dst_ref=dst, send_sem=send, recv_sem=recv, device_id=device, device_id_type=MESH
    )


def meet(devices):
    barrier = pltpu.get_barrier_semaphore()
    for device in devices:
        pl.semaphore_signal(barrier, inc=1, device_id=device, device_id_type=MESH)
    pl.semaphore_wait(barrier, len(devices))


def ring_friends():
    _, _, _, z, k = place()
    other = z + 1 - 2 * (z % 2)
    return [
        on_ring((z + 1) % 4, k),
        on_ring((z + 3) % 4, k),
        on_ring(z, 1 - k),
        on_ring(other, 1 - k),
    ]


def dp_friends():
    p = lax.axis_index("dp")
    return [{"dp": (p + o) % DP} for o in range(1, DP)]


def tile_at(buf):
    def loc(j, half=None):
        row, col = j // 4, j % 4
        first = pl.multiple_of(row * TILE, TILE)
        rows = pl.ds(first, TILE)
        if half is not None:
            rows = pl.ds(first + half * (TILE // 2), TILE // 2)
        return buf.at[rows, pl.ds(pl.multiple_of(col * TILE, TILE), TILE)]

    return loc


def rows_at(buf):
    def loc(j, half=None):
        first = pl.multiple_of(j * OWN, OWN)
        rows = pl.ds(first, OWN)
        if half is not None:
            rows = pl.ds(first + half * (OWN // 2), OWN // 2)
        return buf.at[rows]

    return loc


class Gather:
    def __init__(self, loc, send, recv, own=None):
        _, _, _, z, k = place()
        up, down, far = (z + 1) % 4, (z + 3) % 4, (z + 2) % 4
        to_up, to_down, peer = on_ring(up, k), on_ring(down, k), on_ring(z, 1 - k)

        def out(slot, src, dst, device):
            return remote(src, dst, send.at[slot], recv.at[slot], device)

        def into(slot, dst):
            return remote(dst, dst, send.at[slot], recv.at[slot], peer)

        mine = loc(2 * z + k)
        own = mine if own is None else own
        left, right, across = 2 * down + k, 2 * up + k, 2 * far + k
        self.first = [out(0, own, mine, to_up), out(1, own, mine, to_down), out(4, own, mine, peer)]
        self.from_left = [
            out(2, loc(left, 0), loc(left, 0), to_up),
            out(5, loc(left), loc(left), peer),
        ]
        self.from_right = [
            out(3, loc(right, 1), loc(right, 1), to_down),
            out(6, loc(right), loc(right), peer),
        ]
        self.from_far = [
            out(7, loc(across, 0), loc(across, 0), peer),
            out(8, loc(across, 1), loc(across, 1), peer),
        ]
        theirs = [2 * z + 1 - k, 2 * down + 1 - k, 2 * up + 1 - k, 2 * far + 1 - k]
        self.arrivals = {
            0: into(0, loc(left)),
            1: into(1, loc(right)),
            2: into(2, loc(across, 0)),
            3: into(3, loc(across, 1)),
            4: into(4, loc(theirs[0])),
            5: into(5, loc(theirs[1])),
            6: into(6, loc(theirs[2])),
            7: into(7, loc(theirs[3], 0)),
            8: into(8, loc(theirs[3], 1)),
        }

    def start(self):
        for copy in self.first:
            copy.start()

    def forward(self):
        self.arrivals[0].wait_recv()
        for copy in self.from_left:
            copy.start()
        self.arrivals[1].wait_recv()
        for copy in self.from_right:
            copy.start()

    def share(self):
        for half in range(2):
            self.arrivals[2 + half].wait_recv()
            self.from_far[half].start()

    def finish(self):
        for slot in range(4, 9):
            self.arrivals[slot].wait_recv()

    def drain(self):
        for copy in self.first + self.from_left + self.from_right + self.from_far:
            copy.wait_send()


GATHER_SEMS = [pltpu.SemaphoreType.DMA((9,)), pltpu.SemaphoreType.DMA((9,))]


class Scatter:
    def __init__(self, parts, theirs, sums, near, full, send, recv):
        _, _, _, z, k = place()
        self.parts, self.theirs, self.sums, self.near, self.full = parts, theirs, sums, near, full
        self.k = k
        to_up, to_down = on_ring((z + 1) % 4, k), on_ring((z + 3) % 4, k)
        peer = on_ring(z, 1 - k)
        half = OWN // 2
        other = pl.ds(pl.multiple_of((1 - k) * OWN, OWN), OWN)

        def copy(slot, src, dst, device):
            return remote(src, dst, send.at[slot], recv.at[slot], device)

        self.copies = [copy(d, parts.at[d, other], theirs.at[d], peer) for d in range(4)] + [
            copy(4, sums.at[0, pl.ds(0, half)], near.at[0], to_up),
            copy(5, sums.at[0, pl.ds(half, half)], near.at[1], to_down),
            copy(6, sums.at[1], full.at[0], to_up),
            copy(7, sums.at[2], full.at[1], to_down),
        ]

    def put(self, d):
        self.copies[d].start()

    def own(self, d, rows, count):
        first = pl.multiple_of(self.k * OWN + rows, count)
        return self.parts[d, pl.ds(first, count)].astype(F32) + self.theirs[
            d, pl.ds(rows, count)
        ].astype(F32)

    def across(self):
        self.copies[2].wait_recv()

        @pl.loop(0, OWN // 16)
        def _(i):
            rows = pl.multiple_of(i * 16, 16)
            self.sums[0, pl.ds(rows, 16)] = self.own(2, rows, 16).astype(BF)

        self.copies[4].start()
        self.copies[5].start()

    def beside(self, side):
        d, half = (1, 3)[side], OWN // 2
        self.copies[d].wait_recv()
        self.copies[4 + side].wait_recv()

        @pl.loop(0, half // 16)
        def _(i):
            rows = pl.multiple_of(i * 16, 16)
            here = pl.multiple_of(rows + side * half, 16)
            there = pl.multiple_of(rows + (1 - side) * half, 16)
            added = self.own(d, here, 16) + self.near[side, pl.ds(rows, 16)].astype(F32)
            self.sums[1 + side, pl.ds(here, 16)] = added.astype(BF)
            self.sums[1 + side, pl.ds(there, 16)] = self.own(d, there, 16).astype(BF)

        self.copies[6 + side].start()

    def arrive(self):
        self.copies[0].wait_recv()
        self.copies[6].wait_recv()
        self.copies[7].wait_recv()

    def total(self, rows, count):
        return (
            self.own(0, rows, count)
            + self.full[0, pl.ds(rows, count)].astype(F32)
            + self.full[1, pl.ds(rows, count)].astype(F32)
        )

    def drain(self):
        for copy in self.copies:
            copy.wait_send()


def scatter_scratch():
    return [
        pltpu.VMEM((4, 2 * OWN, WIDTH), BF),
        pltpu.VMEM((4, OWN, WIDTH), BF),
        pltpu.VMEM((3, OWN, WIDTH), BF),
        pltpu.VMEM((2, OWN // 2, WIDTH), BF),
        pltpu.VMEM((2, OWN, WIDTH), BF),
        pltpu.SemaphoreType.DMA((8,)),
        pltpu.SemaphoreType.DMA((8,)),
    ]


def head_norm(value):
    return lax.rsqrt(jnp.mean(value * value, axis=1, keepdims=True) + EPS)


def turn(value, cosine, sine):
    return value * cosine + pltpu.roll(value, HEAD // 2, 1) * sine


def turn_back(value, cosine, sine):
    return value * cosine - pltpu.roll(value, HEAD // 2, 1) * sine


LOG2 = math.log2(math.e)
SCALE = 1.0 / math.sqrt(HEAD)
QROWS = 256


def allowed_keys(start, first, keys):
    slots = lax.broadcasted_iota(jnp.int32, (QROWS, keys), 1)
    query = lax.broadcasted_iota(jnp.int32, (QROWS, keys), 0) + first
    return (slots >= start) & (slots <= query)


def forward_kernel(
    tok, og, gains, q_gain, k_gain, start, cosine, sine, wq_pair, wq_part, wg_pair, wg_part, w_out, w_down,
    h2_o, g_o, wq_o, wo_o, wg_o, wd_o, h1t_o, raw_o, q_o, k_o, att_o, lse_o, mid_o, gain_o, x_o,
    x, h1, h1t, h2, g, wq, wo, raw, qs, ks, att, lse, mid, gain,
    xs, xr, gs, gr, hs, hr,
    parts, theirs, sums, near, full, rs_s, rs_r,
    zs, zr, ps, pr, ys, yr, ns, nr, loc_s, out_s,
):
    p, row, col, z, k = place()
    me = 2 * z + k
    lo = z % 2
    other = z + 1 - 2 * lo
    peer = on_ring(z, 1 - k)
    meet(ring_friends() + dp_friends())

    gain[col] = gains[...]
    gain_copies = [
        remote(gains, gain.at[col], ns.at[i], nr.at[col], device)
        for i, device in enumerate([peer, on_ring(other, k), on_ring(other, 1 - k)])
    ]
    for copy in gain_copies:
        copy.start()

    def part(weight, rows, index):
        return weight.at[:, pl.ds(pl.multiple_of(index * rows, 16), rows)]

    rows_of = [32, 16, 32, 48]
    weights = [wq, wo, wg_o, wd_o]

    def crossing(a, kk):
        target = 2 * (1 - lo) + kk
        src = [
            wq_part.at[kk],
            w_out.at[pl.ds(pl.multiple_of(target * 256 + p * 16, 16), 16)],
            wg_part.at[kk],
            w_down.at[pl.ds(pl.multiple_of(target * UNITS + p * 48, 16), 48)],
        ][a]
        dst = weights[a].at[col, pl.ds(pl.multiple_of(p * rows_of[a], 16), rows_of[a])]
        return remote(src, dst, zs.at[a, kk], zr.at[a, k], on_ring(other, kk))

    def crossed(a, kk):
        source = 2 * (1 - lo) + kk
        dst = weights[a].at[source, pl.ds(pl.multiple_of(p * rows_of[a], 16), rows_of[a])]
        return remote(dst, dst, zs.at[a, kk], zr.at[a, kk], peer)

    def beside(a):
        src = [
            lambda c, kk: wq_pair.at[kk],
            lambda c, kk: w_out.at[pl.ds(pl.multiple_of(c * 256, 256), 256)],
            lambda c, kk: wg_pair.at[kk],
            lambda c, kk: w_down.at[pl.ds(pl.multiple_of(c * UNITS, 256), UNITS)],
        ][a]
        there = 2 * lo + 1 - k
        keep = pltpu.make_async_copy(src(col, k), weights[a].at[col], loc_s.at[a])
        give = remote(src(there, 1 - k), weights[a].at[col], ps.at[a], pr.at[a], peer)
        take = remote(weights[a].at[there], weights[a].at[there], ps.at[a], pr.at[a], peer)
        return keep, give, take

    def spread(a, o):
        q = (p + o) % DP
        pair = pl.ds(2 * (1 - lo), 2)
        rows = rows_of[a]
        mine = weights[a].at[pair, pl.ds(pl.multiple_of(p * rows, 16), rows)]
        arriving = weights[a].at[pair, pl.ds(pl.multiple_of(q * rows, 16), rows)]
        send = remote(mine, mine, ys.at[a, q], yr.at[a, p], {"dp": q})
        take = remote(arriving, arriving, ys.at[a, q], yr.at[a, q], {"dp": q})
        return send, take

    def spread_start(a):
        @pl.loop(1, DP)
        def _(o):
            spread(a, o)[0].start()

    def spread_wait(a):
        @pl.loop(1, DP)
        def _(o):
            send, take = spread(a, o)
            take.wait_recv()
            send.wait_send()

    for a in (0, 1):
        for kk in range(2):
            crossing(a, kk).start()
    x_gather = Gather(tile_at(x), xs, xr, tok)
    x_gather.start()
    for a in range(2):
        beside(a)[0].start()
        beside(a)[1].start()
    keep_x = pltpu.make_async_copy(tok, tile_at(x)(me), loc_s.at[4])
    keep_x.start()
    keep_g = pltpu.make_async_copy(og, tile_at(g)(me), loc_s.at[5])
    keep_g.start()
    for a in (0, 1):
        for kk in range(2):
            crossed(a, kk).wait_recv()
        spread_start(a)
    for a in (2, 3):
        beside(a)[0].start()
        beside(a)[1].start()
    x_gather.forward()
    for a in (2, 3):
        for kk in range(2):
            crossing(a, kk).start()
    x_gather.share()
    g_gather = Gather(tile_at(g), gs, gr, og)
    g_gather.start()
    for c in range(4):

        @pl.when(c != col)
        def _():
            remote(gain.at[c], gain.at[c], ns.at[0], nr.at[c], peer).wait_recv()

    keep_x.wait()
    x_gather.finish()
    for a in (2, 3):
        for kk in range(2):
            crossed(a, kk).wait_recv()
        spread_start(a)

    def gain_row(which):
        return jnp.concatenate([gain[c, which : which + 1] for c in range(4)], axis=1)

    gain_one = gain_row(0)

    @pl.loop(0, GROUP // 64)
    def _(i):
        rows = pl.ds(pl.multiple_of(i * 64, 64), 64)
        value = x[rows].astype(F32)
        h1[rows] = (value * head_norm(value) * gain_one).astype(BF)

    for a in range(2):
        keep, _, take = beside(a)
        keep.wait()
        take.wait_recv()
        spread_wait(a)

    @pl.loop(0, GROUP // 256)
    def _(i):
        rows = pl.ds(pl.multiple_of(i * 256, 256), 256)
        mixed = mm(h1[rows], wq[...].reshape(WIDTH, 4 * HEAD)).astype(BF)
        raw[rows] = mixed
        cos_rows, sin_rows = cosine[rows], sine[rows]
        for piece in range(3):
            value = mixed[:, piece * HEAD : (piece + 1) * HEAD].astype(F32)
            by = q_gain[...] if piece < 2 else k_gain[...]
            turned = turn(value * head_norm(value) * by, cos_rows, sin_rows).astype(BF)
            if piece < 2:
                qs[piece, rows] = turned
            else:
                ks[rows] = turned

    g_gather.forward()
    saves = [
        pltpu.make_async_copy(src, dst, out_s.at[i])
        for i, (src, dst) in enumerate(
            [
                (wq, wq_o), (raw, raw_o), (qs, q_o), (ks, k_o), (gain, gain_o),
                (x.at[pl.ds(pl.multiple_of(me * OWN, OWN), OWN)], x_o), (wo, wo_o),
                (att, att_o), (lse, lse_o), (g, g_o), (mid, mid_o), (h2, h2_o), (h1t, h1t_o),
            ]
        )
    ]
    for i in range(7):
        saves[i].start()

    for block in range(GROUP // QROWS):
        first, keys = block * QROWS, (block + 1) * QROWS
        rows = pl.ds(first, QROWS)
        allowed = allowed_keys(start[rows], first, keys)

        @pl.loop(0, 2)
        def _(h):
            score = mm_t(qs[h, rows], ks[:keys]) * (SCALE * LOG2)
            score = jnp.where(allowed, score, -1e30)
            peak = jnp.max(score, axis=1, keepdims=True)
            weight = jnp.exp2(score - peak)
            total = jnp.sum(weight, axis=1, keepdims=True)
            out = mm(weight.astype(BF), raw[:keys, 3 * HEAD :]) / total
            att[h, rows] = out.astype(BF)
            lse[h, rows] = jnp.broadcast_to(peak + jnp.log2(total), (QROWS, HEAD))

    saves[7].start()
    saves[8].start()
    g_gather.share()

    scatter = Scatter(parts, theirs, sums, near, full, rs_s, rs_r)

    def project(d):
        rows = pl.ds(pl.multiple_of((z + d) % 4 * 256, 256), 256)
        left = jnp.concatenate([att[0, rows], att[1, rows]], axis=1)
        for c in range(4):
            parts[d, :, c * TILE : (c + 1) * TILE] = mm(left, wo[c]).astype(BF)
        scatter.put(d)

    project(2)
    project(1)
    scatter.across()
    project(3)
    project(0)
    scatter.beside(0)
    scatter.beside(1)

    @pl.loop(0, 8)
    def _(i):
        cols = pl.ds(pl.multiple_of(i * 256, 256), 256)
        h1t[cols] = h1[:, cols].T

    saves[12].start()
    g_gather.finish()
    keep_g.wait()
    saves[9].start()
    scatter.arrive()
    gain_two = gain_row(1)

    @pl.loop(0, OWN // 16)
    def _(i):
        first = pl.multiple_of(i * 16, 16)
        there = pl.ds(pl.multiple_of(me * OWN + first, 16), 16)
        value = x[there].astype(F32) + scatter.total(first, 16)
        mid[pl.ds(first, 16)] = value
        h2[there] = (value * head_norm(value) * gain_two).astype(BF)

    saves[10].start()
    h2_gather = Gather(rows_at(h2), hs, hr)
    h2_gather.start()
    h2_gather.forward()
    for a in (2, 3):
        keep, _, take = beside(a)
        keep.wait()
        take.wait_recv()
        spread_wait(a)
    h2_gather.share()
    h2_gather.finish()
    saves[11].start()
    for copy in gain_copies:
        copy.wait_send()
    for a in range(4):
        beside(a)[1].wait_send()
        for kk in range(2):
            crossing(a, kk).wait_send()
    x_gather.drain()
    g_gather.drain()
    h2_gather.drain()
    scatter.drain()
    for copy in saves:
        copy.wait()


def forward_call(tok, og, gains, q_gain, k_gain, start, cosine, sine, wq_pair, wq_part, wg_pair, wg_part, w_out, w_down):
    hbm = pl.BlockSpec(memory_space=pl.ANY)
    vmem = pl.BlockSpec(memory_space=pltpu.VMEM)
    dma = pltpu.SemaphoreType.DMA

    def out(shape, dtype=BF):
        return jax.ShapeDtypeStruct(shape, dtype)

    wide = (GROUP, WIDTH)
    return pl.pallas_call(
        forward_kernel,
        out_shape=[
            out(wide), out(wide), out((4, TILE, 512)), out((4, 256, TILE)), out((4, TILE, 2 * UNITS)),
            out((4, UNITS, TILE)), out((WIDTH, GROUP)), out((GROUP, 512)), out((2, GROUP, HEAD)), out((GROUP, HEAD)),
            out((2, GROUP, HEAD)), out((2, GROUP, HEAD), F32), out((OWN, WIDTH), F32), out((4, 8, TILE), F32),
            out((OWN, WIDTH)),
        ],
        in_specs=[vmem] * 8 + [hbm] * 6,
        out_specs=[hbm] * 15,
        scratch_shapes=[
            pltpu.VMEM(wide, BF), pltpu.VMEM(wide, BF), pltpu.VMEM((WIDTH, GROUP), BF), pltpu.VMEM(wide, BF), pltpu.VMEM(wide, BF),
            pltpu.VMEM((4, TILE, 512), BF), pltpu.VMEM((4, 256, TILE), BF), pltpu.VMEM((GROUP, 512), BF),
            pltpu.VMEM((2, GROUP, HEAD), BF), pltpu.VMEM((GROUP, HEAD), BF), pltpu.VMEM((2, GROUP, HEAD), BF),
            pltpu.VMEM((2, GROUP, HEAD), F32), pltpu.VMEM((OWN, WIDTH), F32), pltpu.VMEM((4, 8, TILE), F32),
        ]
        + GATHER_SEMS * 3
        + scatter_scratch()
        + [dma((4, 2)), dma((4, 2)), dma((4,)), dma((4,)), dma((4, DP)), dma((4, DP)), dma((3,)), dma((4,)), dma((6,)), dma((13,))],
        compiler_params=pltpu.CompilerParams(
            collective_id=1, has_side_effects=True, vmem_limit_bytes=VMEM_LIMIT
        ),
        cost_estimate=pl.CostEstimate(flops=4_000_000_000, bytes_accessed=60_000_000, transcendentals=2_000_000),
        name="forward",
    )(tok, og, gains, q_gain, k_gain, start, cosine, sine, wq_pair, wq_part, wg_pair, wg_part, w_out, w_down)


def middle_kernel(h2, g, wg, wd, grads, ggu, hid, h2_t):
    @pl.when(pl.program_id(0) == 0)
    def _():
        @pl.loop(0, 8)
        def _(i):
            cols = pl.ds(pl.multiple_of(i * 256, 256), 256)
            h2_t[cols] = h2[:, cols].T

    @pl.loop(0, GROUP // 256)
    def _(i):
        rows = pl.ds(pl.multiple_of(i * 256, 256), 256)
        pair = mm(h2[rows], wg[...].reshape(WIDTH, 512))
        back = mm_t(g[rows, :TILE], wd[0])
        for c in range(1, 4):
            back += mm_t(g[rows, c * TILE : (c + 1) * TILE], wd[c])
        gate, up = pair[:, :256], pair[:, 256:]
        sig = 1.0 / (1.0 + jnp.exp(-gate))
        silu = gate * sig
        hid[rows] = (silu * up).astype(BF)
        ggu[rows, :256] = (back * up * sig * (1.0 + gate * (1.0 - sig))).astype(BF)
        ggu[rows, 256:] = (back * silu).astype(BF)

    hid_t = hid[...].T

    @pl.loop(0, 4)
    def _(c):
        cols = pl.ds(pl.multiple_of(c * TILE, TILE), TILE)
        up_grad = mm(h2_t[cols], ggu[...]).astype(BF).reshape(DP, 1, 32, 512)
        down_grad = mm(hid_t, g[:, cols]).astype(BF).reshape(DP, 1, 16, 512)
        grads[:, 0, pl.ds(c, 1), :32] = up_grad
        grads[:, 0, pl.ds(c, 1), 32:] = down_grad


def middle_call(h2, g, wg, wd):
    once = pl.Buffered(1)
    wide = pl.BlockSpec((GROUP, WIDTH), lambda u: (0, 0), pipeline_mode=once)
    return pl.pallas_call(
        middle_kernel,
        grid=(3,),
        out_shape=[
            jax.ShapeDtypeStruct((DP, 3, 4, 48, 512), BF),
            jax.ShapeDtypeStruct((GROUP, 2 * UNITS), BF),
            jax.ShapeDtypeStruct((GROUP, UNITS), BF),
        ],
        in_specs=[
            wide,
            wide,
            pl.BlockSpec((4, TILE, 512), lambda u: (0, 0, u)),
            pl.BlockSpec((4, 256, TILE), lambda u: (0, u, 0)),
        ],
        out_specs=[
            pl.BlockSpec((DP, 1, 4, 48, 512), lambda u: (0, u, 0, 0, 0)),
            pl.BlockSpec((GROUP, 512), lambda u: (0, u)),
            pl.BlockSpec((GROUP, 256), lambda u: (0, u)),
        ],
        scratch_shapes=[pltpu.VMEM((WIDTH, GROUP), BF)],
        compiler_params=pltpu.CompilerParams(vmem_limit_bytes=VMEM_LIMIT),
        cost_estimate=pl.CostEstimate(flops=19_000_000_000, bytes_accessed=32_000_000, transcendentals=800_000),
        name="feed_forward",
    )(h2, g, wg, wd)


def dp_place():
    p = lax.axis_index("dp")
    return p // 4, p % 4


def along(axis, o):
    px, py = dp_place()
    return {"dp": (px + o) % 4 * 4 + py} if axis == 0 else {"dp": px * 4 + (py + o) % 4}


def xy_friends():
    return [along(axis, o) for axis in range(2) for o in range(1, 4)]


class Spread:
    def __init__(self, at, send, recv):
        px, py = dp_place()
        here = (px, py)
        self.out, self.into = {}, {}
        for half in range(2):
            for phase in range(2):
                axis = half ^ phase
                for o in range(1, 4):
                    came = [px, py]
                    came[axis] = (here[axis] - o + 4) % 4
                    mine = [px, py]
                    if phase:
                        mine[1 - axis] = came[1 - axis] = None
                    src, dst = at(half, *mine), at(half, *came)
                    sems = (send.at[half, phase, o - 1], recv.at[half, phase, o - 1])
                    self.out[half, phase, o] = remote(src, src, *sems, along(axis, o))
                    self.into[half, phase, o] = remote(dst, dst, *sems, along(axis, o))

    def start(self, phase):
        for half in range(2):
            for o in range(1, 4):
                self.out[half, phase, o].start()

    def wait(self, phase):
        for half in range(2):
            for o in range(1, 4):
                self.into[half, phase, o].wait_recv()

    def drain(self):
        for copy in self.out.values():
            copy.wait_send()


class Collapse:
    def __init__(self, src, got, sums, got2, done, send, recv, own):
        px, py = dp_place()
        here = (px, py)
        self.got, self.sums, self.got2, self.done, self.here = got, sums, got2, done, here
        self.units = src.shape[2]

        def cut(axis, index, half):
            pair = pl.ds(2 * half, 2)
            return src.at[index, :, :, pair] if axis == 0 else src.at[:, index, :, pair]

        self.keep, self.copies = [], {}
        for half in range(2):
            axis = half
            self.keep.append(pltpu.make_async_copy(cut(axis, here[axis], half), sums.at[half], own.at[half]))
            for o in range(1, 4):
                there = (here[axis] + o) % 4
                self.copies[half, 0, o] = remote(
                    cut(axis, there, half), got.at[half, o - 1],
                    send.at[half, 0, o - 1], recv.at[half, 0, o - 1], along(axis, o),
                )
                there = (here[1 - axis] + o) % 4
                self.copies[half, 1, o] = remote(
                    sums.at[half, there], got2.at[half, o - 1],
                    send.at[half, 1, o - 1], recv.at[half, 1, o - 1], along(1 - axis, o),
                )

    def start(self):
        for half in range(2):
            for o in range(1, 4):
                self.copies[half, 0, o].start()
            self.keep[half].start()

    def first(self):
        units = self.units
        for half in range(2):
            self.keep[half].wait()
            for o in range(1, 4):
                self.copies[half, 0, o].wait_recv()

            @pl.loop(0, 4 * units)
            def _(i):
                a, u = i // units, i % units
                for c in range(2):
                    total = self.sums[half, a, u, c].astype(F32)
                    for o in range(3):
                        total += self.got[half, o, a, u, c].astype(F32)
                    self.sums[half, a, u, c] = total.astype(BF)

            for o in range(1, 4):
                self.copies[half, 1, o].start()

    def second(self):
        for half in range(2):
            for o in range(1, 4):
                self.copies[half, 1, o].wait_recv()

            @pl.loop(0, self.units)
            def _(u):
                for c in range(2):
                    total = self.sums[half, self.here[1 - half], u, c].astype(F32)
                    for o in range(3):
                        total += self.got2[half, o, u, c].astype(F32)
                    self.done[2 * half + c, u] = total.astype(BF)

    def drain(self):
        for copy in self.copies.values():
            copy.wait_send()


def collapse_scratch(units):
    dma = pltpu.SemaphoreType.DMA
    return [
        pltpu.VMEM((2, 3, 4, units, 2, 48, 512), BF),
        pltpu.VMEM((2, 4, units, 2, 48, 512), BF),
        pltpu.VMEM((2, 3, units, 2, 48, 512), BF),
        pltpu.VMEM((4, units, 48, 512), BF),
        dma((2, 2, 3)), dma((2, 2, 3)), dma((2,)),
        dma((3,)), dma((4,)), dma((2, 2, 3)), dma((2, 2, 3)),
    ]


class Trade:
    def __init__(self, block, slot, send, recv):
        _, row, col, z, k = place()
        self.col, self.peer = col, on_ring(z, 1 - k)
        self.recv, self.send, self.slot = recv, send, slot
        self.copies = [
            remote(block((col + o) % 4), slot(col), send.at[o - 1], recv.at[o - 1], {"col": (col + o) % 4})
            for o in range(1, 4)
        ]
        self.keep = pltpu.make_async_copy(block(col), slot(col), recv.at[3])

    def start(self):
        for copy in self.copies:
            copy.start()
        self.keep.start()

    def finish(self):
        for o in range(1, 4):
            dst = self.slot((self.col - o + 4) % 4)
            remote(dst, dst, self.send.at[o - 1], self.recv.at[o - 1], self.peer).wait_recv()
        self.keep.wait()

    def drain(self):
        for copy in self.copies:
            copy.wait_send()


def norm_back(grad, value, gain):
    scale = head_norm(value)
    weighted = grad * gain
    inner = jnp.mean(weighted * value, axis=1, keepdims=True)
    return scale * weighted - value * (scale * scale * scale * inner), grad * value * scale


def backward_kernel(
    big, ggu_i, hid_i, g_i, wg_i, wd_i, wo_i, wq_i, h1t_i, raw_i, q_i, k_i, att_i, lse_i, mid_i, gain_i, x_i,
    q_gain, k_gain, start, cosine, sine,
    result_o, stream_o, big_o, small_o, sums_o,
    m, gm, dqkv, small, mid, gain, x_own, g_own, acc, head_acc, tile_f, tile_b, totals, heard,
    ms, mr,
    parts, theirs, psums, near, full, rs_s, rs_r,
    b_got, b_sums, b_got2, b_done, b_s, b_r, b_own, b_ts, b_tr, b_gs, b_gr,
    s_got, s_sums, s_got2, s_done, s_s, s_r, s_own, s_ts, s_tr, s_gs, s_gr,
    fs, fr, ls, lr, as_, ar, in_s, free,
):
    p, row, col, z, k = place()
    px, py = dp_place()
    me = 2 * z + k
    up, down, peer = on_ring((z + 1) % 4, k), on_ring((z + 3) % 4, k), on_ring(z, 1 - k)
    far = on_ring((z + 2) % 4, k)
    meet(ring_friends() + [far] + xy_friends())

    loads = {}

    def load(src, dst):
        i = len(loads)
        copy = pltpu.make_async_copy(src, dst, in_s.at[i])
        copy.start()
        loads[i] = copy
        return copy

    def small_slot(units_ref):
        return units_ref

    big_sum = Collapse(big, b_got, b_sums, b_got2, b_done, b_s, b_r, b_own)
    big_trade = Trade(lambda c: b_done.at[c], lambda c: big_o.at[px, py, c], b_ts, b_tr)

    def big_at(half, x, y):
        xs = slice(None) if x is None else x
        ys = slice(None) if y is None else y
        return big_o.at[xs, ys, pl.ds(2 * half, 2)]

    def small_at(half, x, y):
        xs = slice(None) if x is None else x
        ys = slice(None) if y is None else y
        return small_o.at[xs, ys, pl.ds(2 * half, 2)]

    big_all = Spread(big_at, b_gs, b_gr)
    small_sum = Collapse(small, s_got, s_sums, s_got2, s_done, s_s, s_r, s_own)
    small_trade = Trade(lambda c: s_done.at[c], lambda c: small_o.at[px, py, c], s_ts, s_tr)
    small_all = Spread(small_at, s_gs, s_gr)
    scatter = Scatter(parts, theirs, psums, near, full, rs_s, rs_r)
    stream_trade = Trade(
        lambda c: tile_f.at[:, pl.ds(pl.multiple_of(c * TILE, TILE), TILE)],
        lambda c: stream_o.at[pl.ds(pl.multiple_of(c * OWN, OWN), OWN)], fs, fr,
    )
    result_trade = Trade(
        lambda c: tile_b.at[:, pl.ds(pl.multiple_of(c * TILE, TILE), TILE)],
        lambda c: result_o.at[pl.ds(pl.multiple_of(c * OWN, OWN), OWN)], ls, lr,
    )

    def release():
        scatter.drain()
        for device in (up, down, peer):
            pl.semaphore_signal(free, inc=1, device_id=device, device_id_type=MESH)

    def project(d, product):
        rows = pl.ds(pl.multiple_of((z + d) % 4 * 256, 256), 256)

        @pl.loop(0, 4)
        def _(c):
            cols = pl.ds(pl.multiple_of(c * TILE, TILE), TILE)
            parts[d, :, cols] = product(rows, c, cols).astype(BF)

        scatter.put(d)

    big_sum.start()
    own_rows = pl.ds(pl.multiple_of(me * OWN, OWN), OWN)
    early = [load(mid_i, mid), load(gain_i, gain), load(x_i, x_own), load(g_i.at[own_rows], g_own)]

    def gain_row(which):
        return jnp.concatenate([gain[c, which : which + 1] for c in range(4)], axis=1)

    def stage_one(wg, ggu):
        waits = [load(wg_i, wg), load(ggu_i, ggu)]
        for copy in waits:
            copy.wait()

        def product(rows, c, cols):
            return mm_t(ggu[rows], wg[c])

        project(2, product)
        project(1, product)
        scatter.across()
        project(3, product)
        project(0, product)

    pl.run_scoped(stage_one, pltpu.VMEM((4, TILE, 2 * UNITS), BF), pltpu.VMEM((GROUP, 2 * UNITS), BF))

    def stage_two(wo, att, qs, ks, raw, lse, ga, dk, dv, h1t, wq, att_t):
        l_wo, l_att = load(wo_i, wo), load(att_i, att)
        l_heads = [load(q_i, qs), load(k_i, ks), load(raw_i, raw), load(lse_i, lse)]
        l_last = [load(h1t_i, h1t), load(wq_i, wq)]
        scatter.beside(0)
        scatter.beside(1)
        for copy in early:
            copy.wait()
        acc[...] = jnp.zeros_like(acc)
        head_acc[...] = jnp.zeros_like(head_acc)
        dk[...] = jnp.zeros_like(dk)
        dv[...] = jnp.zeros_like(dv)
        totals[0] = jnp.zeros((8, WIDTH), F32)
        gain_two = gain_row(1)
        scatter.arrive()

        @pl.loop(0, OWN // 16)
        def _(i):
            rows = pl.ds(pl.multiple_of(i * 16, 16), 16)
            back, gained = norm_back(scatter.total(pl.multiple_of(i * 16, 16), 16), mid[rows], gain_two)
            acc[1] += gained
            back = back + g_own[rows].astype(F32)
            gm[rows] = back
            m[pl.ds(pl.multiple_of(me * OWN + i * 16, 16), 16)] = back.astype(BF)

        m_gather = Gather(rows_at(m), ms, mr)
        m_gather.start()
        release()
        l_att.wait()
        for h in range(2):
            att_t[h * HEAD : (h + 1) * HEAD] = att[h].T
        m_gather.forward()
        l_wo.wait()
        for copy in l_heads:
            copy.wait()
        m_gather.share()
        m_gather.finish()

        @pl.loop(0, 4)
        def _(i):
            rows = pl.ds(pl.multiple_of(i * 256, 256), 256)
            back = mm_t(m[rows, :TILE], wo[0])
            for c in range(1, 4):
                back += mm_t(m[rows, c * TILE : (c + 1) * TILE], wo[c])
            for h in range(2):
                ga[h, rows] = back[:, h * HEAD : (h + 1) * HEAD].astype(BF)

        @pl.loop(0, 4)
        def _(c):
            cols = pl.ds(pl.multiple_of(c * TILE, TILE), TILE)
            grad = mm(att_t[...], m[:, cols]).astype(BF)
            small[:, :, 0, pl.ds(c, 1), 32:] = grad.reshape(4, 4, 1, 16, TILE)

        for block in range(GROUP // QROWS):
            first, keys = block * QROWS, (block + 1) * QROWS
            rows = pl.ds(first, QROWS)
            allowed = allowed_keys(start[rows], first, keys)

            @pl.loop(0, 2)
            def _(h):
                cols = pl.ds(pl.multiple_of(h * HEAD, HEAD), HEAD)
                score = mm_t(qs[h, rows], ks[:keys]) * (SCALE * LOG2)
                prob = jnp.exp2(jnp.where(allowed, score, -1e30) - lse[h, rows, :1])
                grad = ga[h, rows]
                delta = jnp.sum(grad.astype(F32) * att[h, rows].astype(F32), axis=1, keepdims=True)
                prob_grad = mm_t(grad, raw[:keys, 3 * HEAD :])
                score_grad = (prob * (prob_grad - delta)).astype(BF)
                dk[:keys] += t_mm(score_grad, qs[h, rows])
                dv[:keys] += t_mm(prob.astype(BF), grad)
                back = turn_back(mm(score_grad, ks[:keys]) * SCALE, cosine[rows], sine[rows])
                back, gained = norm_back(back, raw[rows, cols].astype(F32), q_gain[...])
                dqkv[rows, cols] = back.astype(BF)
                head_acc[0:1] += jnp.sum(gained, axis=0, keepdims=True)

        @pl.loop(0, 4)
        def _(i):
            rows = pl.ds(pl.multiple_of(i * 256, 256), 256)
            back = turn_back(dk[rows] * SCALE, cosine[rows], sine[rows])
            back, gained = norm_back(back, raw[rows, 2 * HEAD : 3 * HEAD].astype(F32), k_gain[...])
            dqkv[rows, 2 * HEAD : 3 * HEAD] = back.astype(BF)
            dqkv[rows, 3 * HEAD :] = dv[rows].astype(BF)
            head_acc[1:2] += jnp.sum(gained, axis=0, keepdims=True)

        big_sum.first()
        for copy in l_last:
            copy.wait()
        pl.semaphore_wait(free, 3)

        def product(rows, c, cols):
            return mm_t(dqkv[rows], wq[c])

        project(2, product)
        project(1, product)

        @pl.loop(0, 4)
        def _(c):
            cols = pl.ds(pl.multiple_of(c * TILE, TILE), TILE)
            small[:, :, 0, pl.ds(c, 1), :32] = mm(h1t[cols], dqkv[...]).astype(BF).reshape(4, 4, 1, 32, 512)

        small_sum.start()
        scatter.across()
        project(3, product)
        project(0, product)
        m_gather.drain()

    pl.run_scoped(
        stage_two,
        pltpu.VMEM((4, 256, TILE), BF), pltpu.VMEM((2, GROUP, HEAD), BF), pltpu.VMEM((2, GROUP, HEAD), BF),
        pltpu.VMEM((GROUP, HEAD), BF), pltpu.VMEM((GROUP, 512), BF), pltpu.VMEM((2, GROUP, HEAD), F32),
        pltpu.VMEM((2, GROUP, HEAD), BF), pltpu.VMEM((GROUP, HEAD), F32), pltpu.VMEM((GROUP, HEAD), F32),
        pltpu.VMEM((WIDTH, GROUP), BF), pltpu.VMEM((4, TILE, 512), BF), pltpu.VMEM((2 * HEAD, GROUP), BF),
    )

    def stage_three(hid, wd):
        waits = [load(hid_i, hid), load(wd_i, wd)]
        big_sum.second()
        big_trade.start()
        scatter.beside(0)
        scatter.beside(1)
        small_sum.first()
        big_trade.finish()
        big_all.start(0)
        gain_one = gain_row(0)
        scatter.arrive()

        @pl.loop(0, OWN // 16)
        def _(i):
            rows = pl.ds(pl.multiple_of(i * 16, 16), 16)
            back, gained = norm_back(
                scatter.total(pl.multiple_of(i * 16, 16), 16), x_own[rows].astype(F32), gain_one
            )
            acc[0] += gained
            tile_f[rows] = gm[rows] + back

        stream_trade.start()
        release()
        totals[0, 0:1] = jnp.sum(acc[0], axis=0, keepdims=True)
        totals[0, 1:2] = jnp.sum(acc[1], axis=0, keepdims=True)
        totals[0, 2:3, 0:HEAD] = head_acc[0:1]
        totals[0, 2:3, HEAD : 2 * HEAD] = head_acc[1:2]
        sent = []

        def tell(phase, devices, slots):
            for device, slot in zip(devices, slots):
                copy = remote(totals.at[phase], heard.at[slot], as_.at[slot], ar.at[slot], device)
                copy.start()
                sent.append(copy)

        def listen(phase, slots):
            total = totals[phase]
            for slot in slots:
                remote(heard.at[slot], heard.at[slot], as_.at[slot], ar.at[slot], peer).wait_recv()
                total += heard[slot]
            totals[phase + 1] = total

        tell(0, [peer], [0])
        big_all.wait(0)
        big_all.start(1)
        small_sum.second()
        small_trade.start()
        listen(0, [0])
        tell(1, [up, down, far], [1, 2, 3])
        for copy in waits:
            copy.wait()
        pl.semaphore_wait(free, 3)

        def product(rows, c, cols):
            return mm(hid[rows], wd[c])

        project(2, product)
        project(1, product)
        small_trade.finish()
        small_all.start(0)
        scatter.across()
        project(3, product)
        project(0, product)
        listen(1, [1, 2, 3])
        tell(2, [along(0, o) for o in range(1, 4)], [4, 5, 6])
        scatter.beside(0)
        scatter.beside(1)
        small_all.wait(0)
        small_all.start(1)
        scatter.arrive()

        @pl.loop(0, OWN // 16)
        def _(i):
            rows = pl.ds(pl.multiple_of(i * 16, 16), 16)
            tile_b[rows] = (mid[rows] + scatter.total(pl.multiple_of(i * 16, 16), 16)).astype(BF)

        result_trade.start()
        listen(2, [4, 5, 6])
        tell(3, [along(1, o) for o in range(1, 4)], [7, 8, 9])
        stream_trade.finish()
        listen(3, [7, 8, 9])
        sums_o[...] = totals[4]
        result_trade.finish()
        big_all.wait(1)
        small_all.wait(1)
        scatter.drain()
        for thing in (big_sum, big_trade, big_all, small_sum, small_trade, small_all, stream_trade, result_trade):
            thing.drain()
        for copy in sent:
            copy.wait_send()

    pl.run_scoped(stage_three, pltpu.VMEM((GROUP, UNITS), BF), pltpu.VMEM((4, UNITS, TILE), BF))


def backward_call(*args):
    hbm = pl.BlockSpec(memory_space=pl.ANY)
    vmem = pl.BlockSpec(memory_space=pltpu.VMEM)
    dma = pltpu.SemaphoreType.DMA
    out = jax.ShapeDtypeStruct
    return pl.pallas_call(
        backward_kernel,
        out_shape=[
            out((TILE, TILE), BF), out((TILE, TILE), F32), out((4, 4, 4, 3, 48, 512), BF),
            out((4, 4, 4, 1, 48, 512), BF), out((8, WIDTH), F32),
        ],
        in_specs=[hbm] * 17 + [vmem] * 5,
        out_specs=[hbm] * 4 + [vmem],
        scratch_shapes=[
            pltpu.VMEM((GROUP, WIDTH), BF), pltpu.VMEM((OWN, WIDTH), F32), pltpu.VMEM((GROUP, 512), BF),
            pltpu.VMEM((4, 4, 1, 4, 48, 512), BF), pltpu.VMEM((OWN, WIDTH), F32), pltpu.VMEM((4, 8, TILE), F32),
            pltpu.VMEM((OWN, WIDTH), BF), pltpu.VMEM((OWN, WIDTH), BF), pltpu.VMEM((2, 16, WIDTH), F32),
            pltpu.VMEM((8, HEAD), F32), pltpu.VMEM((OWN, WIDTH), F32), pltpu.VMEM((OWN, WIDTH), BF),
            pltpu.VMEM((5, 8, WIDTH), F32), pltpu.VMEM((10, 8, WIDTH), F32),
        ]
        + GATHER_SEMS
        + scatter_scratch()
        + collapse_scratch(3)
        + collapse_scratch(1)
        + [dma((3,)), dma((4,)), dma((3,)), dma((4,)), dma((10,)), dma((10,)), dma((20,)), pltpu.SemaphoreType.REGULAR],
        compiler_params=pltpu.CompilerParams(
            collective_id=2, has_side_effects=True, vmem_limit_bytes=63 * 1024 * 1024
        ),
        cost_estimate=pl.CostEstimate(flops=15_000_000_000, bytes_accessed=100_000_000, transcendentals=2_000_000),
        name="backward",
    )(*args)


def place_big_kernel(grads, gate_up, down):
    value = grads[:, 0, 0, :32].reshape(TILE, 512).astype(F32)
    for g in range(2):
        gate_up[:, g, :] = value[:, g * 256 : (g + 1) * 256]
    down[...] = grads[:, 0, 0, 32:].reshape(256, TILE).astype(F32)


def place_big(grads):
    return pl.pallas_call(
        place_big_kernel,
        grid=(4, 3),
        in_specs=[pl.BlockSpec((DP, 1, 1, 48, 512), lambda c, u: (0, c, u, 0, 0))],
        out_specs=[
            pl.BlockSpec((TILE, 2, 256), lambda c, u: (0, 0, c * 3 + u)),
            pl.BlockSpec((256, TILE), lambda c, u: (c * 3 + u, 0)),
        ],
        out_shape=[
            jax.ShapeDtypeStruct((TILE, 2, 4 * UNITS), F32),
            jax.ShapeDtypeStruct((4 * UNITS, TILE), F32),
        ],
        compiler_params=pltpu.CompilerParams(vmem_limit_bytes=40 * 1024 * 1024),
        cost_estimate=pl.CostEstimate(flops=0, bytes_accessed=29_000_000, transcendentals=0),
        name="place_big",
    )(grads)


def place_small_kernel(grads, qkv, out):
    for c in range(4):
        qkv[:, c, :] = grads[:, c, :32].reshape(128, 512).astype(F32)
        out[c] = grads[:, c, 32:].reshape(64, TILE).astype(F32)


def place_small(grads):
    return pl.pallas_call(
        place_small_kernel,
        grid=(4,),
        in_specs=[pl.BlockSpec((4, 4, 48, 512), lambda i: (i, 0, 0, 0))],
        out_specs=[
            pl.BlockSpec((128, 4, 512), lambda i: (i, 0, 0)),
            pl.BlockSpec((4, 64, TILE), lambda i: (0, i, 0)),
        ],
        out_shape=[
            jax.ShapeDtypeStruct((TILE, 4, 512), F32),
            jax.ShapeDtypeStruct((4, 256, TILE), F32),
        ],
        compiler_params=pltpu.CompilerParams(vmem_limit_bytes=40 * 1024 * 1024),
        cost_estimate=pl.CostEstimate(flops=0, bytes_accessed=9_000_000, transcendentals=0),
        name="place_small",
    )(grads)


def starts_of(seq_lengths, seq_group, seq_start, group_index):
    slots = jnp.arange(GROUP, dtype=jnp.int32)
    inside = (
        (seq_group[None, :] == group_index)
        & (seq_start[None, :] <= slots[:, None])
        & (slots[:, None] < (seq_start + seq_lengths)[None, :])
    )
    return (jnp.sum(jnp.where(inside, seq_start[None, :], 0), axis=1), slots)


def angles(position):
    half = HEAD // 2
    freq = THETA ** (-(jnp.arange(half, dtype=F32) * 2.0 / HEAD))
    angle = position.astype(F32)[:, None] * freq[None, :]
    return (jnp.cos(angle), jnp.sin(angle))


def body(
    tokens, norm1_gain, w_qkv, q_gain, k_gain, w_out, norm2_gain, w_gate_up, w_down, out_grad,
    seq_lengths, seq_group, seq_start,
):
    me = lax.axis_index("row") * 4 + lax.axis_index("col")
    p = lax.axis_index("dp")
    lo = lax.axis_index("col") // 2
    start, slots = starts_of(seq_lengths, seq_group, seq_start, p)
    cosine, sine = angles(slots - start)
    cos_wide = jnp.concatenate([cosine, cosine], axis=1)
    sin_wide = jnp.concatenate([-sine, sine], axis=1)
    gains = jnp.concatenate([norm1_gain[None], norm2_gain[None], jnp.zeros((6, TILE), F32)])

    def pair(weight, index, cut):
        return lax.dynamic_index_in_dim(weight, index, cut, keepdims=False)

    wq5 = w_qkv.reshape(TILE, 2, 2, 512)
    wq_pair = pair(wq5, lo, 1).transpose(1, 0, 2)
    wq_part = pair(lax.dynamic_slice_in_dim(wq5, p * 32, 32, 0), 1 - lo, 1).transpose(1, 0, 2)
    wg7 = w_gate_up.reshape(TILE, 2, 2, 2, 3, 256)

    def order(block):
        return block.transpose(2, 0, 3, 1, 4).reshape(2, -1, 2 * UNITS)

    wg_pair = order(pair(wg7, lo, 2))
    wg_part = order(pair(lax.dynamic_slice_in_dim(wg7, p * 32, 32, 0), 1 - lo, 2))

    (h2, g, wq, wo, wg, wd, h1t, raw, qs, ks, att, lse, middle, gain, x_own) = forward_call(
        tokens, out_grad, gains, q_gain[None], k_gain[None], start[:, None], cos_wide, sin_wide,
        wq_pair, wq_part, wg_pair, wg_part, w_out, w_down,
    )
    big, ggu, hid = middle_call(h2, g, wg, wd)
    result, stream_grad, big, small, totals = backward_call(
        big.reshape(4, 4, 3, 4, 48, 512), ggu, hid, g, wg, wd, wo, wq, h1t, raw, qs, ks, att, lse, middle, gain,
        x_own, q_gain[None], k_gain[None], start[:, None], cos_wide, sin_wide,
    )
    g_gate_up, g_down = place_big(big.reshape(DP, 4, 3, 48, 512))
    g_qkv, g_out = place_small(small.reshape(DP, 4, 48, 512))
    return (
        result,
        stream_grad,
        totals[0],
        g_qkv,
        totals[2, :HEAD],
        totals[2, HEAD : 2 * HEAD],
        g_out.reshape(w_out.shape),
        totals[1],
        g_gate_up,
        g_down,
    )


def solution(mesh):
    in_specs = (
        P(("dp", "row"), "col"),
        P("col"),
        P("col", "row", None),
        P(),
        P(),
        P("row", "col"),
        P("col"),
        P("col", None, "row"),
        P("row", "col"),
        P(("dp", "row"), "col"),
        P(),
        P(),
        P(),
    )
    out_specs = (
        P(("dp", "row"), "col"),
        P(("dp", "row"), "col"),
        P(),
        P("col", "row", None),
        P(),
        P(),
        P("row", "col"),
        P(),
        P("col", None, "row"),
        P("row", "col"),
    )
    return jax.shard_map(body, mesh=mesh, in_specs=in_specs, out_specs=out_specs, check_vma=False)
```

```python
import math

import jax
import jax.numpy as jnp
import numpy as np
from jax import lax
from jax.experimental import pallas as pl
from jax.experimental.pallas import tpu as pltpu
from jax.sharding import PartitionSpec as P

EPS = 1e-06
THETA = 1000000.0
BF = jnp.bfloat16
F32 = jnp.float32
Z = ("row", "col")
MESH = pl.DeviceIdType.MESH
VMEM_LIMIT = 63 * 1024 * 1024

GROUP, WIDTH, TILE, UNITS, HEAD = 1024, 2048, 512, 768, 128
OWN = GROUP // 8
DP = 16


def dot(left, right, dims):
    return lax.dot_general(left, right, (dims, ((), ())), preferred_element_type=F32)


def mm(left, right):
    return dot(left, right, ((1,), (0,)))


def mm_t(left, right):
    return dot(left, right, ((1,), (1,)))


def t_mm(left, right):
    return dot(left, right, ((0,), (0,)))


def place():
    row, col = lax.axis_index("row"), lax.axis_index("col")
    j = 4 * row + col
    return lax.axis_index("dp"), row, col, j // 2, j % 2


def on_ring(z, k):
    j = 2 * z + k
    return {"row": j // 4, "col": j % 4}


def remote(src, dst, send, recv, device):
    return pltpu.make_async_remote_copy(
        src_ref=src, dst_ref=dst, send_sem=send, recv_sem=recv, device_id=device, device_id_type=MESH
    )


def meet(devices):
    barrier = pltpu.get_barrier_semaphore()
    for device in devices:
        pl.semaphore_signal(barrier, inc=1, device_id=device, device_id_type=MESH)
    pl.semaphore_wait(barrier, len(devices))


def ring_friends():
    _, _, _, z, k = place()
    other = z + 1 - 2 * (z % 2)
    return [
        on_ring((z + 1) % 4, k),
        on_ring((z + 3) % 4, k),
        on_ring(z, 1 - k),
        on_ring(other, 1 - k),
    ]


def dp_place():
    p = lax.axis_index("dp")
    return p // 4, p % 4


def along(axis, o):
    px, py = dp_place()
    return {"dp": (px + o) % 4 * 4 + py} if axis == 0 else {"dp": px * 4 + (py + o) % 4}


def xy_friends():
    return [along(axis, o) for axis in range(2) for o in range(1, 4)]


def tile_at(buf):
    def loc(j, half=None):
        row, col = j // 4, j % 4
        first = pl.multiple_of(row * TILE, TILE)
        rows = pl.ds(first, TILE)
        if half is not None:
            rows = pl.ds(first + half * (TILE // 2), TILE // 2)
        return buf.at[rows, pl.ds(pl.multiple_of(col * TILE, TILE), TILE)]

    return loc


def rows_at(buf):
    def loc(j, half=None):
        first = pl.multiple_of(j * OWN, OWN)
        rows = pl.ds(first, OWN)
        if half is not None:
            rows = pl.ds(first + half * (OWN // 2), OWN // 2)
        return buf.at[rows]

    return loc


class Gather:
    def __init__(self, loc, send, recv, own=None):
        _, _, _, z, k = place()
        up, down, far = (z + 1) % 4, (z + 3) % 4, (z + 2) % 4
        to_up, to_down, peer = on_ring(up, k), on_ring(down, k), on_ring(z, 1 - k)

        def out(slot, src, dst, device):
            return remote(src, dst, send.at[slot], recv.at[slot], device)

        def into(slot, dst):
            return remote(dst, dst, send.at[slot], recv.at[slot], peer)

        mine = loc(2 * z + k)
        own = mine if own is None else own
        left, right, across = 2 * down + k, 2 * up + k, 2 * far + k
        self.first = [out(0, own, mine, to_up), out(1, own, mine, to_down), out(4, own, mine, peer)]
        self.from_left = [
            out(2, loc(left, 0), loc(left, 0), to_up),
            out(5, loc(left), loc(left), peer),
        ]
        self.from_right = [
            out(3, loc(right, 1), loc(right, 1), to_down),
            out(6, loc(right), loc(right), peer),
        ]
        self.from_far = [
            out(7, loc(across, 0), loc(across, 0), peer),
            out(8, loc(across, 1), loc(across, 1), peer),
        ]
        theirs = [2 * z + 1 - k, 2 * down + 1 - k, 2 * up + 1 - k, 2 * far + 1 - k]
        self.arrivals = {
            0: into(0, loc(left)),
            1: into(1, loc(right)),
            2: into(2, loc(across, 0)),
            3: into(3, loc(across, 1)),
            4: into(4, loc(theirs[0])),
            5: into(5, loc(theirs[1])),
            6: into(6, loc(theirs[2])),
            7: into(7, loc(theirs[3], 0)),
            8: into(8, loc(theirs[3], 1)),
        }

    def start(self):
        for copy in self.first:
            copy.start()

    def forward(self):
        self.arrivals[0].wait_recv()
        for copy in self.from_left:
            copy.start()
        self.arrivals[1].wait_recv()
        for copy in self.from_right:
            copy.start()

    def share(self):
        for half in range(2):
            self.arrivals[2 + half].wait_recv()
            self.from_far[half].start()

    def finish(self):
        for slot in range(4, 9):
            self.arrivals[slot].wait_recv()

    def drain(self):
        for copy in self.first + self.from_left + self.from_right + self.from_far:
            copy.wait_send()


GATHER_SEMS = [pltpu.SemaphoreType.DMA((9,)), pltpu.SemaphoreType.DMA((9,))]


class Spread:
    def __init__(self, at, send, recv, which=()):
        px, py = dp_place()
        here = (px, py)
        self.out, self.into = {}, {}
        for half in range(2):
            for phase in range(2):
                axis = half ^ phase

                def block(o, part=None):
                    whose = [px, py]
                    whose[axis] = (here[axis] + o) % 4
                    if phase:
                        whose[1 - axis] = None
                    return at(half, *whose, part)

                def copy(slot, ref, o):
                    index = (*which, half, phase, slot)
                    sems = (send.at[index], recv.at[index])
                    return remote(ref, ref, *sems, along(axis, o))

                self.out[half, phase] = [
                    copy(0, block(0), 1), copy(1, block(0), 3),
                    copy(2, block(3, 0), 1), copy(3, block(1, 1), 3),
                ]
                self.into[half, phase] = [
                    copy(0, block(3), 1), copy(1, block(1), 3),
                    copy(2, block(2, 0), 1), copy(3, block(2, 1), 3),
                ]

    def start(self, phase):
        for half in range(2):
            for slot in range(2):
                self.out[half, phase][slot].start()

    def pass_on(self, phase):
        for half in range(2):
            for slot in range(2):
                self.into[half, phase][slot].wait_recv()
                self.out[half, phase][2 + slot].start()

    def wait(self, phase):
        for half in range(2):
            for slot in range(2, 4):
                self.into[half, phase][slot].wait_recv()

    def drain(self):
        for copies in self.out.values():
            for copy in copies:
                copy.wait_send()


SPREAD_SEMS = [pltpu.SemaphoreType.DMA((2, 2, 4)), pltpu.SemaphoreType.DMA((2, 2, 4))]


class Scatter:
    def __init__(self, parts, theirs, sums, near, full, send, recv):
        _, _, _, z, k = place()
        self.parts, self.theirs, self.sums, self.near, self.full = parts, theirs, sums, near, full
        self.k = k
        to_up, to_down = on_ring((z + 1) % 4, k), on_ring((z + 3) % 4, k)
        peer = on_ring(z, 1 - k)
        half = OWN // 2
        other = pl.ds(pl.multiple_of((1 - k) * OWN, OWN), OWN)

        def copy(slot, src, dst, device):
            return remote(src, dst, send.at[slot], recv.at[slot], device)

        self.copies = [copy(d, parts.at[d, other], theirs.at[d], peer) for d in range(4)] + [
            copy(4, sums.at[0, pl.ds(0, half)], near.at[0], to_up),
            copy(5, sums.at[0, pl.ds(half, half)], near.at[1], to_down),
            copy(6, sums.at[1], full.at[0], to_up),
            copy(7, sums.at[2], full.at[1], to_down),
        ]

    def put(self, d):
        self.copies[d].start()

    def own(self, d, rows, count):
        first = pl.multiple_of(self.k * OWN + rows, count)
        return self.parts[d, pl.ds(first, count)].astype(F32) + self.theirs[
            d, pl.ds(rows, count)
        ].astype(F32)

    def across(self):
        self.copies[2].wait_recv()

        @pl.loop(0, OWN // 16)
        def _(i):
            rows = pl.multiple_of(i * 16, 16)
            self.sums[0, pl.ds(rows, 16)] = self.own(2, rows, 16).astype(BF)

        self.copies[4].start()
        self.copies[5].start()

    def beside(self, side):
        d, half = (1, 3)[side], OWN // 2
        self.copies[d].wait_recv()
        self.copies[4 + side].wait_recv()

        @pl.loop(0, half // 16)
        def _(i):
            rows = pl.multiple_of(i * 16, 16)
            here = pl.multiple_of(rows + side * half, 16)
            there = pl.multiple_of(rows + (1 - side) * half, 16)
            added = self.own(d, here, 16) + self.near[side, pl.ds(rows, 16)].astype(F32)
            self.sums[1 + side, pl.ds(here, 16)] = added.astype(BF)
            self.sums[1 + side, pl.ds(there, 16)] = self.own(d, there, 16).astype(BF)

        self.copies[6 + side].start()

    def arrive(self):
        self.copies[0].wait_recv()
        self.copies[6].wait_recv()
        self.copies[7].wait_recv()

    def total(self, rows, count):
        return (
            self.own(0, rows, count)
            + self.full[0, pl.ds(rows, count)].astype(F32)
            + self.full[1, pl.ds(rows, count)].astype(F32)
        )

    def drain(self):
        for copy in self.copies:
            copy.wait_send()


def scatter_scratch():
    return [
        pltpu.VMEM((4, 2 * OWN, WIDTH), BF),
        pltpu.VMEM((4, OWN, WIDTH), BF),
        pltpu.VMEM((3, OWN, WIDTH), BF),
        pltpu.VMEM((2, OWN // 2, WIDTH), BF),
        pltpu.VMEM((2, OWN, WIDTH), BF),
        pltpu.SemaphoreType.DMA((8,)),
        pltpu.SemaphoreType.DMA((8,)),
    ]


def head_norm(value):
    return lax.rsqrt(jnp.mean(value * value, axis=1, keepdims=True) + EPS)


def turn(value, cosine, sine):
    return value * cosine + pltpu.roll(value, HEAD // 2, 1) * sine


def turn_back(value, cosine, sine):
    return value * cosine - pltpu.roll(value, HEAD // 2, 1) * sine


LOG2 = math.log2(math.e)
SCALE = 1.0 / math.sqrt(HEAD)
QROWS = 256


def allowed_keys(start, first, keys):
    slots = lax.broadcasted_iota(jnp.int32, (QROWS, keys), 1)
    query = lax.broadcasted_iota(jnp.int32, (QROWS, keys), 0) + first
    return (slots >= start) & (slots <= query)


FREQ = np.tile(THETA ** (-(np.arange(HEAD // 2) * 2.0 / HEAD)), 2)[None].astype(np.float32)


def forward_kernel(
    tok, og, norm1, norm2, q_gain, k_gain, freq, lengths, groups, starts, w_qkv, w_gu, w_out, w_down,
    h2_o, g_o, wq_o, wo_o, wg_o, wd_o, h1t_o, raw_o, q_o, k_o, att_o, lse_o, mid_o, gain_o, x_o, start_o, cos_o, sin_o,
    x, h1, h1t, h2, g, wq, wo, raw, qs, ks, att, lse, mid, gain, gains, start, cosine, sine,
    q_raw, q_cut, q_raw_part, q_part, g_raw, g_cut, g_raw_part, g_part,
    xs, xr, gs, gr, hs, hr,
    parts, theirs, sums, near, full, rs_s, rs_r,
    zs, zr, ps, pr, ns, nr, loc_s, out_s, raw_s,
    y0s, y0r, y1s, y1r, y2s, y2r, y3s, y3r,
):
    p, row, col, z, k = place()
    px, py = dp_place()
    me = 2 * z + k
    lo = z % 2
    other = z + 1 - 2 * lo
    peer = on_ring(z, 1 - k)
    piece_rows = pl.ds(pl.multiple_of(p * 32, 32), 32)

    def lanes(first, count):
        return pl.ds(pl.multiple_of(first, 256), count)

    raws = [
        pltpu.make_async_copy(src, dst, raw_s.at[i])
        for i, (src, dst) in enumerate(
            [
                (w_qkv.at[piece_rows], q_raw_part),
                (w_gu.at[piece_rows, :, lanes((1 - lo) * 2 * UNITS, 2 * UNITS)], g_raw_part),
                (w_qkv, q_raw),
                (w_gu.at[:, :, lanes(lo * 2 * UNITS, 2 * UNITS)], g_raw),
            ]
        )
    ]
    for copy in raws:
        copy.start()
    gains[0:1] = norm1[...]
    gains[1:2] = norm2[...]
    raws[0].wait()
    for kk in range(2):
        q_part[kk] = jnp.where(lo == 0, q_raw_part[:, 2 + kk, :], q_raw_part[:, kk, :])
    meet(ring_friends() + xy_friends())

    gain[col] = gains[...]
    gain_copies = [
        remote(gains, gain.at[col], ns.at[i], nr.at[col], device)
        for i, device in enumerate([peer, on_ring(other, k), on_ring(other, 1 - k)])
    ]
    weights = [wq, wo, wg_o, wd_o]
    sources = [q_part, w_out, g_part, w_down]
    blocks = [q_cut, w_out, g_cut, w_down]

    def crossing(a, kk):
        target = 2 * (1 - lo) + kk
        src = sources[a].at[kk] if a % 2 == 0 else w_out.at[target, px, py] if a == 1 else w_down.at[target, px, py]
        return remote(src, weights[a].at[col, px, py], zs.at[a, kk], zr.at[a, k], on_ring(other, kk))

    def crossed(a, kk):
        dst = weights[a].at[2 * (1 - lo) + kk, px, py]
        return remote(dst, dst, zs.at[a, kk], zr.at[a, kk], peer)

    def beside(a):
        there = 2 * lo + 1 - k
        src, dst = (blocks[a].at[k], blocks[a].at[1 - k]) if a % 2 == 0 else (blocks[a].at[col], blocks[a].at[there])
        keep = pltpu.make_async_copy(src, weights[a].at[col], loc_s.at[a])
        give = remote(dst, weights[a].at[col], ps.at[a], pr.at[a], peer)
        take = remote(weights[a].at[there], weights[a].at[there], ps.at[a], pr.at[a], peer)
        return keep, give, take

    def spread_at(a):
        weight = weights[a]
        half_lanes = weight.shape[-1] // 2

        def at(half, xx, yy, part):
            xs_ = slice(None) if xx is None else xx
            ys_ = slice(None) if yy is None else yy
            cols = slice(None) if part is None else pl.ds(part * half_lanes, half_lanes)
            return weight.at[2 * (1 - lo) + half, xs_, ys_, :, cols]

        return at

    spreads = [
        Spread(spread_at(a), send, recv)
        for a, (send, recv) in enumerate([(y0s, y0r), (y1s, y1r), (y2s, y2r), (y3s, y3r)])
    ]

    for a in (0, 1):
        for kk in range(2):
            crossing(a, kk).start()
    x_gather = Gather(tile_at(x), xs, xr, tok)
    x_gather.start()
    for copy in gain_copies:
        copy.start()
    keep_x = pltpu.make_async_copy(tok, tile_at(x)(me), loc_s.at[4])
    keep_x.start()
    keep_g = pltpu.make_async_copy(og, tile_at(g)(me), loc_s.at[5])
    keep_g.start()
    raws[2].wait()

    @pl.loop(0, 16)
    def _(i):
        rows = pl.ds(pl.multiple_of(i * 32, 32), 32)
        for kk in range(2):
            q_cut[kk, i // 4, i % 4] = jnp.where(lo == 0, q_raw[rows, kk, :], q_raw[rows, 2 + kk, :])

    for a in (0, 1):
        beside(a)[0].start()
        beside(a)[1].start()
    for a in (0, 1):
        for kk in range(2):
            crossed(a, kk).wait_recv()
        spreads[a].start(0)
    for a in (1, 3):
        raws[a].wait()
    slot = (
        lax.broadcasted_iota(jnp.int32, (8, HEAD), 0) * HEAD + lax.broadcasted_iota(jnp.int32, (8, HEAD), 1)
    ).astype(F32)

    def one_sequence(i, begun):
        first = starts[i].astype(F32)
        last = first + jnp.where(groups[i] == p, lengths[i], 0).astype(F32)
        return jnp.where((slot >= first) & (slot < last), first, begun)

    begun = lax.fori_loop(0, lengths.shape[0], one_sequence, jnp.zeros((8, HEAD), F32))
    for i in range(8):
        rows = slice(i * HEAD, (i + 1) * HEAD)
        begin = jnp.broadcast_to(begun[i : i + 1], (HEAD, HEAD)).T
        there = lax.broadcasted_iota(jnp.int32, (HEAD, HEAD), 0).astype(F32) + float(i * HEAD)
        angle = (there - begin) * freq[...]
        start[rows] = begin.astype(jnp.int32)
        cosine[rows] = jnp.cos(angle)
        lane = lax.broadcasted_iota(jnp.int32, (HEAD, HEAD), 1)
        sine[rows] = jnp.where(lane < HEAD // 2, -1.0, 1.0) * jnp.sin(angle)
    for a in (0, 1):
        spreads[a].pass_on(0)
    for u in range(3):
        for half in range(2):
            into = slice(u * 512 + half * 256, u * 512 + half * 256 + 256)
            for kk in range(2):
                cols = slice(kk * UNITS + u * 256, kk * UNITS + u * 256 + 256)
                g_part[kk, :, into] = g_raw_part[:, half, cols]
    for a in (0, 1):
        spreads[a].wait(0)
        spreads[a].start(1)
    x_gather.forward()

    @pl.loop(0, 16)
    def _(i):
        rows = pl.ds(pl.multiple_of(i * 32, 32), 32)
        for u in range(3):
            for half in range(2):
                into = slice(u * 512 + half * 256, u * 512 + half * 256 + 256)
                for kk in range(2):
                    cols = slice(kk * UNITS + u * 256, kk * UNITS + u * 256 + 256)
                    g_cut[kk, i // 4, i % 4, :, into] = g_raw[rows, half, cols]

    for a in (0, 1):
        spreads[a].pass_on(1)
    x_gather.share()
    for a in (2, 3):
        for kk in range(2):
            crossing(a, kk).start()
    for a in (2, 3):
        beside(a)[0].start()
        beside(a)[1].start()
    for c in range(4):

        @pl.when(c != col)
        def _():
            remote(gain.at[c], gain.at[c], ns.at[0], nr.at[c], peer).wait_recv()

    keep_x.wait()
    x_gather.finish()
    g_gather = Gather(tile_at(g), gs, gr, og)
    g_gather.start()

    def gain_row(which):
        return jnp.concatenate([gain[c, which : which + 1] for c in range(4)], axis=1)

    gain_one = gain_row(0)

    @pl.loop(0, GROUP // 64)
    def _(i):
        rows = pl.ds(pl.multiple_of(i * 64, 64), 64)
        value = x[rows].astype(F32)
        h1[rows] = (value * head_norm(value) * gain_one).astype(BF)

    for a in (2, 3):
        for kk in range(2):
            crossed(a, kk).wait_recv()
        spreads[a].start(0)
    for a in range(2):
        keep, _, take = beside(a)
        keep.wait()
        take.wait_recv()
        spreads[a].wait(1)

    @pl.loop(0, GROUP // 256)
    def _(i):
        rows = pl.ds(pl.multiple_of(i * 256, 256), 256)
        mixed = mm(h1[rows], wq[...].reshape(WIDTH, 4 * HEAD)).astype(BF)
        raw[rows] = mixed
        cos_rows, sin_rows = cosine[rows], sine[rows]
        for piece in range(3):
            value = mixed[:, piece * HEAD : (piece + 1) * HEAD].astype(F32)
            by = q_gain[...] if piece < 2 else k_gain[...]
            turned = turn(value * head_norm(value) * by, cos_rows, sin_rows).astype(BF)
            if piece < 2:
                qs[piece, rows] = turned
            else:
                ks[rows] = turned

    for a in (2, 3):
        spreads[a].pass_on(0)
    g_gather.forward()
    saves = [
        pltpu.make_async_copy(src, dst, out_s.at[i])
        for i, (src, dst) in enumerate(
            [
                (wq, wq_o), (raw, raw_o), (qs, q_o), (ks, k_o), (gain, gain_o),
                (x.at[pl.ds(pl.multiple_of(me * OWN, OWN), OWN)], x_o), (wo, wo_o),
                (att, att_o), (lse, lse_o), (g, g_o), (mid, mid_o), (h2, h2_o), (h1t, h1t_o), (start, start_o), (cosine, cos_o), (sine, sin_o),
            ]
        )
    ]
    for i in (0, 1, 2, 3, 4, 5, 6, 13, 14, 15):
        saves[i].start()

    for block in range(GROUP // QROWS):
        first, keys = block * QROWS, (block + 1) * QROWS
        rows = pl.ds(first, QROWS)
        allowed = allowed_keys(start[rows, :1], first, keys)

        @pl.loop(0, 2)
        def _(h):
            score = mm_t(qs[h, rows], ks[:keys]) * (SCALE * LOG2)
            score = jnp.where(allowed, score, -1e30)
            peak = jnp.max(score, axis=1, keepdims=True)
            weight = jnp.exp2(score - peak)
            total = jnp.sum(weight, axis=1, keepdims=True)
            out = mm(weight.astype(BF), raw[:keys, 3 * HEAD :]) / total
            att[h, rows] = out.astype(BF)
            lse[h, rows] = jnp.broadcast_to(peak + jnp.log2(total), (QROWS, HEAD))

    for a in (2, 3):
        spreads[a].wait(0)
        spreads[a].start(1)
    saves[7].start()
    saves[8].start()
    g_gather.share()

    scatter = Scatter(parts, theirs, sums, near, full, rs_s, rs_r)

    def project(d):
        rows = pl.ds(pl.multiple_of((z + d) % 4 * 256, 256), 256)
        left = jnp.concatenate([att[0, rows], att[1, rows]], axis=1)
        for c in range(4):
            parts[d, :, c * TILE : (c + 1) * TILE] = mm(left, wo[c].reshape(256, TILE)).astype(BF)
        scatter.put(d)

    project(2)
    project(1)
    scatter.across()
    project(3)
    project(0)
    scatter.beside(0)
    scatter.beside(1)

    @pl.loop(0, 8)
    def _(i):
        cols = pl.ds(pl.multiple_of(i * 256, 256), 256)
        h1t[cols] = h1[:, cols].T

    saves[12].start()
    for a in (2, 3):
        spreads[a].pass_on(1)
    g_gather.finish()
    keep_g.wait()
    saves[9].start()
    scatter.arrive()
    gain_two = gain_row(1)

    @pl.loop(0, OWN // 16)
    def _(i):
        first = pl.multiple_of(i * 16, 16)
        there = pl.ds(pl.multiple_of(me * OWN + first, 16), 16)
        value = x[there].astype(F32) + scatter.total(first, 16)
        mid[pl.ds(first, 16)] = value
        h2[there] = (value * head_norm(value) * gain_two).astype(BF)

    saves[10].start()
    h2_gather = Gather(rows_at(h2), hs, hr)
    h2_gather.start()
    h2_gather.forward()
    for a in (2, 3):
        keep, _, take = beside(a)
        keep.wait()
        take.wait_recv()
        spreads[a].wait(1)
    h2_gather.share()
    h2_gather.finish()
    saves[11].start()
    for copy in gain_copies:
        copy.wait_send()
    for a in range(4):
        beside(a)[1].wait_send()
        for kk in range(2):
            crossing(a, kk).wait_send()
    for spread in spreads:
        spread.drain()
    x_gather.drain()
    g_gather.drain()
    h2_gather.drain()
    scatter.drain()
    for copy in saves:
        copy.wait()


def forward_call(*args):
    hbm = pl.BlockSpec(memory_space=pl.ANY)
    vmem = pl.BlockSpec(memory_space=pltpu.VMEM)
    smem = pl.BlockSpec(memory_space=pltpu.SMEM)
    dma = pltpu.SemaphoreType.DMA

    def out(shape, dtype=BF):
        return jax.ShapeDtypeStruct(shape, dtype)

    wide = (GROUP, WIDTH)
    return pl.pallas_call(
        forward_kernel,
        out_shape=[
            out(wide), out(wide), out((4, 4, 4, 32, 512)), out((4, 4, 4, 16, TILE)), out((4, 4, 4, 32, 2 * UNITS)),
            out((4, 4, 4, 48, TILE)), out((WIDTH, GROUP)), out((GROUP, 512)), out((2, GROUP, HEAD)), out((GROUP, HEAD)),
            out((2, GROUP, HEAD)), out((2, GROUP, HEAD), F32), out((OWN, WIDTH), F32), out((4, 8, TILE), F32),
            out((OWN, WIDTH)), out((GROUP, HEAD), jnp.int32), out((GROUP, HEAD), F32), out((GROUP, HEAD), F32),
        ],
        in_specs=[vmem] * 7 + [smem] * 3 + [hbm] * 4,
        out_specs=[hbm] * 18,
        scratch_shapes=[
            pltpu.VMEM(wide, BF), pltpu.VMEM(wide, BF), pltpu.VMEM((WIDTH, GROUP), BF), pltpu.VMEM(wide, BF),
            pltpu.VMEM(wide, BF), pltpu.VMEM((4, 4, 4, 32, 512), BF), pltpu.VMEM((4, 4, 4, 16, TILE), BF),
            pltpu.VMEM((GROUP, 512), BF), pltpu.VMEM((2, GROUP, HEAD), BF), pltpu.VMEM((GROUP, HEAD), BF),
            pltpu.VMEM((2, GROUP, HEAD), BF), pltpu.VMEM((2, GROUP, HEAD), F32), pltpu.VMEM((OWN, WIDTH), F32),
            pltpu.VMEM((4, 8, TILE), F32), pltpu.VMEM((8, TILE), F32), pltpu.VMEM((GROUP, HEAD), jnp.int32),
            pltpu.VMEM((GROUP, HEAD), F32), pltpu.VMEM((GROUP, HEAD), F32),
            pltpu.VMEM((TILE, 4, 512), BF), pltpu.VMEM((2, 4, 4, 32, 512), BF), pltpu.VMEM((32, 4, 512), BF),
            pltpu.VMEM((2, 32, 512), BF), pltpu.VMEM((TILE, 2, 2 * UNITS), BF), pltpu.VMEM((2, 4, 4, 32, 2 * UNITS), BF),
            pltpu.VMEM((32, 2, 2 * UNITS), BF), pltpu.VMEM((2, 32, 2 * UNITS), BF),
        ]
        + GATHER_SEMS * 3
        + scatter_scratch()
        + [dma((4, 2)), dma((4, 2)), dma((4,)), dma((4,)), dma((3,)), dma((4,)), dma((6,)), dma((16,)), dma((4,))]
        + SPREAD_SEMS * 4,
        compiler_params=pltpu.CompilerParams(
            collective_id=1, has_side_effects=True, vmem_limit_bytes=VMEM_LIMIT
        ),
        cost_estimate=pl.CostEstimate(flops=4_000_000_000, bytes_accessed=60_000_000, transcendentals=2_000_000),
        name="forward",
    )(*args)


def middle_kernel(h2, g, wg, wd, ggu, hid):
    @pl.loop(0, GROUP // 256)
    def _(i):
        rows = pl.ds(pl.multiple_of(i * 256, 256), 256)
        pair = mm(h2[rows], wg[...].reshape(WIDTH, 512))
        back = mm_t(g[rows, :TILE], wd[0])
        for c in range(1, 4):
            back += mm_t(g[rows, c * TILE : (c + 1) * TILE], wd[c])
        gate, up = pair[:, :256], pair[:, 256:]
        sig = 1.0 / (1.0 + jnp.exp(-gate))
        silu = gate * sig
        hid[rows] = (silu * up).astype(BF)
        ggu[rows, :256] = (back * up * sig * (1.0 + gate * (1.0 - sig))).astype(BF)
        ggu[rows, 256:] = (back * silu).astype(BF)


def middle_call(h2, g, wg, wd):
    wide = pl.BlockSpec((GROUP, WIDTH), lambda u: (0, 0), pipeline_mode=pl.Buffered(1))
    return pl.pallas_call(
        middle_kernel,
        grid=(3,),
        out_shape=[
            jax.ShapeDtypeStruct((GROUP, 2 * UNITS), BF),
            jax.ShapeDtypeStruct((GROUP, UNITS), BF),
        ],
        in_specs=[
            wide,
            wide,
            pl.BlockSpec((4, TILE, 512), lambda u: (0, 0, u)),
            pl.BlockSpec((4, 256, TILE), lambda u: (0, u, 0)),
        ],
        out_specs=[
            pl.BlockSpec((GROUP, 512), lambda u: (0, u)),
            pl.BlockSpec((GROUP, 256), lambda u: (0, u)),
        ],
        compiler_params=pltpu.CompilerParams(vmem_limit_bytes=VMEM_LIMIT),
        cost_estimate=pl.CostEstimate(flops=9_600_000_000, bytes_accessed=22_000_000, transcendentals=800_000),
        name="feed_forward",
    )(h2, g, wg, wd)


class Collapse:
    def __init__(self, which, src, got, sums, got2, done, send, recv, own):
        px, py = dp_place()
        here = (px, py)
        self.which = which
        self.got, self.sums, self.got2, self.done, self.here = got, sums, got2, done, here

        def cut(axis, index, half):
            pair = pl.ds(2 * half, 2)
            return src.at[which, index, :, pair] if axis == 0 else src.at[which, :, index, pair]

        self.keep, self.copies = [], {}
        for half in range(2):
            axis = half
            self.keep.append(pltpu.make_async_copy(cut(axis, here[axis], half), sums.at[which, half], own.at[which, half]))
            for o in range(1, 4):
                there = (here[axis] + o) % 4
                self.copies[half, 0, o] = remote(
                    cut(axis, there, half), got.at[which, half, o - 1],
                    send.at[which, half, 0, o - 1], recv.at[which, half, 0, o - 1], along(axis, o),
                )
                there = (here[1 - axis] + o) % 4
                self.copies[half, 1, o] = remote(
                    sums.at[which, half, there], got2.at[which, half, o - 1],
                    send.at[which, half, 1, o - 1], recv.at[which, half, 1, o - 1], along(1 - axis, o),
                )

    def start(self):
        for half in range(2):
            for o in range(1, 4):
                self.copies[half, 0, o].start()
            self.keep[half].start()

    def first(self):
        for half in range(2):
            self.keep[half].wait()
            for o in range(1, 4):
                self.copies[half, 0, o].wait_recv()

            @pl.loop(0, 8)
            def _(i):
                a, c = i // 2, i % 2
                total = self.sums[self.which, half, a, c].astype(F32)
                for o in range(3):
                    total += self.got[self.which, half, o, a, c].astype(F32)
                self.sums[self.which, half, a, c] = total.astype(BF)

            for o in range(1, 4):
                self.copies[half, 1, o].start()

    def second(self):
        for half in range(2):
            for o in range(1, 4):
                self.copies[half, 1, o].wait_recv()
            for c in range(2):
                total = self.sums[self.which, half, self.here[1 - half], c].astype(F32)
                for o in range(3):
                    total += self.got2[self.which, half, o, c].astype(F32)
                self.done[self.which, 2 * half + c] = total.astype(BF)

    def drain(self):
        for copy in self.copies.values():
            copy.wait_send()


CHUNKS = 4


def collapse_scratch():
    dma = pltpu.SemaphoreType.DMA
    return [
        pltpu.VMEM((CHUNKS, 2, 3, 4, 2, 48, 512), BF),
        pltpu.VMEM((CHUNKS, 2, 4, 2, 48, 512), BF),
        pltpu.VMEM((CHUNKS, 2, 3, 2, 48, 512), BF),
        pltpu.VMEM((CHUNKS, 4, 48, 512), BF),
        dma((CHUNKS, 2, 2, 3)), dma((CHUNKS, 2, 2, 3)), dma((CHUNKS, 2)),
        dma((CHUNKS, 3)), dma((CHUNKS, 4)), dma((CHUNKS, 2, 2, 4)), dma((CHUNKS, 2, 2, 4)),
    ]


class Trade:
    def __init__(self, block, slot, send, recv, which=()):
        _, row, col, z, k = place()
        self.col, self.peer = col, on_ring(z, 1 - k)
        self.recv, self.send, self.slot, self.which = recv, send, slot, which
        self.copies = [
            remote(block((col + o) % 4), slot(col), send.at[(*which, o - 1)], recv.at[(*which, o - 1)], {"col": (col + o) % 4})
            for o in range(1, 4)
        ]
        self.keep = pltpu.make_async_copy(block(col), slot(col), recv.at[(*which, 3)])

    def start(self):
        for copy in self.copies:
            copy.start()
        self.keep.start()

    def finish(self):
        for o in range(1, 4):
            dst = self.slot((self.col - o + 4) % 4)
            sems = (self.send.at[(*self.which, o - 1)], self.recv.at[(*self.which, o - 1)])
            remote(dst, dst, *sems, self.peer).wait_recv()
        self.keep.wait()

    def drain(self):
        for copy in self.copies:
            copy.wait_send()


def norm_back(grad, value, gain):
    scale = head_norm(value)
    weighted = grad * gain
    inner = jnp.mean(weighted * value, axis=1, keepdims=True)
    return scale * weighted - value * (scale * scale * scale * inner), grad * value * scale


def norm_back(grad, value, gain):
    scale = head_norm(value)
    weighted = grad * gain
    inner = jnp.mean(weighted * value, axis=1, keepdims=True)
    return scale * weighted - value * (scale * scale * scale * inner), grad * value * scale


def backward_kernel(
    h2_i, ggu_i, hid_i, g_i, wg_i, wd_i, wo_i, wq_i, h1t_i, raw_i, q_i, k_i, att_i, lse_i, mid_i, gain_i, x_i,
    start_i, cos_i, sin_i, q_gain, k_gain,
    result_o, stream_o, grads_o, local_o, sums_o,
    m, gm, dqkv, stage, mid, gain, x_own, g_own, acc, head_acc, tile_f, tile_b, totals, heard,
    ms, mr,
    parts, theirs, psums, near, full, rs_s, rs_r,
    got, sums, got2, done, c_s, c_r, c_own, t_s, t_r, a_s, a_r,
    fs, fr, ls, lr, as_, ar, in_s, stage_s, free,
):
    p, row, col, z, k = place()
    px, py = dp_place()
    me = 2 * z + k
    up, down, peer = on_ring((z + 1) % 4, k), on_ring((z + 3) % 4, k), on_ring(z, 1 - k)
    far = on_ring((z + 2) % 4, k)
    loads = []

    def load(src, dst):
        copy = pltpu.make_async_copy(src, dst, in_s.at[len(loads)])
        copy.start()
        loads.append(copy)
        return copy

    def wait(copies):
        for copy in copies:
            copy.wait()

    collapses, trades, spreads = [], [], []

    def chunk(i):
        def at(half, x, y, part):
            xs = slice(None) if x is None else x
            ys = slice(None) if y is None else y
            which = pl.ds(2 * half, 2) if part is None else 2 * half + part
            return grads_o.at[i, xs, ys, which]

        collapses.append(
            Collapse(
                i, local_o, got, sums, got2, done, c_s, c_r, c_own
            )
        )
        trades.append(
            Trade(lambda c: done.at[i, c], lambda c: grads_o.at[i, px, py, c], t_s, t_r, (i,))
        )
        spreads.append(Spread(at, a_s, a_r, (i,)))

    for i in range(CHUNKS):
        chunk(i)
    scatter = Scatter(parts, theirs, psums, near, full, rs_s, rs_r)
    stream_trade = Trade(
        lambda c: tile_f.at[:, pl.ds(pl.multiple_of(c * TILE, TILE), TILE)],
        lambda c: stream_o.at[pl.ds(pl.multiple_of(c * OWN, OWN), OWN)], fs, fr,
    )
    result_trade = Trade(
        lambda c: tile_b.at[:, pl.ds(pl.multiple_of(c * TILE, TILE), TILE)],
        lambda c: result_o.at[pl.ds(pl.multiple_of(c * OWN, OWN), OWN)], ls, lr,
    )

    def release():
        scatter.drain()
        for device in (up, down, peer):
            pl.semaphore_signal(free, inc=1, device_id=device, device_id_type=MESH)

    def project(d, product):
        rows = pl.ds(pl.multiple_of((z + d) % 4 * 256, 256), 256)

        @pl.loop(0, 4)
        def _(c):
            cols = pl.ds(pl.multiple_of(c * TILE, TILE), TILE)
            parts[d, :, cols] = product(rows, c, cols).astype(BF)

        scatter.put(d)

    def weight_grads(i, first, second):
        copies = [
            pltpu.make_async_copy(stage.at[c % 2], local_o.at[i, :, :, c], stage_s.at[i, c]) for c in range(4)
        ]
        for c in range(4):
            if c >= 2:
                copies[c - 2].wait()
            cols = slice(c * TILE, (c + 1) * TILE)
            stage[c % 2, :, :, :32] = first(cols).astype(BF).reshape(4, 4, 32, 512)
            stage[c % 2, :, :, 32:] = second(cols).astype(BF).reshape(4, 4, 16, 512)
            copies[c].start()
        copies[2].wait()
        copies[3].wait()
        collapses[i].start()

    def gain_row(which):
        return jnp.concatenate([gain[c, which : which + 1] for c in range(4)], axis=1)

    own_rows = pl.ds(pl.multiple_of(me * OWN, OWN), OWN)

    def stage_one(h2, g, ggu, hid, wg):
        needed = [load(ggu_i, ggu), load(h2_i, h2), load(hid_i, hid), load(g_i, g)]
        l_wg = load(wg_i, wg)
        meet(ring_friends() + [far] + xy_friends())
        wait(needed)

        def grads(u):
            weight_grads(
                u,
                lambda cols: t_mm(h2[:, cols], ggu[:, u * 512 : (u + 1) * 512]),
                lambda cols: t_mm(hid[:, u * 256 : (u + 1) * 256], g[:, cols]),
            )

        def product(rows, c, cols):
            return mm_t(ggu[rows], wg[c])

        grads(0)
        l_wg.wait()
        project(2, product)
        project(1, product)
        scatter.across()
        project(3, product)
        project(0, product)
        grads(1)
        scatter.beside(0)
        scatter.beside(1)
        grads(2)

    early = [load(mid_i, mid), load(gain_i, gain), load(x_i, x_own), load(g_i.at[own_rows], g_own)]
    pl.run_scoped(
        stage_one,
        pltpu.VMEM((GROUP, WIDTH), BF), pltpu.VMEM((GROUP, WIDTH), BF), pltpu.VMEM((GROUP, 2 * UNITS), BF),
        pltpu.VMEM((GROUP, UNITS), BF), pltpu.VMEM((4, TILE, 2 * UNITS), BF),
    )

    def stage_two(wo, att, qs, ks, raw, lse, ga, dk, dv, h1t, wq, att_t, start, cosine, sine):
        l_wo, l_att = load(wo_i, wo), load(att_i, att)
        l_heads = [
            load(q_i, qs), load(k_i, ks), load(raw_i, raw), load(lse_i, lse),
            load(start_i, start), load(cos_i, cosine), load(sin_i, sine),
        ]
        l_last = [load(h1t_i, h1t), load(wq_i, wq)]
        wait(early)
        acc[...] = jnp.zeros_like(acc)
        head_acc[...] = jnp.zeros_like(head_acc)
        dk[...] = jnp.zeros_like(dk)
        dv[...] = jnp.zeros_like(dv)
        totals[0] = jnp.zeros((8, WIDTH), F32)
        gain_two = gain_row(1)
        scatter.arrive()

        @pl.loop(0, OWN // 16)
        def _(i):
            rows = pl.ds(pl.multiple_of(i * 16, 16), 16)
            back, gained = norm_back(scatter.total(pl.multiple_of(i * 16, 16), 16), mid[rows], gain_two)
            acc[1] += gained
            back = back + g_own[rows].astype(F32)
            gm[rows] = back
            m[pl.ds(pl.multiple_of(me * OWN + i * 16, 16), 16)] = back.astype(BF)

        m_gather = Gather(rows_at(m), ms, mr)
        m_gather.start()
        release()
        collapses[0].first()
        l_att.wait()
        for h in range(2):
            att_t[h * HEAD : (h + 1) * HEAD] = att[h].T
        m_gather.forward()
        l_wo.wait()
        wait(l_heads)
        m_gather.share()
        m_gather.finish()

        @pl.loop(0, 4)
        def _(i):
            rows = pl.ds(pl.multiple_of(i * 256, 256), 256)
            back = mm_t(m[rows, :TILE], wo[0])
            for c in range(1, 4):
                back += mm_t(m[rows, c * TILE : (c + 1) * TILE], wo[c])
            for h in range(2):
                ga[h, rows] = back[:, h * HEAD : (h + 1) * HEAD].astype(BF)

        collapses[1].first()
        collapses[0].second()
        trades[0].start()
        for block in range(GROUP // QROWS):
            first, keys = block * QROWS, (block + 1) * QROWS
            rows = pl.ds(first, QROWS)
            allowed = allowed_keys(start[rows, :1], first, keys)

            @pl.loop(0, 2)
            def _(h):
                cols = pl.ds(pl.multiple_of(h * HEAD, HEAD), HEAD)
                score = mm_t(qs[h, rows], ks[:keys]) * (SCALE * LOG2)
                prob = jnp.exp2(jnp.where(allowed, score, -1e30) - lse[h, rows, :1])
                grad = ga[h, rows]
                delta = jnp.sum(grad.astype(F32) * att[h, rows].astype(F32), axis=1, keepdims=True)
                prob_grad = mm_t(grad, raw[:keys, 3 * HEAD :])
                score_grad = (prob * (prob_grad - delta)).astype(BF)
                dk[:keys] += t_mm(score_grad, qs[h, rows])
                dv[:keys] += t_mm(prob.astype(BF), grad)
                back = turn_back(mm(score_grad, ks[:keys]) * SCALE, cosine[rows], sine[rows])
                back, gained = norm_back(back, raw[rows, cols].astype(F32), q_gain[...])
                dqkv[rows, cols] = back.astype(BF)
                head_acc[0:1] += jnp.sum(gained, axis=0, keepdims=True)

            if block == 1:
                trades[0].finish()
                spreads[0].start(0)
            if block == 2:
                collapses[2].first()


        @pl.loop(0, 4)
        def _(i):
            rows = pl.ds(pl.multiple_of(i * 256, 256), 256)
            back = turn_back(dk[rows] * SCALE, cosine[rows], sine[rows])
            back, gained = norm_back(back, raw[rows, 2 * HEAD : 3 * HEAD].astype(F32), k_gain[...])
            dqkv[rows, 2 * HEAD : 3 * HEAD] = back.astype(BF)
            dqkv[rows, 3 * HEAD :] = dv[rows].astype(BF)
            head_acc[1:2] += jnp.sum(gained, axis=0, keepdims=True)

        wait(l_last)
        pl.semaphore_wait(free, 3)

        def product(rows, c, cols):
            return mm_t(dqkv[rows], wq[c])

        project(2, product)
        project(1, product)
        weight_grads(3, lambda cols: mm(h1t[cols], dqkv[...]), lambda cols: mm(att_t[...], m[:, cols]))
        spreads[0].pass_on(0)
        scatter.across()
        project(3, product)
        project(0, product)
        collapses[1].second()
        trades[1].start()
        spreads[0].wait(0)
        spreads[0].start(1)
        m_gather.drain()

    pl.run_scoped(
        stage_two,
        pltpu.VMEM((4, 256, TILE), BF), pltpu.VMEM((2, GROUP, HEAD), BF), pltpu.VMEM((2, GROUP, HEAD), BF),
        pltpu.VMEM((GROUP, HEAD), BF), pltpu.VMEM((GROUP, 512), BF), pltpu.VMEM((2, GROUP, HEAD), F32),
        pltpu.VMEM((2, GROUP, HEAD), BF), pltpu.VMEM((GROUP, HEAD), F32), pltpu.VMEM((GROUP, HEAD), F32),
        pltpu.VMEM((WIDTH, GROUP), BF), pltpu.VMEM((4, TILE, 512), BF), pltpu.VMEM((2 * HEAD, GROUP), BF),
        pltpu.VMEM((GROUP, HEAD), jnp.int32), pltpu.VMEM((GROUP, HEAD), F32), pltpu.VMEM((GROUP, HEAD), F32),
    )

    def stage_three(hid, wd):
        last = [load(hid_i, hid), load(wd_i, wd)]
        scatter.beside(0)
        scatter.beside(1)
        collapses[2].second()
        trades[2].start()
        trades[1].finish()
        spreads[1].start(0)
        gain_one = gain_row(0)
        scatter.arrive()

        @pl.loop(0, OWN // 16)
        def _(i):
            rows = pl.ds(pl.multiple_of(i * 16, 16), 16)
            back, gained = norm_back(
                scatter.total(pl.multiple_of(i * 16, 16), 16), x_own[rows].astype(F32), gain_one
            )
            acc[0] += gained
            tile_f[rows] = gm[rows] + back

        stream_trade.start()
        release()
        totals[0, 0:1] = jnp.sum(acc[0], axis=0, keepdims=True)
        totals[0, 1:2] = jnp.sum(acc[1], axis=0, keepdims=True)
        totals[0, 2:3, 0:HEAD] = head_acc[0:1]
        totals[0, 2:3, HEAD : 2 * HEAD] = head_acc[1:2]
        sent = []

        def tell(phase, devices, slots):
            for device, slot in zip(devices, slots):
                copy = remote(totals.at[phase], heard.at[slot], as_.at[slot], ar.at[slot], device)
                copy.start()
                sent.append(copy)

        def listen(phase, slots):
            total = totals[phase]
            for slot in slots:
                remote(heard.at[slot], heard.at[slot], as_.at[slot], ar.at[slot], peer).wait_recv()
                total += heard[slot]
            totals[phase + 1] = total

        tell(0, [peer], [0])
        trades[2].finish()
        spreads[2].start(0)
        collapses[3].first()
        spreads[1].pass_on(0)
        listen(0, [0])
        tell(1, [up, down, far], [1, 2, 3])
        wait(last)
        pl.semaphore_wait(free, 3)

        def product(rows, c, cols):
            return mm(hid[rows], wd[c])

        project(2, product)
        project(1, product)
        spreads[0].pass_on(1)
        spreads[1].wait(0)
        spreads[1].start(1)
        spreads[2].pass_on(0)
        scatter.across()
        project(3, product)
        project(0, product)
        listen(1, [1, 2, 3])
        tell(2, [along(0, o) for o in range(1, 4)], [4, 5, 6])
        collapses[3].second()
        trades[3].start()
        scatter.beside(0)
        scatter.beside(1)
        spreads[2].wait(0)
        spreads[2].start(1)
        trades[3].finish()
        spreads[3].start(0)
        scatter.arrive()

        @pl.loop(0, OWN // 16)
        def _(i):
            rows = pl.ds(pl.multiple_of(i * 16, 16), 16)
            tile_b[rows] = (mid[rows] + scatter.total(pl.multiple_of(i * 16, 16), 16)).astype(BF)

        result_trade.start()
        spreads[1].pass_on(1)
        spreads[3].pass_on(0)
        listen(2, [4, 5, 6])
        tell(3, [along(1, o) for o in range(1, 4)], [7, 8, 9])
        spreads[3].wait(0)
        spreads[3].start(1)
        spreads[2].pass_on(1)
        stream_trade.finish()
        result_trade.finish()
        listen(3, [7, 8, 9])
        sums_o[...] = totals[4]
        spreads[3].pass_on(1)
        for spread in spreads:
            spread.wait(1)
        scatter.drain()
        for thing in collapses + trades + spreads + [stream_trade, result_trade]:
            thing.drain()
        for copy in sent:
            copy.wait_send()

    pl.run_scoped(stage_three, pltpu.VMEM((GROUP, UNITS), BF), pltpu.VMEM((4, UNITS, TILE), BF))


def backward_call(*args):
    hbm = pl.BlockSpec(memory_space=pl.ANY)
    vmem = pl.BlockSpec(memory_space=pltpu.VMEM)
    dma = pltpu.SemaphoreType.DMA
    out = jax.ShapeDtypeStruct
    grads = out((CHUNKS, 4, 4, 4, 48, 512), BF)
    return pl.pallas_call(
        backward_kernel,
        out_shape=[out((TILE, TILE), BF), out((TILE, TILE), F32), grads, grads, out((8, WIDTH), F32)],
        in_specs=[hbm] * 20 + [vmem] * 2,
        out_specs=[hbm] * 4 + [vmem],
        scratch_shapes=[
            pltpu.VMEM((GROUP, WIDTH), BF), pltpu.VMEM((OWN, WIDTH), F32), pltpu.VMEM((GROUP, 512), BF),
            pltpu.VMEM((2, 4, 4, 48, 512), BF), pltpu.VMEM((OWN, WIDTH), F32), pltpu.VMEM((4, 8, TILE), F32),
            pltpu.VMEM((OWN, WIDTH), BF), pltpu.VMEM((OWN, WIDTH), BF), pltpu.VMEM((2, 16, WIDTH), F32),
            pltpu.VMEM((8, HEAD), F32), pltpu.VMEM((OWN, WIDTH), F32), pltpu.VMEM((OWN, WIDTH), BF),
            pltpu.VMEM((5, 8, WIDTH), F32), pltpu.VMEM((10, 8, WIDTH), F32),
        ]
        + GATHER_SEMS
        + scatter_scratch()
        + collapse_scratch()
        + [
            dma((3,)), dma((4,)), dma((3,)), dma((4,)), dma((10,)), dma((10,)), dma((24,)), dma((CHUNKS, 4)),
            pltpu.SemaphoreType.REGULAR,
        ],
        compiler_params=pltpu.CompilerParams(
            collective_id=2, has_side_effects=True, vmem_limit_bytes=VMEM_LIMIT
        ),
        cost_estimate=pl.CostEstimate(flops=25_000_000_000, bytes_accessed=100_000_000, transcendentals=2_000_000),
        name="backward",
    )(*args)


def place_big_kernel(grads, result, stream, totals, gate_up, down, result_o, stream_o, one, two, head):
    value = grads[0, :, 0, :32].reshape(TILE, 512).astype(F32)
    for g in range(2):
        gate_up[:, g, :] = value[:, g * 256 : (g + 1) * 256]
    down[...] = grads[0, :, 0, 32:].reshape(256, TILE).astype(F32)
    result_o[...] = result[...]
    stream_o[...] = stream[...]
    one[...] = totals[0:1]
    two[...] = totals[1:2]
    head[...] = totals[2:3, : 2 * HEAD]


def place_big(grads, result, stream, totals):
    rows = pl.BlockSpec((OWN, TILE), lambda c, u: (c, 0))

    def whole(*shape):
        return pl.BlockSpec(shape, lambda c, u: (0, 0))

    return pl.pallas_call(
        place_big_kernel,
        grid=(4, 3),
        in_specs=[
            pl.BlockSpec((1, DP, 1, 48, 512), lambda c, u: (u, 0, c, 0, 0)), rows, rows, whole(8, WIDTH),
        ],
        out_specs=[
            pl.BlockSpec((TILE, 2, 256), lambda c, u: (0, 0, c * 3 + u)),
            pl.BlockSpec((256, TILE), lambda c, u: (c * 3 + u, 0)),
            rows, rows, whole(1, WIDTH), whole(1, WIDTH), whole(1, 2 * HEAD),
        ],
        out_shape=[
            jax.ShapeDtypeStruct((TILE, 2, 4 * UNITS), F32),
            jax.ShapeDtypeStruct((4 * UNITS, TILE), F32),
            jax.ShapeDtypeStruct((TILE, TILE), BF),
            jax.ShapeDtypeStruct((TILE, TILE), F32),
            jax.ShapeDtypeStruct((1, WIDTH), F32),
            jax.ShapeDtypeStruct((1, WIDTH), F32),
            jax.ShapeDtypeStruct((1, 2 * HEAD), F32),
        ],
        compiler_params=pltpu.CompilerParams(vmem_limit_bytes=40 * 1024 * 1024),
        cost_estimate=pl.CostEstimate(flops=0, bytes_accessed=32_000_000, transcendentals=0),
        name="place_big",
    )(grads, result, stream, totals)


def place_small_kernel(grads, qkv, out):
    for c in range(4):
        qkv[:, c, :] = grads[0, :, c, :32].reshape(128, 512).astype(F32)
        out[c] = grads[0, :, c, 32:].reshape(64, TILE).astype(F32)


def place_small(grads):
    return pl.pallas_call(
        place_small_kernel,
        grid=(4,),
        in_specs=[pl.BlockSpec((1, 4, 4, 48, 512), lambda i: (3, i, 0, 0, 0))],
        out_specs=[
            pl.BlockSpec((128, 4, 512), lambda i: (i, 0, 0)),
            pl.BlockSpec((4, 64, TILE), lambda i: (0, i, 0)),
        ],
        out_shape=[
            jax.ShapeDtypeStruct((TILE, 4, 512), F32),
            jax.ShapeDtypeStruct((4, 256, TILE), F32),
        ],
        compiler_params=pltpu.CompilerParams(vmem_limit_bytes=40 * 1024 * 1024),
        cost_estimate=pl.CostEstimate(flops=0, bytes_accessed=9_000_000, transcendentals=0),
        name="place_small",
    )(grads)


def body(
    tokens, norm1_gain, w_qkv, q_gain, k_gain, w_out, norm2_gain, w_gate_up, w_down, out_grad,
    seq_lengths, seq_group, seq_start,
):
    (h2, g, wq, wo, wg, wd, h1t, raw, qs, ks, att, lse, middle, gain, x_own, start, cosine, sine) = forward_call(
        tokens, out_grad, norm1_gain[None], norm2_gain[None], q_gain[None], k_gain[None], jnp.asarray(FREQ),
        seq_lengths, seq_group, seq_start, w_qkv, w_gate_up,
        w_out.reshape(4, 4, 4, 16, TILE), w_down.reshape(4, 4, 4, 48, TILE),
    )
    wg = wg.reshape(4, TILE, 2 * UNITS)
    wd = wd.reshape(4, UNITS, TILE)
    ggu, hid = middle_call(h2, g, wg, wd)
    result, stream, grads, _, totals = backward_call(
        h2, ggu, hid, g, wg, wd, wo.reshape(4, 256, TILE), wq.reshape(4, TILE, 512), h1t, raw, qs, ks, att, lse,
        middle, gain, x_own, start, cosine, sine, q_gain[None], k_gain[None],
    )
    grads = grads.reshape(CHUNKS, DP, 4, 48, 512)
    g_gate_up, g_down, result, stream, one, two, head = place_big(grads, result, stream, totals)
    g_qkv, g_out = place_small(grads)
    return (
        result,
        stream,
        one.reshape(WIDTH),
        g_qkv,
        head[0, :HEAD],
        head[0, HEAD:],
        g_out.reshape(w_out.shape),
        two.reshape(WIDTH),
        g_gate_up,
        g_down,
    )


def solution(mesh):
    in_specs = (
        P(("dp", "row"), "col"),
        P("col"),
        P("col", "row", None),
        P(),
        P(),
        P("row", "col"),
        P("col"),
        P("col", None, "row"),
        P("row", "col"),
        P(("dp", "row"), "col"),
        P(),
        P(),
        P(),
    )
    out_specs = (
        P(("dp", "row"), "col"),
        P(("dp", "row"), "col"),
        P(),
        P("col", "row", None),
        P(),
        P(),
        P("row", "col"),
        P(),
        P("col", None, "row"),
        P("row", "col"),
    )
    return jax.shard_map(body, mesh=mesh, in_specs=in_specs, out_specs=out_specs, check_vma=False)
```

```python
import math

import jax
import jax.numpy as jnp
import numpy as np
from jax import lax
from jax.experimental import pallas as pl
from jax.experimental.pallas import tpu as pltpu
from jax.sharding import PartitionSpec as P

EPS = 1e-06
THETA = 1000000.0
BF = jnp.bfloat16
F32 = jnp.float32
Z = ("row", "col")
MESH = pl.DeviceIdType.MESH
VMEM_LIMIT = 63 * 1024 * 1024

GROUP, WIDTH, TILE, UNITS, HEAD = 1024, 2048, 512, 768, 128
OWN = GROUP // 8
DP = 16


def dot(left, right, dims):
    return lax.dot_general(left, right, (dims, ((), ())), preferred_element_type=F32)


def mm(left, right):
    return dot(left, right, ((1,), (0,)))


def mm_t(left, right):
    return dot(left, right, ((1,), (1,)))


def t_mm(left, right):
    return dot(left, right, ((0,), (0,)))


def place():
    row, col = lax.axis_index("row"), lax.axis_index("col")
    j = 4 * row + col
    return lax.axis_index("dp"), row, col, j // 2, j % 2


def on_ring(z, k):
    j = 2 * z + k
    return {"row": j // 4, "col": j % 4}


def remote(src, dst, send, recv, device):
    return pltpu.make_async_remote_copy(
        src_ref=src, dst_ref=dst, send_sem=send, recv_sem=recv, device_id=device, device_id_type=MESH
    )


def meet(devices):
    barrier = pltpu.get_barrier_semaphore()
    for device in devices:
        pl.semaphore_signal(barrier, inc=1, device_id=device, device_id_type=MESH)
    pl.semaphore_wait(barrier, len(devices))


def ring_friends():
    _, _, _, z, k = place()
    other = z + 1 - 2 * (z % 2)
    return [
        on_ring((z + 1) % 4, k),
        on_ring((z + 3) % 4, k),
        on_ring(z, 1 - k),
        on_ring(other, 1 - k),
    ]


def dp_place():
    p = lax.axis_index("dp")
    return p // 4, p % 4


def along(axis, o):
    px, py = dp_place()
    return {"dp": (px + o) % 4 * 4 + py} if axis == 0 else {"dp": px * 4 + (py + o) % 4}


def xy_friends():
    return [along(axis, o) for axis in range(2) for o in range(1, 4)]


def tile_at(buf):
    def loc(j, half=None):
        row, col = j // 4, j % 4
        first = pl.multiple_of(row * TILE, TILE)
        rows = pl.ds(first, TILE)
        if half is not None:
            rows = pl.ds(first + half * (TILE // 2), TILE // 2)
        return buf.at[rows, pl.ds(pl.multiple_of(col * TILE, TILE), TILE)]

    return loc


def rows_at(buf):
    def loc(j, half=None):
        first = pl.multiple_of(j * OWN, OWN)
        rows = pl.ds(first, OWN)
        if half is not None:
            rows = pl.ds(first + half * (OWN // 2), OWN // 2)
        return buf.at[rows]

    return loc


class Gather:
    def __init__(self, loc, send, recv, own=None):
        _, _, _, z, k = place()
        up, down, far = (z + 1) % 4, (z + 3) % 4, (z + 2) % 4
        to_up, to_down, peer = on_ring(up, k), on_ring(down, k), on_ring(z, 1 - k)

        def out(slot, src, dst, device):
            return remote(src, dst, send.at[slot], recv.at[slot], device)

        def into(slot, dst):
            return remote(dst, dst, send.at[slot], recv.at[slot], peer)

        mine = loc(2 * z + k)
        own = mine if own is None else own
        left, right, across = 2 * down + k, 2 * up + k, 2 * far + k
        self.first = [out(0, own, mine, to_up), out(1, own, mine, to_down), out(4, own, mine, peer)]
        self.from_left = [
            out(2, loc(left, 0), loc(left, 0), to_up),
            out(5, loc(left), loc(left), peer),
        ]
        self.from_right = [
            out(3, loc(right, 1), loc(right, 1), to_down),
            out(6, loc(right), loc(right), peer),
        ]
        self.from_far = [
            out(7, loc(across, 0), loc(across, 0), peer),
            out(8, loc(across, 1), loc(across, 1), peer),
        ]
        theirs = [2 * z + 1 - k, 2 * down + 1 - k, 2 * up + 1 - k, 2 * far + 1 - k]
        self.arrivals = {
            0: into(0, loc(left)),
            1: into(1, loc(right)),
            2: into(2, loc(across, 0)),
            3: into(3, loc(across, 1)),
            4: into(4, loc(theirs[0])),
            5: into(5, loc(theirs[1])),
            6: into(6, loc(theirs[2])),
            7: into(7, loc(theirs[3], 0)),
            8: into(8, loc(theirs[3], 1)),
        }

    def start(self):
        for copy in self.first:
            copy.start()

    def forward(self):
        self.arrivals[0].wait_recv()
        for copy in self.from_left:
            copy.start()
        self.arrivals[1].wait_recv()
        for copy in self.from_right:
            copy.start()

    def share(self):
        for half in range(2):
            self.arrivals[2 + half].wait_recv()
            self.from_far[half].start()

    def finish(self, slots=range(4, 9)):
        for slot in slots:
            self.arrivals[slot].wait_recv()

    def drain(self):
        for copy in self.first + self.from_left + self.from_right + self.from_far:
            copy.wait_send()


GATHER_SEMS = [pltpu.SemaphoreType.DMA((9,)), pltpu.SemaphoreType.DMA((9,))]


class Spread:
    def __init__(self, at, send, recv, which=()):
        px, py = dp_place()
        here = (px, py)
        self.out, self.into = {}, {}
        for half in range(2):
            for phase in range(2):
                axis = half ^ phase

                def block(o, part=None):
                    whose = [px, py]
                    whose[axis] = (here[axis] + o) % 4
                    if phase:
                        whose[1 - axis] = None
                    return at(half, *whose, part)

                def copy(slot, ref, o):
                    index = (*which, half, phase, slot)
                    sems = (send.at[index], recv.at[index])
                    return remote(ref, ref, *sems, along(axis, o))

                self.out[half, phase] = [
                    copy(0, block(0), 1), copy(1, block(0), 3),
                    copy(2, block(3, 0), 1), copy(3, block(1, 1), 3),
                ]
                self.into[half, phase] = [
                    copy(0, block(3), 1), copy(1, block(1), 3),
                    copy(2, block(2, 0), 1), copy(3, block(2, 1), 3),
                ]

    def start(self, phase):
        for half in range(2):
            for slot in range(2):
                self.out[half, phase][slot].start()

    def pass_on(self, phase):
        for half in range(2):
            for slot in range(2):
                self.into[half, phase][slot].wait_recv()
                self.out[half, phase][2 + slot].start()

    def wait(self, phase):
        for half in range(2):
            for slot in range(2, 4):
                self.into[half, phase][slot].wait_recv()

    def drain(self):
        for copies in self.out.values():
            for copy in copies:
                copy.wait_send()


SPREAD_SEMS = [pltpu.SemaphoreType.DMA((2, 2, 4)), pltpu.SemaphoreType.DMA((2, 2, 4))]


class Scatter:
    def __init__(self, parts, theirs, sums, near, full, send, recv):
        _, _, _, z, k = place()
        self.parts, self.theirs, self.sums, self.near, self.full = parts, theirs, sums, near, full
        self.k = k
        to_up, to_down = on_ring((z + 1) % 4, k), on_ring((z + 3) % 4, k)
        peer = on_ring(z, 1 - k)
        half = OWN // 2
        other = pl.ds(pl.multiple_of((1 - k) * OWN, OWN), OWN)

        def copy(slot, src, dst, device):
            return remote(src, dst, send.at[slot], recv.at[slot], device)

        self.copies = [copy(d, parts.at[d, other], theirs.at[d], peer) for d in range(4)] + [
            copy(4, sums.at[0, pl.ds(0, half)], near.at[0], to_up),
            copy(5, sums.at[0, pl.ds(half, half)], near.at[1], to_down),
            copy(6, sums.at[1], full.at[0], to_up),
            copy(7, sums.at[2], full.at[1], to_down),
        ]

    def put(self, d):
        self.copies[d].start()

    def own(self, d, rows, count):
        first = pl.multiple_of(self.k * OWN + rows, count)
        return self.parts[d, pl.ds(first, count)].astype(F32) + self.theirs[
            d, pl.ds(rows, count)
        ].astype(F32)

    def across(self):
        self.copies[2].wait_recv()

        @pl.loop(0, OWN // 16)
        def _(i):
            rows = pl.multiple_of(i * 16, 16)
            self.sums[0, pl.ds(rows, 16)] = self.own(2, rows, 16).astype(BF)

        self.copies[4].start()
        self.copies[5].start()

    def beside(self, side):
        d, half = (1, 3)[side], OWN // 2
        self.copies[d].wait_recv()
        self.copies[4 + side].wait_recv()

        @pl.loop(0, half // 16)
        def _(i):
            rows = pl.multiple_of(i * 16, 16)
            here = pl.multiple_of(rows + side * half, 16)
            there = pl.multiple_of(rows + (1 - side) * half, 16)
            added = self.own(d, here, 16) + self.near[side, pl.ds(rows, 16)].astype(F32)
            self.sums[1 + side, pl.ds(here, 16)] = added.astype(BF)
            self.sums[1 + side, pl.ds(there, 16)] = self.own(d, there, 16).astype(BF)

        self.copies[6 + side].start()

    def arrive(self):
        self.copies[0].wait_recv()
        self.copies[6].wait_recv()
        self.copies[7].wait_recv()

    def total(self, rows, count):
        return (
            self.own(0, rows, count)
            + self.full[0, pl.ds(rows, count)].astype(F32)
            + self.full[1, pl.ds(rows, count)].astype(F32)
        )

    def drain(self):
        for copy in self.copies:
            copy.wait_send()


def scatter_scratch():
    return [
        pltpu.VMEM((4, 2 * OWN, WIDTH), BF),
        pltpu.VMEM((4, OWN, WIDTH), BF),
        pltpu.VMEM((3, OWN, WIDTH), BF),
        pltpu.VMEM((2, OWN // 2, WIDTH), BF),
        pltpu.VMEM((2, OWN, WIDTH), BF),
        pltpu.SemaphoreType.DMA((8,)),
        pltpu.SemaphoreType.DMA((8,)),
    ]


def head_norm(value):
    return lax.rsqrt(jnp.mean(value * value, axis=1, keepdims=True) + EPS)


def turn(value, cosine, sine):
    return value * cosine + pltpu.roll(value, HEAD // 2, 1) * sine


def turn_back(value, cosine, sine):
    return value * cosine - pltpu.roll(value, HEAD // 2, 1) * sine


LOG2 = math.log2(math.e)
SCALE = 1.0 / math.sqrt(HEAD)
QROWS = 256


def allowed_keys(start, first, keys):
    slots = lax.broadcasted_iota(jnp.int32, (QROWS, keys), 1)
    query = lax.broadcasted_iota(jnp.int32, (QROWS, keys), 0) + first
    return (slots >= start) & (slots <= query)


FREQ = np.tile(THETA ** (-(np.arange(HEAD // 2) * 2.0 / HEAD)), 2)[None].astype(np.float32)


def forward_kernel(
    tok, og, norm1, norm2, q_gain, k_gain, freq, lengths, groups, starts, w_qkv, w_gu, w_out, w_down,
    h2_o, g_o, wq_o, wo_o, wg_o, wd_o, h1t_o, raw_o, q_o, k_o, att_o, lse_o, mid_o, gain_o, x_o, start_o, cos_o, sin_o, ggu_o, hid_o,
    x, h1, h1t, h2, g, wq, wo, wg, wd, raw, qs, ks, att, lse, mid, gain, gains, start, cosine, sine,
    q_raw, q_cut, q_raw_part, q_part, g_raw, g_cut, g_raw_part, g_part,
    xs, xr, gs, gr, hs, hr,
    parts, theirs, sums, near, full, rs_s, rs_r,
    zs, zr, ps, pr, ns, nr, loc_s, out_s, raw_s, row_s,
    y0s, y0r, y1s, y1r, y2s, y2r, y3s, y3r,
):
    p, row, col, z, k = place()
    px, py = dp_place()
    me = 2 * z + k
    lo = z % 2
    other = z + 1 - 2 * lo
    peer = on_ring(z, 1 - k)
    piece_rows = pl.ds(pl.multiple_of(p * 32, 32), 32)

    def lanes(first, count):
        return pl.ds(pl.multiple_of(first, 256), count)

    raws = [
        pltpu.make_async_copy(src, dst, raw_s.at[i])
        for i, (src, dst) in enumerate(
            [
                (w_qkv.at[piece_rows], q_raw_part),
                (w_gu.at[piece_rows, :, lanes((1 - lo) * 2 * UNITS, 2 * UNITS)], g_raw_part),
                (w_qkv, q_raw),
                (w_gu.at[:, :, lanes(lo * 2 * UNITS, 2 * UNITS)], g_raw),
            ]
        )
    ]
    for copy in raws:
        copy.start()
    gains[0:1] = norm1[...]
    gains[1:2] = norm2[...]
    meet(ring_friends() + xy_friends())

    raws[0].wait()
    for kk in range(2):
        q_part[kk] = jnp.where(lo == 0, q_raw_part[:, 2 + kk, :], q_raw_part[:, kk, :])

    gain[col] = gains[...]
    gain_copies = [
        remote(gains, gain.at[col], ns.at[i], nr.at[col], device)
        for i, device in enumerate([peer, on_ring(other, k), on_ring(other, 1 - k)])
    ]
    weights = [wq, wo, wg, wd]
    sources = [q_part, w_out, g_part, w_down]
    blocks = [q_cut, w_out, g_cut, w_down]

    def cell(weight, c, xx, yy, cols=slice(None)):
        between = (slice(None),) * (len(weight.shape) - 5)
        return weight.at[(c, *between, xx, yy, slice(None), cols)]

    def crossing(a, kk):
        target = 2 * (1 - lo) + kk
        src = sources[a].at[kk] if a % 2 == 0 else cell(sources[a], target, px, py)
        return remote(src, cell(weights[a], col, px, py), zs.at[a, kk], zr.at[a, k], on_ring(other, kk))

    def crossed(a, kk):
        dst = cell(weights[a], 2 * (1 - lo) + kk, px, py)
        return remote(dst, dst, zs.at[a, kk], zr.at[a, kk], peer)

    def beside(a):
        there = 2 * lo + 1 - k
        src, dst = (blocks[a].at[k], blocks[a].at[1 - k]) if a % 2 == 0 else (blocks[a].at[col], blocks[a].at[there])
        keep = pltpu.make_async_copy(src, weights[a].at[col], loc_s.at[a])
        give = remote(dst, weights[a].at[col], ps.at[a], pr.at[a], peer)
        take = remote(weights[a].at[there], weights[a].at[there], ps.at[a], pr.at[a], peer)
        return keep, give, take

    def spread_at(a):
        weight = weights[a]
        half_lanes = weight.shape[-1] // 2

        def at(half, xx, yy, part):
            xs_ = slice(None) if xx is None else xx
            ys_ = slice(None) if yy is None else yy
            cols = slice(None) if part is None else pl.ds(part * half_lanes, half_lanes)
            return cell(weight, 2 * (1 - lo) + half, xs_, ys_, cols)

        return at

    spreads = [
        Spread(spread_at(a), send, recv)
        for a, (send, recv) in enumerate([(y0s, y0r), (y1s, y1r), (y2s, y2r), (y3s, y3r)])
    ]

    for a in (0, 1):
        for kk in range(2):
            crossing(a, kk).start()
    x_gather = Gather(tile_at(x), xs, xr, tok)
    x_gather.start()
    for copy in gain_copies:
        copy.start()
    keep_x = pltpu.make_async_copy(tok, tile_at(x)(me), loc_s.at[4])
    keep_x.start()
    keep_g = pltpu.make_async_copy(og, tile_at(g)(me), loc_s.at[5])
    keep_g.start()
    raws[2].wait()

    @pl.loop(0, 16)
    def _(i):
        rows = pl.ds(pl.multiple_of(i * 32, 32), 32)
        for kk in range(2):
            q_cut[kk, i // 4, i % 4] = jnp.where(lo == 0, q_raw[rows, kk, :], q_raw[rows, 2 + kk, :])

    for a in (0, 1):
        beside(a)[0].start()
        beside(a)[1].start()
    for a in (0, 1):
        for kk in range(2):
            crossed(a, kk).wait_recv()
        spreads[a].start(0)
    for a in (1, 3):
        raws[a].wait()
    slot = (
        lax.broadcasted_iota(jnp.int32, (8, HEAD), 0) * HEAD + lax.broadcasted_iota(jnp.int32, (8, HEAD), 1)
    ).astype(F32)

    def one_sequence(i, begun):
        first = starts[i].astype(F32)
        last = first + jnp.where(groups[i] == p, lengths[i], 0).astype(F32)
        return jnp.where((slot >= first) & (slot < last), first, begun)

    begun = lax.fori_loop(0, lengths.shape[0], one_sequence, jnp.zeros((8, HEAD), F32))
    for i in range(8):
        rows = slice(i * HEAD, (i + 1) * HEAD)
        begin = jnp.broadcast_to(begun[i : i + 1], (HEAD, HEAD)).T
        there = lax.broadcasted_iota(jnp.int32, (HEAD, HEAD), 0).astype(F32) + float(i * HEAD)
        angle = (there - begin) * freq[...]
        start[rows] = begin.astype(jnp.int32)
        cosine[rows] = jnp.cos(angle)
        lane = lax.broadcasted_iota(jnp.int32, (HEAD, HEAD), 1)
        sine[rows] = jnp.where(lane < HEAD // 2, -1.0, 1.0) * jnp.sin(angle)
    for a in (0, 1):
        spreads[a].pass_on(0)
    for u in range(3):
        for half in range(2):
            into = slice(u * 512 + half * 256, u * 512 + half * 256 + 256)
            for kk in range(2):
                cols = slice(kk * UNITS + u * 256, kk * UNITS + u * 256 + 256)
                g_part[kk, :, into] = g_raw_part[:, half, cols]
    for a in (0, 1):
        spreads[a].wait(0)
        spreads[a].start(1)
    for a in (0, 1):
        spreads[a].pass_on(1)
    x_gather.forward()
    for c in range(4):

        @pl.when(c != col)
        def _():
            remote(gain.at[c], gain.at[c], ns.at[0], nr.at[c], peer).wait_recv()

    keep_x.wait()
    x_gather.finish([4, 5, 6])

    def gain_row(which):
        return jnp.concatenate([gain[c, which : which + 1] for c in range(4)], axis=1)

    gain_one = gain_row(0)

    def norm_one(half):
        @pl.loop(0, TILE // 64)
        def _(i):
            rows = pl.ds(pl.multiple_of(half * TILE + i * 64, 64), 64)
            value = x[rows].astype(F32)
            h1[rows] = (value * head_norm(value) * gain_one).astype(BF)

    def heads(half):
        @pl.loop(0, TILE // 256)
        def _(i):
            rows = pl.ds(pl.multiple_of(half * TILE + i * 256, 256), 256)
            mixed = mm(h1[rows], wq[...].reshape(WIDTH, 4 * HEAD)).astype(BF)
            raw[rows] = mixed
            cos_rows, sin_rows = cosine[rows], sine[rows]
            for piece in range(3):
                value = mixed[:, piece * HEAD : (piece + 1) * HEAD].astype(F32)
                by = q_gain[...] if piece < 2 else k_gain[...]
                turned = turn(value * head_norm(value) * by, cos_rows, sin_rows).astype(BF)
                if piece < 2:
                    qs[piece, rows] = turned
                else:
                    ks[rows] = turned

    norm_one(row)
    for a in range(2):
        keep, _, take = beside(a)
        keep.wait()
        take.wait_recv()
        spreads[a].wait(1)
    heads(row)
    x_gather.share()
    for a in (2, 3):
        for kk in range(2):
            crossing(a, kk).start()
    beside(3)[0].start()
    beside(3)[1].start()
    x_gather.finish([7, 8])
    norm_one(1 - row)
    heads(1 - row)
    g_gather = Gather(tile_at(g), gs, gr, og)
    g_gather.start()
    saves = [
        pltpu.make_async_copy(src, dst, out_s.at[i])
        for i, (src, dst) in enumerate(
            [
                (wq, wq_o), (raw, raw_o), (qs, q_o), (ks, k_o), (gain, gain_o),
                (x.at[pl.ds(pl.multiple_of(me * OWN, OWN), OWN)], x_o), (wo, wo_o),
                (att, att_o), (lse, lse_o), (g, g_o), (mid, mid_o), (h2, h2_o), (h1t, h1t_o), (start, start_o), (cosine, cos_o), (sine, sin_o),
            ]
        )
    ]
    for i in (0, 1, 2, 3, 4, 5, 6, 13, 14, 15):
        saves[i].start()

    for block in range(GROUP // QROWS):
        first, keys = block * QROWS, (block + 1) * QROWS
        rows = pl.ds(first, QROWS)
        allowed = allowed_keys(start[rows, :1], first, keys)

        @pl.loop(0, 2)
        def _(h):
            score = mm_t(qs[h, rows], ks[:keys]) * (SCALE * LOG2)
            score = jnp.where(allowed, score, -1e30)
            peak = jnp.max(score, axis=1, keepdims=True)
            weight = jnp.exp2(score - peak)
            total = jnp.sum(weight, axis=1, keepdims=True)
            out = mm(weight.astype(BF), raw[:keys, 3 * HEAD :]) / total
            att[h, rows] = out.astype(BF)
            lse[h, rows] = jnp.broadcast_to(peak + jnp.log2(total), (QROWS, HEAD))

    saves[7].start()
    saves[8].start()
    for a in (2, 3):
        for kk in range(2):
            crossed(a, kk).wait_recv()
        spreads[a].start(0)

    scatter = Scatter(parts, theirs, sums, near, full, rs_s, rs_r)

    def project(d):
        rows = pl.ds(pl.multiple_of((z + d) % 4 * 256, 256), 256)
        left = jnp.concatenate([att[0, rows], att[1, rows]], axis=1)
        for c in range(4):
            parts[d, :, c * TILE : (c + 1) * TILE] = mm(left, wo[c].reshape(256, TILE)).astype(BF)
        scatter.put(d)

    project(2)
    project(1)
    scatter.across()
    project(3)
    project(0)
    for a in (2, 3):
        spreads[a].pass_on(0)

    @pl.loop(0, 8)
    def _(i):
        cols = pl.ds(pl.multiple_of(i * 256, 256), 256)
        h1t[cols] = h1[:, cols].T

    saves[12].start()
    scatter.beside(0)
    scatter.beside(1)
    g_gather.forward()
    for a in (2, 3):
        spreads[a].wait(0)
        spreads[a].start(1)


    @pl.loop(0, 16)
    def _(i):
        rows = pl.ds(pl.multiple_of(i * 32, 32), 32)
        for u in range(3):
            for half in range(2):
                into = slice(u * 512 + half * 256, u * 512 + half * 256 + 256)
                for kk in range(2):
                    cols = slice(kk * UNITS + u * 256, kk * UNITS + u * 256 + 256)
                    g_cut[kk, i // 4, i % 4, :, into] = g_raw[rows, half, cols]

    beside(2)[0].start()
    beside(2)[1].start()
    for a in (2, 3):
        spreads[a].pass_on(1)
    g_gather.share()
    scatter.arrive()
    gain_two = gain_row(1)

    @pl.loop(0, OWN // 16)
    def _(i):
        first = pl.multiple_of(i * 16, 16)
        there = pl.ds(pl.multiple_of(me * OWN + first, 16), 16)
        value = x[there].astype(F32) + scatter.total(first, 16)
        mid[pl.ds(first, 16)] = value
        h2[there] = (value * head_norm(value) * gain_two).astype(BF)

    saves[10].start()
    h2_gather = Gather(rows_at(h2), hs, hr)
    h2_gather.start()
    x_gather.drain()
    saves[5].wait()
    for a in (2, 3):
        keep, _, take = beside(a)
        keep.wait()
        take.wait_recv()
        spreads[a].wait(1)
    weight_saves = [pltpu.make_async_copy(weights[a], (wg_o, wd_o)[a - 2], loc_s.at[a + 4]) for a in (2, 3)]
    for copy in weight_saves:
        copy.start()
    row_saves = []

    def feed(d):
        rows = pl.ds(pl.multiple_of((z + d) % 4 * 256, 256), 256)

        @pl.loop(0, 3)
        def _(u):
            wide = pl.ds(pl.multiple_of(u * 512, 512), 512)
            gate_cols = pl.ds(pl.multiple_of(u * 512, 256), 256)
            up_cols = pl.ds(pl.multiple_of(u * 512 + 256, 256), 256)
            pair = mm(h2[rows], wg[:, :, :, :, wide].reshape(WIDTH, 512))
            back = mm_t(g[rows, :TILE], wd[0, u].reshape(256, TILE))
            for c in range(1, 4):
                back += mm_t(g[rows, c * TILE : (c + 1) * TILE], wd[c, u].reshape(256, TILE))
            gate, up = pair[:, :256], pair[:, 256:]
            sig = 1.0 / (1.0 + jnp.exp(-gate))
            silu = gate * sig
            h1[rows, pl.ds(pl.multiple_of(u * 256, 256), 256)] = (silu * up).astype(BF)
            x[rows, gate_cols] = (back * up * sig * (1.0 + gate * (1.0 - sig))).astype(BF)
            x[rows, up_cols] = (back * silu).astype(BF)

        for i, (src, dst) in enumerate(
            [
                (h2.at[rows], h2_o.at[rows]),
                (x.at[rows, pl.ds(0, 2 * UNITS)], ggu_o.at[rows]),
                (h1.at[rows, pl.ds(0, UNITS)], hid_o.at[rows]),
            ]
        ):
            copy = pltpu.make_async_copy(src, dst, row_s.at[d, i])
            copy.start()
            row_saves.append(copy)

    g_gather.finish()
    keep_g.wait()
    saves[9].start()
    h2_gather.finish([4])
    feed(0)
    h2_gather.forward()
    h2_gather.finish([5, 6])
    feed(1)
    h2_gather.share()
    feed(3)
    h2_gather.finish([7, 8])
    feed(2)
    for copy in gain_copies:
        copy.wait_send()
    for a in range(4):
        beside(a)[1].wait_send()
        for kk in range(2):
            crossing(a, kk).wait_send()
    for spread in spreads:
        spread.drain()
    g_gather.drain()
    h2_gather.drain()
    scatter.drain()
    for i, copy in enumerate(saves):
        if i not in (5, 11):
            copy.wait()
    for copy in weight_saves + row_saves:
        copy.wait()


def forward_call(*args):
    hbm = pl.BlockSpec(memory_space=pl.ANY)
    vmem = pl.BlockSpec(memory_space=pltpu.VMEM)
    smem = pl.BlockSpec(memory_space=pltpu.SMEM)
    dma = pltpu.SemaphoreType.DMA

    def out(shape, dtype=BF):
        return jax.ShapeDtypeStruct(shape, dtype)

    wide = (GROUP, WIDTH)
    return pl.pallas_call(
        forward_kernel,
        out_shape=[
            out(wide), out(wide), out((4, 4, 4, 32, 512)), out((4, 4, 4, 16, TILE)), out((4, 4, 4, 32, 2 * UNITS)),
            out((4, 3, 4, 4, 16, TILE)), out((WIDTH, GROUP)), out((GROUP, 512)), out((2, GROUP, HEAD)), out((GROUP, HEAD)),
            out((2, GROUP, HEAD)), out((2, GROUP, HEAD), F32), out((OWN, WIDTH), F32), out((4, 8, TILE), F32),
            out((OWN, WIDTH)), out((GROUP, HEAD), jnp.int32), out((GROUP, HEAD), F32), out((GROUP, HEAD), F32),
            out((GROUP, 2 * UNITS)), out((GROUP, UNITS)),
        ],
        in_specs=[vmem] * 7 + [smem] * 3 + [hbm] * 4,
        out_specs=[hbm] * 20,
        scratch_shapes=[
            pltpu.VMEM(wide, BF), pltpu.VMEM(wide, BF), pltpu.VMEM((WIDTH, GROUP), BF), pltpu.VMEM(wide, BF),
            pltpu.VMEM(wide, BF), pltpu.VMEM((4, 4, 4, 32, 512), BF), pltpu.VMEM((4, 4, 4, 16, TILE), BF),
            pltpu.VMEM((4, 4, 4, 32, 2 * UNITS), BF), pltpu.VMEM((4, 3, 4, 4, 16, TILE), BF),
            pltpu.VMEM((GROUP, 512), BF), pltpu.VMEM((2, GROUP, HEAD), BF), pltpu.VMEM((GROUP, HEAD), BF),
            pltpu.VMEM((2, GROUP, HEAD), BF), pltpu.VMEM((2, GROUP, HEAD), F32), pltpu.VMEM((OWN, WIDTH), F32),
            pltpu.VMEM((4, 8, TILE), F32), pltpu.VMEM((8, TILE), F32), pltpu.VMEM((GROUP, HEAD), jnp.int32),
            pltpu.VMEM((GROUP, HEAD), F32), pltpu.VMEM((GROUP, HEAD), F32),
            pltpu.VMEM((TILE, 4, 512), BF), pltpu.VMEM((2, 4, 4, 32, 512), BF), pltpu.VMEM((32, 4, 512), BF),
            pltpu.VMEM((2, 32, 512), BF), pltpu.VMEM((TILE, 2, 2 * UNITS), BF), pltpu.VMEM((2, 4, 4, 32, 2 * UNITS), BF),
            pltpu.VMEM((32, 2, 2 * UNITS), BF), pltpu.VMEM((2, 32, 2 * UNITS), BF),
        ]
        + GATHER_SEMS * 3
        + scatter_scratch()
        + [dma((4, 2)), dma((4, 2)), dma((4,)), dma((4,)), dma((3,)), dma((4,)), dma((8,)), dma((16,)), dma((4,)), dma((4, 3))]
        + SPREAD_SEMS * 4,
        compiler_params=pltpu.CompilerParams(
            collective_id=1, has_side_effects=True, vmem_limit_bytes=VMEM_LIMIT
        ),
        cost_estimate=pl.CostEstimate(flops=14_000_000_000, bytes_accessed=60_000_000, transcendentals=2_000_000),
        name="forward",
    )(*args)


class Collapse:
    def __init__(self, which, data, near, full, done, send, recv):
        here = dp_place()
        self.which, self.data, self.near, self.full, self.done, self.here = which, data, near, full, done, here
        self.copies = {}
        for half in range(2):
            for phase in range(2):
                axis = half ^ phase

                def copy(slot, src, dst, o):
                    index = (which, half, phase, slot)
                    return remote(src, dst, send.at[index], recv.at[index], along(axis, o))

                self.copies[half, phase] = [
                    copy(0, self.block(half, phase, 2, 0), near[phase].at[half, 0], 1),
                    copy(1, self.block(half, phase, 2, 1), near[phase].at[half, 1], 3),
                    copy(2, self.block(half, phase, 1), full[phase].at[half, 0], 1),
                    copy(3, self.block(half, phase, 3), full[phase].at[half, 1], 3),
                ]

    def at(self, half, phase, o):
        there = (self.here[half ^ phase] + o) % 4
        if phase == 0:
            return (there, slice(None)) if half == 0 else (slice(None), there)
        return (self.here[0], there) if half == 0 else (there, self.here[1])

    def block(self, half, phase, o, part=None):
        which = pl.ds(2 * half, 2) if part is None else 2 * half + part
        return self.data.at[(*self.at(half, phase, o), which)]

    def cell(self, half, phase, o, a, c):
        x, y = self.at(half, phase, o)
        x, y = (a if isinstance(x, slice) else x), (a if isinstance(y, slice) else y)
        return (x, y, 2 * half + c)

    def start(self, phase=0):
        for half in range(2):
            for slot in range(2):
                self.copies[half, phase][slot].start()

    def mid(self, phase=0):
        for half in range(2):
            for slot in range(2):
                self.copies[half, phase][slot].wait_recv()

                def add(a):
                    index = self.cell(half, phase, (1, 3)[slot], a, slot)
                    here = (half, slot, a) if phase == 0 else (half, slot)
                    self.data[index] = (
                        self.data[index].astype(F32) + self.near[phase][here].astype(F32)
                    ).astype(BF)

                if phase == 0:
                    pl.loop(0, 4)(add)
                else:
                    add(0)
                self.copies[half, phase][2 + slot].start()

    def first(self):
        for half in range(2):
            for slot in range(2):
                self.copies[half, 0][2 + slot].wait_recv()

            @pl.loop(0, 4)
            def _(a):
                for c in range(2):
                    index = self.cell(half, 0, 0, a, c)
                    total = self.data[index].astype(F32)
                    for slot in range(2):
                        total += self.full[0][half, slot, a, c].astype(F32)
                    self.data[index] = total.astype(BF)

        self.start(1)

    def second(self):
        for half in range(2):
            for slot in range(2):
                self.copies[half, 1][2 + slot].wait_recv()
            for c in range(2):
                total = self.data[self.cell(half, 1, 0, 0, c)].astype(F32)
                for slot in range(2):
                    total += self.full[1][half, slot, c].astype(F32)
                self.done[self.which, 2 * half + c] = total.astype(BF)

    def drain(self):
        for copies in self.copies.values():
            for copy in copies:
                copy.wait_send()


CHUNKS, BUFFERS = 4, 3


def collapse_scratch():
    dma = pltpu.SemaphoreType.DMA
    return (
        [pltpu.VMEM((4, 4, 4, 48, 512), BF)] * BUFFERS
        + [pltpu.VMEM((2, 2, 4, 48, 512), BF)] * BUFFERS
        + [pltpu.VMEM((2, 2, 48, 512), BF)] * BUFFERS
        + [pltpu.VMEM((2, 2, 4, 2, 48, 512), BF)] * BUFFERS
        + [pltpu.VMEM((2, 2, 2, 48, 512), BF)] * BUFFERS
        + [pltpu.VMEM((CHUNKS, 4, 48, 512), BF), dma((CHUNKS, 2, 2, 4)), dma((CHUNKS, 2, 2, 4))]
        + [dma((CHUNKS, 3)), dma((CHUNKS, 4)), dma((CHUNKS, 2, 2, 4)), dma((CHUNKS, 2, 2, 4))]
    )


class Trade:
    def __init__(self, block, slot, send, recv, which=()):
        _, row, col, z, k = place()
        self.col, self.peer = col, on_ring(z, 1 - k)
        self.recv, self.send, self.slot, self.which = recv, send, slot, which
        self.copies = [
            remote(block((col + o) % 4), slot(col), send.at[(*which, o - 1)], recv.at[(*which, o - 1)], {"col": (col + o) % 4})
            for o in range(1, 4)
        ]
        self.keep = pltpu.make_async_copy(block(col), slot(col), recv.at[(*which, 3)])

    def start(self):
        for copy in self.copies:
            copy.start()
        self.keep.start()

    def finish(self):
        for o in range(1, 4):
            dst = self.slot((self.col - o + 4) % 4)
            sems = (self.send.at[(*self.which, o - 1)], self.recv.at[(*self.which, o - 1)])
            remote(dst, dst, *sems, self.peer).wait_recv()
        self.keep.wait()

    def drain(self):
        for copy in self.copies:
            copy.wait_send()


def norm_back(grad, value, gain):
    scale = head_norm(value)
    weighted = grad * gain
    inner = jnp.mean(weighted * value, axis=1, keepdims=True)
    return scale * weighted - value * (scale * scale * scale * inner), grad * value * scale


def norm_back(grad, value, gain):
    scale = head_norm(value)
    weighted = grad * gain
    inner = jnp.mean(weighted * value, axis=1, keepdims=True)
    return scale * weighted - value * (scale * scale * scale * inner), grad * value * scale


def backward_kernel(
    h2_i, ggu_i, hid_i, g_i, wg_i, wd_i, wo_i, wq_i, h1t_i, raw_i, q_i, k_i, att_i, lse_i, mid_i, gain_i, x_i,
    start_i, cos_i, sin_i, q_gain, k_gain,
    result_o, stream_o, grads_o, sums_o,
    m, gm, dqkv, mid, gain, x_own, g_own, acc, head_acc, tile_f, tile_b, totals, heard,
    ms, mr,
    parts, theirs, psums, near, full, rs_s, rs_r,
    data0, data1, data2, near0, near1, near2, next0, next1, next2, full0, full1, full2, last0, last1, last2,
    done, c_s, c_r, t_s, t_r, a_s, a_r,
    fs, fr, ls, lr, as_, ar, in_s, free,
):
    p, row, col, z, k = place()
    px, py = dp_place()
    me = 2 * z + k
    up, down, peer = on_ring((z + 1) % 4, k), on_ring((z + 3) % 4, k), on_ring(z, 1 - k)
    far = on_ring((z + 2) % 4, k)
    loads = []

    def load(src, dst):
        copy = pltpu.make_async_copy(src, dst, in_s.at[len(loads)])
        copy.start()
        loads.append(copy)
        return copy

    def wait(copies):
        for copy in copies:
            copy.wait()

    collapses, trades, spreads = [], [], []
    datas, nears, nexts = (data0, data1, data2), (near0, near1, near2), (next0, next1, next2)
    fulls, lasts = (full0, full1, full2), (last0, last1, last2)

    def chunk(i):
        def at(half, x, y, part):
            xs = slice(None) if x is None else x
            ys = slice(None) if y is None else y
            which = pl.ds(2 * half, 2) if part is None else 2 * half + part
            return grads_o.at[i, xs, ys, which]

        b = i % BUFFERS
        collapses.append(Collapse(i, datas[b], (nears[b], nexts[b]), (fulls[b], lasts[b]), done, c_s, c_r))
        trades.append(
            Trade(lambda c: done.at[i, c], lambda c: grads_o.at[i, px, py, c], t_s, t_r, (i,))
        )
        spreads.append(Spread(at, a_s, a_r, (i,)))

    for i in range(CHUNKS):
        chunk(i)
    scatter = Scatter(parts, theirs, psums, near, full, rs_s, rs_r)
    stream_trade = Trade(
        lambda c: tile_f.at[:, pl.ds(pl.multiple_of(c * TILE, TILE), TILE)],
        lambda c: stream_o.at[pl.ds(pl.multiple_of(c * OWN, OWN), OWN)], fs, fr,
    )
    result_trade = Trade(
        lambda c: tile_b.at[:, pl.ds(pl.multiple_of(c * TILE, TILE), TILE)],
        lambda c: result_o.at[pl.ds(pl.multiple_of(c * OWN, OWN), OWN)], ls, lr,
    )

    def release():
        scatter.drain()
        for device in (up, down, peer):
            pl.semaphore_signal(free, inc=1, device_id=device, device_id_type=MESH)

    def project(d, product):
        rows = pl.ds(pl.multiple_of((z + d) % 4 * 256, 256), 256)

        @pl.loop(0, 4)
        def _(c):
            cols = pl.ds(pl.multiple_of(c * TILE, TILE), TILE)
            parts[d, :, cols] = product(rows, c, cols).astype(BF)

        scatter.put(d)

    def weight_grads(i, first, second):
        data = datas[i % BUFFERS]
        for c in range(4):
            cols = slice(c * TILE, (c + 1) * TILE)
            data[:, :, c, :32] = first(cols).astype(BF).reshape(4, 4, 32, 512)
            data[:, :, c, 32:] = second(cols).astype(BF).reshape(4, 4, 16, 512)
        collapses[i].start()

    def gain_row(which):
        return jnp.concatenate([gain[c, which : which + 1] for c in range(4)], axis=1)

    own_rows = pl.ds(pl.multiple_of(me * OWN, OWN), OWN)

    def stage_one(h2, g, ggu, hid, wg):
        first_loads = [load(ggu_i, ggu), load(wg_i, wg)]
        more_loads = [load(h2_i, h2), load(hid_i, hid), load(g_i, g)]
        meet(ring_friends() + [far] + xy_friends())
        def grads(u):
            weight_grads(
                u,
                lambda cols: t_mm(h2[:, cols], ggu[:, u * 512 : (u + 1) * 512]),
                lambda cols: t_mm(hid[:, u * 256 : (u + 1) * 256], g[:, cols]),
            )

        def product(rows, c, cols):
            return mm_t(ggu[rows], wg[c])

        wait(first_loads)
        project(2, product)
        project(1, product)
        wait(more_loads)
        grads(0)
        scatter.across()
        project(3, product)
        project(0, product)
        collapses[0].mid()
        scatter.beside(0)
        scatter.beside(1)
        grads(1)
        grads(2)
        collapses[0].first()

    early = [load(mid_i, mid), load(gain_i, gain), load(x_i, x_own), load(g_i.at[own_rows], g_own)]
    pl.run_scoped(
        stage_one,
        pltpu.VMEM((GROUP, WIDTH), BF), pltpu.VMEM((GROUP, WIDTH), BF), pltpu.VMEM((GROUP, 2 * UNITS), BF),
        pltpu.VMEM((GROUP, UNITS), BF), pltpu.VMEM((4, TILE, 2 * UNITS), BF),
    )

    def stage_two(wo, att, qs, ks, raw, lse, ga, dk, dv, h1t, wq, att_t, start, cosine, sine):
        l_wo, l_att = load(wo_i, wo), load(att_i, att)
        l_heads = [
            load(q_i, qs), load(k_i, ks), load(raw_i, raw), load(lse_i, lse),
            load(start_i, start), load(cos_i, cosine), load(sin_i, sine),
        ]
        l_last = [load(h1t_i, h1t), load(wq_i, wq)]
        wait(early)
        acc[...] = jnp.zeros_like(acc)
        head_acc[...] = jnp.zeros_like(head_acc)
        dk[...] = jnp.zeros_like(dk)
        dv[...] = jnp.zeros_like(dv)
        totals[0] = jnp.zeros((8, WIDTH), F32)
        gain_two = gain_row(1)
        scatter.arrive()

        @pl.loop(0, OWN // 16)
        def _(i):
            rows = pl.ds(pl.multiple_of(i * 16, 16), 16)
            back, gained = norm_back(scatter.total(pl.multiple_of(i * 16, 16), 16), mid[rows], gain_two)
            acc[1] += gained
            back = back + g_own[rows].astype(F32)
            gm[rows] = back
            m[pl.ds(pl.multiple_of(me * OWN + i * 16, 16), 16)] = back.astype(BF)

        m_gather = Gather(rows_at(m), ms, mr)
        m_gather.start()
        release()
        collapses[1].mid()
        collapses[2].mid()
        collapses[0].mid(1)
        l_att.wait()
        for h in range(2):
            att_t[h * HEAD : (h + 1) * HEAD] = att[h].T
        collapses[1].first()
        m_gather.forward()
        l_wo.wait()
        wait(l_heads)
        m_gather.share()
        collapses[2].first()
        m_gather.finish()
        collapses[0].second()
        trades[0].start()

        @pl.loop(0, 4)
        def _(i):
            rows = pl.ds(pl.multiple_of(i * 256, 256), 256)
            back = mm_t(m[rows, :TILE], wo[0])
            for c in range(1, 4):
                back += mm_t(m[rows, c * TILE : (c + 1) * TILE], wo[c])
            for h in range(2):
                ga[h, rows] = back[:, h * HEAD : (h + 1) * HEAD].astype(BF)

        collapses[1].mid(1)
        collapses[2].mid(1)
        for block in range(GROUP // QROWS):
            first, keys = block * QROWS, (block + 1) * QROWS
            rows = pl.ds(first, QROWS)
            allowed = allowed_keys(start[rows, :1], first, keys)

            @pl.loop(0, 2)
            def _(h):
                cols = pl.ds(pl.multiple_of(h * HEAD, HEAD), HEAD)
                score = mm_t(qs[h, rows], ks[:keys]) * (SCALE * LOG2)
                prob = jnp.exp2(jnp.where(allowed, score, -1e30) - lse[h, rows, :1])
                grad = ga[h, rows]
                delta = jnp.sum(grad.astype(F32) * att[h, rows].astype(F32), axis=1, keepdims=True)
                prob_grad = mm_t(grad, raw[:keys, 3 * HEAD :])
                score_grad = (prob * (prob_grad - delta)).astype(BF)
                dk[:keys] += t_mm(score_grad, qs[h, rows])
                dv[:keys] += t_mm(prob.astype(BF), grad)
                back = turn_back(mm(score_grad, ks[:keys]) * SCALE, cosine[rows], sine[rows])
                back, gained = norm_back(back, raw[rows, cols].astype(F32), q_gain[...])
                dqkv[rows, cols] = back.astype(BF)
                head_acc[0:1] += jnp.sum(gained, axis=0, keepdims=True)

            if block == 0:
                trades[0].finish()
                spreads[0].start(0)
                collapses[1].second()
                trades[1].start()
            if block == 1:
                spreads[0].pass_on(0)
                collapses[2].second()
                trades[2].start()
            if block == 2:
                spreads[0].wait(0)
                spreads[0].start(1)
                trades[1].finish()
                spreads[1].start(0)


        @pl.loop(0, 4)
        def _(i):
            rows = pl.ds(pl.multiple_of(i * 256, 256), 256)
            back = turn_back(dk[rows] * SCALE, cosine[rows], sine[rows])
            back, gained = norm_back(back, raw[rows, 2 * HEAD : 3 * HEAD].astype(F32), k_gain[...])
            dqkv[rows, 2 * HEAD : 3 * HEAD] = back.astype(BF)
            dqkv[rows, 3 * HEAD :] = dv[rows].astype(BF)
            head_acc[1:2] += jnp.sum(gained, axis=0, keepdims=True)

        trades[2].finish()
        spreads[2].start(0)
        wait(l_last)
        collapses[0].drain()
        weight_grads(3, lambda cols: mm(h1t[cols], dqkv[...]), lambda cols: mm(att_t[...], m[:, cols]))
        pl.semaphore_wait(free, 3)

        def product(rows, c, cols):
            return mm_t(dqkv[rows], wq[c])

        project(2, product)
        project(1, product)
        spreads[0].pass_on(1)
        spreads[1].pass_on(0)
        scatter.across()
        project(3, product)
        project(0, product)
        spreads[2].pass_on(0)
        collapses[3].mid()
        scatter.beside(0)
        scatter.beside(1)
        spreads[1].wait(0)
        spreads[1].start(1)
        m_gather.drain()

    pl.run_scoped(
        stage_two,
        pltpu.VMEM((4, 256, TILE), BF), pltpu.VMEM((2, GROUP, HEAD), BF), pltpu.VMEM((2, GROUP, HEAD), BF),
        pltpu.VMEM((GROUP, HEAD), BF), pltpu.VMEM((GROUP, 512), BF), pltpu.VMEM((2, GROUP, HEAD), F32),
        pltpu.VMEM((2, GROUP, HEAD), BF), pltpu.VMEM((GROUP, HEAD), F32), pltpu.VMEM((GROUP, HEAD), F32),
        pltpu.VMEM((WIDTH, GROUP), BF), pltpu.VMEM((4, TILE, 512), BF), pltpu.VMEM((2 * HEAD, GROUP), BF),
        pltpu.VMEM((GROUP, HEAD), jnp.int32), pltpu.VMEM((GROUP, HEAD), F32), pltpu.VMEM((GROUP, HEAD), F32),
    )

    def stage_three(hid, wd):
        last = [load(hid_i, hid), load(wd_i, wd)]
        gain_one = gain_row(0)
        scatter.arrive()

        @pl.loop(0, OWN // 16)
        def _(i):
            rows = pl.ds(pl.multiple_of(i * 16, 16), 16)
            back, gained = norm_back(
                scatter.total(pl.multiple_of(i * 16, 16), 16), x_own[rows].astype(F32), gain_one
            )
            acc[0] += gained
            tile_f[rows] = gm[rows] + back

        stream_trade.start()
        release()
        totals[0, 0:1] = jnp.sum(acc[0], axis=0, keepdims=True)
        totals[0, 1:2] = jnp.sum(acc[1], axis=0, keepdims=True)
        totals[0, 2:3, 0:HEAD] = head_acc[0:1]
        totals[0, 2:3, HEAD : 2 * HEAD] = head_acc[1:2]
        sent = []

        def tell(phase, devices, slots):
            for device, slot in zip(devices, slots):
                copy = remote(totals.at[phase], heard.at[slot], as_.at[slot], ar.at[slot], device)
                copy.start()
                sent.append(copy)

        def listen(phase, slots):
            total = totals[phase]
            for slot in slots:
                remote(heard.at[slot], heard.at[slot], as_.at[slot], ar.at[slot], peer).wait_recv()
                total += heard[slot]
            totals[phase + 1] = total

        tell(0, [peer], [0])
        collapses[3].first()
        spreads[2].wait(0)
        listen(0, [0])
        tell(1, [up, down, far], [1, 2, 3])
        wait(last)
        pl.semaphore_wait(free, 3)

        def product(rows, c, cols):
            return mm(hid[rows], wd[c])

        project(2, product)
        project(1, product)
        collapses[3].mid(1)
        spreads[2].start(1)
        scatter.across()
        project(3, product)
        project(0, product)
        spreads[1].pass_on(1)
        collapses[3].second()
        trades[3].start()
        listen(1, [1, 2, 3])
        tell(2, [along(0, o) for o in range(1, 4)], [4, 5, 6])
        scatter.beside(0)
        scatter.beside(1)
        trades[3].finish()
        spreads[3].start(0)
        spreads[2].pass_on(1)
        spreads[3].pass_on(0)
        spreads[3].wait(0)
        spreads[3].start(1)
        listen(2, [4, 5, 6])
        tell(3, [along(1, o) for o in range(1, 4)], [7, 8, 9])
        scatter.arrive()

        @pl.loop(0, OWN // 16)
        def _(i):
            rows = pl.ds(pl.multiple_of(i * 16, 16), 16)
            tile_b[rows] = (mid[rows] + scatter.total(pl.multiple_of(i * 16, 16), 16)).astype(BF)

        result_trade.start()
        spreads[3].pass_on(1)
        listen(3, [7, 8, 9])
        sums_o[...] = totals[4]
        stream_trade.finish()
        result_trade.finish()
        for spread in spreads:
            spread.wait(1)
        scatter.drain()
        for thing in collapses[1:] + trades + spreads + [stream_trade, result_trade]:
            thing.drain()
        for copy in sent:
            copy.wait_send()

    pl.run_scoped(stage_three, pltpu.VMEM((GROUP, UNITS), BF), pltpu.VMEM((4, UNITS, TILE), BF))


def backward_call(*args):
    hbm = pl.BlockSpec(memory_space=pl.ANY)
    vmem = pl.BlockSpec(memory_space=pltpu.VMEM)
    dma = pltpu.SemaphoreType.DMA
    out = jax.ShapeDtypeStruct
    grads = out((CHUNKS, 4, 4, 4, 48, 512), BF)
    return pl.pallas_call(
        backward_kernel,
        out_shape=[out((TILE, TILE), BF), out((TILE, TILE), F32), grads, out((8, WIDTH), F32)],
        in_specs=[hbm] * 20 + [vmem] * 2,
        out_specs=[hbm] * 3 + [vmem],
        scratch_shapes=[
            pltpu.VMEM((GROUP, WIDTH), BF), pltpu.VMEM((OWN, WIDTH), F32), pltpu.VMEM((GROUP, 512), BF),
            pltpu.VMEM((OWN, WIDTH), F32), pltpu.VMEM((4, 8, TILE), F32),
            pltpu.VMEM((OWN, WIDTH), BF), pltpu.VMEM((OWN, WIDTH), BF), pltpu.VMEM((2, 16, WIDTH), F32),
            pltpu.VMEM((8, HEAD), F32), pltpu.VMEM((OWN, WIDTH), F32), pltpu.VMEM((OWN, WIDTH), BF),
            pltpu.VMEM((5, 8, WIDTH), F32), pltpu.VMEM((10, 8, WIDTH), F32),
        ]
        + GATHER_SEMS
        + scatter_scratch()
        + collapse_scratch()
        + [
            dma((3,)), dma((4,)), dma((3,)), dma((4,)), dma((10,)), dma((10,)), dma((24,)), pltpu.SemaphoreType.REGULAR,
        ],
        compiler_params=pltpu.CompilerParams(
            collective_id=2, has_side_effects=True, vmem_limit_bytes=VMEM_LIMIT
        ),
        cost_estimate=pl.CostEstimate(flops=25_000_000_000, bytes_accessed=100_000_000, transcendentals=2_000_000),
        name="backward",
    )(*args)


PLACE = 4


def place_kernel(grads, result, stream, totals, gate_up, down, qkv, out, result_o, stream_o, one, two, head):
    for c in range(4):
        for u in range(3):
            t = c * 3 + u
            value = grads[u, :, c, :32].reshape(PLACE * 32, 512).astype(F32)
            for g in range(2):
                gate_up[:, g, t * 256 : (t + 1) * 256] = value[:, g * 256 : (g + 1) * 256]
            down[t] = grads[u, :, c, 32:].astype(F32)
        qkv[:, c, :] = grads[3, :, c, :32].reshape(PLACE * 32, 512).astype(F32)
        out[c] = grads[3, :, c, 32:].astype(F32)
    result_o[...] = result[...]
    stream_o[...] = stream[...]
    one[...] = totals[0:1]
    two[...] = totals[1:2]
    head[...] = totals[2:3, : 2 * HEAD]


def place_grads(grads, result, stream, totals):
    tile = pl.BlockSpec((32 * PLACE, TILE), lambda p: (p, 0))

    def whole(*shape):
        return pl.BlockSpec(shape, lambda p: (0,) * len(shape))

    return pl.pallas_call(
        place_kernel,
        grid=(DP // PLACE,),
        in_specs=[
            pl.BlockSpec((CHUNKS, PLACE, 4, 48, 512), lambda p: (0, p, 0, 0, 0)), tile, tile, whole(8, WIDTH),
        ],
        out_specs=[
            pl.BlockSpec((32 * PLACE, 2, 4 * UNITS), lambda p: (p, 0, 0)),
            pl.BlockSpec((12, PLACE, 16, TILE), lambda p: (0, p, 0, 0)),
            pl.BlockSpec((32 * PLACE, 4, 512), lambda p: (p, 0, 0)),
            pl.BlockSpec((4, PLACE, 16, TILE), lambda p: (0, p, 0, 0)),
            tile, tile, whole(1, WIDTH), whole(1, WIDTH), whole(1, 2 * HEAD),
        ],
        out_shape=[
            jax.ShapeDtypeStruct((TILE, 2, 4 * UNITS), F32),
            jax.ShapeDtypeStruct((12, DP, 16, TILE), F32),
            jax.ShapeDtypeStruct((TILE, 4, 512), F32),
            jax.ShapeDtypeStruct((4, DP, 16, TILE), F32),
            jax.ShapeDtypeStruct((TILE, TILE), BF),
            jax.ShapeDtypeStruct((TILE, TILE), F32),
            jax.ShapeDtypeStruct((1, WIDTH), F32),
            jax.ShapeDtypeStruct((1, WIDTH), F32),
            jax.ShapeDtypeStruct((1, 2 * HEAD), F32),
        ],
        compiler_params=pltpu.CompilerParams(vmem_limit_bytes=VMEM_LIMIT),
        cost_estimate=pl.CostEstimate(flops=0, bytes_accessed=41_000_000, transcendentals=0),
        name="place",
    )(grads, result, stream, totals)


def body(
    tokens, norm1_gain, w_qkv, q_gain, k_gain, w_out, norm2_gain, w_gate_up, w_down, out_grad,
    seq_lengths, seq_group, seq_start,
):
    (h2, g, wq, wo, wg, wd, h1t, raw, qs, ks, att, lse, middle, gain, x_own, start, cosine, sine, ggu, hid) = forward_call(
        tokens, out_grad, norm1_gain[None], norm2_gain[None], q_gain[None], k_gain[None], jnp.asarray(FREQ),
        seq_lengths, seq_group, seq_start, w_qkv, w_gate_up,
        w_out.reshape(4, 4, 4, 16, TILE), w_down.reshape(4, 3, 4, 4, 16, TILE),
    )
    wg = wg.reshape(4, TILE, 2 * UNITS)
    wd = wd.reshape(4, UNITS, TILE)
    result, stream, grads, totals = backward_call(
        h2, ggu, hid, g, wg, wd, wo.reshape(4, 256, TILE), wq.reshape(4, TILE, 512), h1t, raw, qs, ks, att, lse,
        middle, gain, x_own, start, cosine, sine, q_gain[None], k_gain[None],
    )
    grads = grads.reshape(CHUNKS, DP, 4, 48, 512)
    g_gate_up, g_down, g_qkv, g_out, result, stream, one, two, head = place_grads(grads, result, stream, totals)
    return (
        result,
        stream,
        one.reshape(WIDTH),
        g_qkv,
        head[0, :HEAD],
        head[0, HEAD:],
        g_out.reshape(w_out.shape),
        two.reshape(WIDTH),
        g_gate_up,
        g_down.reshape(w_down.shape),
    )


def solution(mesh):
    in_specs = (
        P(("dp", "row"), "col"),
        P("col"),
        P("col", "row", None),
        P(),
        P(),
        P("row", "col"),
        P("col"),
        P("col", None, "row"),
        P("row", "col"),
        P(("dp", "row"), "col"),
        P(),
        P(),
        P(),
    )
    out_specs = (
        P(("dp", "row"), "col"),
        P(("dp", "row"), "col"),
        P(),
        P("col", "row", None),
        P(),
        P(),
        P("row", "col"),
        P(),
        P("col", None, "row"),
        P("row", "col"),
    )
    return jax.shard_map(body, mesh=mesh, in_specs=in_specs, out_specs=out_specs, check_vma=False)
```

```python
import math

import jax
import jax.numpy as jnp
import numpy as np
from jax import lax
from jax.experimental import pallas as pl
from jax.experimental.pallas import tpu as pltpu
from jax.sharding import PartitionSpec as P

EPS = 1e-06
THETA = 1000000.0
BF = jnp.bfloat16
F32 = jnp.float32
Z = ("row", "col")
MESH = pl.DeviceIdType.MESH
VMEM_LIMIT = 63 * 1024 * 1024

GROUP, WIDTH, TILE, UNITS, HEAD = 1024, 2048, 512, 768, 128
OWN = GROUP // 8
DP = 16


def dot(left, right, dims):
    return lax.dot_general(left, right, (dims, ((), ())), preferred_element_type=F32)


def mm(left, right):
    return dot(left, right, ((1,), (0,)))


def mm_t(left, right):
    return dot(left, right, ((1,), (1,)))


def t_mm(left, right):
    return dot(left, right, ((0,), (0,)))


def place():
    row, col = lax.axis_index("row"), lax.axis_index("col")
    j = 4 * row + col
    return lax.axis_index("dp"), row, col, j // 2, j % 2


def on_ring(z, k):
    j = 2 * z + k
    return {"row": j // 4, "col": j % 4}


def remote(src, dst, send, recv, device):
    return pltpu.make_async_remote_copy(
        src_ref=src, dst_ref=dst, send_sem=send, recv_sem=recv, device_id=device, device_id_type=MESH
    )


def meet(devices):
    barrier = pltpu.get_barrier_semaphore()
    for device in devices:
        pl.semaphore_signal(barrier, inc=1, device_id=device, device_id_type=MESH)
    pl.semaphore_wait(barrier, len(devices))


def ring_friends():
    _, _, _, z, k = place()
    other = z + 1 - 2 * (z % 2)
    return [
        on_ring((z + 1) % 4, k),
        on_ring((z + 3) % 4, k),
        on_ring(z, 1 - k),
        on_ring(other, 1 - k),
    ]


def column_friends():
    _, _, _, z, k = place()
    me = 2 * z + k
    return [on_ring((me + o) % 8 // 2, (me + o) % 2) for o in range(1, 8)]


def dp_place():
    p = lax.axis_index("dp")
    return p // 4, p % 4


def along(axis, o):
    px, py = dp_place()
    return {"dp": (px + o) % 4 * 4 + py} if axis == 0 else {"dp": px * 4 + (py + o) % 4}


def xy_friends():
    return [along(axis, o) for axis in range(2) for o in range(1, 4)]


def tile_at(buf):
    def loc(j, half=None):
        row, col = j // 4, j % 4
        first = pl.multiple_of(row * TILE, TILE)
        rows = pl.ds(first, TILE)
        if half is not None:
            rows = pl.ds(first + half * (TILE // 2), TILE // 2)
        return buf.at[rows, pl.ds(pl.multiple_of(col * TILE, TILE), TILE)]

    return loc


def rows_at(buf):
    def loc(j, half=None):
        first = pl.multiple_of(j * OWN, OWN)
        rows = pl.ds(first, OWN)
        if half is not None:
            rows = pl.ds(first + half * (OWN // 2), OWN // 2)
        return buf.at[rows]

    return loc


class Gather:
    def __init__(self, loc, send, recv, own=None):
        _, _, _, z, k = place()
        up, down, far = (z + 1) % 4, (z + 3) % 4, (z + 2) % 4
        to_up, to_down, peer = on_ring(up, k), on_ring(down, k), on_ring(z, 1 - k)

        def out(slot, src, dst, device):
            return remote(src, dst, send.at[slot], recv.at[slot], device)

        def into(slot, dst):
            return remote(dst, dst, send.at[slot], recv.at[slot], peer)

        mine = loc(2 * z + k)
        own = mine if own is None else own
        left, right, across = 2 * down + k, 2 * up + k, 2 * far + k
        self.first = [out(0, own, mine, to_up), out(1, own, mine, to_down), out(4, own, mine, peer)]
        self.from_left = [
            out(2, loc(left, 0), loc(left, 0), to_up),
            out(5, loc(left), loc(left), peer),
        ]
        self.from_right = [
            out(3, loc(right, 1), loc(right, 1), to_down),
            out(6, loc(right), loc(right), peer),
        ]
        self.from_far = [
            out(7, loc(across, 0), loc(across, 0), peer),
            out(8, loc(across, 1), loc(across, 1), peer),
        ]
        theirs = [2 * z + 1 - k, 2 * down + 1 - k, 2 * up + 1 - k, 2 * far + 1 - k]
        self.arrivals = {
            0: into(0, loc(left)),
            1: into(1, loc(right)),
            2: into(2, loc(across, 0)),
            3: into(3, loc(across, 1)),
            4: into(4, loc(theirs[0])),
            5: into(5, loc(theirs[1])),
            6: into(6, loc(theirs[2])),
            7: into(7, loc(theirs[3], 0)),
            8: into(8, loc(theirs[3], 1)),
        }

    def start(self):
        for copy in self.first:
            copy.start()

    def forward(self):
        self.arrivals[0].wait_recv()
        for copy in self.from_left:
            copy.start()
        self.arrivals[1].wait_recv()
        for copy in self.from_right:
            copy.start()

    def share(self):
        for half in range(2):
            self.arrivals[2 + half].wait_recv()
            self.from_far[half].start()

    def finish(self, slots=range(4, 9)):
        for slot in slots:
            self.arrivals[slot].wait_recv()

    def drain(self):
        for copy in self.first + self.from_left + self.from_right + self.from_far:
            copy.wait_send()


GATHER_SEMS = [pltpu.SemaphoreType.DMA((9,)), pltpu.SemaphoreType.DMA((9,))]


class Spread:
    def __init__(self, at, send, recv, which=()):
        px, py = dp_place()
        here = (px, py)
        self.out, self.into = {}, {}
        for half in range(2):
            for phase in range(2):
                axis = half ^ phase

                def block(o, part=None):
                    whose = [px, py]
                    whose[axis] = (here[axis] + o) % 4
                    if phase:
                        whose[1 - axis] = None
                    return at(half, *whose, part)

                def copy(slot, ref, o):
                    index = (*which, half, phase, slot)
                    sems = (send.at[index], recv.at[index])
                    return remote(ref, ref, *sems, along(axis, o))

                self.out[half, phase] = [
                    copy(0, block(0), 1), copy(1, block(0), 3),
                    copy(2, block(3, 0), 1), copy(3, block(1, 1), 3),
                ]
                self.into[half, phase] = [
                    copy(0, block(3), 1), copy(1, block(1), 3),
                    copy(2, block(2, 0), 1), copy(3, block(2, 1), 3),
                ]

    def start(self, phase):
        for half in range(2):
            for slot in range(2):
                self.out[half, phase][slot].start()

    def pass_on(self, phase):
        for half in range(2):
            for slot in range(2):
                self.into[half, phase][slot].wait_recv()
                self.out[half, phase][2 + slot].start()

    def wait(self, phase):
        for half in range(2):
            for slot in range(2, 4):
                self.into[half, phase][slot].wait_recv()

    def drain(self):
        for copies in self.out.values():
            for copy in copies:
                copy.wait_send()


SPREAD_SEMS = [pltpu.SemaphoreType.DMA((2, 2, 4)), pltpu.SemaphoreType.DMA((2, 2, 4))]


class Scatter:
    def __init__(self, parts, theirs, sums, near, full, send, recv):
        _, _, _, z, k = place()
        self.parts, self.theirs, self.sums, self.near, self.full = parts, theirs, sums, near, full
        self.k = k
        to_up, to_down = on_ring((z + 1) % 4, k), on_ring((z + 3) % 4, k)
        peer = on_ring(z, 1 - k)
        half = OWN // 2
        other = pl.ds(pl.multiple_of((1 - k) * OWN, OWN), OWN)

        def copy(slot, src, dst, device):
            return remote(src, dst, send.at[slot], recv.at[slot], device)

        self.copies = [copy(d, parts.at[d, other], theirs.at[d], peer) for d in range(4)] + [
            copy(4, sums.at[0, pl.ds(0, half)], near.at[0], to_up),
            copy(5, sums.at[0, pl.ds(half, half)], near.at[1], to_down),
            copy(6, sums.at[1], full.at[0], to_up),
            copy(7, sums.at[2], full.at[1], to_down),
        ]

    def put(self, d):
        self.copies[d].start()

    def own(self, d, rows, count):
        first = pl.multiple_of(self.k * OWN + rows, count)
        return self.parts[d, pl.ds(first, count)].astype(F32) + self.theirs[
            d, pl.ds(rows, count)
        ].astype(F32)

    def across(self):
        self.copies[2].wait_recv()

        @pl.loop(0, OWN // 16)
        def _(i):
            rows = pl.multiple_of(i * 16, 16)
            self.sums[0, pl.ds(rows, 16)] = self.own(2, rows, 16).astype(BF)

        self.copies[4].start()
        self.copies[5].start()

    def beside(self, side):
        d, half = (1, 3)[side], OWN // 2
        self.copies[d].wait_recv()
        self.copies[4 + side].wait_recv()

        @pl.loop(0, half // 16)
        def _(i):
            rows = pl.multiple_of(i * 16, 16)
            here = pl.multiple_of(rows + side * half, 16)
            there = pl.multiple_of(rows + (1 - side) * half, 16)
            added = self.own(d, here, 16) + self.near[side, pl.ds(rows, 16)].astype(F32)
            self.sums[1 + side, pl.ds(here, 16)] = added.astype(BF)
            self.sums[1 + side, pl.ds(there, 16)] = self.own(d, there, 16).astype(BF)

        self.copies[6 + side].start()

    def arrive(self):
        self.copies[0].wait_recv()
        self.copies[6].wait_recv()
        self.copies[7].wait_recv()

    def total(self, rows, count):
        return (
            self.own(0, rows, count)
            + self.full[0, pl.ds(rows, count)].astype(F32)
            + self.full[1, pl.ds(rows, count)].astype(F32)
        )

    def drain(self):
        for copy in self.copies:
            copy.wait_send()


def scatter_scratch():
    return [
        pltpu.VMEM((4, 2 * OWN, WIDTH), BF),
        pltpu.VMEM((4, OWN, WIDTH), BF),
        pltpu.VMEM((3, OWN, WIDTH), BF),
        pltpu.VMEM((2, OWN // 2, WIDTH), BF),
        pltpu.VMEM((2, OWN, WIDTH), BF),
        pltpu.SemaphoreType.DMA((8,)),
        pltpu.SemaphoreType.DMA((8,)),
    ]


def head_norm(value):
    return lax.rsqrt(jnp.mean(value * value, axis=1, keepdims=True) + EPS)


def turn(value, cosine, sine):
    return value * cosine + pltpu.roll(value, HEAD // 2, 1) * sine


def turn_back(value, cosine, sine):
    return value * cosine - pltpu.roll(value, HEAD // 2, 1) * sine


LOG2 = math.log2(math.e)
SCALE = 1.0 / math.sqrt(HEAD)
QROWS = 256


def allowed_keys(start, first, keys):
    slots = lax.broadcasted_iota(jnp.int32, (QROWS, keys), 1)
    query = lax.broadcasted_iota(jnp.int32, (QROWS, keys), 0) + first
    return (slots >= start) & (slots <= query)


FREQ = np.tile(THETA ** (-(np.arange(HEAD // 2) * 2.0 / HEAD)), 2)[None].astype(np.float32)


def forward_kernel(
    tok, og, norm1, norm2, q_gain, k_gain, freq, lengths, groups, starts, w_qkv, w_gu, w_out, w_down,
    h2_o, g_o, wq_o, wo_o, wg_o, wd_o, h1t_o, raw_o, q_o, k_o, att_o, lse_o, mid_o, gain_o, x_o, start_o, cos_o, sin_o,
    ggu_o, hid_o,
    x, h1, h1t, h2, g, wq, wg, wd, w_all, raw, qs, ks, att, heard, lse, mid, gain, gains, start, cosine, sine,
    q_raw, q_cut, q_raw_part, q_part, g_raw, g_cut, g_raw_part, g_part,
    xs, xr, gs, gr, hs, hr,
    zs, zr, ps, pr, ns, nr, loc_s, out_s, raw_s, row_s, os_, or_, ts, tr,
    y0s, y0r, y1s, y1r, y2s, y2r, y3s, y3r, y4s, y4r,
):
    p, row, col, z, k = place()
    px, py = dp_place()
    me = 2 * z + k
    lo = z % 2
    other = z + 1 - 2 * lo
    peer = on_ring(z, 1 - k)
    beside_col = 2 * lo + 1 - k
    piece_rows = pl.ds(pl.multiple_of(p * 32, 32), 32)

    def lanes(first, count):
        return pl.ds(pl.multiple_of(first, 256), count)

    raws = [
        pltpu.make_async_copy(src, dst, raw_s.at[i])
        for i, (src, dst) in enumerate(
            [
                (w_qkv.at[piece_rows], q_raw_part),
                (w_gu.at[piece_rows, :, lanes((1 - lo) * 2 * UNITS, 2 * UNITS)], g_raw_part),
                (w_qkv, q_raw),
                (w_gu.at[:, :, lanes(lo * 2 * UNITS, 2 * UNITS)], g_raw),
            ]
        )
    ]
    for copy in raws:
        copy.start()
    gains[0:1] = norm1[...]
    gains[1:2] = norm2[...]
    meet(column_friends() + xy_friends())
    raws[0].wait()
    for kk in range(2):
        q_part[kk] = jnp.where(lo == 0, q_raw_part[:, 2 + kk, :], q_raw_part[:, kk, :])

    gain[col] = gains[...]
    gain_copies = [
        remote(gains, gain.at[col], ns.at[i], nr.at[col], device)
        for i, device in enumerate([peer, on_ring(other, k), on_ring(other, 1 - k)])
    ]

    weights = [wq, wg, wd]
    blocks = [q_cut, g_cut, w_down]

    def cell(weight, c, xx, yy, cols=slice(None)):
        between = (slice(None),) * (len(weight.shape) - 5)
        return weight.at[(c, *between, xx, yy, slice(None), cols)]

    def crossing(a, kk):
        src = (q_part.at[kk], g_part.at[kk], cell(w_down, 2 * (1 - lo) + kk, px, py))[a]
        return remote(src, cell(weights[a], col, px, py), zs.at[a, kk], zr.at[a, k], on_ring(other, kk))

    def crossed(a, kk):
        dst = cell(weights[a], 2 * (1 - lo) + kk, px, py)
        return remote(dst, dst, zs.at[a, kk], zr.at[a, kk], peer)

    def beside(a):
        mine, theirs = (col, beside_col) if a == 2 else (k, 1 - k)
        keep = pltpu.make_async_copy(blocks[a].at[mine], weights[a].at[col], loc_s.at[a])
        give = remote(blocks[a].at[theirs], weights[a].at[col], ps.at[a], pr.at[a], peer)
        take = remote(weights[a].at[beside_col], weights[a].at[beside_col], ps.at[a], pr.at[a], peer)
        return keep, give, take

    def spread_at(a):
        weight = weights[a]
        half_lanes = weight.shape[-1] // 2

        def at(half, xx, yy, part):
            xs_ = slice(None) if xx is None else xx
            ys_ = slice(None) if yy is None else yy
            cols = slice(None) if part is None else pl.ds(part * half_lanes, half_lanes)
            return cell(weight, 2 * (1 - lo) + half, xs_, ys_, cols)

        return at

    spreads = [
        Spread(spread_at(a), send, recv) for a, (send, recv) in enumerate([(y0s, y0r), (y1s, y1r), (y2s, y2r)])
    ]

    pair = pl.ds(2 * (1 - lo), 2)
    groups_of = [(1 - row, slice(None)), (row, pair)]

    def out_at(which):
        def at(half, xx, yy, part):
            xs_ = slice(None) if xx is None else xx
            ys_ = slice(None) if yy is None else yy
            cols = pl.ds(half * 256, 256) if part is None else pl.ds(half * 256 + part * HEAD, HEAD)
            return w_all.at[(*groups_of[which], xs_, ys_, k, slice(None), cols)]

        return at

    out_spreads = [Spread(out_at(0), y3s, y3r), Spread(out_at(1), y4s, y4r)]
    out_pieces = [
        remote(
            w_out.at[px, py, kk], w_all.at[row, col, px, py, kk],
            os_.at[2 * dz + kk], or_.at[me], on_ring((z + dz) % 4, kk),
        )
        for dz in (1, 3, 2)
        for kk in range(2)
    ]
    keep_out = pltpu.make_async_copy(w_out, w_all.at[row, col], loc_s.at[3])
    give_out = remote(w_out, w_all.at[row, col], os_.at[0], or_.at[me], peer)

    def out_arrived(j):
        dst = w_all.at[j // 4, j % 4, px, py, k]
        return remote(dst, dst, os_.at[0], or_.at[j], peer)

    def out_share(which, core):
        ref = w_all.at[(*groups_of[which], slice(None), slice(None), core)]
        return remote(ref, ref, ts.at[7 + which], tr.at[7 + which], peer)

    def hand(o):
        there = (me + o) % 8
        rows = pl.ds(pl.multiple_of(there * OWN, OWN), OWN)
        device = {"row": there // 4, "col": there % 4}
        return remote(att.at[:, rows], heard.at[me], ts.at[o - 1], tr.at[o - 1], device)

    def handed(o):
        dst = heard.at[(me + 8 - o) % 8]
        return remote(dst, dst, ts.at[o - 1], tr.at[o - 1], peer)

    for kk in range(2):
        crossing(0, kk).start()
    for copy in out_pieces:
        copy.start()
    x_gather = Gather(tile_at(x), xs, xr, tok)
    x_gather.start()
    for copy in gain_copies:
        copy.start()
    keep_x = pltpu.make_async_copy(tok, tile_at(x)(me), loc_s.at[4])
    keep_x.start()
    keep_g = pltpu.make_async_copy(og, tile_at(g)(me), loc_s.at[5])
    keep_g.start()
    keep_out.start()
    give_out.start()
    raws[2].wait()

    @pl.loop(0, 16)
    def _(i):
        rows = pl.ds(pl.multiple_of(i * 32, 32), 32)
        for kk in range(2):
            q_cut[kk, i // 4, i % 4] = jnp.where(lo == 0, q_raw[rows, kk, :], q_raw[rows, 2 + kk, :])

    beside(0)[0].start()
    beside(0)[1].start()
    for kk in range(2):
        crossed(0, kk).wait_recv()
    spreads[0].start(0)
    for dz in (1, 3, 2):
        for kk in range(2):
            out_arrived(2 * ((z + dz) % 4) + kk).wait_recv()
    for spread in out_spreads:
        spread.start(0)
    for a in (1, 3):
        raws[a].wait()
    slot = (
        lax.broadcasted_iota(jnp.int32, (8, HEAD), 0) * HEAD + lax.broadcasted_iota(jnp.int32, (8, HEAD), 1)
    ).astype(F32)

    def one_sequence(i, begun):
        first = starts[i].astype(F32)
        last = first + jnp.where(groups[i] == p, lengths[i], 0).astype(F32)
        return jnp.where((slot >= first) & (slot < last), first, begun)

    begun = lax.fori_loop(0, lengths.shape[0], one_sequence, jnp.zeros((8, HEAD), F32))
    for i in range(8):
        rows = slice(i * HEAD, (i + 1) * HEAD)
        begin = jnp.broadcast_to(begun[i : i + 1], (HEAD, HEAD)).T
        there = lax.broadcasted_iota(jnp.int32, (HEAD, HEAD), 0).astype(F32) + float(i * HEAD)
        angle = (there - begin) * freq[...]
        start[rows] = begin.astype(jnp.int32)
        cosine[rows] = jnp.cos(angle)
        lane = lax.broadcasted_iota(jnp.int32, (HEAD, HEAD), 1)
        sine[rows] = jnp.where(lane < HEAD // 2, -1.0, 1.0) * jnp.sin(angle)
    spreads[0].pass_on(0)
    for spread in out_spreads:
        spread.pass_on(0)
    for u in range(3):
        for half in range(2):
            into = slice(u * 512 + half * 256, u * 512 + half * 256 + 256)
            for kk in range(2):
                cols = slice(kk * UNITS + u * 256, kk * UNITS + u * 256 + 256)
                g_part[kk, :, into] = g_raw_part[:, half, cols]
    spreads[0].wait(0)
    spreads[0].start(1)
    x_gather.forward()
    spreads[0].pass_on(1)
    for spread in out_spreads:
        spread.wait(0)
        spread.start(1)
    for c in range(4):

        @pl.when(c != col)
        def _():
            remote(gain.at[c], gain.at[c], ns.at[0], nr.at[c], peer).wait_recv()

    keep_x.wait()
    x_gather.finish([4, 5, 6])

    def gain_row(which):
        return jnp.concatenate([gain[c, which : which + 1] for c in range(4)], axis=1)

    gain_one = gain_row(0)

    def norm_one(half):
        @pl.loop(0, TILE // 64)
        def _(i):
            rows = pl.ds(pl.multiple_of(half * TILE + i * 64, 64), 64)
            value = x[rows].astype(F32)
            h1[rows] = (value * head_norm(value) * gain_one).astype(BF)

    def heads(half):
        @pl.loop(0, TILE // 256)
        def _(i):
            rows = pl.ds(pl.multiple_of(half * TILE + i * 256, 256), 256)
            mixed = mm(h1[rows], wq[...].reshape(WIDTH, 4 * HEAD)).astype(BF)
            raw[rows] = mixed
            cos_rows, sin_rows = cosine[rows], sine[rows]
            for piece in range(3):
                value = mixed[:, piece * HEAD : (piece + 1) * HEAD].astype(F32)
                by = q_gain[...] if piece < 2 else k_gain[...]
                turned = turn(value * head_norm(value) * by, cos_rows, sin_rows).astype(BF)
                if piece < 2:
                    qs[piece, rows] = turned
                else:
                    ks[rows] = turned

    norm_one(row)
    keep, _, take = beside(0)
    keep.wait()
    take.wait_recv()
    spreads[0].wait(1)
    heads(row)
    x_gather.share()
    for a in (1, 2):
        for kk in range(2):
            crossing(a, kk).start()
    beside(2)[0].start()
    beside(2)[1].start()
    x_gather.finish([7, 8])
    g_gather = Gather(tile_at(g), gs, gr, og)
    g_gather.start()
    for spread in out_spreads:
        spread.pass_on(1)
    norm_one(1 - row)
    heads(1 - row)
    mine = pl.ds(pl.multiple_of(me * OWN, OWN), OWN)
    saves = [
        pltpu.make_async_copy(src, dst, out_s.at[i])
        for i, (src, dst) in enumerate(
            [
                (wq, wq_o), (raw, raw_o), (qs, q_o), (ks, k_o), (gain, gain_o), (x.at[mine], x_o),
                (start, start_o), (cosine, cos_o), (sine, sin_o),
                (att, att_o), (lse, lse_o), (h1t, h1t_o), (g, g_o), (mid, mid_o),
                (w_all.at[row, :, pl.ds(col, 1)], wo_o),
            ]
        )
    ]
    for i in range(9):
        saves[i].start()

    for block in range(GROUP // QROWS):
        first, keys = block * QROWS, (block + 1) * QROWS
        rows = pl.ds(first, QROWS)
        allowed = allowed_keys(start[rows, :1], first, keys)

        @pl.loop(0, 2)
        def _(h):
            score = mm_t(qs[h, rows], ks[:keys]) * (SCALE * LOG2)
            score = jnp.where(allowed, score, -1e30)
            peak = jnp.max(score, axis=1, keepdims=True)
            weight = jnp.exp2(score - peak)
            total = jnp.sum(weight, axis=1, keepdims=True)
            out = mm(weight.astype(BF), raw[:keys, 3 * HEAD :]) / total
            att[h, rows] = out.astype(BF)
            lse[h, rows] = jnp.broadcast_to(peak + jnp.log2(total), (QROWS, HEAD))

        if block == 1:
            for a in (1, 2):
                for kk in range(2):
                    crossed(a, kk).wait_recv()
                spreads[a].start(0)

    for which, spread in enumerate(out_spreads):
        spread.wait(1)
        out_share(which, k).start()
    for o in range(1, 8):
        hand(o).start()
    for h in range(2):
        heard[me, h] = att[h, mine]
    saves[9].start()
    saves[10].start()
    for a in (1, 2):
        spreads[a].pass_on(0)
    for a in (1, 2):
        spreads[a].wait(0)
        spreads[a].start(1)

    @pl.loop(0, 16)
    def _(i):
        rows = pl.ds(pl.multiple_of(i * 32, 32), 32)
        for u in range(3):
            for half in range(2):
                into = slice(u * 512 + half * 256, u * 512 + half * 256 + 256)
                for kk in range(2):
                    cols = slice(kk * UNITS + u * 256, kk * UNITS + u * 256 + 256)
                    g_cut[kk, i // 4, i % 4, :, into] = g_raw[rows, half, cols]

    beside(1)[0].start()
    beside(1)[1].start()
    keep_out.wait()
    out_arrived_peer = w_all.at[row, beside_col]
    remote(out_arrived_peer, out_arrived_peer, os_.at[0], or_.at[2 * z + 1 - k], peer).wait_recv()
    for which in range(2):
        out_share(which, 1 - k).wait_recv()
    saves[14].start()
    for o in range(1, 8):
        handed(o).wait_recv()
    left = [
        jnp.concatenate([heard[4 * half + c, h] for c in range(4) for h in range(2)], axis=1) for half in range(2)
    ]
    for c in range(4):
        mid[:, c * TILE : (c + 1) * TILE] = mm(left[0], w_all[0, c].reshape(2 * TILE, TILE)) + mm(
            left[1], w_all[1, c].reshape(2 * TILE, TILE)
        )
    gain_two = gain_row(1)

    @pl.loop(0, OWN // 16)
    def _(i):
        first = pl.multiple_of(i * 16, 16)
        there = pl.ds(pl.multiple_of(me * OWN + first, 16), 16)
        value = x[there].astype(F32) + mid[pl.ds(first, 16)]
        mid[pl.ds(first, 16)] = value
        h2[there] = (value * head_norm(value) * gain_two).astype(BF)

    h2_gather = Gather(rows_at(h2), hs, hr)
    h2_gather.start()
    saves[13].start()

    @pl.loop(0, 8)
    def _(i):
        cols = pl.ds(pl.multiple_of(i * 256, 256), 256)
        h1t[cols] = h1[:, cols].T

    saves[11].start()
    g_gather.forward()
    for a in (1, 2):
        spreads[a].pass_on(1)
    x_gather.drain()
    saves[5].wait()
    g_gather.share()
    row_saves = []

    def feed(d):
        rows = pl.ds(pl.multiple_of((z + d) % 4 * 256, 256), 256)

        @pl.loop(0, 3)
        def _(u):
            wide = pl.ds(pl.multiple_of(u * 512, 512), 512)
            gate_cols = pl.ds(pl.multiple_of(u * 512, 256), 256)
            up_cols = pl.ds(pl.multiple_of(u * 512 + 256, 256), 256)
            pair_ = mm(h2[rows], wg[:, :, :, :, wide].reshape(WIDTH, 512))
            back = mm_t(g[rows, :TILE], wd[0, u].reshape(256, TILE))
            for c in range(1, 4):
                back += mm_t(g[rows, c * TILE : (c + 1) * TILE], wd[c, u].reshape(256, TILE))
            gate, up = pair_[:, :256], pair_[:, 256:]
            sig = 1.0 / (1.0 + jnp.exp(-gate))
            silu = gate * sig
            h1[rows, pl.ds(pl.multiple_of(u * 256, 256), 256)] = (silu * up).astype(BF)
            x[rows, gate_cols] = (back * up * sig * (1.0 + gate * (1.0 - sig))).astype(BF)
            x[rows, up_cols] = (back * silu).astype(BF)

        for i, (src, dst) in enumerate(
            [
                (h2.at[rows], h2_o.at[rows]),
                (x.at[rows, pl.ds(0, 2 * UNITS)], ggu_o.at[rows]),
                (h1.at[rows, pl.ds(0, UNITS)], hid_o.at[rows]),
            ]
        ):
            copy = pltpu.make_async_copy(src, dst, row_s.at[d, i])
            copy.start()
            row_saves.append(copy)

    for a in (1, 2):
        keep, _, take = beside(a)
        keep.wait()
        take.wait_recv()
        spreads[a].wait(1)
    h2_gather.forward()
    weight_saves = [pltpu.make_async_copy(weights[a], (wg_o, wd_o)[a - 1], loc_s.at[a + 5]) for a in (1, 2)]
    for copy in weight_saves:
        copy.start()
    g_gather.finish()
    keep_g.wait()
    saves[12].start()
    h2_gather.finish([4])
    feed(0)
    h2_gather.finish([5, 6])
    feed(1)
    h2_gather.share()
    feed(3)
    h2_gather.finish([7, 8])
    feed(2)
    for copy in gain_copies + out_pieces + [give_out]:
        copy.wait_send()
    for a in range(3):
        beside(a)[1].wait_send()
        for kk in range(2):
            crossing(a, kk).wait_send()
    for o in range(1, 8):
        hand(o).wait_send()
    for which in range(2):
        out_share(which, k).wait_send()
    for spread in spreads + out_spreads:
        spread.drain()
    g_gather.drain()
    h2_gather.drain()
    for i, copy in enumerate(saves):
        if i != 5:
            copy.wait()
    for copy in weight_saves + row_saves:
        copy.wait()


def forward_call(*args):
    hbm = pl.BlockSpec(memory_space=pl.ANY)
    vmem = pl.BlockSpec(memory_space=pltpu.VMEM)
    smem = pl.BlockSpec(memory_space=pltpu.SMEM)
    dma = pltpu.SemaphoreType.DMA

    def out(shape, dtype=BF):
        return jax.ShapeDtypeStruct(shape, dtype)

    wide = (GROUP, WIDTH)
    return pl.pallas_call(
        forward_kernel,
        out_shape=[
            out(wide), out(wide), out((4, 4, 4, 32, 512)), out((4, 1, 4, 2, 32, TILE)), out((4, 4, 4, 32, 2 * UNITS)),
            out((4, 3, 4, 4, 16, TILE)), out((WIDTH, GROUP)), out((GROUP, 512)), out((2, GROUP, HEAD)), out((GROUP, HEAD)),
            out((2, GROUP, HEAD)), out((2, GROUP, HEAD), F32), out((OWN, WIDTH), F32), out((4, 8, TILE), F32),
            out((OWN, WIDTH)), out((GROUP, HEAD), jnp.int32), out((GROUP, HEAD), F32), out((GROUP, HEAD), F32),
            out((GROUP, 2 * UNITS)), out((GROUP, UNITS)),
        ],
        in_specs=[vmem] * 7 + [smem] * 3 + [hbm] * 4,
        out_specs=[hbm] * 20,
        scratch_shapes=[
            pltpu.VMEM(wide, BF), pltpu.VMEM(wide, BF), pltpu.VMEM((WIDTH, GROUP), BF), pltpu.VMEM(wide, BF),
            pltpu.VMEM(wide, BF), pltpu.VMEM((4, 4, 4, 32, 512), BF), pltpu.VMEM((4, 4, 4, 32, 2 * UNITS), BF),
            pltpu.VMEM((4, 3, 4, 4, 16, TILE), BF), pltpu.VMEM((2, 4, 4, 4, 2, 32, TILE), BF),
            pltpu.VMEM((GROUP, 512), BF), pltpu.VMEM((2, GROUP, HEAD), BF), pltpu.VMEM((GROUP, HEAD), BF),
            pltpu.VMEM((2, GROUP, HEAD), BF), pltpu.VMEM((8, 2, OWN, HEAD), BF), pltpu.VMEM((2, GROUP, HEAD), F32),
            pltpu.VMEM((OWN, WIDTH), F32), pltpu.VMEM((4, 8, TILE), F32), pltpu.VMEM((8, TILE), F32),
            pltpu.VMEM((GROUP, HEAD), jnp.int32), pltpu.VMEM((GROUP, HEAD), F32), pltpu.VMEM((GROUP, HEAD), F32),
            pltpu.VMEM((TILE, 4, 512), BF), pltpu.VMEM((2, 4, 4, 32, 512), BF), pltpu.VMEM((32, 4, 512), BF),
            pltpu.VMEM((2, 32, 512), BF), pltpu.VMEM((TILE, 2, 2 * UNITS), BF), pltpu.VMEM((2, 4, 4, 32, 2 * UNITS), BF),
            pltpu.VMEM((32, 2, 2 * UNITS), BF), pltpu.VMEM((2, 32, 2 * UNITS), BF),
        ]
        + GATHER_SEMS * 3
        + [
            dma((3, 2)), dma((3, 2)), dma((3,)), dma((3,)), dma((3,)), dma((4,)), dma((8,)), dma((15,)), dma((4,)),
            dma((4, 3)), dma((8,)), dma((8,)), dma((9,)), dma((9,)),
        ]
        + SPREAD_SEMS * 5,
        compiler_params=pltpu.CompilerParams(
            collective_id=1, has_side_effects=True, vmem_limit_bytes=VMEM_LIMIT
        ),
        cost_estimate=pl.CostEstimate(flops=14_000_000_000, bytes_accessed=60_000_000, transcendentals=2_000_000),
        name="forward",
    )(*args)


class Collapse:
    def __init__(self, which, data, near, full, done, send, recv):
        here = dp_place()
        self.which, self.data, self.near, self.full, self.done, self.here = which, data, near, full, done, here
        self.copies = {}
        for half in range(2):
            for phase in range(2):
                axis = half ^ phase

                def copy(slot, src, dst, o):
                    index = (which, half, phase, slot)
                    return remote(src, dst, send.at[index], recv.at[index], along(axis, o))

                self.copies[half, phase] = [
                    copy(0, self.block(half, phase, 2, 0), near[phase].at[half, 0], 1),
                    copy(1, self.block(half, phase, 2, 1), near[phase].at[half, 1], 3),
                    copy(2, self.block(half, phase, 1), full[phase].at[half, 0], 1),
                    copy(3, self.block(half, phase, 3), full[phase].at[half, 1], 3),
                ]

    def at(self, half, phase, o):
        there = (self.here[half ^ phase] + o) % 4
        if phase == 0:
            return (there, slice(None)) if half == 0 else (slice(None), there)
        return (self.here[0], there) if half == 0 else (there, self.here[1])

    def block(self, half, phase, o, part=None):
        which = pl.ds(2 * half, 2) if part is None else 2 * half + part
        return self.data.at[(*self.at(half, phase, o), which)]

    def cell(self, half, phase, o, a, c):
        x, y = self.at(half, phase, o)
        x, y = (a if isinstance(x, slice) else x), (a if isinstance(y, slice) else y)
        return (x, y, 2 * half + c)

    def start(self, phase=0):
        for half in range(2):
            for slot in range(2):
                self.copies[half, phase][slot].start()

    def mid(self, phase=0):
        for half in range(2):
            for slot in range(2):
                self.copies[half, phase][slot].wait_recv()

                def add(a):
                    index = self.cell(half, phase, (1, 3)[slot], a, slot)
                    here = (half, slot, a) if phase == 0 else (half, slot)
                    self.data[index] = (
                        self.data[index].astype(F32) + self.near[phase][here].astype(F32)
                    ).astype(BF)

                if phase == 0:
                    pl.loop(0, 4)(add)
                else:
                    add(0)
                self.copies[half, phase][2 + slot].start()

    def first(self):
        for half in range(2):
            for slot in range(2):
                self.copies[half, 0][2 + slot].wait_recv()

            @pl.loop(0, 4)
            def _(a):
                for c in range(2):
                    index = self.cell(half, 0, 0, a, c)
                    total = self.data[index].astype(F32)
                    for slot in range(2):
                        total += self.full[0][half, slot, a, c].astype(F32)
                    self.data[index] = total.astype(BF)

        self.start(1)

    def second(self):
        for half in range(2):
            for slot in range(2):
                self.copies[half, 1][2 + slot].wait_recv()
            for c in range(2):
                total = self.data[self.cell(half, 1, 0, 0, c)].astype(F32)
                for slot in range(2):
                    total += self.full[1][half, slot, c].astype(F32)
                self.done[self.which, 2 * half + c] = total.astype(BF)

    def drain(self):
        for copies in self.copies.values():
            for copy in copies:
                copy.wait_send()


CHUNKS, BUFFERS = 4, 3


def collapse_scratch():
    dma = pltpu.SemaphoreType.DMA
    return (
        [pltpu.VMEM((4, 4, 4, 48, 512), BF)] * BUFFERS
        + [pltpu.VMEM((2, 2, 4, 48, 512), BF)] * BUFFERS
        + [pltpu.VMEM((2, 2, 48, 512), BF)] * BUFFERS
        + [pltpu.VMEM((2, 2, 4, 2, 48, 512), BF)] * BUFFERS
        + [pltpu.VMEM((2, 2, 2, 48, 512), BF)] * BUFFERS
        + [pltpu.VMEM((CHUNKS, 4, 48, 512), BF), dma((CHUNKS, 2, 2, 4)), dma((CHUNKS, 2, 2, 4))]
        + [dma((CHUNKS, 3)), dma((CHUNKS, 4)), dma((CHUNKS, 2, 2, 4)), dma((CHUNKS, 2, 2, 4))]
    )


class Trade:
    def __init__(self, block, slot, send, recv, which=()):
        _, row, col, z, k = place()
        self.col, self.peer = col, on_ring(z, 1 - k)
        self.recv, self.send, self.slot, self.which = recv, send, slot, which
        self.copies = [
            remote(block((col + o) % 4), slot(col), send.at[(*which, o - 1)], recv.at[(*which, o - 1)], {"col": (col + o) % 4})
            for o in range(1, 4)
        ]
        self.keep = pltpu.make_async_copy(block(col), slot(col), recv.at[(*which, 3)])

    def start(self):
        for copy in self.copies:
            copy.start()
        self.keep.start()

    def finish(self):
        for o in range(1, 4):
            dst = self.slot((self.col - o + 4) % 4)
            sems = (self.send.at[(*self.which, o - 1)], self.recv.at[(*self.which, o - 1)])
            remote(dst, dst, *sems, self.peer).wait_recv()
        self.keep.wait()

    def drain(self):
        for copy in self.copies:
            copy.wait_send()


def norm_back(grad, value, gain):
    scale = head_norm(value)
    weighted = grad * gain
    inner = jnp.mean(weighted * value, axis=1, keepdims=True)
    return scale * weighted - value * (scale * scale * scale * inner), grad * value * scale


def norm_back(grad, value, gain):
    scale = head_norm(value)
    weighted = grad * gain
    inner = jnp.mean(weighted * value, axis=1, keepdims=True)
    return scale * weighted - value * (scale * scale * scale * inner), grad * value * scale


def backward_kernel(
    h2_i, ggu_i, hid_i, g_i, wg_i, wd_i, wo_i, wq_i, h1t_i, raw_i, q_i, k_i, att_i, lse_i, mid_i, gain_i, x_i,
    start_i, cos_i, sin_i, q_gain, k_gain,
    result_o, stream_o, grads_o, sums_o,
    m, gm, dqkv, mid, gain, x_own, g_own, acc, head_acc, tile_f, tile_b, totals, heard,
    ms, mr,
    parts, theirs, psums, near, full, rs_s, rs_r,
    data0, data1, data2, near0, near1, near2, next0, next1, next2, full0, full1, full2, last0, last1, last2,
    done, c_s, c_r, t_s, t_r, a_s, a_r,
    fs, fr, ls, lr, as_, ar, in_s, free,
):
    p, row, col, z, k = place()
    px, py = dp_place()
    me = 2 * z + k
    up, down, peer = on_ring((z + 1) % 4, k), on_ring((z + 3) % 4, k), on_ring(z, 1 - k)
    far = on_ring((z + 2) % 4, k)
    loads = []

    def load(src, dst):
        copy = pltpu.make_async_copy(src, dst, in_s.at[len(loads)])
        copy.start()
        loads.append(copy)
        return copy

    def wait(copies):
        for copy in copies:
            copy.wait()

    collapses, trades, spreads = [], [], []
    datas, nears, nexts = (data0, data1, data2), (near0, near1, near2), (next0, next1, next2)
    fulls, lasts = (full0, full1, full2), (last0, last1, last2)

    def chunk(i):
        def at(half, x, y, part):
            xs = slice(None) if x is None else x
            ys = slice(None) if y is None else y
            which = pl.ds(2 * half, 2) if part is None else 2 * half + part
            return grads_o.at[i, xs, ys, which]

        b = i % BUFFERS
        collapses.append(Collapse(i, datas[b], (nears[b], nexts[b]), (fulls[b], lasts[b]), done, c_s, c_r))
        trades.append(
            Trade(lambda c: done.at[i, c], lambda c: grads_o.at[i, px, py, c], t_s, t_r, (i,))
        )
        spreads.append(Spread(at, a_s, a_r, (i,)))

    for i in range(CHUNKS):
        chunk(i)
    scatter = Scatter(parts, theirs, psums, near, full, rs_s, rs_r)
    stream_trade = Trade(
        lambda c: tile_f.at[:, pl.ds(pl.multiple_of(c * TILE, TILE), TILE)],
        lambda c: stream_o.at[pl.ds(pl.multiple_of(c * OWN, OWN), OWN)], fs, fr,
    )
    result_trade = Trade(
        lambda c: tile_b.at[:, pl.ds(pl.multiple_of(c * TILE, TILE), TILE)],
        lambda c: result_o.at[pl.ds(pl.multiple_of(c * OWN, OWN), OWN)], ls, lr,
    )

    def release():
        scatter.drain()
        for device in (up, down, peer):
            pl.semaphore_signal(free, inc=1, device_id=device, device_id_type=MESH)

    def project(d, product):
        rows = pl.ds(pl.multiple_of((z + d) % 4 * 256, 256), 256)

        @pl.loop(0, 4)
        def _(c):
            cols = pl.ds(pl.multiple_of(c * TILE, TILE), TILE)
            parts[d, :, cols] = product(rows, c, cols).astype(BF)

        scatter.put(d)

    def weight_grads(i, first, second):
        data = datas[i % BUFFERS]
        for c in range(4):
            cols = slice(c * TILE, (c + 1) * TILE)
            data[:, :, c, :32] = first(cols).astype(BF).reshape(4, 4, 32, 512)
            data[:, :, c, 32:] = second(cols).astype(BF).reshape(4, 4, 16, 512)
        collapses[i].start()

    def gain_row(which):
        return jnp.concatenate([gain[c, which : which + 1] for c in range(4)], axis=1)

    own_rows = pl.ds(pl.multiple_of(me * OWN, OWN), OWN)

    def stage_one(h2, g, ggu, hid, wg):
        first_loads = [load(ggu_i, ggu), load(wg_i, wg)]
        more_loads = [load(h2_i, h2), load(hid_i, hid), load(g_i, g)]
        meet(ring_friends() + [far] + xy_friends())
        def grads(u):
            weight_grads(
                u,
                lambda cols: t_mm(h2[:, cols], ggu[:, u * 512 : (u + 1) * 512]),
                lambda cols: t_mm(hid[:, u * 256 : (u + 1) * 256], g[:, cols]),
            )

        def product(rows, c, cols):
            return mm_t(ggu[rows], wg[c])

        wait(first_loads)
        project(2, product)
        wait(more_loads)
        grads(0)
        scatter.across()
        project(1, product)
        project(3, product)
        project(0, product)
        scatter.beside(0)
        scatter.beside(1)
        collapses[0].mid()
        grads(1)
        grads(2)
        collapses[0].first()

    early = [load(mid_i, mid), load(gain_i, gain), load(x_i, x_own), load(g_i.at[own_rows], g_own)]
    pl.run_scoped(
        stage_one,
        pltpu.VMEM((GROUP, WIDTH), BF), pltpu.VMEM((GROUP, WIDTH), BF), pltpu.VMEM((GROUP, 2 * UNITS), BF),
        pltpu.VMEM((GROUP, UNITS), BF), pltpu.VMEM((4, TILE, 2 * UNITS), BF),
    )

    def stage_two(wo, att, qs, ks, raw, lse, ga, dk, dv, h1t, wq, att_t, start, cosine, sine):
        l_wo, l_att = load(wo_i, wo), load(att_i, att)
        l_heads = [
            load(q_i, qs), load(k_i, ks), load(raw_i, raw), load(lse_i, lse),
            load(start_i, start), load(cos_i, cosine), load(sin_i, sine),
        ]
        l_last = [load(h1t_i, h1t), load(wq_i, wq)]
        wait(early)
        acc[...] = jnp.zeros_like(acc)
        head_acc[...] = jnp.zeros_like(head_acc)
        dk[...] = jnp.zeros_like(dk)
        dv[...] = jnp.zeros_like(dv)
        totals[0] = jnp.zeros((8, TILE + HEAD), F32)
        gain_two = gain_row(1)
        scatter.arrive()

        @pl.loop(0, OWN // 16)
        def _(i):
            rows = pl.ds(pl.multiple_of(i * 16, 16), 16)
            back, gained = norm_back(scatter.total(pl.multiple_of(i * 16, 16), 16), mid[rows], gain_two)
            acc[1] += gained
            back = back + g_own[rows].astype(F32)
            gm[rows] = back
            m[pl.ds(pl.multiple_of(me * OWN + i * 16, 16), 16)] = back.astype(BF)

        m_gather = Gather(rows_at(m), ms, mr)
        m_gather.start()
        release()
        collapses[1].mid()
        l_att.wait()
        for h in range(2):
            att_t[h * HEAD : (h + 1) * HEAD] = att[h].T
        l_wo.wait()
        wait(l_heads)

        def attend(d):
            block = (z + d) % 4
            first = pl.multiple_of(block * QROWS, QROWS)
            rows = pl.ds(first, QROWS)
            back = mm_t(m[rows, :TILE], wo[0])
            for c in range(1, 4):
                back += mm_t(m[rows, c * TILE : (c + 1) * TILE], wo[c])
            for h in range(2):
                ga[h, rows] = back[:, h * HEAD : (h + 1) * HEAD].astype(BF)

            def over(keys):
                allowed = allowed_keys(start[rows, :1], first, keys)

                @pl.loop(0, 2)
                def _(h):
                    cols = pl.ds(pl.multiple_of(h * HEAD, HEAD), HEAD)
                    score = mm_t(qs[h, rows], ks[:keys]) * (SCALE * LOG2)
                    prob = jnp.exp2(jnp.where(allowed, score, -1e30) - lse[h, rows, :1])
                    grad = ga[h, rows]
                    delta = jnp.sum(grad.astype(F32) * att[h, rows].astype(F32), axis=1, keepdims=True)
                    prob_grad = mm_t(grad, raw[:keys, 3 * HEAD :])
                    score_grad = (prob * (prob_grad - delta)).astype(BF)
                    dk[:keys] += t_mm(score_grad, qs[h, rows])
                    dv[:keys] += t_mm(prob.astype(BF), grad)
                    back = turn_back(mm(score_grad, ks[:keys]) * SCALE, cosine[rows], sine[rows])
                    back, gained = norm_back(back, raw[rows, cols].astype(F32), q_gain[...])
                    dqkv[rows, cols] = back.astype(BF)
                    head_acc[0:1] += jnp.sum(gained, axis=0, keepdims=True)

            @pl.when(block < 2)
            def _():
                over(2 * QROWS)

            @pl.when(block >= 2)
            def _():
                over(4 * QROWS)

        m_gather.finish([4])
        attend(0)
        collapses[0].mid(1)
        collapses[2].mid()
        m_gather.forward()
        collapses[1].first()
        m_gather.finish([5, 6])
        attend(1)
        collapses[0].second()
        trades[0].start()
        m_gather.share()
        attend(3)
        m_gather.finish([7, 8])
        attend(2)
        collapses[2].first()
        trades[0].finish()
        spreads[0].start(0)
        collapses[1].mid(1)

        @pl.loop(0, 4)
        def _(i):
            rows = pl.ds(pl.multiple_of(i * 256, 256), 256)
            back = turn_back(dk[rows] * SCALE, cosine[rows], sine[rows])
            back, gained = norm_back(back, raw[rows, 2 * HEAD : 3 * HEAD].astype(F32), k_gain[...])
            dqkv[rows, 2 * HEAD : 3 * HEAD] = back.astype(BF)
            dqkv[rows, 3 * HEAD :] = dv[rows].astype(BF)
            head_acc[1:2] += jnp.sum(gained, axis=0, keepdims=True)

        wait(l_last)
        collapses[0].drain()
        weight_grads(3, lambda cols: mm(h1t[cols], dqkv[...]), lambda cols: mm(att_t[...], m[:, cols]))
        collapses[2].mid(1)
        pl.semaphore_wait(free, 3)

        def product(rows, c, cols):
            return mm_t(dqkv[rows], wq[c])

        project(2, product)
        project(1, product)
        collapses[1].second()
        trades[1].start()
        project(3, product)
        project(0, product)
        collapses[3].mid()
        scatter.across()
        spreads[0].pass_on(0)
        collapses[2].second()
        trades[2].start()
        trades[1].finish()
        spreads[1].start(0)
        scatter.beside(0)
        scatter.beside(1)
        m_gather.drain()

    pl.run_scoped(
        stage_two,
        pltpu.VMEM((4, 256, TILE), BF), pltpu.VMEM((2, GROUP, HEAD), BF), pltpu.VMEM((2, GROUP, HEAD), BF),
        pltpu.VMEM((GROUP, HEAD), BF), pltpu.VMEM((GROUP, 512), BF), pltpu.VMEM((2, GROUP, HEAD), F32),
        pltpu.VMEM((2, GROUP, HEAD), BF), pltpu.VMEM((GROUP, HEAD), F32), pltpu.VMEM((GROUP, HEAD), F32),
        pltpu.VMEM((WIDTH, GROUP), BF), pltpu.VMEM((4, TILE, 512), BF), pltpu.VMEM((2 * HEAD, GROUP), BF),
        pltpu.VMEM((GROUP, HEAD), jnp.int32), pltpu.VMEM((GROUP, HEAD), F32), pltpu.VMEM((GROUP, HEAD), F32),
    )

    def stage_three(hid, wd):
        last = [load(hid_i, hid), load(wd_i, wd)]
        gain_one = gain_row(0)
        collapses[3].first()
        spreads[0].wait(0)
        spreads[0].start(1)
        spreads[1].pass_on(0)
        collapses[3].mid(1)
        trades[2].finish()
        spreads[2].start(0)
        spreads[0].pass_on(1)
        spreads[1].wait(0)
        spreads[1].start(1)
        collapses[3].second()
        trades[3].start()
        scatter.arrive()

        @pl.loop(0, OWN // 16)
        def _(i):
            rows = pl.ds(pl.multiple_of(i * 16, 16), 16)
            back, gained = norm_back(
                scatter.total(pl.multiple_of(i * 16, 16), 16), x_own[rows].astype(F32), gain_one
            )
            acc[0] += gained
            tile_f[rows] = gm[rows] + back

        stream_trade.start()
        release()
        for c in range(4):
            for which in range(2):
                part = jnp.sum(acc[which, :, c * TILE : (c + 1) * TILE], axis=0, keepdims=True)
                totals[0, 4 * which + c : 4 * which + c + 1, :TILE] = part
        totals[0, 0:2, TILE:] = head_acc[0:2]
        sent = []

        def tell(phase, devices, slots):
            for device, slot in zip(devices, slots):
                copy = remote(totals.at[phase], heard.at[slot], as_.at[slot], ar.at[slot], device)
                copy.start()
                sent.append(copy)

        def listen(phase, slots):
            total = totals[phase]
            for slot in slots:
                remote(heard.at[slot], heard.at[slot], as_.at[slot], ar.at[slot], peer).wait_recv()
                total += heard[slot]
            totals[phase + 1] = total

        tell(0, [peer], [0])
        wait(last)
        pl.semaphore_wait(free, 3)

        def product(rows, c, cols):
            return mm(hid[rows], wd[c])

        project(2, product)
        project(1, product)
        project(3, product)
        scatter.across()
        listen(0, [0])
        tell(1, [up, down, far], [1, 2, 3])
        trades[3].finish()
        spreads[3].start(0)
        spreads[2].pass_on(0)
        project(0, product)
        spreads[1].pass_on(1)
        spreads[3].pass_on(0)
        spreads[2].wait(0)
        spreads[2].start(1)
        scatter.beside(0)
        scatter.beside(1)
        listen(1, [1, 2, 3])
        tell(2, [along(0, o) for o in range(1, 4)], [4, 5, 6])
        spreads[3].wait(0)
        spreads[3].start(1)
        spreads[2].pass_on(1)
        listen(2, [4, 5, 6])
        tell(3, [along(1, o) for o in range(1, 4)], [7, 8, 9])
        scatter.arrive()

        @pl.loop(0, OWN // 16)
        def _(i):
            rows = pl.ds(pl.multiple_of(i * 16, 16), 16)
            tile_b[rows] = (mid[rows] + scatter.total(pl.multiple_of(i * 16, 16), 16)).astype(BF)

        result_trade.start()
        spreads[3].pass_on(1)
        listen(3, [7, 8, 9])
        sums_o[...] = totals[4]
        stream_trade.finish()
        result_trade.finish()
        for spread in spreads:
            spread.wait(1)
        scatter.drain()
        for thing in collapses[1:] + trades + spreads + [stream_trade, result_trade]:
            thing.drain()
        for copy in sent:
            copy.wait_send()

    pl.run_scoped(stage_three, pltpu.VMEM((GROUP, UNITS), BF), pltpu.VMEM((4, UNITS, TILE), BF))


def backward_call(*args):
    hbm = pl.BlockSpec(memory_space=pl.ANY)
    vmem = pl.BlockSpec(memory_space=pltpu.VMEM)
    dma = pltpu.SemaphoreType.DMA
    out = jax.ShapeDtypeStruct
    grads = out((CHUNKS, 4, 4, 4, 48, 512), BF)
    return pl.pallas_call(
        backward_kernel,
        out_shape=[out((TILE, TILE), BF), out((TILE, TILE), F32), grads, out((8, TILE + HEAD), F32)],
        in_specs=[hbm] * 20 + [vmem] * 2,
        out_specs=[hbm] * 3 + [vmem],
        scratch_shapes=[
            pltpu.VMEM((GROUP, WIDTH), BF), pltpu.VMEM((OWN, WIDTH), F32), pltpu.VMEM((GROUP, 512), BF),
            pltpu.VMEM((OWN, WIDTH), F32), pltpu.VMEM((4, 8, TILE), F32),
            pltpu.VMEM((OWN, WIDTH), BF), pltpu.VMEM((OWN, WIDTH), BF), pltpu.VMEM((2, 16, WIDTH), F32),
            pltpu.VMEM((8, HEAD), F32), pltpu.VMEM((OWN, WIDTH), F32), pltpu.VMEM((OWN, WIDTH), BF),
            pltpu.VMEM((5, 8, TILE + HEAD), F32), pltpu.VMEM((10, 8, TILE + HEAD), F32),
        ]
        + GATHER_SEMS
        + scatter_scratch()
        + collapse_scratch()
        + [
            dma((3,)), dma((4,)), dma((3,)), dma((4,)), dma((10,)), dma((10,)), dma((24,)), pltpu.SemaphoreType.REGULAR,
        ],
        compiler_params=pltpu.CompilerParams(
            collective_id=2, has_side_effects=True, vmem_limit_bytes=VMEM_LIMIT
        ),
        cost_estimate=pl.CostEstimate(flops=25_000_000_000, bytes_accessed=100_000_000, transcendentals=2_000_000),
        name="backward",
    )(*args)


PLACE = 4


def place_kernel(grads, result, stream, totals, gate_up, down, qkv, out, result_o, stream_o, one, two, q_o, k_o):
    for c in range(4):
        for u in range(3):
            t = c * 3 + u
            value = grads[u, :, c, :32].reshape(PLACE * 32, 512).astype(F32)
            for g in range(2):
                gate_up[:, g, t * 256 : (t + 1) * 256] = value[:, g * 256 : (g + 1) * 256]
            down[t] = grads[u, :, c, 32:].astype(F32)
        qkv[:, c, :] = grads[3, :, c, :32].reshape(PLACE * 32, 512).astype(F32)
        out[c] = grads[3, :, c, 32:].astype(F32)
    result_o[...] = result[...]
    stream_o[...] = stream[...]
    for c in range(4):
        one[:, c * TILE : (c + 1) * TILE] = totals[c : c + 1, :TILE]
        two[:, c * TILE : (c + 1) * TILE] = totals[4 + c : 5 + c, :TILE]
    q_o[...] = totals[0:1, TILE:]
    k_o[...] = totals[1:2, TILE:]


def place_grads(grads, result, stream, totals):
    tile = pl.BlockSpec((32 * PLACE, TILE), lambda p: (p, 0))

    def whole(*shape):
        return pl.BlockSpec(shape, lambda p: (0,) * len(shape))

    return pl.pallas_call(
        place_kernel,
        grid=(DP // PLACE,),
        in_specs=[
            pl.BlockSpec((CHUNKS, PLACE, 4, 48, 512), lambda p: (0, p, 0, 0, 0)), tile, tile, whole(8, TILE + HEAD),
        ],
        out_specs=[
            pl.BlockSpec((32 * PLACE, 2, 4 * UNITS), lambda p: (p, 0, 0)),
            pl.BlockSpec((12, PLACE, 16, TILE), lambda p: (0, p, 0, 0)),
            pl.BlockSpec((32 * PLACE, 4, 512), lambda p: (p, 0, 0)),
            pl.BlockSpec((4, PLACE, 16, TILE), lambda p: (0, p, 0, 0)),
            tile, tile, whole(1, WIDTH), whole(1, WIDTH), whole(1, HEAD), whole(1, HEAD),
        ],
        out_shape=[
            jax.ShapeDtypeStruct((TILE, 2, 4 * UNITS), F32),
            jax.ShapeDtypeStruct((12, DP, 16, TILE), F32),
            jax.ShapeDtypeStruct((TILE, 4, 512), F32),
            jax.ShapeDtypeStruct((4, DP, 16, TILE), F32),
            jax.ShapeDtypeStruct((TILE, TILE), BF),
            jax.ShapeDtypeStruct((TILE, TILE), F32),
            jax.ShapeDtypeStruct((1, WIDTH), F32),
            jax.ShapeDtypeStruct((1, WIDTH), F32),
            jax.ShapeDtypeStruct((1, HEAD), F32),
            jax.ShapeDtypeStruct((1, HEAD), F32),
        ],
        compiler_params=pltpu.CompilerParams(vmem_limit_bytes=VMEM_LIMIT),
        cost_estimate=pl.CostEstimate(flops=0, bytes_accessed=41_000_000, transcendentals=0),
        name="place",
    )(grads, result, stream, totals)


def body(
    tokens, norm1_gain, w_qkv, q_gain, k_gain, w_out, norm2_gain, w_gate_up, w_down, out_grad,
    seq_lengths, seq_group, seq_start,
):
    (h2, g, wq, wo, wg, wd, h1t, raw, qs, ks, att, lse, middle, gain, x_own, start, cosine, sine, ggu, hid) = forward_call(
        tokens, out_grad, norm1_gain[None], norm2_gain[None], q_gain[None], k_gain[None], jnp.asarray(FREQ),
        seq_lengths, seq_group, seq_start, w_qkv, w_gate_up,
        w_out.reshape(4, 4, 2, 32, TILE), w_down.reshape(4, 3, 4, 4, 16, TILE),
    )
    wg = wg.reshape(4, TILE, 2 * UNITS)
    wd = wd.reshape(4, UNITS, TILE)
    result, stream, grads, totals = backward_call(
        h2, ggu, hid, g, wg, wd, wo.reshape(4, 256, TILE), wq.reshape(4, TILE, 512), h1t, raw, qs, ks, att, lse,
        middle, gain, x_own, start, cosine, sine, q_gain[None], k_gain[None],
    )
    grads = grads.reshape(CHUNKS, DP, 4, 48, 512)
    g_gate_up, g_down, g_qkv, g_out, result, stream, one, two, q_grad, k_grad = place_grads(grads, result, stream, totals)
    return (
        result,
        stream,
        one.reshape(WIDTH),
        g_qkv,
        q_grad.reshape(HEAD),
        k_grad.reshape(HEAD),
        g_out.reshape(w_out.shape),
        two.reshape(WIDTH),
        g_gate_up,
        g_down.reshape(w_down.shape),
    )


def solution(mesh):
    in_specs = (
        P(("dp", "row"), "col"),
        P("col"),
        P("col", "row", None),
        P(),
        P(),
        P("row", "col"),
        P("col"),
        P("col", None, "row"),
        P("row", "col"),
        P(("dp", "row"), "col"),
        P(),
        P(),
        P(),
    )
    out_specs = (
        P(("dp", "row"), "col"),
        P(("dp", "row"), "col"),
        P(),
        P("col", "row", None),
        P(),
        P(),
        P("row", "col"),
        P(),
        P("col", None, "row"),
        P("row", "col"),
    )
    return jax.shard_map(body, mesh=mesh, in_specs=in_specs, out_specs=out_specs, check_vma=False)
```

```python
import math

import jax
import jax.numpy as jnp
import numpy as np
from jax import lax
from jax.experimental import pallas as pl
from jax.experimental.pallas import tpu as pltpu
from jax.sharding import PartitionSpec as P

EPS = 1e-06
THETA = 1000000.0
BF = jnp.bfloat16
F32 = jnp.float32
Z = ("row", "col")
MESH = pl.DeviceIdType.MESH
VMEM_LIMIT = 63 * 1024 * 1024

GROUP, WIDTH, TILE, UNITS, HEAD = 1024, 2048, 512, 768, 128
OWN = GROUP // 8
DP = 16


def dot(left, right, dims):
    return lax.dot_general(left, right, (dims, ((), ())), preferred_element_type=F32)


def mm(left, right):
    return dot(left, right, ((1,), (0,)))


def mm_t(left, right):
    return dot(left, right, ((1,), (1,)))


def t_mm(left, right):
    return dot(left, right, ((0,), (0,)))


def place():
    row, col = lax.axis_index("row"), lax.axis_index("col")
    j = 4 * row + col
    return lax.axis_index("dp"), row, col, j // 2, j % 2


def on_ring(z, k):
    j = 2 * z + k
    return {"row": j // 4, "col": j % 4}


def remote(src, dst, send, recv, device):
    return pltpu.make_async_remote_copy(
        src_ref=src, dst_ref=dst, send_sem=send, recv_sem=recv, device_id=device, device_id_type=MESH
    )


def meet(devices):
    barrier = pltpu.get_barrier_semaphore()
    for device in devices:
        pl.semaphore_signal(barrier, inc=1, device_id=device, device_id_type=MESH)
    pl.semaphore_wait(barrier, len(devices))


def ring_friends():
    _, _, _, z, k = place()
    other = z + 1 - 2 * (z % 2)
    return [
        on_ring((z + 1) % 4, k),
        on_ring((z + 3) % 4, k),
        on_ring(z, 1 - k),
        on_ring(other, 1 - k),
    ]


def column_friends():
    _, _, _, z, k = place()
    me = 2 * z + k
    return [on_ring((me + o) % 8 // 2, (me + o) % 2) for o in range(1, 8)]


def dp_place():
    p = lax.axis_index("dp")
    return p // 4, p % 4


def along(axis, o):
    px, py = dp_place()
    return {"dp": (px + o) % 4 * 4 + py} if axis == 0 else {"dp": px * 4 + (py + o) % 4}


def xy_friends():
    return [along(axis, o) for axis in range(2) for o in range(1, 4)]


def tile_at(buf):
    def loc(j, half=None):
        row, col = j // 4, j % 4
        first = pl.multiple_of(row * TILE, TILE)
        rows = pl.ds(first, TILE)
        if half is not None:
            rows = pl.ds(first + half * (TILE // 2), TILE // 2)
        return buf.at[rows, pl.ds(pl.multiple_of(col * TILE, TILE), TILE)]

    return loc


def rows_at(buf):
    def loc(j, half=None):
        first = pl.multiple_of(j * OWN, OWN)
        rows = pl.ds(first, OWN)
        if half is not None:
            rows = pl.ds(first + half * (OWN // 2), OWN // 2)
        return buf.at[rows]

    return loc


class Gather:
    def __init__(self, loc, send, recv, own=None):
        _, _, _, z, k = place()
        up, down, far = (z + 1) % 4, (z + 3) % 4, (z + 2) % 4
        to_up, to_down, peer = on_ring(up, k), on_ring(down, k), on_ring(z, 1 - k)

        def out(slot, src, dst, device):
            return remote(src, dst, send.at[slot], recv.at[slot], device)

        def into(slot, dst):
            return remote(dst, dst, send.at[slot], recv.at[slot], peer)

        mine = loc(2 * z + k)
        own = mine if own is None else own
        left, right, across = 2 * down + k, 2 * up + k, 2 * far + k
        self.first = [out(0, own, mine, to_up), out(1, own, mine, to_down), out(4, own, mine, peer)]
        self.from_left = [
            out(2, loc(left, 0), loc(left, 0), to_up),
            out(5, loc(left), loc(left), peer),
        ]
        self.from_right = [
            out(3, loc(right, 1), loc(right, 1), to_down),
            out(6, loc(right), loc(right), peer),
        ]
        self.from_far = [
            out(7, loc(across, 0), loc(across, 0), peer),
            out(8, loc(across, 1), loc(across, 1), peer),
        ]
        theirs = [2 * z + 1 - k, 2 * down + 1 - k, 2 * up + 1 - k, 2 * far + 1 - k]
        self.arrivals = {
            0: into(0, loc(left)),
            1: into(1, loc(right)),
            2: into(2, loc(across, 0)),
            3: into(3, loc(across, 1)),
            4: into(4, loc(theirs[0])),
            5: into(5, loc(theirs[1])),
            6: into(6, loc(theirs[2])),
            7: into(7, loc(theirs[3], 0)),
            8: into(8, loc(theirs[3], 1)),
        }

    def start(self):
        for copy in self.first:
            copy.start()

    def forward(self):
        self.arrivals[0].wait_recv()
        for copy in self.from_left:
            copy.start()
        self.arrivals[1].wait_recv()
        for copy in self.from_right:
            copy.start()

    def share(self):
        for half in range(2):
            self.arrivals[2 + half].wait_recv()
            self.from_far[half].start()

    def finish(self, slots=range(4, 9)):
        for slot in slots:
            self.arrivals[slot].wait_recv()

    def drain(self):
        for copy in self.first + self.from_left + self.from_right + self.from_far:
            copy.wait_send()


GATHER_SEMS = [pltpu.SemaphoreType.DMA((9,)), pltpu.SemaphoreType.DMA((9,))]


class Spread:
    def __init__(self, at, bulk, send, recv, which=()):
        px, py = dp_place()
        here = (px, py)
        self.bulk, self.send, self.recv, self.which = bulk, send, recv, which
        self.out = {}
        for phase in range(2):
            for step in range(2):
                self.out[phase, step] = []
            for half in range(2):
                axis = half ^ phase

                def block(o, part=None):
                    whose = [px, py]
                    whose[axis] = (here[axis] + o) % 4
                    if phase:
                        whose[1 - axis] = None
                    return at(half, *whose, part)

                def copy(step, ref, o):
                    sems = (send.at[(*which, phase)], recv.at[(*which, phase, step)])
                    self.out[phase, step].append(remote(ref, ref, *sems, along(axis, o)))

                copy(0, block(0), 1)
                copy(0, block(0), 3)
                copy(1, block(3, 0), 1)
                copy(1, block(1, 1), 3)

    def sized(self, phase, count, step=0):
        ref = self.bulk(phase, count)
        sems = (self.send.at[(*self.which, phase)], self.recv.at[(*self.which, phase, step)])
        return remote(ref, ref, *sems, along(0, 1))

    def start(self, phase):
        for copy in self.out[phase, 0]:
            copy.start()

    def pass_on(self, phase):
        self.sized(phase, 4).wait_recv()
        for copy in self.out[phase, 1]:
            copy.start()

    def wait(self, phase):
        self.sized(phase, 2, 1).wait_recv()

    def drain(self):
        for phase in range(2):
            self.sized(phase, 6).wait_send()


SPREAD_SEMS = [pltpu.SemaphoreType.DMA((2,)), pltpu.SemaphoreType.DMA((2, 2))]


class Scatter:
    def __init__(self, parts, theirs, sums, near, full, send, recv):
        _, _, _, z, k = place()
        self.parts, self.theirs, self.sums, self.near, self.full = parts, theirs, sums, near, full
        self.k = k
        to_up, to_down = on_ring((z + 1) % 4, k), on_ring((z + 3) % 4, k)
        peer = on_ring(z, 1 - k)
        half = OWN // 2
        other = pl.ds(pl.multiple_of((1 - k) * OWN, OWN), OWN)

        def copy(slot, src, dst, device):
            return remote(src, dst, send.at[slot], recv.at[slot], device)

        self.copies = [copy(d, parts.at[d, other], theirs.at[d], peer) for d in range(4)] + [
            copy(4, sums.at[0, pl.ds(0, half)], near.at[0], to_up),
            copy(5, sums.at[0, pl.ds(half, half)], near.at[1], to_down),
            copy(6, sums.at[1], full.at[0], to_up),
            copy(7, sums.at[2], full.at[1], to_down),
        ]

    def put(self, d):
        self.copies[d].start()

    def own(self, d, rows, count):
        first = pl.multiple_of(self.k * OWN + rows, count)
        return self.parts[d, pl.ds(first, count)].astype(F32) + self.theirs[
            d, pl.ds(rows, count)
        ].astype(F32)

    def across(self):
        self.copies[2].wait_recv()

        @pl.loop(0, OWN // 16)
        def _(i):
            rows = pl.multiple_of(i * 16, 16)
            self.sums[0, pl.ds(rows, 16)] = self.own(2, rows, 16).astype(BF)

        self.copies[4].start()
        self.copies[5].start()

    def beside(self, side):
        d, half = (1, 3)[side], OWN // 2
        self.copies[d].wait_recv()
        self.copies[4 + side].wait_recv()

        @pl.loop(0, half // 16)
        def _(i):
            rows = pl.multiple_of(i * 16, 16)
            here = pl.multiple_of(rows + side * half, 16)
            there = pl.multiple_of(rows + (1 - side) * half, 16)
            added = self.own(d, here, 16) + self.near[side, pl.ds(rows, 16)].astype(F32)
            self.sums[1 + side, pl.ds(here, 16)] = added.astype(BF)
            self.sums[1 + side, pl.ds(there, 16)] = self.own(d, there, 16).astype(BF)

        self.copies[6 + side].start()

    def arrive(self):
        self.copies[0].wait_recv()
        self.copies[6].wait_recv()
        self.copies[7].wait_recv()

    def total(self, rows, count):
        return (
            self.own(0, rows, count)
            + self.full[0, pl.ds(rows, count)].astype(F32)
            + self.full[1, pl.ds(rows, count)].astype(F32)
        )

    def drain(self):
        for copy in self.copies:
            copy.wait_send()


def scatter_scratch():
    return [
        pltpu.VMEM((4, 2 * OWN, WIDTH), BF),
        pltpu.VMEM((4, OWN, WIDTH), BF),
        pltpu.VMEM((3, OWN, WIDTH), BF),
        pltpu.VMEM((2, OWN // 2, WIDTH), BF),
        pltpu.VMEM((2, OWN, WIDTH), BF),
        pltpu.SemaphoreType.DMA((8,)),
        pltpu.SemaphoreType.DMA((8,)),
    ]


def head_norm(value):
    return lax.rsqrt(jnp.mean(value * value, axis=1, keepdims=True) + EPS)


def turn(value, cosine, sine):
    return value * cosine + pltpu.roll(value, HEAD // 2, 1) * sine


def turn_back(value, cosine, sine):
    return value * cosine - pltpu.roll(value, HEAD // 2, 1) * sine


LOG2 = math.log2(math.e)
SCALE = 1.0 / math.sqrt(HEAD)
QROWS = 256


def allowed_keys(start, first, keys):
    slots = lax.broadcasted_iota(jnp.int32, (QROWS, keys), 1)
    query = lax.broadcasted_iota(jnp.int32, (QROWS, keys), 0) + first
    return (slots >= start) & (slots <= query)


FREQ = np.tile(THETA ** (-(np.arange(HEAD // 2) * 2.0 / HEAD)), 2)[None].astype(np.float32)


def forward_kernel(
    tok, og, norm1, norm2, q_gain, k_gain, freq, lengths, groups, starts, w_qkv, w_gu, w_out, w_down,
    h2_o, g_o, wq_o, wo_o, wg_o, wd_o, h1t_o, raw_o, q_o, k_o, att_o, lse_o, mid_o, gain_o, x_o, start_o, cos_o, sin_o,
    ggu_o, hid_o,
    x, h1, h1t, h2, g, wq, wg, wd, w_all, raw, qs, ks, att, heard, lse, mid, gain, gains, start, cosine, sine,
    q_raw, q_cut, q_raw_part, q_part, g_raw, g_cut, g_raw_part, g_part,
    xs, xr, gs, gr, hs, hr,
    zs, zr, ps, pr, ns, nr, loc_s, out_s, raw_s, row_s, os_, or_, ts, tr,
    y0s, y0r, y1s, y1r, y2s, y2r, y3s, y3r, y4s, y4r,
):
    p, row, col, z, k = place()
    px, py = dp_place()
    me = 2 * z + k
    lo = z % 2
    other = z + 1 - 2 * lo
    peer = on_ring(z, 1 - k)
    beside_col = 2 * lo + 1 - k
    piece_rows = pl.ds(pl.multiple_of(p * 32, 32), 32)

    def lanes(first, count):
        return pl.ds(pl.multiple_of(first, 256), count)

    raws = [
        pltpu.make_async_copy(src, dst, raw_s.at[i])
        for i, (src, dst) in enumerate(
            [
                (w_qkv.at[piece_rows], q_raw_part),
                (w_gu.at[piece_rows, :, lanes((1 - lo) * 2 * UNITS, 2 * UNITS)], g_raw_part),
                (w_qkv, q_raw),
                (w_gu.at[:, :, lanes(lo * 2 * UNITS, 2 * UNITS)], g_raw),
            ]
        )
    ]
    for copy in raws:
        copy.start()
    gains[0:1] = norm1[...]
    gains[1:2] = norm2[...]
    meet(column_friends() + xy_friends())
    raws[0].wait()
    for kk in range(2):
        q_part[kk] = jnp.where(lo == 0, q_raw_part[:, 2 + kk, :], q_raw_part[:, kk, :])

    gain[col] = gains[...]
    gain_copies = [
        remote(gains, gain.at[col], ns.at[i], nr.at[col], device)
        for i, device in enumerate([peer, on_ring(other, k), on_ring(other, 1 - k)])
    ]

    weights = [wq, wg, wd]
    blocks = [q_cut, g_cut, w_down]

    def cell(weight, c, xx, yy, cols=slice(None)):
        between = (slice(None),) * (len(weight.shape) - 5)
        return weight.at[(c, *between, xx, yy, slice(None), cols)]

    def crossing(a, kk):
        src = (q_part.at[kk], g_part.at[kk], cell(w_down, 2 * (1 - lo) + kk, px, py))[a]
        return remote(src, cell(weights[a], col, px, py), zs.at[a, kk], zr.at[a, k], on_ring(other, kk))

    def crossed(a, kk):
        dst = cell(weights[a], 2 * (1 - lo) + kk, px, py)
        return remote(dst, dst, zs.at[a, kk], zr.at[a, kk], peer)

    def beside(a):
        mine, theirs = (col, beside_col) if a == 2 else (k, 1 - k)
        keep = pltpu.make_async_copy(blocks[a].at[mine], weights[a].at[col], loc_s.at[a])
        give = remote(blocks[a].at[theirs], weights[a].at[col], ps.at[a], pr.at[a], peer)
        take = remote(weights[a].at[beside_col], weights[a].at[beside_col], ps.at[a], pr.at[a], peer)
        return keep, give, take

    def spread_at(a):
        weight = weights[a]
        half_lanes = weight.shape[-1] // 2

        def at(half, xx, yy, part):
            xs_ = slice(None) if xx is None else xx
            ys_ = slice(None) if yy is None else yy
            cols = slice(None) if part is None else pl.ds(part * half_lanes, half_lanes)
            return cell(weight, 2 * (1 - lo) + half, xs_, ys_, cols)

        return at

    def spread_bulk(a):
        weight = weights[a]
        between = (slice(None),) * (len(weight.shape) - 5)

        def bulk(phase, count):
            cs, long, short = {2: (1, 2, 1), 4: (1, 4, 1), 6: (2, 3, 1)}[count]
            xs_, ys_ = (long, 4) if phase else (short, long)
            return weight.at[(pl.ds(0, cs), *between, pl.ds(0, xs_), pl.ds(0, ys_))]

        return bulk

    spreads = [
        Spread(spread_at(a), spread_bulk(a), send, recv)
        for a, (send, recv) in enumerate([(y0s, y0r), (y1s, y1r), (y2s, y2r)])
    ]

    pair = pl.ds(2 * (1 - lo), 2)
    groups_of = [(1 - row, slice(None)), (row, pair)]

    def out_at(which):
        def at(half, xx, yy, part):
            xs_ = slice(None) if xx is None else xx
            ys_ = slice(None) if yy is None else yy
            cols = pl.ds(half * 256, 256) if part is None else pl.ds(half * 256 + part * HEAD, HEAD)
            return w_all.at[(*groups_of[which], xs_, ys_, k, slice(None), cols)]

        return at

    def out_bulk(which):
        def bulk(phase, count):
            xs_, ys_ = (count // 2, 4) if phase else (1, count // 2)
            return w_all.at[0, pl.ds(0, 4 - 2 * which), pl.ds(0, xs_), pl.ds(0, ys_), 0]

        return bulk

    out_spreads = [Spread(out_at(0), out_bulk(0), y3s, y3r), Spread(out_at(1), out_bulk(1), y4s, y4r)]
    out_pieces = [
        remote(
            w_out.at[px, py, kk], w_all.at[row, col, px, py, kk],
            os_.at[2 * dz + kk], or_.at[me], on_ring((z + dz) % 4, kk),
        )
        for dz in (1, 3, 2)
        for kk in range(2)
    ]
    keep_out = pltpu.make_async_copy(w_out, w_all.at[row, col], loc_s.at[3])
    give_out = remote(w_out, w_all.at[row, col], os_.at[0], or_.at[me], peer)

    def out_arrived(j):
        dst = w_all.at[j // 4, j % 4, px, py, k]
        return remote(dst, dst, os_.at[0], or_.at[j], peer)

    def out_share(which, core):
        ref = w_all.at[(*groups_of[which], slice(None), slice(None), core)]
        return remote(ref, ref, ts.at[7 + which], tr.at[7 + which], peer)

    def hand(o):
        there = (me + o) % 8
        rows = pl.ds(pl.multiple_of(there * OWN, OWN), OWN)
        device = {"row": there // 4, "col": there % 4}
        return remote(att.at[:, rows], heard.at[me], ts.at[o - 1], tr.at[o - 1], device)

    def handed(o):
        dst = heard.at[(me + 8 - o) % 8]
        return remote(dst, dst, ts.at[o - 1], tr.at[o - 1], peer)

    for kk in range(2):
        crossing(0, kk).start()
    for copy in out_pieces:
        copy.start()
    x_gather = Gather(tile_at(x), xs, xr, tok)
    x_gather.start()
    for copy in gain_copies:
        copy.start()
    keep_x = pltpu.make_async_copy(tok, tile_at(x)(me), loc_s.at[4])
    keep_x.start()
    keep_g = pltpu.make_async_copy(og, tile_at(g)(me), loc_s.at[5])
    keep_g.start()
    keep_out.start()
    give_out.start()
    raws[2].wait()

    @pl.loop(0, 16)
    def _(i):
        rows = pl.ds(pl.multiple_of(i * 32, 32), 32)
        for kk in range(2):
            q_cut[kk, i // 4, i % 4] = jnp.where(lo == 0, q_raw[rows, kk, :], q_raw[rows, 2 + kk, :])

    beside(0)[0].start()
    beside(0)[1].start()
    for kk in range(2):
        crossed(0, kk).wait_recv()
    spreads[0].start(0)
    for dz in (1, 3, 2):
        for kk in range(2):
            out_arrived(2 * ((z + dz) % 4) + kk).wait_recv()
    for spread in out_spreads:
        spread.start(0)
    for a in (1, 3):
        raws[a].wait()
    slot = (
        lax.broadcasted_iota(jnp.int32, (8, HEAD), 0) * HEAD + lax.broadcasted_iota(jnp.int32, (8, HEAD), 1)
    ).astype(F32)

    def one_sequence(i, begun):
        first = starts[i].astype(F32)
        last = first + jnp.where(groups[i] == p, lengths[i], 0).astype(F32)
        return jnp.where((slot >= first) & (slot < last), first, begun)

    begun = lax.fori_loop(0, lengths.shape[0], one_sequence, jnp.zeros((8, HEAD), F32))
    for i in range(8):
        rows = slice(i * HEAD, (i + 1) * HEAD)
        begin = jnp.broadcast_to(begun[i : i + 1], (HEAD, HEAD)).T
        there = lax.broadcasted_iota(jnp.int32, (HEAD, HEAD), 0).astype(F32) + float(i * HEAD)
        angle = (there - begin) * freq[...]
        start[rows] = begin.astype(jnp.int32)
        cosine[rows] = jnp.cos(angle)
        lane = lax.broadcasted_iota(jnp.int32, (HEAD, HEAD), 1)
        sine[rows] = jnp.where(lane < HEAD // 2, -1.0, 1.0) * jnp.sin(angle)
    spreads[0].pass_on(0)
    for spread in out_spreads:
        spread.pass_on(0)
    for u in range(3):
        for half in range(2):
            into = slice(u * 512 + half * 256, u * 512 + half * 256 + 256)
            for kk in range(2):
                cols = slice(kk * UNITS + u * 256, kk * UNITS + u * 256 + 256)
                g_part[kk, :, into] = g_raw_part[:, half, cols]
    spreads[0].wait(0)
    spreads[0].start(1)
    x_gather.forward()
    spreads[0].pass_on(1)
    for spread in out_spreads:
        spread.wait(0)
        spread.start(1)
    for c in range(4):

        @pl.when(c != col)
        def _():
            remote(gain.at[c], gain.at[c], ns.at[0], nr.at[c], peer).wait_recv()

    keep_x.wait()
    x_gather.finish([4, 5, 6])

    def gain_row(which):
        return jnp.concatenate([gain[c, which : which + 1] for c in range(4)], axis=1)

    gain_one = gain_row(0)

    def norm_one(half):
        @pl.loop(0, TILE // 64)
        def _(i):
            rows = pl.ds(pl.multiple_of(half * TILE + i * 64, 64), 64)
            value = x[rows].astype(F32)
            h1[rows] = (value * head_norm(value) * gain_one).astype(BF)

    def heads(half):
        @pl.loop(0, TILE // 256)
        def _(i):
            rows = pl.ds(pl.multiple_of(half * TILE + i * 256, 256), 256)
            mixed = mm(h1[rows], wq[...].reshape(WIDTH, 4 * HEAD)).astype(BF)
            raw[rows] = mixed
            cos_rows, sin_rows = cosine[rows], sine[rows]
            for piece in range(3):
                value = mixed[:, piece * HEAD : (piece + 1) * HEAD].astype(F32)
                by = q_gain[...] if piece < 2 else k_gain[...]
                turned = turn(value * head_norm(value) * by, cos_rows, sin_rows).astype(BF)
                if piece < 2:
                    qs[piece, rows] = turned
                else:
                    ks[rows] = turned

    norm_one(row)
    keep, _, take = beside(0)
    keep.wait()
    take.wait_recv()
    spreads[0].wait(1)
    heads(row)
    x_gather.share()
    for a in (1, 2):
        for kk in range(2):
            crossing(a, kk).start()
    beside(2)[0].start()
    beside(2)[1].start()
    g_gather = Gather(tile_at(g), gs, gr, og)
    g_gather.start()
    x_gather.finish([7, 8])
    for spread in out_spreads:
        spread.pass_on(1)
    norm_one(1 - row)
    heads(1 - row)
    mine = pl.ds(pl.multiple_of(me * OWN, OWN), OWN)
    saves = [
        pltpu.make_async_copy(src, dst, out_s.at[i])
        for i, (src, dst) in enumerate(
            [
                (wq, wq_o), (raw, raw_o), (qs, q_o), (ks, k_o), (gain, gain_o), (x.at[mine], x_o),
                (start, start_o), (cosine, cos_o), (sine, sin_o),
                (att, att_o), (lse, lse_o), (h1t, h1t_o), (g, g_o), (mid, mid_o),
                (w_all.at[row, :, pl.ds(col, 1)], wo_o),
            ]
        )
    ]
    for i in range(9):
        saves[i].start()

    for block in range(GROUP // QROWS):
        first, keys = block * QROWS, (block + 1) * QROWS
        rows = pl.ds(first, QROWS)
        allowed = allowed_keys(start[rows, :1], first, keys)

        @pl.loop(0, 2)
        def _(h):
            score = mm_t(qs[h, rows], ks[:keys]) * (SCALE * LOG2)
            score = jnp.where(allowed, score, -1e30)
            peak = jnp.max(score, axis=1, keepdims=True)
            weight = jnp.exp2(score - peak)
            total = jnp.sum(weight, axis=1, keepdims=True)
            out = mm(weight.astype(BF), raw[:keys, 3 * HEAD :]) / total
            att[h, rows] = out.astype(BF)
            lse[h, rows] = jnp.broadcast_to(peak + jnp.log2(total), (QROWS, HEAD))

        if block == 1:
            for a in (1, 2):
                for kk in range(2):
                    crossed(a, kk).wait_recv()
                spreads[a].start(0)

    for which, spread in enumerate(out_spreads):
        spread.wait(1)
        out_share(which, k).start()
    for o in range(1, 8):
        hand(o).start()
    for h in range(2):
        heard[me, h] = att[h, mine]
    saves[9].start()
    saves[10].start()
    for a in (1, 2):
        spreads[a].pass_on(0)
    for a in (1, 2):
        spreads[a].wait(0)
        spreads[a].start(1)
    def cut(i):
        rows = pl.ds(pl.multiple_of(i * 32, 32), 32)
        for u in range(3):
            for half in range(2):
                into = slice(u * 512 + half * 256, u * 512 + half * 256 + 256)
                for kk in range(2):
                    cols = slice(kk * UNITS + u * 256, kk * UNITS + u * 256 + 256)
                    g_cut[kk, i // 4, i % 4, :, into] = g_raw[rows, half, cols]

    pl.loop(0, 8)(cut)
    g_gather.forward()
    pl.loop(8, 16)(cut)
    beside(1)[0].start()
    beside(1)[1].start()
    keep_out.wait()
    out_arrived_peer = w_all.at[row, beside_col]
    remote(out_arrived_peer, out_arrived_peer, os_.at[0], or_.at[2 * z + 1 - k], peer).wait_recv()
    for which in range(2):
        out_share(which, 1 - k).wait_recv()
    saves[14].start()
    for o in range(1, 8):
        handed(o).wait_recv()
    left = [
        jnp.concatenate([heard[4 * half + c, h] for c in range(4) for h in range(2)], axis=1) for half in range(2)
    ]
    for c in range(4):
        mid[:, c * TILE : (c + 1) * TILE] = mm(left[0], w_all[0, c].reshape(2 * TILE, TILE)) + mm(
            left[1], w_all[1, c].reshape(2 * TILE, TILE)
        )
    gain_two = gain_row(1)

    @pl.loop(0, OWN // 16)
    def _(i):
        first = pl.multiple_of(i * 16, 16)
        there = pl.ds(pl.multiple_of(me * OWN + first, 16), 16)
        value = x[there].astype(F32) + mid[pl.ds(first, 16)]
        mid[pl.ds(first, 16)] = value
        h2[there] = (value * head_norm(value) * gain_two).astype(BF)

    h2_gather = Gather(rows_at(h2), hs, hr)
    h2_gather.start()
    saves[13].start()

    @pl.loop(0, 8)
    def _(i):
        cols = pl.ds(pl.multiple_of(i * 256, 256), 256)
        h1t[cols] = h1[:, cols].T

    saves[11].start()
    g_gather.share()
    for a in (1, 2):
        spreads[a].pass_on(1)
    x_gather.drain()
    saves[5].wait()
    row_saves = []

    def feed(d):
        rows = pl.ds(pl.multiple_of((z + d) % 4 * 256, 256), 256)

        @pl.loop(0, 3)
        def _(u):
            wide = pl.ds(pl.multiple_of(u * 512, 512), 512)
            gate_cols = pl.ds(pl.multiple_of(u * 512, 256), 256)
            up_cols = pl.ds(pl.multiple_of(u * 512 + 256, 256), 256)
            pair_ = mm(h2[rows], wg[:, :, :, :, wide].reshape(WIDTH, 512))
            back = mm_t(g[rows, :TILE], wd[0, u].reshape(256, TILE))
            for c in range(1, 4):
                back += mm_t(g[rows, c * TILE : (c + 1) * TILE], wd[c, u].reshape(256, TILE))
            gate, up = pair_[:, :256], pair_[:, 256:]
            sig = 1.0 / (1.0 + jnp.exp(-gate))
            silu = gate * sig
            h1[rows, pl.ds(pl.multiple_of(u * 256, 256), 256)] = (silu * up).astype(BF)
            x[rows, gate_cols] = (back * up * sig * (1.0 + gate * (1.0 - sig))).astype(BF)
            x[rows, up_cols] = (back * silu).astype(BF)

        for i, (src, dst) in enumerate(
            [
                (h2.at[rows], h2_o.at[rows]),
                (x.at[rows, pl.ds(0, 2 * UNITS)], ggu_o.at[rows]),
                (h1.at[rows, pl.ds(0, UNITS)], hid_o.at[rows]),
            ]
        ):
            copy = pltpu.make_async_copy(src, dst, row_s.at[d, i])
            copy.start()
            row_saves.append(copy)

    for a in (1, 2):
        keep, _, take = beside(a)
        keep.wait()
        take.wait_recv()
        spreads[a].wait(1)
    g_gather.finish()
    keep_g.wait()
    saves[12].start()
    h2_gather.finish([4])
    feed(0)
    h2_gather.forward()
    h2_gather.finish([5, 6])
    feed(1)
    weight_saves = [pltpu.make_async_copy(weights[a], (wg_o, wd_o)[a - 1], loc_s.at[a + 5]) for a in (1, 2)]
    for copy in weight_saves:
        copy.start()
    h2_gather.share()
    feed(3)
    h2_gather.finish([7, 8])
    feed(2)
    for copy in gain_copies + out_pieces + [give_out]:
        copy.wait_send()
    for a in range(3):
        beside(a)[1].wait_send()
        for kk in range(2):
            crossing(a, kk).wait_send()
    for o in range(1, 8):
        hand(o).wait_send()
    for which in range(2):
        out_share(which, k).wait_send()
    for spread in spreads + out_spreads:
        spread.drain()
    g_gather.drain()
    h2_gather.drain()
    for i, copy in enumerate(saves):
        if i != 5:
            copy.wait()
    for copy in weight_saves + row_saves:
        copy.wait()


def forward_call(*args):
    hbm = pl.BlockSpec(memory_space=pl.ANY)
    vmem = pl.BlockSpec(memory_space=pltpu.VMEM)
    smem = pl.BlockSpec(memory_space=pltpu.SMEM)
    dma = pltpu.SemaphoreType.DMA

    def out(shape, dtype=BF):
        return jax.ShapeDtypeStruct(shape, dtype)

    wide = (GROUP, WIDTH)
    return pl.pallas_call(
        forward_kernel,
        out_shape=[
            out(wide), out(wide), out((4, 4, 4, 32, 512)), out((4, 1, 4, 2, 32, TILE)), out((4, 4, 4, 32, 2 * UNITS)),
            out((4, 3, 4, 4, 16, TILE)), out((WIDTH, GROUP)), out((GROUP, 512)), out((2, GROUP, HEAD)), out((GROUP, HEAD)),
            out((2, GROUP, HEAD)), out((2, GROUP, HEAD), F32), out((OWN, WIDTH), F32), out((4, 8, TILE), F32),
            out((OWN, WIDTH)), out((GROUP, HEAD), jnp.int32), out((GROUP, HEAD), F32), out((GROUP, HEAD), F32),
            out((GROUP, 2 * UNITS)), out((GROUP, UNITS)),
        ],
        in_specs=[hbm] * 2 + [vmem] * 5 + [smem] * 3 + [hbm] * 4,
        out_specs=[hbm] * 20,
        scratch_shapes=[
            pltpu.VMEM(wide, BF), pltpu.VMEM(wide, BF), pltpu.VMEM((WIDTH, GROUP), BF), pltpu.VMEM(wide, BF),
            pltpu.VMEM(wide, BF), pltpu.VMEM((4, 4, 4, 32, 512), BF), pltpu.VMEM((4, 4, 4, 32, 2 * UNITS), BF),
            pltpu.VMEM((4, 3, 4, 4, 16, TILE), BF), pltpu.VMEM((2, 4, 4, 4, 2, 32, TILE), BF),
            pltpu.VMEM((GROUP, 512), BF), pltpu.VMEM((2, GROUP, HEAD), BF), pltpu.VMEM((GROUP, HEAD), BF),
            pltpu.VMEM((2, GROUP, HEAD), BF), pltpu.VMEM((8, 2, OWN, HEAD), BF), pltpu.VMEM((2, GROUP, HEAD), F32),
            pltpu.VMEM((OWN, WIDTH), F32), pltpu.VMEM((4, 8, TILE), F32), pltpu.VMEM((8, TILE), F32),
            pltpu.VMEM((GROUP, HEAD), jnp.int32), pltpu.VMEM((GROUP, HEAD), F32), pltpu.VMEM((GROUP, HEAD), F32),
            pltpu.VMEM((TILE, 4, 512), BF), pltpu.VMEM((2, 4, 4, 32, 512), BF), pltpu.VMEM((32, 4, 512), BF),
            pltpu.VMEM((2, 32, 512), BF), pltpu.VMEM((TILE, 2, 2 * UNITS), BF), pltpu.VMEM((2, 4, 4, 32, 2 * UNITS), BF),
            pltpu.VMEM((32, 2, 2 * UNITS), BF), pltpu.VMEM((2, 32, 2 * UNITS), BF),
        ]
        + GATHER_SEMS * 3
        + [
            dma((3, 2)), dma((3, 2)), dma((3,)), dma((3,)), dma((3,)), dma((4,)), dma((8,)), dma((15,)), dma((4,)),
            dma((4, 3)), dma((8,)), dma((8,)), dma((9,)), dma((9,)),
        ]
        + SPREAD_SEMS * 5,
        compiler_params=pltpu.CompilerParams(
            collective_id=1, has_side_effects=True, vmem_limit_bytes=VMEM_LIMIT
        ),
        cost_estimate=pl.CostEstimate(flops=14_000_000_000, bytes_accessed=60_000_000, transcendentals=2_000_000),
        name="forward",
    )(*args)


class Collapse:
    def __init__(self, which, data, near, full, done, send, recv):
        here = dp_place()
        self.which, self.data, self.near, self.full, self.done, self.here = which, data, near, full, done, here
        self.copies, self.send, self.recv = {}, send, recv
        for half in range(2):
            for phase in range(2):
                axis = half ^ phase

                def copy(slot, src, dst, o):
                    return remote(src, dst, send.at[which, phase], recv.at[which, phase, slot // 2], along(axis, o))

                self.copies[half, phase] = [
                    copy(0, self.block(half, phase, 2, 0), near[phase].at[half, 0], 1),
                    copy(1, self.block(half, phase, 2, 1), near[phase].at[half, 1], 3),
                    copy(2, self.block(half, phase, 1), full[phase].at[half, 0], 1),
                    copy(3, self.block(half, phase, 3), full[phase].at[half, 1], 3),
                ]

    def at(self, half, phase, o):
        there = (self.here[half ^ phase] + o) % 4
        if phase == 0:
            return (there, slice(None)) if half == 0 else (slice(None), there)
        return (self.here[0], there) if half == 0 else (there, self.here[1])

    def block(self, half, phase, o, part=None):
        which = pl.ds(2 * half, 2) if part is None else 2 * half + part
        return self.data.at[(*self.at(half, phase, o), which)]

    def cell(self, half, phase, o, a, c):
        x, y = self.at(half, phase, o)
        x, y = (a if isinstance(x, slice) else x), (a if isinstance(y, slice) else y)
        return (x, y, 2 * half + c)

    def arrived(self, phase, step):
        ref = (self.near, self.full)[step][phase]
        sems = (self.send.at[self.which, phase], self.recv.at[self.which, phase, step])
        remote(ref, ref, *sems, along(0, 1)).wait_recv()

    def start(self, phase=0):
        for half in range(2):
            for slot in range(2):
                self.copies[half, phase][slot].start()

    def mid(self, phase=0):
        self.arrived(phase, 0)
        for half in range(2):
            for slot in range(2):

                def add(a):
                    index = self.cell(half, phase, (1, 3)[slot], a, slot)
                    here = (half, slot, a) if phase == 0 else (half, slot)
                    self.data[index] = (
                        self.data[index].astype(F32) + self.near[phase][here].astype(F32)
                    ).astype(BF)

                if phase == 0:
                    pl.loop(0, 4)(add)
                else:
                    add(0)
                self.copies[half, phase][2 + slot].start()

    def first(self):
        self.arrived(0, 1)
        for half in range(2):

            @pl.loop(0, 4)
            def _(a):
                for c in range(2):
                    index = self.cell(half, 0, 0, a, c)
                    total = self.data[index].astype(F32)
                    for slot in range(2):
                        total += self.full[0][half, slot, a, c].astype(F32)
                    self.data[index] = total.astype(BF)

        self.start(1)

    def second(self):
        self.arrived(1, 1)
        for half in range(2):
            for c in range(2):
                total = self.data[self.cell(half, 1, 0, 0, c)].astype(F32)
                for slot in range(2):
                    total += self.full[1][half, slot, c].astype(F32)
                self.done[self.which, 2 * half + c] = total.astype(BF)

    def drain(self):
        for phase in range(2):
            ref = self.data.at[0, pl.ds(0, 3)] if phase else self.data.at[pl.ds(0, 3)]
            sems = (self.send.at[self.which, phase], self.recv.at[self.which, phase, 0])
            remote(ref, ref, *sems, along(0, 1)).wait_send()


CHUNKS, BUFFERS = 4, 3


def collapse_scratch():
    dma = pltpu.SemaphoreType.DMA
    return (
        [pltpu.VMEM((4, 4, 4, 48, 512), BF)] * BUFFERS
        + [pltpu.VMEM((2, 2, 4, 48, 512), BF)] * BUFFERS
        + [pltpu.VMEM((2, 2, 48, 512), BF)] * BUFFERS
        + [pltpu.VMEM((2, 2, 4, 2, 48, 512), BF)] * BUFFERS
        + [pltpu.VMEM((2, 2, 2, 48, 512), BF)] * BUFFERS
        + [pltpu.VMEM((CHUNKS, 4, 48, 512), BF), dma((CHUNKS, 2)), dma((CHUNKS, 2, 2))]
        + [dma((CHUNKS, 3)), dma((CHUNKS, 4)), dma((CHUNKS, 2)), dma((CHUNKS, 2, 2))]
    )


class Trade:
    def __init__(self, block, slot, send, recv, which=()):
        _, row, col, z, k = place()
        self.col, self.peer = col, on_ring(z, 1 - k)
        self.recv, self.send, self.slot, self.which = recv, send, slot, which
        self.copies = [
            remote(block((col + o) % 4), slot(col), send.at[(*which, o - 1)], recv.at[(*which, o - 1)], {"col": (col + o) % 4})
            for o in range(1, 4)
        ]
        self.keep = pltpu.make_async_copy(block(col), slot(col), recv.at[(*which, 3)])

    def start(self):
        for copy in self.copies:
            copy.start()
        self.keep.start()

    def finish(self):
        for o in range(1, 4):
            dst = self.slot((self.col - o + 4) % 4)
            sems = (self.send.at[(*self.which, o - 1)], self.recv.at[(*self.which, o - 1)])
            remote(dst, dst, *sems, self.peer).wait_recv()
        self.keep.wait()

    def drain(self):
        for copy in self.copies:
            copy.wait_send()


def norm_back(grad, value, gain):
    scale = head_norm(value)
    weighted = grad * gain
    inner = jnp.mean(weighted * value, axis=1, keepdims=True)
    return scale * weighted - value * (scale * scale * scale * inner), grad * value * scale


def norm_back(grad, value, gain):
    scale = head_norm(value)
    weighted = grad * gain
    inner = jnp.mean(weighted * value, axis=1, keepdims=True)
    return scale * weighted - value * (scale * scale * scale * inner), grad * value * scale


def backward_kernel(
    h2_i, ggu_i, hid_i, g_i, wg_i, wd_i, wo_i, wq_i, h1t_i, raw_i, q_i, k_i, att_i, lse_i, mid_i, gain_i, x_i,
    start_i, cos_i, sin_i, q_gain, k_gain,
    result_o, stream_o, grads_o, sums_o,
    m, gm, dqkv, mid, gain, x_own, g_own, acc, head_acc, tile_f, tile_b, totals, heard,
    ms, mr,
    parts, theirs, psums, near, full, rs_s, rs_r,
    data0, data1, data2, near0, near1, near2, next0, next1, next2, full0, full1, full2, last0, last1, last2,
    done, c_s, c_r, t_s, t_r, a_s, a_r,
    fs, fr, ls, lr, as_, ar, in_s, free,
):
    p, row, col, z, k = place()
    px, py = dp_place()
    me = 2 * z + k
    up, down, peer = on_ring((z + 1) % 4, k), on_ring((z + 3) % 4, k), on_ring(z, 1 - k)
    far = on_ring((z + 2) % 4, k)
    loads = []

    def load(src, dst):
        copy = pltpu.make_async_copy(src, dst, in_s.at[len(loads)])
        copy.start()
        loads.append(copy)
        return copy

    def wait(copies):
        for copy in copies:
            copy.wait()

    collapses, trades, spreads = [], [], []
    datas, nears, nexts = (data0, data1, data2), (near0, near1, near2), (next0, next1, next2)
    fulls, lasts = (full0, full1, full2), (last0, last1, last2)

    def chunk(i):
        def at(half, x, y, part):
            xs = slice(None) if x is None else x
            ys = slice(None) if y is None else y
            which = pl.ds(2 * half, 2) if part is None else 2 * half + part
            return grads_o.at[i, xs, ys, which]

        b = i % BUFFERS
        collapses.append(Collapse(i, datas[b], (nears[b], nexts[b]), (fulls[b], lasts[b]), done, c_s, c_r))
        trades.append(
            Trade(lambda c: done.at[i, c], lambda c: grads_o.at[i, px, py, c], t_s, t_r, (i,))
        )
        def bulk(phase, count):
            xs_, ys_ = (count // 2, 4) if phase else (1, count // 2)
            return grads_o.at[i, pl.ds(0, xs_), pl.ds(0, ys_)]

        spreads.append(Spread(at, bulk, a_s, a_r, (i,)))

    for i in range(CHUNKS):
        chunk(i)
    scatter = Scatter(parts, theirs, psums, near, full, rs_s, rs_r)
    stream_trade = Trade(
        lambda c: tile_f.at[:, pl.ds(pl.multiple_of(c * TILE, TILE), TILE)],
        lambda c: stream_o.at[pl.ds(pl.multiple_of(c * OWN, OWN), OWN)], fs, fr,
    )
    result_trade = Trade(
        lambda c: tile_b.at[:, pl.ds(pl.multiple_of(c * TILE, TILE), TILE)],
        lambda c: result_o.at[pl.ds(pl.multiple_of(c * OWN, OWN), OWN)], ls, lr,
    )

    def release():
        scatter.drain()
        for device in (up, down, peer):
            pl.semaphore_signal(free, inc=1, device_id=device, device_id_type=MESH)

    def project(d, product):
        rows = pl.ds(pl.multiple_of((z + d) % 4 * 256, 256), 256)

        @pl.loop(0, 4)
        def _(c):
            cols = pl.ds(pl.multiple_of(c * TILE, TILE), TILE)
            parts[d, :, cols] = product(rows, c, cols).astype(BF)

        scatter.put(d)

    def weight_grads(i, first, second):
        data = datas[i % BUFFERS]
        for c in range(4):
            cols = slice(c * TILE, (c + 1) * TILE)
            data[:, :, c, :32] = first(cols).astype(BF).reshape(4, 4, 32, 512)
            data[:, :, c, 32:] = second(cols).astype(BF).reshape(4, 4, 16, 512)
        collapses[i].start()

    def gain_row(which):
        return jnp.concatenate([gain[c, which : which + 1] for c in range(4)], axis=1)

    own_rows = pl.ds(pl.multiple_of(me * OWN, OWN), OWN)

    def stage_one(h2, g, ggu, hid, wg):
        first_loads = [load(ggu_i, ggu), load(wg_i, wg)]
        more_loads = [load(h2_i, h2), load(hid_i, hid), load(g_i, g)]
        meet(ring_friends() + [far] + xy_friends())
        def grads(u):
            weight_grads(
                u,
                lambda cols: t_mm(h2[:, cols], ggu[:, u * 512 : (u + 1) * 512]),
                lambda cols: t_mm(hid[:, u * 256 : (u + 1) * 256], g[:, cols]),
            )

        def product(rows, c, cols):
            return mm_t(ggu[rows], wg[c])

        wait(first_loads)
        project(2, product)
        wait(more_loads)
        grads(0)
        scatter.across()
        project(1, product)
        project(3, product)
        project(0, product)
        scatter.beside(0)
        scatter.beside(1)
        collapses[0].mid()
        grads(1)
        grads(2)
        collapses[0].first()

    early = [load(mid_i, mid), load(gain_i, gain), load(x_i, x_own), load(g_i.at[own_rows], g_own)]
    pl.run_scoped(
        stage_one,
        pltpu.VMEM((GROUP, WIDTH), BF), pltpu.VMEM((GROUP, WIDTH), BF), pltpu.VMEM((GROUP, 2 * UNITS), BF),
        pltpu.VMEM((GROUP, UNITS), BF), pltpu.VMEM((4, TILE, 2 * UNITS), BF),
    )

    def stage_two(wo, att, qs, ks, raw, lse, ga, dk, dv, h1t, wq, att_t, start, cosine, sine):
        l_wo, l_att = load(wo_i, wo), load(att_i, att)
        l_heads = [
            load(q_i, qs), load(k_i, ks), load(raw_i, raw), load(lse_i, lse),
            load(start_i, start), load(cos_i, cosine), load(sin_i, sine),
        ]
        l_last = [load(h1t_i, h1t), load(wq_i, wq)]
        wait(early)
        acc[...] = jnp.zeros_like(acc)
        head_acc[...] = jnp.zeros_like(head_acc)
        dk[...] = jnp.zeros_like(dk)
        dv[...] = jnp.zeros_like(dv)
        totals[0] = jnp.zeros((8, TILE + HEAD), F32)
        gain_two = gain_row(1)
        scatter.arrive()

        @pl.loop(0, OWN // 16)
        def _(i):
            rows = pl.ds(pl.multiple_of(i * 16, 16), 16)
            back, gained = norm_back(scatter.total(pl.multiple_of(i * 16, 16), 16), mid[rows], gain_two)
            acc[1] += gained
            back = back + g_own[rows].astype(F32)
            gm[rows] = back
            m[pl.ds(pl.multiple_of(me * OWN + i * 16, 16), 16)] = back.astype(BF)

        m_gather = Gather(rows_at(m), ms, mr)
        m_gather.start()
        release()
        collapses[1].mid()
        l_att.wait()
        for h in range(2):
            att_t[h * HEAD : (h + 1) * HEAD] = att[h].T
        l_wo.wait()
        wait(l_heads)

        def attend(d):
            block = (z + d) % 4
            first = pl.multiple_of(block * QROWS, QROWS)
            rows = pl.ds(first, QROWS)
            back = mm_t(m[rows, :TILE], wo[0])
            for c in range(1, 4):
                back += mm_t(m[rows, c * TILE : (c + 1) * TILE], wo[c])
            for h in range(2):
                ga[h, rows] = back[:, h * HEAD : (h + 1) * HEAD].astype(BF)

            def over(keys):
                allowed = allowed_keys(start[rows, :1], first, keys)

                @pl.loop(0, 2)
                def _(h):
                    cols = pl.ds(pl.multiple_of(h * HEAD, HEAD), HEAD)
                    score = mm_t(qs[h, rows], ks[:keys]) * (SCALE * LOG2)
                    prob = jnp.exp2(jnp.where(allowed, score, -1e30) - lse[h, rows, :1])
                    grad = ga[h, rows]
                    delta = jnp.sum(grad.astype(F32) * att[h, rows].astype(F32), axis=1, keepdims=True)
                    prob_grad = mm_t(grad, raw[:keys, 3 * HEAD :])
                    score_grad = (prob * (prob_grad - delta)).astype(BF)
                    dk[:keys] += t_mm(score_grad, qs[h, rows])
                    dv[:keys] += t_mm(prob.astype(BF), grad)
                    back = turn_back(mm(score_grad, ks[:keys]) * SCALE, cosine[rows], sine[rows])
                    back, gained = norm_back(back, raw[rows, cols].astype(F32), q_gain[...])
                    dqkv[rows, cols] = back.astype(BF)
                    head_acc[0:1] += jnp.sum(gained, axis=0, keepdims=True)

            @pl.when(block < 2)
            def _():
                over(2 * QROWS)

            @pl.when(block >= 2)
            def _():
                over(4 * QROWS)

        m_gather.finish([4])
        attend(0)
        collapses[0].mid(1)
        collapses[2].mid()
        m_gather.forward()
        collapses[1].first()
        m_gather.finish([5, 6])
        attend(1)
        collapses[0].second()
        trades[0].start()
        m_gather.share()
        attend(3)
        m_gather.finish([7, 8])
        attend(2)
        collapses[2].first()
        trades[0].finish()
        spreads[0].start(0)
        collapses[1].mid(1)

        @pl.loop(0, 4)
        def _(i):
            rows = pl.ds(pl.multiple_of(i * 256, 256), 256)
            back = turn_back(dk[rows] * SCALE, cosine[rows], sine[rows])
            back, gained = norm_back(back, raw[rows, 2 * HEAD : 3 * HEAD].astype(F32), k_gain[...])
            dqkv[rows, 2 * HEAD : 3 * HEAD] = back.astype(BF)
            dqkv[rows, 3 * HEAD :] = dv[rows].astype(BF)
            head_acc[1:2] += jnp.sum(gained, axis=0, keepdims=True)

        wait(l_last)
        collapses[0].drain()
        weight_grads(3, lambda cols: mm(h1t[cols], dqkv[...]), lambda cols: mm(att_t[...], m[:, cols]))
        collapses[2].mid(1)
        pl.semaphore_wait(free, 3)

        def product(rows, c, cols):
            return mm_t(dqkv[rows], wq[c])

        project(2, product)
        project(1, product)
        collapses[1].second()
        trades[1].start()
        project(3, product)
        project(0, product)
        collapses[3].mid()
        scatter.across()
        spreads[0].pass_on(0)
        collapses[2].second()
        trades[2].start()
        trades[1].finish()
        spreads[1].start(0)
        scatter.beside(0)
        scatter.beside(1)
        m_gather.drain()

    pl.run_scoped(
        stage_two,
        pltpu.VMEM((4, 256, TILE), BF), pltpu.VMEM((2, GROUP, HEAD), BF), pltpu.VMEM((2, GROUP, HEAD), BF),
        pltpu.VMEM((GROUP, HEAD), BF), pltpu.VMEM((GROUP, 512), BF), pltpu.VMEM((2, GROUP, HEAD), F32),
        pltpu.VMEM((2, GROUP, HEAD), BF), pltpu.VMEM((GROUP, HEAD), F32), pltpu.VMEM((GROUP, HEAD), F32),
        pltpu.VMEM((WIDTH, GROUP), BF), pltpu.VMEM((4, TILE, 512), BF), pltpu.VMEM((2 * HEAD, GROUP), BF),
        pltpu.VMEM((GROUP, HEAD), jnp.int32), pltpu.VMEM((GROUP, HEAD), F32), pltpu.VMEM((GROUP, HEAD), F32),
    )

    def stage_three(hid, wd):
        last = [load(hid_i, hid), load(wd_i, wd)]
        gain_one = gain_row(0)
        collapses[3].first()
        spreads[0].wait(0)
        spreads[0].start(1)
        spreads[1].pass_on(0)
        collapses[3].mid(1)
        trades[2].finish()
        spreads[2].start(0)
        spreads[0].pass_on(1)
        spreads[1].wait(0)
        spreads[1].start(1)
        collapses[3].second()
        trades[3].start()
        scatter.arrive()

        @pl.loop(0, OWN // 16)
        def _(i):
            rows = pl.ds(pl.multiple_of(i * 16, 16), 16)
            back, gained = norm_back(
                scatter.total(pl.multiple_of(i * 16, 16), 16), x_own[rows].astype(F32), gain_one
            )
            acc[0] += gained
            tile_f[rows] = gm[rows] + back

        stream_trade.start()
        release()
        for c in range(4):
            for which in range(2):
                part = jnp.sum(acc[which, :, c * TILE : (c + 1) * TILE], axis=0, keepdims=True)
                totals[0, 4 * which + c : 4 * which + c + 1, :TILE] = part
        totals[0, 0:2, TILE:] = head_acc[0:2]
        sent = []

        def tell(phase, devices, slots):
            for device, slot in zip(devices, slots):
                copy = remote(totals.at[phase], heard.at[slot], as_.at[slot], ar.at[slot], device)
                copy.start()
                sent.append(copy)

        def listen(phase, slots):
            total = totals[phase]
            for slot in slots:
                remote(heard.at[slot], heard.at[slot], as_.at[slot], ar.at[slot], peer).wait_recv()
                total += heard[slot]
            totals[phase + 1] = total

        tell(0, [peer], [0])
        wait(last)
        pl.semaphore_wait(free, 3)

        def product(rows, c, cols):
            return mm(hid[rows], wd[c])

        project(2, product)
        project(1, product)
        project(3, product)
        scatter.across()
        listen(0, [0])
        tell(1, [up, down, far], [1, 2, 3])
        trades[3].finish()
        spreads[3].start(0)
        spreads[2].pass_on(0)
        project(0, product)
        spreads[1].pass_on(1)
        spreads[3].pass_on(0)
        spreads[2].wait(0)
        spreads[2].start(1)
        scatter.beside(0)
        scatter.beside(1)
        listen(1, [1, 2, 3])
        tell(2, [along(0, o) for o in range(1, 4)], [4, 5, 6])
        spreads[3].wait(0)
        spreads[3].start(1)
        spreads[2].pass_on(1)
        listen(2, [4, 5, 6])
        tell(3, [along(1, o) for o in range(1, 4)], [7, 8, 9])
        scatter.arrive()

        @pl.loop(0, OWN // 16)
        def _(i):
            rows = pl.ds(pl.multiple_of(i * 16, 16), 16)
            tile_b[rows] = (mid[rows] + scatter.total(pl.multiple_of(i * 16, 16), 16)).astype(BF)

        result_trade.start()
        spreads[3].pass_on(1)
        listen(3, [7, 8, 9])
        sums_o[...] = totals[4]
        stream_trade.finish()
        result_trade.finish()
        for spread in spreads:
            spread.wait(1)
        scatter.drain()
        for thing in collapses[1:] + trades + spreads + [stream_trade, result_trade]:
            thing.drain()
        for copy in sent:
            copy.wait_send()

    pl.run_scoped(stage_three, pltpu.VMEM((GROUP, UNITS), BF), pltpu.VMEM((4, UNITS, TILE), BF))


def backward_call(*args):
    hbm = pl.BlockSpec(memory_space=pl.ANY)
    vmem = pl.BlockSpec(memory_space=pltpu.VMEM)
    dma = pltpu.SemaphoreType.DMA
    out = jax.ShapeDtypeStruct
    grads = out((CHUNKS, 4, 4, 4, 48, 512), BF)
    return pl.pallas_call(
        backward_kernel,
        out_shape=[out((TILE, TILE), BF), out((TILE, TILE), F32), grads, out((8, TILE + HEAD), F32)],
        in_specs=[hbm] * 20 + [vmem] * 2,
        out_specs=[hbm] * 3 + [vmem],
        scratch_shapes=[
            pltpu.VMEM((GROUP, WIDTH), BF), pltpu.VMEM((OWN, WIDTH), F32), pltpu.VMEM((GROUP, 512), BF),
            pltpu.VMEM((OWN, WIDTH), F32), pltpu.VMEM((4, 8, TILE), F32),
            pltpu.VMEM((OWN, WIDTH), BF), pltpu.VMEM((OWN, WIDTH), BF), pltpu.VMEM((2, 16, WIDTH), F32),
            pltpu.VMEM((8, HEAD), F32), pltpu.VMEM((OWN, WIDTH), F32), pltpu.VMEM((OWN, WIDTH), BF),
            pltpu.VMEM((5, 8, TILE + HEAD), F32), pltpu.VMEM((10, 8, TILE + HEAD), F32),
        ]
        + GATHER_SEMS
        + scatter_scratch()
        + collapse_scratch()
        + [
            dma((3,)), dma((4,)), dma((3,)), dma((4,)), dma((10,)), dma((10,)), dma((24,)), pltpu.SemaphoreType.REGULAR,
        ],
        compiler_params=pltpu.CompilerParams(
            collective_id=2, has_side_effects=True, vmem_limit_bytes=VMEM_LIMIT
        ),
        cost_estimate=pl.CostEstimate(flops=25_000_000_000, bytes_accessed=100_000_000, transcendentals=2_000_000),
        name="backward",
    )(*args)


PLACE = 4


def place_kernel(grads, result, stream, totals, gate_up, down, qkv, out, result_o, stream_o, one, two, q_o, k_o):
    for c in range(4):
        for u in range(3):
            t = c * 3 + u
            value = grads[u, :, c, :32].reshape(PLACE * 32, 512).astype(F32)
            for g in range(2):
                gate_up[:, g, t * 256 : (t + 1) * 256] = value[:, g * 256 : (g + 1) * 256]
            down[t] = grads[u, :, c, 32:].astype(F32)
        qkv[:, c, :] = grads[3, :, c, :32].reshape(PLACE * 32, 512).astype(F32)
        out[c] = grads[3, :, c, 32:].astype(F32)
    result_o[...] = result[...]
    stream_o[...] = stream[...]
    for c in range(4):
        one[:, c * TILE : (c + 1) * TILE] = totals[c : c + 1, :TILE]
        two[:, c * TILE : (c + 1) * TILE] = totals[4 + c : 5 + c, :TILE]
    q_o[...] = totals[0:1, TILE:]
    k_o[...] = totals[1:2, TILE:]


def place_grads(grads, result, stream, totals):
    tile = pl.BlockSpec((32 * PLACE, TILE), lambda p: (p, 0))

    def whole(*shape):
        return pl.BlockSpec(shape, lambda p: (0,) * len(shape))

    return pl.pallas_call(
        place_kernel,
        grid=(DP // PLACE,),
        in_specs=[
            pl.BlockSpec((CHUNKS, PLACE, 4, 48, 512), lambda p: (0, p, 0, 0, 0)), tile, tile, whole(8, TILE + HEAD),
        ],
        out_specs=[
            pl.BlockSpec((32 * PLACE, 2, 4 * UNITS), lambda p: (p, 0, 0)),
            pl.BlockSpec((12, PLACE, 16, TILE), lambda p: (0, p, 0, 0)),
            pl.BlockSpec((32 * PLACE, 4, 512), lambda p: (p, 0, 0)),
            pl.BlockSpec((4, PLACE, 16, TILE), lambda p: (0, p, 0, 0)),
            tile, tile, whole(1, WIDTH), whole(1, WIDTH), whole(1, HEAD), whole(1, HEAD),
        ],
        out_shape=[
            jax.ShapeDtypeStruct((TILE, 2, 4 * UNITS), F32),
            jax.ShapeDtypeStruct((12, DP, 16, TILE), F32),
            jax.ShapeDtypeStruct((TILE, 4, 512), F32),
            jax.ShapeDtypeStruct((4, DP, 16, TILE), F32),
            jax.ShapeDtypeStruct((TILE, TILE), BF),
            jax.ShapeDtypeStruct((TILE, TILE), F32),
            jax.ShapeDtypeStruct((1, WIDTH), F32),
            jax.ShapeDtypeStruct((1, WIDTH), F32),
            jax.ShapeDtypeStruct((1, HEAD), F32),
            jax.ShapeDtypeStruct((1, HEAD), F32),
        ],
        compiler_params=pltpu.CompilerParams(vmem_limit_bytes=VMEM_LIMIT),
        cost_estimate=pl.CostEstimate(flops=0, bytes_accessed=41_000_000, transcendentals=0),
        name="place",
    )(grads, result, stream, totals)


def body(
    tokens, norm1_gain, w_qkv, q_gain, k_gain, w_out, norm2_gain, w_gate_up, w_down, out_grad,
    seq_lengths, seq_group, seq_start,
):
    (h2, g, wq, wo, wg, wd, h1t, raw, qs, ks, att, lse, middle, gain, x_own, start, cosine, sine, ggu, hid) = forward_call(
        tokens, out_grad, norm1_gain[None], norm2_gain[None], q_gain[None], k_gain[None], jnp.asarray(FREQ),
        seq_lengths, seq_group, seq_start, w_qkv, w_gate_up,
        w_out.reshape(4, 4, 2, 32, TILE), w_down.reshape(4, 3, 4, 4, 16, TILE),
    )
    wg = wg.reshape(4, TILE, 2 * UNITS)
    wd = wd.reshape(4, UNITS, TILE)
    result, stream, grads, totals = backward_call(
        h2, ggu, hid, g, wg, wd, wo.reshape(4, 256, TILE), wq.reshape(4, TILE, 512), h1t, raw, qs, ks, att, lse,
        middle, gain, x_own, start, cosine, sine, q_gain[None], k_gain[None],
    )
    grads = grads.reshape(CHUNKS, DP, 4, 48, 512)
    g_gate_up, g_down, g_qkv, g_out, result, stream, one, two, q_grad, k_grad = place_grads(grads, result, stream, totals)
    return (
        result,
        stream,
        one.reshape(WIDTH),
        g_qkv,
        q_grad.reshape(HEAD),
        k_grad.reshape(HEAD),
        g_out.reshape(w_out.shape),
        two.reshape(WIDTH),
        g_gate_up,
        g_down.reshape(w_down.shape),
    )


def solution(mesh):
    in_specs = (
        P(("dp", "row"), "col"),
        P("col"),
        P("col", "row", None),
        P(),
        P(),
        P("row", "col"),
        P("col"),
        P("col", None, "row"),
        P("row", "col"),
        P(("dp", "row"), "col"),
        P(),
        P(),
        P(),
    )
    out_specs = (
        P(("dp", "row"), "col"),
        P(("dp", "row"), "col"),
        P(),
        P("col", "row", None),
        P(),
        P(),
        P("row", "col"),
        P(),
        P("col", None, "row"),
        P("row", "col"),
    )
    return jax.shard_map(body, mesh=mesh, in_specs=in_specs, out_specs=out_specs, check_vma=False)
```

```python
import math

import jax
import jax.numpy as jnp
import numpy as np
from jax import lax
from jax.experimental import pallas as pl
from jax.experimental.pallas import tpu as pltpu
from jax.sharding import PartitionSpec as P

EPS = 1e-06
THETA = 1000000.0
BF = jnp.bfloat16
F32 = jnp.float32
Z = ("row", "col")
MESH = pl.DeviceIdType.MESH
VMEM_LIMIT = 63 * 1024 * 1024

GROUP, WIDTH, TILE, UNITS, HEAD = 1024, 2048, 512, 768, 128
OWN = GROUP // 8
DP = 16


def dot(left, right, dims):
    return lax.dot_general(left, right, (dims, ((), ())), preferred_element_type=F32)


def mm(left, right):
    return dot(left, right, ((1,), (0,)))


def mm_t(left, right):
    return dot(left, right, ((1,), (1,)))


def t_mm(left, right):
    return dot(left, right, ((0,), (0,)))


def place():
    row, col = lax.axis_index("row"), lax.axis_index("col")
    j = 4 * row + col
    return lax.axis_index("dp"), row, col, j // 2, j % 2


def on_ring(z, k):
    j = 2 * z + k
    return {"row": j // 4, "col": j % 4}


def remote(src, dst, send, recv, device):
    return pltpu.make_async_remote_copy(
        src_ref=src, dst_ref=dst, send_sem=send, recv_sem=recv, device_id=device, device_id_type=MESH
    )


def meet(devices):
    barrier = pltpu.get_barrier_semaphore()
    for device in devices:
        pl.semaphore_signal(barrier, inc=1, device_id=device, device_id_type=MESH)
    pl.semaphore_wait(barrier, len(devices))


def ring_friends():
    _, _, _, z, k = place()
    other = z + 1 - 2 * (z % 2)
    return [
        on_ring((z + 1) % 4, k),
        on_ring((z + 3) % 4, k),
        on_ring(z, 1 - k),
        on_ring(other, 1 - k),
    ]


def column_friends():
    _, _, _, z, k = place()
    me = 2 * z + k
    return [on_ring((me + o) % 8 // 2, (me + o) % 2) for o in range(1, 8)]


def dp_place():
    p = lax.axis_index("dp")
    return p // 4, p % 4


def along(axis, o):
    px, py = dp_place()
    return {"dp": (px + o) % 4 * 4 + py} if axis == 0 else {"dp": px * 4 + (py + o) % 4}


def xy_friends():
    return [along(axis, o) for axis in range(2) for o in range(1, 4)]


def tile_at(buf):
    def loc(j, half=None):
        row, col = j // 4, j % 4
        first = pl.multiple_of(row * TILE, TILE)
        rows = pl.ds(first, TILE)
        if half is not None:
            rows = pl.ds(first + half * (TILE // 2), TILE // 2)
        return buf.at[rows, pl.ds(pl.multiple_of(col * TILE, TILE), TILE)]

    return loc


def rows_at(buf):
    def loc(j, half=None):
        first = pl.multiple_of(j * OWN, OWN)
        rows = pl.ds(first, OWN)
        if half is not None:
            rows = pl.ds(first + half * (OWN // 2), OWN // 2)
        return buf.at[rows]

    return loc


class Gather:
    def __init__(self, loc, send, recv, own=None):
        _, _, _, z, k = place()
        up, down, far = (z + 1) % 4, (z + 3) % 4, (z + 2) % 4
        to_up, to_down, peer = on_ring(up, k), on_ring(down, k), on_ring(z, 1 - k)

        def out(slot, src, dst, device):
            return remote(src, dst, send.at[slot], recv.at[slot], device)

        def into(slot, dst):
            return remote(dst, dst, send.at[slot], recv.at[slot], peer)

        mine = loc(2 * z + k)
        own = mine if own is None else own
        left, right, across = 2 * down + k, 2 * up + k, 2 * far + k
        self.first = [out(0, own, mine, to_up), out(1, own, mine, to_down), out(4, own, mine, peer)]
        self.from_left = [
            out(2, loc(left, 0), loc(left, 0), to_up),
            out(5, loc(left), loc(left), peer),
        ]
        self.from_right = [
            out(3, loc(right, 1), loc(right, 1), to_down),
            out(6, loc(right), loc(right), peer),
        ]
        self.from_far = [
            out(7, loc(across, 0), loc(across, 0), peer),
            out(8, loc(across, 1), loc(across, 1), peer),
        ]
        theirs = [2 * z + 1 - k, 2 * down + 1 - k, 2 * up + 1 - k, 2 * far + 1 - k]
        self.arrivals = {
            0: into(0, loc(left)),
            1: into(1, loc(right)),
            2: into(2, loc(across, 0)),
            3: into(3, loc(across, 1)),
            4: into(4, loc(theirs[0])),
            5: into(5, loc(theirs[1])),
            6: into(6, loc(theirs[2])),
            7: into(7, loc(theirs[3], 0)),
            8: into(8, loc(theirs[3], 1)),
        }

    def start(self):
        for copy in self.first:
            copy.start()

    def forward(self):
        self.arrivals[0].wait_recv()
        for copy in self.from_left:
            copy.start()
        self.arrivals[1].wait_recv()
        for copy in self.from_right:
            copy.start()

    def share(self):
        for half in range(2):
            self.arrivals[2 + half].wait_recv()
            self.from_far[half].start()

    def finish(self, slots=range(4, 9)):
        for slot in slots:
            self.arrivals[slot].wait_recv()

    def drain(self):
        for copy in self.first + self.from_left + self.from_right + self.from_far:
            copy.wait_send()


GATHER_SEMS = [pltpu.SemaphoreType.DMA((9,)), pltpu.SemaphoreType.DMA((9,))]


class Spread:
    def __init__(self, at, bulk, send, recv, which=()):
        px, py = dp_place()
        here = (px, py)
        self.bulk, self.send, self.recv, self.which = bulk, send, recv, which
        self.out = {}
        for phase in range(2):
            for step in range(2):
                self.out[phase, step] = []
            for half in range(2):
                axis = half ^ phase

                def block(o, part=None):
                    whose = [px, py]
                    whose[axis] = (here[axis] + o) % 4
                    if phase:
                        whose[1 - axis] = None
                    return at(half, *whose, part)

                def copy(step, ref, o):
                    sems = (send.at[(*which, phase)], recv.at[(*which, phase, step)])
                    self.out[phase, step].append(remote(ref, ref, *sems, along(axis, o)))

                copy(0, block(0), 1)
                copy(0, block(0), 3)
                copy(1, block(3, 0), 1)
                copy(1, block(1, 1), 3)

    def sized(self, phase, count, step=0):
        ref = self.bulk(phase, count)
        sems = (self.send.at[(*self.which, phase)], self.recv.at[(*self.which, phase, step)])
        return remote(ref, ref, *sems, along(0, 1))

    def start(self, phase):
        for copy in self.out[phase, 0]:
            copy.start()

    def pass_on(self, phase):
        self.sized(phase, 4).wait_recv()
        for copy in self.out[phase, 1]:
            copy.start()

    def wait(self, phase):
        self.sized(phase, 2, 1).wait_recv()

    def drain(self):
        for phase in range(2):
            self.sized(phase, 6).wait_send()


SPREAD_SEMS = [pltpu.SemaphoreType.DMA((2,)), pltpu.SemaphoreType.DMA((2, 2))]


class Scatter:
    def __init__(self, parts, theirs, sums, near, full, send, recv):
        _, _, _, z, k = place()
        self.parts, self.theirs, self.sums, self.near, self.full = parts, theirs, sums, near, full
        self.k = k
        to_up, to_down = on_ring((z + 1) % 4, k), on_ring((z + 3) % 4, k)
        peer = on_ring(z, 1 - k)
        half = OWN // 2
        other = pl.ds(pl.multiple_of((1 - k) * OWN, OWN), OWN)

        def copy(slot, src, dst, device):
            return remote(src, dst, send.at[slot], recv.at[slot], device)

        self.copies = [copy(d, parts.at[d, other], theirs.at[d], peer) for d in range(4)] + [
            copy(4, sums.at[0, pl.ds(0, half)], near.at[0], to_up),
            copy(5, sums.at[0, pl.ds(half, half)], near.at[1], to_down),
            copy(6, sums.at[1], full.at[0], to_up),
            copy(7, sums.at[2], full.at[1], to_down),
        ]

    def put(self, d):
        self.copies[d].start()

    def own(self, d, rows, count):
        first = pl.multiple_of(self.k * OWN + rows, count)
        return self.parts[d, pl.ds(first, count)].astype(F32) + self.theirs[
            d, pl.ds(rows, count)
        ].astype(F32)

    def across(self):
        self.copies[2].wait_recv()

        @pl.loop(0, OWN // 16)
        def _(i):
            rows = pl.multiple_of(i * 16, 16)
            self.sums[0, pl.ds(rows, 16)] = self.own(2, rows, 16).astype(BF)

        self.copies[4].start()
        self.copies[5].start()

    def beside(self, side):
        d, half = (1, 3)[side], OWN // 2
        self.copies[d].wait_recv()
        self.copies[4 + side].wait_recv()

        @pl.loop(0, half // 16)
        def _(i):
            rows = pl.multiple_of(i * 16, 16)
            here = pl.multiple_of(rows + side * half, 16)
            there = pl.multiple_of(rows + (1 - side) * half, 16)
            added = self.own(d, here, 16) + self.near[side, pl.ds(rows, 16)].astype(F32)
            self.sums[1 + side, pl.ds(here, 16)] = added.astype(BF)
            self.sums[1 + side, pl.ds(there, 16)] = self.own(d, there, 16).astype(BF)

        self.copies[6 + side].start()

    def arrive(self):
        self.copies[0].wait_recv()
        self.copies[6].wait_recv()
        self.copies[7].wait_recv()

    def total(self, rows, count):
        return (
            self.own(0, rows, count)
            + self.full[0, pl.ds(rows, count)].astype(F32)
            + self.full[1, pl.ds(rows, count)].astype(F32)
        )

    def drain(self):
        for copy in self.copies:
            copy.wait_send()


def scatter_scratch():
    return [
        pltpu.VMEM((4, 2 * OWN, WIDTH), BF),
        pltpu.VMEM((4, OWN, WIDTH), BF),
        pltpu.VMEM((3, OWN, WIDTH), BF),
        pltpu.VMEM((2, OWN // 2, WIDTH), BF),
        pltpu.VMEM((2, OWN, WIDTH), BF),
        pltpu.SemaphoreType.DMA((8,)),
        pltpu.SemaphoreType.DMA((8,)),
    ]


def head_norm(value):
    return lax.rsqrt(jnp.mean(value * value, axis=1, keepdims=True) + EPS)


def turn(value, cosine, sine):
    return value * cosine + pltpu.roll(value, HEAD // 2, 1) * sine


def turn_back(value, cosine, sine):
    return value * cosine - pltpu.roll(value, HEAD // 2, 1) * sine


LOG2 = math.log2(math.e)
SCALE = 1.0 / math.sqrt(HEAD)
QROWS = 256


def allowed_keys(start, first, keys):
    slots = lax.broadcasted_iota(jnp.int32, (QROWS, keys), 1)
    query = lax.broadcasted_iota(jnp.int32, (QROWS, keys), 0) + first
    return (slots >= start) & (slots <= query)


FREQ = np.tile(THETA ** (-(np.arange(HEAD // 2) * 2.0 / HEAD)), 2)[None].astype(np.float32)


def forward_kernel(
    tok, og, norm1, norm2, q_gain, k_gain, freq, lengths, groups, starts, w_qkv, w_gu, w_out, w_down,
    h2_o, g_o, wq_o, wo_o, wg_o, wd_o, h1t_o, raw_o, q_o, k_o, att_o, lse_o, mid_o, gain_o, x_o, start_o, cos_o, sin_o,
    ggu_o, hid_o,
    x, h1, h1t, h2, g, wq, wg, wd, w_all, raw, qs, ks, att, heard, lse, mid, gain, gains, start, cosine, sine,
    q_raw, q_cut, q_raw_part, q_part, g_raw, g_cut, g_raw_part, g_part,
    xs, xr, gs, gr, hs, hr,
    zs, zr, ps, pr, ns, nr, loc_s, out_s, raw_s, row_s, os_, or_, ts, tr,
    y0s, y0r, y1s, y1r, y2s, y2r, y3s, y3r, y4s, y4r,
):
    p, row, col, z, k = place()
    px, py = dp_place()
    me = 2 * z + k
    lo = z % 2
    other = z + 1 - 2 * lo
    peer = on_ring(z, 1 - k)
    beside_col = 2 * lo + 1 - k
    piece_rows = pl.ds(pl.multiple_of(p * 32, 32), 32)

    def lanes(first, count):
        return pl.ds(pl.multiple_of(first, 256), count)

    raws = [
        pltpu.make_async_copy(src, dst, raw_s.at[i])
        for i, (src, dst) in enumerate(
            [
                (w_qkv.at[piece_rows], q_raw_part),
                (w_gu.at[piece_rows, :, lanes((1 - lo) * 2 * UNITS, 2 * UNITS)], g_raw_part),
                (w_qkv, q_raw),
                (w_gu.at[:, :, lanes(lo * 2 * UNITS, 2 * UNITS)], g_raw),
            ]
        )
    ]
    for copy in raws:
        copy.start()
    gains[0:1] = norm1[...]
    gains[1:2] = norm2[...]
    meet(column_friends() + xy_friends())
    raws[0].wait()
    for kk in range(2):
        q_part[kk] = jnp.where(lo == 0, q_raw_part[:, 2 + kk, :], q_raw_part[:, kk, :])

    gain[col] = gains[...]
    gain_copies = [
        remote(gains, gain.at[col], ns.at[i], nr.at[col], device)
        for i, device in enumerate([peer, on_ring(other, k), on_ring(other, 1 - k)])
    ]

    weights = [wq, wg, wd]
    blocks = [q_cut, g_cut, w_down]

    def cell(weight, c, xx, yy, cols=slice(None)):
        between = (slice(None),) * (len(weight.shape) - 5)
        return weight.at[(c, *between, xx, yy, slice(None), cols)]

    def crossing(a, kk):
        src = (q_part.at[kk], g_part.at[kk], cell(w_down, 2 * (1 - lo) + kk, px, py))[a]
        return remote(src, cell(weights[a], col, px, py), zs.at[a, kk], zr.at[a, k], on_ring(other, kk))

    def crossed(a, kk):
        dst = cell(weights[a], 2 * (1 - lo) + kk, px, py)
        return remote(dst, dst, zs.at[a, kk], zr.at[a, kk], peer)

    def beside(a):
        mine, theirs = (col, beside_col) if a == 2 else (k, 1 - k)
        keep = pltpu.make_async_copy(blocks[a].at[mine], weights[a].at[col], loc_s.at[a])
        give = remote(blocks[a].at[theirs], weights[a].at[col], ps.at[a], pr.at[a], peer)
        take = remote(weights[a].at[beside_col], weights[a].at[beside_col], ps.at[a], pr.at[a], peer)
        return keep, give, take

    def spread_at(a):
        weight = weights[a]
        half_lanes = weight.shape[-1] // 2

        def at(half, xx, yy, part):
            xs_ = slice(None) if xx is None else xx
            ys_ = slice(None) if yy is None else yy
            cols = slice(None) if part is None else pl.ds(part * half_lanes, half_lanes)
            return cell(weight, 2 * (1 - lo) + half, xs_, ys_, cols)

        return at

    def spread_bulk(a):
        weight = weights[a]
        between = (slice(None),) * (len(weight.shape) - 5)

        def bulk(phase, count):
            cs, long, short = {2: (1, 2, 1), 4: (1, 4, 1), 6: (2, 3, 1)}[count]
            xs_, ys_ = (long, 4) if phase else (short, long)
            return weight.at[(pl.ds(0, cs), *between, pl.ds(0, xs_), pl.ds(0, ys_))]

        return bulk

    spreads = [
        Spread(spread_at(a), spread_bulk(a), send, recv)
        for a, (send, recv) in enumerate([(y0s, y0r), (y1s, y1r), (y2s, y2r)])
    ]

    pair = pl.ds(2 * (1 - lo), 2)
    groups_of = [(1 - row, slice(None)), (row, pair)]

    def out_at(which):
        def at(half, xx, yy, part):
            xs_ = slice(None) if xx is None else xx
            ys_ = slice(None) if yy is None else yy
            cols = pl.ds(half * 256, 256) if part is None else pl.ds(half * 256 + part * HEAD, HEAD)
            return w_all.at[(*groups_of[which], xs_, ys_, k, slice(None), cols)]

        return at

    def out_bulk(which):
        def bulk(phase, count):
            xs_, ys_ = (count // 2, 4) if phase else (1, count // 2)
            return w_all.at[0, pl.ds(0, 4 - 2 * which), pl.ds(0, xs_), pl.ds(0, ys_), 0]

        return bulk

    out_spreads = [Spread(out_at(0), out_bulk(0), y3s, y3r), Spread(out_at(1), out_bulk(1), y4s, y4r)]
    out_pieces = [
        remote(
            w_out.at[px, py, kk], w_all.at[row, col, px, py, kk],
            os_.at[2 * dz + kk], or_.at[me], on_ring((z + dz) % 4, kk),
        )
        for dz in (1, 3, 2)
        for kk in range(2)
    ]
    keep_out = pltpu.make_async_copy(w_out, w_all.at[row, col], loc_s.at[3])
    give_out = remote(w_out, w_all.at[row, col], os_.at[0], or_.at[me], peer)

    def out_arrived(j):
        dst = w_all.at[j // 4, j % 4, px, py, k]
        return remote(dst, dst, os_.at[0], or_.at[j], peer)

    def out_share(which, core):
        ref = w_all.at[(*groups_of[which], slice(None), slice(None), core)]
        return remote(ref, ref, ts.at[7 + which], tr.at[7 + which], peer)

    def hand(o):
        there = (me + o) % 8
        rows = pl.ds(pl.multiple_of(there * OWN, OWN), OWN)
        device = {"row": there // 4, "col": there % 4}
        return remote(att.at[:, rows], heard.at[me], ts.at[o - 1], tr.at[o - 1], device)

    def handed(o):
        dst = heard.at[(me + 8 - o) % 8]
        return remote(dst, dst, ts.at[o - 1], tr.at[o - 1], peer)

    for kk in range(2):
        crossing(0, kk).start()
    for copy in out_pieces:
        copy.start()
    x_gather = Gather(tile_at(x), xs, xr, tok)
    x_gather.start()
    for copy in gain_copies:
        copy.start()
    keep_x = pltpu.make_async_copy(tok, tile_at(x)(me), loc_s.at[4])
    keep_x.start()
    keep_g = pltpu.make_async_copy(og, tile_at(g)(me), loc_s.at[5])
    keep_g.start()
    keep_out.start()
    give_out.start()
    raws[2].wait()

    @pl.loop(0, 16)
    def _(i):
        rows = pl.ds(pl.multiple_of(i * 32, 32), 32)
        for kk in range(2):
            q_cut[kk, i // 4, i % 4] = jnp.where(lo == 0, q_raw[rows, kk, :], q_raw[rows, 2 + kk, :])

    beside(0)[0].start()
    beside(0)[1].start()
    for kk in range(2):
        crossed(0, kk).wait_recv()
    spreads[0].start(0)
    for dz in (1, 3, 2):
        for kk in range(2):
            out_arrived(2 * ((z + dz) % 4) + kk).wait_recv()
    for spread in out_spreads:
        spread.start(0)
    for a in (1, 3):
        raws[a].wait()
    slot = (
        lax.broadcasted_iota(jnp.int32, (8, HEAD), 0) * HEAD + lax.broadcasted_iota(jnp.int32, (8, HEAD), 1)
    ).astype(F32)

    def one_sequence(i, begun):
        first = starts[i].astype(F32)
        last = first + jnp.where(groups[i] == p, lengths[i], 0).astype(F32)
        return jnp.where((slot >= first) & (slot < last), first, begun)

    begun = lax.fori_loop(0, lengths.shape[0], one_sequence, jnp.zeros((8, HEAD), F32))
    for i in range(8):
        rows = slice(i * HEAD, (i + 1) * HEAD)
        begin = jnp.broadcast_to(begun[i : i + 1], (HEAD, HEAD)).T
        there = lax.broadcasted_iota(jnp.int32, (HEAD, HEAD), 0).astype(F32) + float(i * HEAD)
        angle = (there - begin) * freq[...]
        start[rows] = begin.astype(jnp.int32)
        cosine[rows] = jnp.cos(angle)
        lane = lax.broadcasted_iota(jnp.int32, (HEAD, HEAD), 1)
        sine[rows] = jnp.where(lane < HEAD // 2, -1.0, 1.0) * jnp.sin(angle)
    spreads[0].pass_on(0)
    for spread in out_spreads:
        spread.pass_on(0)
    for u in range(3):
        for half in range(2):
            into = slice(u * 512 + half * 256, u * 512 + half * 256 + 256)
            for kk in range(2):
                cols = slice(kk * UNITS + u * 256, kk * UNITS + u * 256 + 256)
                g_part[kk, :, into] = g_raw_part[:, half, cols]
    spreads[0].wait(0)
    spreads[0].start(1)
    x_gather.forward()
    spreads[0].pass_on(1)
    for spread in out_spreads:
        spread.wait(0)
        spread.start(1)
    for c in range(4):

        @pl.when(c != col)
        def _():
            remote(gain.at[c], gain.at[c], ns.at[0], nr.at[c], peer).wait_recv()

    keep_x.wait()
    x_gather.finish([4, 5, 6])

    def gain_row(which):
        return jnp.concatenate([gain[c, which : which + 1] for c in range(4)], axis=1)

    gain_one = gain_row(0)

    def norm_one(half):
        @pl.loop(0, TILE // 64)
        def _(i):
            rows = pl.ds(pl.multiple_of(half * TILE + i * 64, 64), 64)
            value = x[rows].astype(F32)
            h1[rows] = (value * head_norm(value) * gain_one).astype(BF)

    def heads(half):
        @pl.loop(0, TILE // 256)
        def _(i):
            rows = pl.ds(pl.multiple_of(half * TILE + i * 256, 256), 256)
            mixed = mm(h1[rows], wq[...].reshape(WIDTH, 4 * HEAD)).astype(BF)
            raw[rows] = mixed
            cos_rows, sin_rows = cosine[rows], sine[rows]
            for piece in range(3):
                value = mixed[:, piece * HEAD : (piece + 1) * HEAD].astype(F32)
                by = q_gain[...] if piece < 2 else k_gain[...]
                turned = turn(value * head_norm(value) * by, cos_rows, sin_rows).astype(BF)
                if piece < 2:
                    qs[piece, rows] = turned
                else:
                    ks[rows] = turned

    norm_one(row)
    keep, _, take = beside(0)
    keep.wait()
    take.wait_recv()
    spreads[0].wait(1)
    heads(row)
    x_gather.share()
    for a in (1, 2):
        for kk in range(2):
            crossing(a, kk).start()
    g_gather = Gather(tile_at(g), gs, gr, og)
    g_gather.start()
    x_gather.finish([7, 8])
    beside(2)[0].start()
    beside(2)[1].start()
    norm_one(1 - row)
    heads(1 - row)
    for spread in out_spreads:
        spread.pass_on(1)
    mine = pl.ds(pl.multiple_of(me * OWN, OWN), OWN)
    saves = [
        pltpu.make_async_copy(src, dst, out_s.at[i])
        for i, (src, dst) in enumerate(
            [
                (wq, wq_o), (raw, raw_o), (qs, q_o), (ks, k_o), (gain, gain_o), (x.at[mine], x_o),
                (start, start_o), (cosine, cos_o), (sine, sin_o),
                (att, att_o), (lse, lse_o), (h1t, h1t_o), (g, g_o), (mid, mid_o),
                (w_all.at[row, :, pl.ds(col, 1)], wo_o),
            ]
        )
    ]
    for i in range(9):
        saves[i].start()

    for block in range(GROUP // QROWS):
        first, keys = block * QROWS, (block + 1) * QROWS
        rows = pl.ds(first, QROWS)
        allowed = allowed_keys(start[rows, :1], first, keys)

        @pl.loop(0, 2)
        def _(h):
            score = mm_t(qs[h, rows], ks[:keys]) * (SCALE * LOG2)
            score = jnp.where(allowed, score, -1e30)
            peak = jnp.max(score, axis=1, keepdims=True)
            weight = jnp.exp2(score - peak)
            total = jnp.sum(weight, axis=1, keepdims=True)
            out = mm(weight.astype(BF), raw[:keys, 3 * HEAD :]) / total
            att[h, rows] = out.astype(BF)
            lse[h, rows] = jnp.broadcast_to(peak + jnp.log2(total), (QROWS, HEAD))

        if block == 1:
            for a in (1, 2):
                for kk in range(2):
                    crossed(a, kk).wait_recv()
                spreads[a].start(0)

    for which, spread in enumerate(out_spreads):
        spread.wait(1)
        out_share(which, k).start()
    for o in range(1, 8):
        hand(o).start()
    for h in range(2):
        heard[me, h] = att[h, mine]
    saves[9].start()
    saves[10].start()
    for a in (1, 2):
        spreads[a].pass_on(0)
    for a in (1, 2):
        spreads[a].wait(0)
        spreads[a].start(1)
    def cut(i):
        rows = pl.ds(pl.multiple_of(i * 32, 32), 32)
        for u in range(3):
            for half in range(2):
                into = slice(u * 512 + half * 256, u * 512 + half * 256 + 256)
                for kk in range(2):
                    cols = slice(kk * UNITS + u * 256, kk * UNITS + u * 256 + 256)
                    g_cut[kk, i // 4, i % 4, :, into] = g_raw[rows, half, cols]

    pl.loop(0, 8)(cut)
    g_gather.forward()
    pl.loop(8, 16)(cut)
    beside(1)[0].start()
    beside(1)[1].start()
    keep_out.wait()
    out_arrived_peer = w_all.at[row, beside_col]
    remote(out_arrived_peer, out_arrived_peer, os_.at[0], or_.at[2 * z + 1 - k], peer).wait_recv()
    for which in range(2):
        out_share(which, 1 - k).wait_recv()
    saves[14].start()
    for o in range(1, 8):
        handed(o).wait_recv()
    left = [
        jnp.concatenate([heard[4 * half + c, h] for c in range(4) for h in range(2)], axis=1) for half in range(2)
    ]
    for c in range(4):
        mid[:, c * TILE : (c + 1) * TILE] = mm(left[0], w_all[0, c].reshape(2 * TILE, TILE)) + mm(
            left[1], w_all[1, c].reshape(2 * TILE, TILE)
        )
    gain_two = gain_row(1)

    @pl.loop(0, OWN // 16)
    def _(i):
        first = pl.multiple_of(i * 16, 16)
        there = pl.ds(pl.multiple_of(me * OWN + first, 16), 16)
        value = x[there].astype(F32) + mid[pl.ds(first, 16)]
        mid[pl.ds(first, 16)] = value
        h2[there] = (value * head_norm(value) * gain_two).astype(BF)

    h2_gather = Gather(rows_at(h2), hs, hr)
    h2_gather.start()
    saves[13].start()

    @pl.loop(0, 8)
    def _(i):
        cols = pl.ds(pl.multiple_of(i * 256, 256), 256)
        h1t[cols] = h1[:, cols].T

    saves[11].start()
    g_gather.share()
    for a in (1, 2):
        spreads[a].pass_on(1)
    x_gather.drain()
    saves[5].wait()
    row_saves = []

    def feed(d):
        rows = pl.ds(pl.multiple_of((z + d) % 4 * 256, 256), 256)

        @pl.loop(0, 3)
        def _(u):
            wide = pl.ds(pl.multiple_of(u * 512, 512), 512)
            gate_cols = pl.ds(pl.multiple_of(u * 512, 256), 256)
            up_cols = pl.ds(pl.multiple_of(u * 512 + 256, 256), 256)
            pair_ = mm(h2[rows], wg[:, :, :, :, wide].reshape(WIDTH, 512))
            back = mm_t(g[rows, :TILE], wd[0, u].reshape(256, TILE))
            for c in range(1, 4):
                back += mm_t(g[rows, c * TILE : (c + 1) * TILE], wd[c, u].reshape(256, TILE))
            gate, up = pair_[:, :256], pair_[:, 256:]
            sig = 1.0 / (1.0 + jnp.exp(-gate))
            silu = gate * sig
            h1[rows, pl.ds(pl.multiple_of(u * 256, 256), 256)] = (silu * up).astype(BF)
            x[rows, gate_cols] = (back * up * sig * (1.0 + gate * (1.0 - sig))).astype(BF)
            x[rows, up_cols] = (back * silu).astype(BF)

        for i, (src, dst) in enumerate(
            [
                (h2.at[rows], h2_o.at[rows]),
                (x.at[rows, pl.ds(0, 2 * UNITS)], ggu_o.at[rows]),
                (h1.at[rows, pl.ds(0, UNITS)], hid_o.at[rows]),
            ]
        ):
            copy = pltpu.make_async_copy(src, dst, row_s.at[d, i])
            copy.start()
            row_saves.append(copy)

    for a in (1, 2):
        keep, _, take = beside(a)
        keep.wait()
        take.wait_recv()
        spreads[a].wait(1)
    g_gather.finish()
    keep_g.wait()
    saves[12].start()
    h2_gather.finish([4])
    feed(0)
    h2_gather.forward()
    h2_gather.finish([5, 6])
    feed(1)
    weight_saves = [pltpu.make_async_copy(weights[a], (wg_o, wd_o)[a - 1], loc_s.at[a + 5]) for a in (1, 2)]
    for copy in weight_saves:
        copy.start()
    h2_gather.share()
    feed(3)
    h2_gather.finish([7, 8])
    feed(2)
    for copy in gain_copies + out_pieces + [give_out]:
        copy.wait_send()
    for a in range(3):
        beside(a)[1].wait_send()
        for kk in range(2):
            crossing(a, kk).wait_send()
    for o in range(1, 8):
        hand(o).wait_send()
    for which in range(2):
        out_share(which, k).wait_send()
    for spread in spreads + out_spreads:
        spread.drain()
    g_gather.drain()
    h2_gather.drain()
    for i, copy in enumerate(saves):
        if i != 5:
            copy.wait()
    for copy in weight_saves + row_saves:
        copy.wait()


def forward_call(*args):
    hbm = pl.BlockSpec(memory_space=pl.ANY)
    vmem = pl.BlockSpec(memory_space=pltpu.VMEM)
    smem = pl.BlockSpec(memory_space=pltpu.SMEM)
    dma = pltpu.SemaphoreType.DMA

    def out(shape, dtype=BF):
        return jax.ShapeDtypeStruct(shape, dtype)

    wide = (GROUP, WIDTH)
    return pl.pallas_call(
        forward_kernel,
        out_shape=[
            out(wide), out(wide), out((4, 4, 4, 32, 512)), out((4, 1, 4, 2, 32, TILE)), out((4, 4, 4, 32, 2 * UNITS)),
            out((4, 3, 4, 4, 16, TILE)), out((WIDTH, GROUP)), out((GROUP, 512)), out((2, GROUP, HEAD)), out((GROUP, HEAD)),
            out((2, GROUP, HEAD)), out((2, GROUP, HEAD), F32), out((OWN, WIDTH), F32), out((4, 8, TILE), F32),
            out((OWN, WIDTH)), out((GROUP, HEAD), jnp.int32), out((GROUP, HEAD), F32), out((GROUP, HEAD), F32),
            out((GROUP, 2 * UNITS)), out((GROUP, UNITS)),
        ],
        in_specs=[hbm] * 2 + [vmem] * 5 + [smem] * 3 + [hbm] * 4,
        out_specs=[hbm] * 20,
        scratch_shapes=[
            pltpu.VMEM(wide, BF), pltpu.VMEM(wide, BF), pltpu.VMEM((WIDTH, GROUP), BF), pltpu.VMEM(wide, BF),
            pltpu.VMEM(wide, BF), pltpu.VMEM((4, 4, 4, 32, 512), BF), pltpu.VMEM((4, 4, 4, 32, 2 * UNITS), BF),
            pltpu.VMEM((4, 3, 4, 4, 16, TILE), BF), pltpu.VMEM((2, 4, 4, 4, 2, 32, TILE), BF),
            pltpu.VMEM((GROUP, 512), BF), pltpu.VMEM((2, GROUP, HEAD), BF), pltpu.VMEM((GROUP, HEAD), BF),
            pltpu.VMEM((2, GROUP, HEAD), BF), pltpu.VMEM((8, 2, OWN, HEAD), BF), pltpu.VMEM((2, GROUP, HEAD), F32),
            pltpu.VMEM((OWN, WIDTH), F32), pltpu.VMEM((4, 8, TILE), F32), pltpu.VMEM((8, TILE), F32),
            pltpu.VMEM((GROUP, HEAD), jnp.int32), pltpu.VMEM((GROUP, HEAD), F32), pltpu.VMEM((GROUP, HEAD), F32),
            pltpu.VMEM((TILE, 4, 512), BF), pltpu.VMEM((2, 4, 4, 32, 512), BF), pltpu.VMEM((32, 4, 512), BF),
            pltpu.VMEM((2, 32, 512), BF), pltpu.VMEM((TILE, 2, 2 * UNITS), BF), pltpu.VMEM((2, 4, 4, 32, 2 * UNITS), BF),
            pltpu.VMEM((32, 2, 2 * UNITS), BF), pltpu.VMEM((2, 32, 2 * UNITS), BF),
        ]
        + GATHER_SEMS * 3
        + [
            dma((3, 2)), dma((3, 2)), dma((3,)), dma((3,)), dma((3,)), dma((4,)), dma((8,)), dma((15,)), dma((4,)),
            dma((4, 3)), dma((8,)), dma((8,)), dma((9,)), dma((9,)),
        ]
        + SPREAD_SEMS * 5,
        compiler_params=pltpu.CompilerParams(
            collective_id=1, has_side_effects=True, vmem_limit_bytes=VMEM_LIMIT
        ),
        cost_estimate=pl.CostEstimate(flops=14_000_000_000, bytes_accessed=60_000_000, transcendentals=2_000_000),
        name="forward",
    )(*args)


class Collapse:
    def __init__(self, which, data, near, full, done, send, recv):
        here = dp_place()
        self.which, self.data, self.near, self.full, self.done, self.here = which, data, near, full, done, here
        self.copies, self.send, self.recv = {}, send, recv
        for half in range(2):
            for phase in range(2):
                axis = half ^ phase

                def copy(slot, src, dst, o):
                    return remote(src, dst, send.at[which, phase], recv.at[which, phase, slot // 2], along(axis, o))

                self.copies[half, phase] = [
                    copy(0, self.block(half, phase, 2, 0), near[phase].at[half, 0], 1),
                    copy(1, self.block(half, phase, 2, 1), near[phase].at[half, 1], 3),
                    copy(2, self.block(half, phase, 1), full[phase].at[half, 0], 1),
                    copy(3, self.block(half, phase, 3), full[phase].at[half, 1], 3),
                ]

    def at(self, half, phase, o):
        there = (self.here[half ^ phase] + o) % 4
        if phase == 0:
            return (there, slice(None)) if half == 0 else (slice(None), there)
        return (self.here[0], there) if half == 0 else (there, self.here[1])

    def block(self, half, phase, o, part=None):
        which = pl.ds(2 * half, 2) if part is None else 2 * half + part
        return self.data.at[(*self.at(half, phase, o), which)]

    def cell(self, half, phase, o, a, c):
        x, y = self.at(half, phase, o)
        x, y = (a if isinstance(x, slice) else x), (a if isinstance(y, slice) else y)
        return (x, y, 2 * half + c)

    def arrived(self, phase, step):
        ref = (self.near, self.full)[step][phase]
        sems = (self.send.at[self.which, phase], self.recv.at[self.which, phase, step])
        remote(ref, ref, *sems, along(0, 1)).wait_recv()

    def start(self, phase=0):
        for half in range(2):
            for slot in range(2):
                self.copies[half, phase][slot].start()

    def mid(self, phase=0):
        self.arrived(phase, 0)
        for half in range(2):
            for slot in range(2):

                def add(a):
                    index = self.cell(half, phase, (1, 3)[slot], a, slot)
                    here = (half, slot, a) if phase == 0 else (half, slot)
                    self.data[index] = (
                        self.data[index].astype(F32) + self.near[phase][here].astype(F32)
                    ).astype(BF)

                if phase == 0:
                    pl.loop(0, 4)(add)
                else:
                    add(0)
                self.copies[half, phase][2 + slot].start()

    def first(self):
        self.arrived(0, 1)
        for half in range(2):

            @pl.loop(0, 4)
            def _(a):
                for c in range(2):
                    index = self.cell(half, 0, 0, a, c)
                    total = self.data[index].astype(F32)
                    for slot in range(2):
                        total += self.full[0][half, slot, a, c].astype(F32)
                    self.data[index] = total.astype(BF)

        self.start(1)

    def second(self):
        self.arrived(1, 1)
        for half in range(2):
            for c in range(2):
                total = self.data[self.cell(half, 1, 0, 0, c)].astype(F32)
                for slot in range(2):
                    total += self.full[1][half, slot, c].astype(F32)
                self.done[self.which, 2 * half + c] = total.astype(BF)

    def drain(self):
        for phase in range(2):
            ref = self.data.at[0, pl.ds(0, 3)] if phase else self.data.at[pl.ds(0, 3)]
            sems = (self.send.at[self.which, phase], self.recv.at[self.which, phase, 0])
            remote(ref, ref, *sems, along(0, 1)).wait_send()


CHUNKS, BUFFERS = 4, 3


def collapse_scratch():
    dma = pltpu.SemaphoreType.DMA
    return (
        [pltpu.VMEM((4, 4, 4, 48, 512), BF)] * BUFFERS
        + [pltpu.VMEM((2, 2, 4, 48, 512), BF)] * BUFFERS
        + [pltpu.VMEM((2, 2, 48, 512), BF)] * BUFFERS
        + [pltpu.VMEM((2, 2, 4, 2, 48, 512), BF)] * BUFFERS
        + [pltpu.VMEM((2, 2, 2, 48, 512), BF)] * BUFFERS
        + [pltpu.VMEM((CHUNKS, 4, 48, 512), BF), dma((CHUNKS, 2)), dma((CHUNKS, 2, 2))]
        + [dma((CHUNKS, 3)), dma((CHUNKS, 4)), dma((CHUNKS, 2)), dma((CHUNKS, 2, 2))]
    )


class Trade:
    def __init__(self, block, slot, send, recv, which=()):
        _, row, col, z, k = place()
        self.col, self.peer = col, on_ring(z, 1 - k)
        self.recv, self.send, self.slot, self.which = recv, send, slot, which
        self.copies = [
            remote(block((col + o) % 4), slot(col), send.at[(*which, o - 1)], recv.at[(*which, o - 1)], {"col": (col + o) % 4})
            for o in range(1, 4)
        ]
        self.keep = pltpu.make_async_copy(block(col), slot(col), recv.at[(*which, 3)])

    def start(self):
        for copy in self.copies:
            copy.start()
        self.keep.start()

    def finish(self):
        for o in range(1, 4):
            dst = self.slot((self.col - o + 4) % 4)
            sems = (self.send.at[(*self.which, o - 1)], self.recv.at[(*self.which, o - 1)])
            remote(dst, dst, *sems, self.peer).wait_recv()
        self.keep.wait()

    def drain(self):
        for copy in self.copies:
            copy.wait_send()


def norm_back(grad, value, gain):
    scale = head_norm(value)
    weighted = grad * gain
    inner = jnp.mean(weighted * value, axis=1, keepdims=True)
    return scale * weighted - value * (scale * scale * scale * inner), grad * value * scale


def norm_back(grad, value, gain):
    scale = head_norm(value)
    weighted = grad * gain
    inner = jnp.mean(weighted * value, axis=1, keepdims=True)
    return scale * weighted - value * (scale * scale * scale * inner), grad * value * scale


def backward_kernel(
    h2_i, ggu_i, hid_i, g_i, wg_i, wd_i, wo_i, wq_i, h1t_i, raw_i, q_i, k_i, att_i, lse_i, mid_i, gain_i, x_i,
    start_i, cos_i, sin_i, q_gain, k_gain,
    result_o, stream_o, grads_o, sums_o,
    m, gm, dqkv, mid, gain, x_own, g_own, acc, head_acc, tile_f, tile_b, totals, heard,
    ms, mr,
    parts, theirs, psums, near, full, rs_s, rs_r,
    data0, data1, data2, near0, near1, near2, next0, next1, next2, full0, full1, full2, last0, last1, last2,
    done, c_s, c_r, t_s, t_r, a_s, a_r,
    fs, fr, ls, lr, as_, ar, in_s, free,
):
    p, row, col, z, k = place()
    px, py = dp_place()
    me = 2 * z + k
    up, down, peer = on_ring((z + 1) % 4, k), on_ring((z + 3) % 4, k), on_ring(z, 1 - k)
    far = on_ring((z + 2) % 4, k)
    loads = []

    def load(src, dst):
        copy = pltpu.make_async_copy(src, dst, in_s.at[len(loads)])
        copy.start()
        loads.append(copy)
        return copy

    def wait(copies):
        for copy in copies:
            copy.wait()

    collapses, trades, spreads = [], [], []
    datas, nears, nexts = (data0, data1, data2), (near0, near1, near2), (next0, next1, next2)
    fulls, lasts = (full0, full1, full2), (last0, last1, last2)

    def chunk(i):
        def at(half, x, y, part):
            xs = slice(None) if x is None else x
            ys = slice(None) if y is None else y
            which = pl.ds(2 * half, 2) if part is None else 2 * half + part
            return grads_o.at[i, xs, ys, which]

        b = i % BUFFERS
        collapses.append(Collapse(i, datas[b], (nears[b], nexts[b]), (fulls[b], lasts[b]), done, c_s, c_r))
        trades.append(
            Trade(lambda c: done.at[i, c], lambda c: grads_o.at[i, px, py, c], t_s, t_r, (i,))
        )
        def bulk(phase, count):
            xs_, ys_ = (count // 2, 4) if phase else (1, count // 2)
            return grads_o.at[i, pl.ds(0, xs_), pl.ds(0, ys_)]

        spreads.append(Spread(at, bulk, a_s, a_r, (i,)))

    for i in range(CHUNKS):
        chunk(i)
    scatter = Scatter(parts, theirs, psums, near, full, rs_s, rs_r)
    stream_trade = Trade(
        lambda c: tile_f.at[:, pl.ds(pl.multiple_of(c * TILE, TILE), TILE)],
        lambda c: stream_o.at[pl.ds(pl.multiple_of(c * OWN, OWN), OWN)], fs, fr,
    )
    result_trade = Trade(
        lambda c: tile_b.at[:, pl.ds(pl.multiple_of(c * TILE, TILE), TILE)],
        lambda c: result_o.at[pl.ds(pl.multiple_of(c * OWN, OWN), OWN)], ls, lr,
    )

    def release():
        scatter.drain()
        for device in (up, down, peer):
            pl.semaphore_signal(free, inc=1, device_id=device, device_id_type=MESH)

    def project(d, product):
        rows = pl.ds(pl.multiple_of((z + d) % 4 * 256, 256), 256)

        @pl.loop(0, 4)
        def _(c):
            cols = pl.ds(pl.multiple_of(c * TILE, TILE), TILE)
            parts[d, :, cols] = product(rows, c, cols).astype(BF)

        scatter.put(d)

    def weight_grads(i, first, second):
        data = datas[i % BUFFERS]
        for c in range(4):
            cols = slice(c * TILE, (c + 1) * TILE)
            data[:, :, c, :32] = first(cols).astype(BF).reshape(4, 4, 32, 512)
            data[:, :, c, 32:] = second(cols).astype(BF).reshape(4, 4, 16, 512)
        collapses[i].start()

    def gain_row(which):
        return jnp.concatenate([gain[c, which : which + 1] for c in range(4)], axis=1)

    own_rows = pl.ds(pl.multiple_of(me * OWN, OWN), OWN)

    def stage_one(h2, g, ggu, hid, wg):
        first_loads = [load(ggu_i, ggu)]
        wg_loads = [load(wg_i.at[c], wg.at[c]) for c in range(4)]
        more_loads = [load(hid_i, hid), load(h2_i, h2), load(g_i, g)]
        meet(ring_friends() + [far] + xy_friends())
        def grads(u):
            weight_grads(
                u,
                lambda cols: t_mm(h2[:, cols], ggu[:, u * 512 : (u + 1) * 512]),
                lambda cols: t_mm(hid[:, u * 256 : (u + 1) * 256], g[:, cols]),
            )

        def product(rows, c, cols):
            return mm_t(ggu[rows], wg[c])

        wait(first_loads)
        far_rows = pl.ds(pl.multiple_of((z + 2) % 4 * 256, 256), 256)
        for c in range(4):
            wg_loads[c].wait()
            parts[2, :, c * TILE : (c + 1) * TILE] = mm_t(ggu[far_rows], wg[c]).astype(BF)
        scatter.put(2)
        wait(more_loads)
        grads(0)
        scatter.across()
        project(1, product)
        project(3, product)
        collapses[0].mid()
        scatter.beside(0)
        scatter.beside(1)
        grads(1)
        project(0, product)
        grads(2)

    early = [load(mid_i, mid), load(gain_i, gain), load(x_i, x_own), load(g_i.at[own_rows], g_own)]
    pl.run_scoped(
        stage_one,
        pltpu.VMEM((GROUP, WIDTH), BF), pltpu.VMEM((GROUP, WIDTH), BF), pltpu.VMEM((GROUP, 2 * UNITS), BF),
        pltpu.VMEM((GROUP, UNITS), BF), pltpu.VMEM((4, TILE, 2 * UNITS), BF),
    )

    def stage_two(wo, att, qs, ks, raw, lse, ga, dk, dv, h1t, wq, att_t, start, cosine, sine):
        l_wo, l_att = load(wo_i, wo), load(att_i, att)
        l_heads = [
            load(q_i, qs), load(k_i, ks), load(raw_i, raw), load(lse_i, lse),
            load(start_i, start), load(cos_i, cosine), load(sin_i, sine),
        ]
        l_last = [load(h1t_i, h1t), load(wq_i, wq)]
        wait(early)
        acc[...] = jnp.zeros_like(acc)
        head_acc[...] = jnp.zeros_like(head_acc)
        dk[...] = jnp.zeros_like(dk)
        dv[...] = jnp.zeros_like(dv)
        totals[0] = jnp.zeros((8, TILE + HEAD), F32)
        gain_two = gain_row(1)
        scatter.arrive()

        @pl.loop(0, OWN // 16)
        def _(i):
            rows = pl.ds(pl.multiple_of(i * 16, 16), 16)
            back, gained = norm_back(scatter.total(pl.multiple_of(i * 16, 16), 16), mid[rows], gain_two)
            acc[1] += gained
            back = back + g_own[rows].astype(F32)
            gm[rows] = back
            m[pl.ds(pl.multiple_of(me * OWN + i * 16, 16), 16)] = back.astype(BF)

        m_gather = Gather(rows_at(m), ms, mr)
        m_gather.start()
        release()
        collapses[0].first()
        collapses[1].mid()
        collapses[0].mid(1)
        l_att.wait()
        for h in range(2):
            att_t[h * HEAD : (h + 1) * HEAD] = att[h].T
        l_wo.wait()
        wait(l_heads)

        def attend(d):
            block = (z + d) % 4
            first = pl.multiple_of(block * QROWS, QROWS)
            rows = pl.ds(first, QROWS)
            back = mm_t(m[rows, :TILE], wo[0])
            for c in range(1, 4):
                back += mm_t(m[rows, c * TILE : (c + 1) * TILE], wo[c])
            for h in range(2):
                ga[h, rows] = back[:, h * HEAD : (h + 1) * HEAD].astype(BF)

            def over(keys):
                allowed = allowed_keys(start[rows, :1], first, keys)

                @pl.loop(0, 2)
                def _(h):
                    cols = pl.ds(pl.multiple_of(h * HEAD, HEAD), HEAD)
                    score = mm_t(qs[h, rows], ks[:keys]) * (SCALE * LOG2)
                    prob = jnp.exp2(jnp.where(allowed, score, -1e30) - lse[h, rows, :1])
                    grad = ga[h, rows]
                    delta = jnp.sum(grad.astype(F32) * att[h, rows].astype(F32), axis=1, keepdims=True)
                    prob_grad = mm_t(grad, raw[:keys, 3 * HEAD :])
                    score_grad = (prob * (prob_grad - delta)).astype(BF)
                    dk[:keys] += t_mm(score_grad, qs[h, rows])
                    dv[:keys] += t_mm(prob.astype(BF), grad)
                    back = turn_back(mm(score_grad, ks[:keys]) * SCALE, cosine[rows], sine[rows])
                    back, gained = norm_back(back, raw[rows, cols].astype(F32), q_gain[...])
                    dqkv[rows, cols] = back.astype(BF)
                    head_acc[0:1] += jnp.sum(gained, axis=0, keepdims=True)

            @pl.when(block < 2)
            def _():
                over(2 * QROWS)

            @pl.when(block >= 2)
            def _():
                over(4 * QROWS)

        m_gather.finish([4])
        attend(0)
        collapses[1].first()
        collapses[2].mid()
        m_gather.forward()
        collapses[1].mid(1)
        collapses[0].second()
        trades[0].start()
        m_gather.finish([5, 6])
        attend(1)
        m_gather.share()
        attend(3)
        collapses[2].first()
        m_gather.finish([7, 8])
        attend(2)
        trades[0].finish()
        spreads[0].start(0)

        @pl.loop(0, 4)
        def _(i):
            rows = pl.ds(pl.multiple_of(i * 256, 256), 256)
            back = turn_back(dk[rows] * SCALE, cosine[rows], sine[rows])
            back, gained = norm_back(back, raw[rows, 2 * HEAD : 3 * HEAD].astype(F32), k_gain[...])
            dqkv[rows, 2 * HEAD : 3 * HEAD] = back.astype(BF)
            dqkv[rows, 3 * HEAD :] = dv[rows].astype(BF)
            head_acc[1:2] += jnp.sum(gained, axis=0, keepdims=True)

        collapses[2].mid(1)
        wait(l_last)
        collapses[0].drain()
        weight_grads(3, lambda cols: mm(h1t[cols], dqkv[...]), lambda cols: mm(att_t[...], m[:, cols]))
        collapses[1].second()
        trades[1].start()
        spreads[0].pass_on(0)
        collapses[2].second()
        trades[2].start()
        pl.semaphore_wait(free, 3)

        def product(rows, c, cols):
            return mm_t(dqkv[rows], wq[c])

        project(2, product)
        project(1, product)
        collapses[3].mid()
        trades[1].finish()
        spreads[1].start(0)
        scatter.across()
        trades[2].finish()
        spreads[2].start(0)
        project(3, product)
        spreads[0].wait(0)
        spreads[0].start(1)
        spreads[1].pass_on(0)
        project(0, product)
        collapses[3].first()
        scatter.beside(0)
        scatter.beside(1)
        m_gather.drain()

    pl.run_scoped(
        stage_two,
        pltpu.VMEM((4, 256, TILE), BF), pltpu.VMEM((2, GROUP, HEAD), BF), pltpu.VMEM((2, GROUP, HEAD), BF),
        pltpu.VMEM((GROUP, HEAD), BF), pltpu.VMEM((GROUP, 512), BF), pltpu.VMEM((2, GROUP, HEAD), F32),
        pltpu.VMEM((2, GROUP, HEAD), BF), pltpu.VMEM((GROUP, HEAD), F32), pltpu.VMEM((GROUP, HEAD), F32),
        pltpu.VMEM((WIDTH, GROUP), BF), pltpu.VMEM((4, TILE, 512), BF), pltpu.VMEM((2 * HEAD, GROUP), BF),
        pltpu.VMEM((GROUP, HEAD), jnp.int32), pltpu.VMEM((GROUP, HEAD), F32), pltpu.VMEM((GROUP, HEAD), F32),
    )

    def stage_three(hid, wd):
        last = [load(hid_i, hid), load(wd_i, wd)]
        gain_one = gain_row(0)
        collapses[3].mid(1)
        spreads[1].wait(0)
        spreads[1].start(1)
        spreads[2].pass_on(0)
        collapses[3].second()
        trades[3].start()
        scatter.arrive()

        @pl.loop(0, OWN // 16)
        def _(i):
            rows = pl.ds(pl.multiple_of(i * 16, 16), 16)
            back, gained = norm_back(
                scatter.total(pl.multiple_of(i * 16, 16), 16), x_own[rows].astype(F32), gain_one
            )
            acc[0] += gained
            tile_f[rows] = gm[rows] + back

        stream_trade.start()
        release()
        for c in range(4):
            for which in range(2):
                part = jnp.sum(acc[which, :, c * TILE : (c + 1) * TILE], axis=0, keepdims=True)
                totals[0, 4 * which + c : 4 * which + c + 1, :TILE] = part
        totals[0, 0:2, TILE:] = head_acc[0:2]
        sent = []

        def tell(phase, devices, slots):
            for device, slot in zip(devices, slots):
                copy = remote(totals.at[phase], heard.at[slot], as_.at[slot], ar.at[slot], device)
                copy.start()
                sent.append(copy)

        def listen(phase, slots):
            total = totals[phase]
            for slot in slots:
                remote(heard.at[slot], heard.at[slot], as_.at[slot], ar.at[slot], peer).wait_recv()
                total += heard[slot]
            totals[phase + 1] = total

        tell(0, [peer], [0])
        spreads[0].pass_on(1)
        wait(last)
        pl.semaphore_wait(free, 3)

        def product(rows, c, cols):
            return mm(hid[rows], wd[c])

        project(2, product)
        project(1, product)
        listen(0, [0])
        tell(1, [up, down, far], [1, 2, 3])
        project(3, product)
        trades[3].finish()
        spreads[3].start(0)
        scatter.across()
        spreads[1].pass_on(1)
        spreads[3].pass_on(0)
        listen(1, [1, 2, 3])
        tell(2, [along(0, o) for o in range(1, 4)], [4, 5, 6])
        spreads[2].wait(0)
        spreads[2].start(1)
        project(0, product)
        scatter.beside(0)
        scatter.beside(1)
        spreads[3].wait(0)
        spreads[3].start(1)
        spreads[2].pass_on(1)
        listen(2, [4, 5, 6])
        tell(3, [along(1, o) for o in range(1, 4)], [7, 8, 9])
        scatter.arrive()

        @pl.loop(0, OWN // 16)
        def _(i):
            rows = pl.ds(pl.multiple_of(i * 16, 16), 16)
            tile_b[rows] = (mid[rows] + scatter.total(pl.multiple_of(i * 16, 16), 16)).astype(BF)

        result_trade.start()
        spreads[3].pass_on(1)
        listen(3, [7, 8, 9])
        sums_o[...] = totals[4]
        stream_trade.finish()
        result_trade.finish()
        for spread in spreads:
            spread.wait(1)
        scatter.drain()
        for thing in collapses[1:] + trades + spreads + [stream_trade, result_trade]:
            thing.drain()
        for copy in sent:
            copy.wait_send()

    pl.run_scoped(stage_three, pltpu.VMEM((GROUP, UNITS), BF), pltpu.VMEM((4, UNITS, TILE), BF))


def backward_call(*args):
    hbm = pl.BlockSpec(memory_space=pl.ANY)
    vmem = pl.BlockSpec(memory_space=pltpu.VMEM)
    dma = pltpu.SemaphoreType.DMA
    out = jax.ShapeDtypeStruct
    grads = out((CHUNKS, 4, 4, 4, 48, 512), BF)
    return pl.pallas_call(
        backward_kernel,
        out_shape=[out((TILE, TILE), BF), out((TILE, TILE), F32), grads, out((8, TILE + HEAD), F32)],
        in_specs=[hbm] * 20 + [vmem] * 2,
        out_specs=[hbm] * 3 + [vmem],
        scratch_shapes=[
            pltpu.VMEM((GROUP, WIDTH), BF), pltpu.VMEM((OWN, WIDTH), F32), pltpu.VMEM((GROUP, 512), BF),
            pltpu.VMEM((OWN, WIDTH), F32), pltpu.VMEM((4, 8, TILE), F32),
            pltpu.VMEM((OWN, WIDTH), BF), pltpu.VMEM((OWN, WIDTH), BF), pltpu.VMEM((2, 16, WIDTH), F32),
            pltpu.VMEM((8, HEAD), F32), pltpu.VMEM((OWN, WIDTH), F32), pltpu.VMEM((OWN, WIDTH), BF),
            pltpu.VMEM((5, 8, TILE + HEAD), F32), pltpu.VMEM((10, 8, TILE + HEAD), F32),
        ]
        + GATHER_SEMS
        + scatter_scratch()
        + collapse_scratch()
        + [
            dma((3,)), dma((4,)), dma((3,)), dma((4,)), dma((10,)), dma((10,)), dma((28,)), pltpu.SemaphoreType.REGULAR,
        ],
        compiler_params=pltpu.CompilerParams(
            collective_id=2, has_side_effects=True, vmem_limit_bytes=VMEM_LIMIT
        ),
        cost_estimate=pl.CostEstimate(flops=25_000_000_000, bytes_accessed=100_000_000, transcendentals=2_000_000),
        name="backward",
    )(*args)


PLACE = 4


def place_kernel(grads, result, stream, totals, gate_up, down, qkv, out, result_o, stream_o, one, two, q_o, k_o):
    for c in range(4):
        for u in range(3):
            t = c * 3 + u
            value = grads[u, :, c, :32].reshape(PLACE * 32, 512).astype(F32)
            for g in range(2):
                gate_up[:, g, t * 256 : (t + 1) * 256] = value[:, g * 256 : (g + 1) * 256]
            down[t] = grads[u, :, c, 32:].astype(F32)
        qkv[:, c, :] = grads[3, :, c, :32].reshape(PLACE * 32, 512).astype(F32)
        out[c] = grads[3, :, c, 32:].astype(F32)
    result_o[...] = result[...]
    stream_o[...] = stream[...]
    for c in range(4):
        one[:, c * TILE : (c + 1) * TILE] = totals[c : c + 1, :TILE]
        two[:, c * TILE : (c + 1) * TILE] = totals[4 + c : 5 + c, :TILE]
    q_o[...] = totals[0:1, TILE:]
    k_o[...] = totals[1:2, TILE:]


def place_grads(grads, result, stream, totals):
    tile = pl.BlockSpec((32 * PLACE, TILE), lambda p: (p, 0))

    def whole(*shape):
        return pl.BlockSpec(shape, lambda p: (0,) * len(shape))

    return pl.pallas_call(
        place_kernel,
        grid=(DP // PLACE,),
        in_specs=[
            pl.BlockSpec((CHUNKS, PLACE, 4, 48, 512), lambda p: (0, p, 0, 0, 0)), tile, tile, whole(8, TILE + HEAD),
        ],
        out_specs=[
            pl.BlockSpec((32 * PLACE, 2, 4 * UNITS), lambda p: (p, 0, 0)),
            pl.BlockSpec((12, PLACE, 16, TILE), lambda p: (0, p, 0, 0)),
            pl.BlockSpec((32 * PLACE, 4, 512), lambda p: (p, 0, 0)),
            pl.BlockSpec((4, PLACE, 16, TILE), lambda p: (0, p, 0, 0)),
            tile, tile, whole(1, WIDTH), whole(1, WIDTH), whole(1, HEAD), whole(1, HEAD),
        ],
        out_shape=[
            jax.ShapeDtypeStruct((TILE, 2, 4 * UNITS), F32),
            jax.ShapeDtypeStruct((12, DP, 16, TILE), F32),
            jax.ShapeDtypeStruct((TILE, 4, 512), F32),
            jax.ShapeDtypeStruct((4, DP, 16, TILE), F32),
            jax.ShapeDtypeStruct((TILE, TILE), BF),
            jax.ShapeDtypeStruct((TILE, TILE), F32),
            jax.ShapeDtypeStruct((1, WIDTH), F32),
            jax.ShapeDtypeStruct((1, WIDTH), F32),
            jax.ShapeDtypeStruct((1, HEAD), F32),
            jax.ShapeDtypeStruct((1, HEAD), F32),
        ],
        compiler_params=pltpu.CompilerParams(vmem_limit_bytes=VMEM_LIMIT),
        cost_estimate=pl.CostEstimate(flops=0, bytes_accessed=41_000_000, transcendentals=0),
        name="place",
    )(grads, result, stream, totals)


def body(
    tokens, norm1_gain, w_qkv, q_gain, k_gain, w_out, norm2_gain, w_gate_up, w_down, out_grad,
    seq_lengths, seq_group, seq_start,
):
    (h2, g, wq, wo, wg, wd, h1t, raw, qs, ks, att, lse, middle, gain, x_own, start, cosine, sine, ggu, hid) = forward_call(
        tokens, out_grad, norm1_gain[None], norm2_gain[None], q_gain[None], k_gain[None], jnp.asarray(FREQ),
        seq_lengths, seq_group, seq_start, w_qkv, w_gate_up,
        w_out.reshape(4, 4, 2, 32, TILE), w_down.reshape(4, 3, 4, 4, 16, TILE),
    )
    wg = wg.reshape(4, TILE, 2 * UNITS)
    wd = wd.reshape(4, UNITS, TILE)
    result, stream, grads, totals = backward_call(
        h2, ggu, hid, g, wg, wd, wo.reshape(4, 256, TILE), wq.reshape(4, TILE, 512), h1t, raw, qs, ks, att, lse,
        middle, gain, x_own, start, cosine, sine, q_gain[None], k_gain[None],
    )
    grads = grads.reshape(CHUNKS, DP, 4, 48, 512)
    g_gate_up, g_down, g_qkv, g_out, result, stream, one, two, q_grad, k_grad = place_grads(grads, result, stream, totals)
    return (
        result,
        stream,
        one.reshape(WIDTH),
        g_qkv,
        q_grad.reshape(HEAD),
        k_grad.reshape(HEAD),
        g_out.reshape(w_out.shape),
        two.reshape(WIDTH),
        g_gate_up,
        g_down.reshape(w_down.shape),
    )


def solution(mesh):
    in_specs = (
        P(("dp", "row"), "col"),
        P("col"),
        P("col", "row", None),
        P(),
        P(),
        P("row", "col"),
        P("col"),
        P("col", None, "row"),
        P("row", "col"),
        P(("dp", "row"), "col"),
        P(),
        P(),
        P(),
    )
    out_specs = (
        P(("dp", "row"), "col"),
        P(("dp", "row"), "col"),
        P(),
        P("col", "row", None),
        P(),
        P(),
        P("row", "col"),
        P(),
        P("col", None, "row"),
        P("row", "col"),
    )
    return jax.shard_map(body, mesh=mesh, in_specs=in_specs, out_specs=out_specs, check_vma=False)
```

```python
import math

import jax
import jax.numpy as jnp
import numpy as np
from jax import lax
from jax.experimental import pallas as pl
from jax.experimental.pallas import tpu as pltpu
from jax.sharding import PartitionSpec as P

EPS = 1e-06
THETA = 1000000.0
BF = jnp.bfloat16
F32 = jnp.float32
Z = ("row", "col")
MESH = pl.DeviceIdType.MESH
VMEM_LIMIT = 63 * 1024 * 1024

GROUP, WIDTH, TILE, UNITS, HEAD = 1024, 2048, 512, 768, 128
OWN = GROUP // 8
DP = 16


def dot(left, right, dims):
    return lax.dot_general(left, right, (dims, ((), ())), preferred_element_type=F32)


def mm(left, right):
    return dot(left, right, ((1,), (0,)))


def mm_t(left, right):
    return dot(left, right, ((1,), (1,)))


def t_mm(left, right):
    return dot(left, right, ((0,), (0,)))


def place():
    row, col = lax.axis_index("row"), lax.axis_index("col")
    j = 4 * row + col
    return lax.axis_index("dp"), row, col, j // 2, j % 2


def on_ring(z, k):
    j = 2 * z + k
    return {"row": j // 4, "col": j % 4}


def remote(src, dst, send, recv, device):
    return pltpu.make_async_remote_copy(
        src_ref=src, dst_ref=dst, send_sem=send, recv_sem=recv, device_id=device, device_id_type=MESH
    )


def meet(devices):
    barrier = pltpu.get_barrier_semaphore()
    for device in devices:
        pl.semaphore_signal(barrier, inc=1, device_id=device, device_id_type=MESH)
    pl.semaphore_wait(barrier, len(devices))


def ring_friends():
    _, _, _, z, k = place()
    other = z + 1 - 2 * (z % 2)
    return [
        on_ring((z + 1) % 4, k),
        on_ring((z + 3) % 4, k),
        on_ring(z, 1 - k),
        on_ring(other, 1 - k),
    ]


def column_friends():
    _, _, _, z, k = place()
    me = 2 * z + k
    return [on_ring((me + o) % 8 // 2, (me + o) % 2) for o in range(1, 8)]


def dp_place():
    p = lax.axis_index("dp")
    return p // 4, p % 4


def along(axis, o):
    px, py = dp_place()
    return {"dp": (px + o) % 4 * 4 + py} if axis == 0 else {"dp": px * 4 + (py + o) % 4}


def xy_friends():
    return [along(axis, o) for axis in range(2) for o in range(1, 4)]


def tile_at(buf):
    def loc(j, half=None):
        row, col = j // 4, j % 4
        first = pl.multiple_of(row * TILE, TILE)
        rows = pl.ds(first, TILE)
        if half is not None:
            rows = pl.ds(first + half * (TILE // 2), TILE // 2)
        return buf.at[rows, pl.ds(pl.multiple_of(col * TILE, TILE), TILE)]

    return loc


def rows_at(buf):
    def loc(j, half=None):
        first = pl.multiple_of(j * OWN, OWN)
        rows = pl.ds(first, OWN)
        if half is not None:
            rows = pl.ds(first + half * (OWN // 2), OWN // 2)
        return buf.at[rows]

    return loc


class Gather:
    def __init__(self, loc, send, recv, own=None):
        _, _, _, z, k = place()
        up, down, far = (z + 1) % 4, (z + 3) % 4, (z + 2) % 4
        to_up, to_down, peer = on_ring(up, k), on_ring(down, k), on_ring(z, 1 - k)

        def out(slot, src, dst, device):
            return remote(src, dst, send.at[slot], recv.at[slot], device)

        def into(slot, dst):
            return remote(dst, dst, send.at[slot], recv.at[slot], peer)

        mine = loc(2 * z + k)
        own = mine if own is None else own
        left, right, across = 2 * down + k, 2 * up + k, 2 * far + k
        self.first = [out(0, own, mine, to_up), out(1, own, mine, to_down), out(4, own, mine, peer)]
        self.from_left = [
            out(2, loc(left, 0), loc(left, 0), to_up),
            out(5, loc(left), loc(left), peer),
        ]
        self.from_right = [
            out(3, loc(right, 1), loc(right, 1), to_down),
            out(6, loc(right), loc(right), peer),
        ]
        self.from_far = [
            out(7, loc(across, 0), loc(across, 0), peer),
            out(8, loc(across, 1), loc(across, 1), peer),
        ]
        theirs = [2 * z + 1 - k, 2 * down + 1 - k, 2 * up + 1 - k, 2 * far + 1 - k]
        self.arrivals = {
            0: into(0, loc(left)),
            1: into(1, loc(right)),
            2: into(2, loc(across, 0)),
            3: into(3, loc(across, 1)),
            4: into(4, loc(theirs[0])),
            5: into(5, loc(theirs[1])),
            6: into(6, loc(theirs[2])),
            7: into(7, loc(theirs[3], 0)),
            8: into(8, loc(theirs[3], 1)),
        }

    def start(self):
        for copy in self.first:
            copy.start()

    def forward(self):
        self.arrivals[0].wait_recv()
        for copy in self.from_left:
            copy.start()
        self.arrivals[1].wait_recv()
        for copy in self.from_right:
            copy.start()

    def share(self):
        for half in range(2):
            self.arrivals[2 + half].wait_recv()
            self.from_far[half].start()

    def finish(self, slots=range(4, 9)):
        for slot in slots:
            self.arrivals[slot].wait_recv()

    def drain(self):
        for copy in self.first + self.from_left + self.from_right + self.from_far:
            copy.wait_send()


GATHER_SEMS = [pltpu.SemaphoreType.DMA((9,)), pltpu.SemaphoreType.DMA((9,))]


class Spread:
    def __init__(self, at, bulk, send, recv, which=()):
        px, py = dp_place()
        here = (px, py)
        self.bulk, self.send, self.recv, self.which = bulk, send, recv, which
        self.out = {}
        for phase in range(2):
            for step in range(2):
                self.out[phase, step] = []
            for half in range(2):
                axis = half ^ phase

                def block(o, part=None):
                    whose = [px, py]
                    whose[axis] = (here[axis] + o) % 4
                    if phase:
                        whose[1 - axis] = None
                    return at(half, *whose, part)

                def copy(step, ref, o):
                    sems = (send.at[(*which, phase)], recv.at[(*which, phase, step)])
                    self.out[phase, step].append(remote(ref, ref, *sems, along(axis, o)))

                copy(0, block(0), 1)
                copy(0, block(0), 3)
                copy(1, block(3, 0), 1)
                copy(1, block(1, 1), 3)

    def sized(self, phase, count, step=0):
        ref = self.bulk(phase, count)
        sems = (self.send.at[(*self.which, phase)], self.recv.at[(*self.which, phase, step)])
        return remote(ref, ref, *sems, along(0, 1))

    def start(self, phase):
        for copy in self.out[phase, 0]:
            copy.start()

    def pass_on(self, phase):
        self.sized(phase, 4).wait_recv()
        for copy in self.out[phase, 1]:
            copy.start()

    def wait(self, phase):
        self.sized(phase, 2, 1).wait_recv()

    def drain(self):
        for phase in range(2):
            self.sized(phase, 6).wait_send()


SPREAD_SEMS = [pltpu.SemaphoreType.DMA((2,)), pltpu.SemaphoreType.DMA((2, 2))]


class Scatter:
    def __init__(self, parts, theirs, sums, near, full, send, recv):
        _, _, _, z, k = place()
        self.parts, self.theirs, self.sums, self.near, self.full = parts, theirs, sums, near, full
        self.k = k
        to_up, to_down = on_ring((z + 1) % 4, k), on_ring((z + 3) % 4, k)
        peer = on_ring(z, 1 - k)
        half = OWN // 2
        other = pl.ds(pl.multiple_of((1 - k) * OWN, OWN), OWN)

        def copy(slot, src, dst, device):
            return remote(src, dst, send.at[slot], recv.at[slot], device)

        self.copies = [copy(d, parts.at[d, other], theirs.at[d], peer) for d in range(4)] + [
            copy(4, sums.at[0, pl.ds(0, half)], near.at[0], to_up),
            copy(5, sums.at[0, pl.ds(half, half)], near.at[1], to_down),
            copy(6, sums.at[1], full.at[0], to_up),
            copy(7, sums.at[2], full.at[1], to_down),
        ]

    def put(self, d):
        self.copies[d].start()

    def own(self, d, rows, count):
        first = pl.multiple_of(self.k * OWN + rows, count)
        return self.parts[d, pl.ds(first, count)].astype(F32) + self.theirs[
            d, pl.ds(rows, count)
        ].astype(F32)

    def across(self):
        self.copies[2].wait_recv()

        @pl.loop(0, OWN // 16)
        def _(i):
            rows = pl.multiple_of(i * 16, 16)
            self.sums[0, pl.ds(rows, 16)] = self.own(2, rows, 16).astype(BF)

        self.copies[4].start()
        self.copies[5].start()

    def beside(self, side):
        d, half = (1, 3)[side], OWN // 2
        self.copies[d].wait_recv()
        self.copies[4 + side].wait_recv()

        @pl.loop(0, half // 16)
        def _(i):
            rows = pl.multiple_of(i * 16, 16)
            here = pl.multiple_of(rows + side * half, 16)
            there = pl.multiple_of(rows + (1 - side) * half, 16)
            added = self.own(d, here, 16) + self.near[side, pl.ds(rows, 16)].astype(F32)
            self.sums[1 + side, pl.ds(here, 16)] = added.astype(BF)
            self.sums[1 + side, pl.ds(there, 16)] = self.own(d, there, 16).astype(BF)

        self.copies[6 + side].start()

    def arrive(self):
        self.copies[0].wait_recv()
        self.copies[6].wait_recv()
        self.copies[7].wait_recv()

    def total(self, rows, count):
        return (
            self.own(0, rows, count)
            + self.full[0, pl.ds(rows, count)].astype(F32)
            + self.full[1, pl.ds(rows, count)].astype(F32)
        )

    def drain(self):
        for copy in self.copies:
            copy.wait_send()


def scatter_scratch():
    return [
        pltpu.VMEM((4, 2 * OWN, WIDTH), BF),
        pltpu.VMEM((4, OWN, WIDTH), BF),
        pltpu.VMEM((3, OWN, WIDTH), BF),
        pltpu.VMEM((2, OWN // 2, WIDTH), BF),
        pltpu.VMEM((2, OWN, WIDTH), BF),
        pltpu.SemaphoreType.DMA((8,)),
        pltpu.SemaphoreType.DMA((8,)),
    ]


def head_norm(value):
    return lax.rsqrt(jnp.mean(value * value, axis=1, keepdims=True) + EPS)


def turn(value, cosine, sine):
    return value * cosine + pltpu.roll(value, HEAD // 2, 1) * sine


def turn_back(value, cosine, sine):
    return value * cosine - pltpu.roll(value, HEAD // 2, 1) * sine


LOG2 = math.log2(math.e)
SCALE = 1.0 / math.sqrt(HEAD)
QROWS = 256


def allowed_keys(start, first, keys):
    slots = lax.broadcasted_iota(jnp.int32, (QROWS, keys), 1)
    query = lax.broadcasted_iota(jnp.int32, (QROWS, keys), 0) + first
    return (slots >= start) & (slots <= query)


FREQ = np.tile(THETA ** (-(np.arange(HEAD // 2) * 2.0 / HEAD)), 2)[None].astype(np.float32)


def forward_kernel(
    tok, og, norm1, norm2, q_gain, k_gain, freq, lengths, groups, starts, w_qkv, w_gu, w_out, w_down,
    h2_o, g_o, wq_o, wo_o, wg_o, wd_o, h1t_o, raw_o, q_o, k_o, att_o, lse_o, mid_o, gain_o, x_o, start_o, cos_o, sin_o,
    ggu_o, hid_o,
    x, h1, h1t, h2, g, wq, wg, wd, w_all, raw, qs, ks, att, heard, lse, mid, gain, gains, start, cosine, sine,
    q_raw, q_cut, q_raw_part, q_part, g_raw, g_cut, g_raw_part, g_part,
    xs, xr, gs, gr, hs, hr,
    zs, zr, ps, pr, ns, nr, loc_s, out_s, raw_s, row_s, os_, or_, ts, tr,
    y0s, y0r, y1s, y1r, y2s, y2r, y3s, y3r, y4s, y4r,
):
    p, row, col, z, k = place()
    px, py = dp_place()
    me = 2 * z + k
    lo = z % 2
    other = z + 1 - 2 * lo
    peer = on_ring(z, 1 - k)
    beside_col = 2 * lo + 1 - k
    piece_rows = pl.ds(pl.multiple_of(p * 32, 32), 32)

    def lanes(first, count):
        return pl.ds(pl.multiple_of(first, 256), count)

    raws = [
        pltpu.make_async_copy(src, dst, raw_s.at[i])
        for i, (src, dst) in enumerate(
            [
                (w_qkv.at[piece_rows], q_raw_part),
                (w_gu.at[piece_rows, :, lanes((1 - lo) * 2 * UNITS, 2 * UNITS)], g_raw_part),
                (w_qkv, q_raw),
                (w_gu.at[:, :, lanes(lo * 2 * UNITS, 2 * UNITS)], g_raw),
            ]
        )
    ]
    for copy in raws:
        copy.start()
    gains[0:1] = norm1[...]
    gains[1:2] = norm2[...]
    meet(column_friends() + xy_friends())
    raws[0].wait()
    for kk in range(2):
        q_part[kk] = jnp.where(lo == 0, q_raw_part[:, 2 + kk, :], q_raw_part[:, kk, :])

    gain[col] = gains[...]
    gain_copies = [
        remote(gains, gain.at[col], ns.at[i], nr.at[col], device)
        for i, device in enumerate([peer, on_ring(other, k), on_ring(other, 1 - k)])
    ]

    weights = [wq, wg, wd]
    blocks = [q_cut, g_cut, w_down]

    def cell(weight, c, xx, yy, cols=slice(None)):
        between = (slice(None),) * (len(weight.shape) - 5)
        return weight.at[(c, *between, xx, yy, slice(None), cols)]

    def crossing(a, kk):
        src = (q_part.at[kk], g_part.at[kk], cell(w_down, 2 * (1 - lo) + kk, px, py))[a]
        return remote(src, cell(weights[a], col, px, py), zs.at[a, kk], zr.at[a, k], on_ring(other, kk))

    def crossed(a, kk):
        dst = cell(weights[a], 2 * (1 - lo) + kk, px, py)
        return remote(dst, dst, zs.at[a, kk], zr.at[a, kk], peer)

    def beside(a):
        mine, theirs = (col, beside_col) if a == 2 else (k, 1 - k)
        keep = pltpu.make_async_copy(blocks[a].at[mine], weights[a].at[col], loc_s.at[a])
        give = remote(blocks[a].at[theirs], weights[a].at[col], ps.at[a], pr.at[a], peer)
        take = remote(weights[a].at[beside_col], weights[a].at[beside_col], ps.at[a], pr.at[a], peer)
        return keep, give, take

    def spread_at(a):
        weight = weights[a]
        half_lanes = weight.shape[-1] // 2

        def at(half, xx, yy, part):
            xs_ = slice(None) if xx is None else xx
            ys_ = slice(None) if yy is None else yy
            cols = slice(None) if part is None else pl.ds(part * half_lanes, half_lanes)
            return cell(weight, 2 * (1 - lo) + half, xs_, ys_, cols)

        return at

    def spread_bulk(a):
        weight = weights[a]
        between = (slice(None),) * (len(weight.shape) - 5)

        def bulk(phase, count):
            cs, long, short = {2: (1, 2, 1), 4: (1, 4, 1), 6: (2, 3, 1)}[count]
            xs_, ys_ = (long, 4) if phase else (short, long)
            return weight.at[(pl.ds(0, cs), *between, pl.ds(0, xs_), pl.ds(0, ys_))]

        return bulk

    spreads = [
        Spread(spread_at(a), spread_bulk(a), send, recv)
        for a, (send, recv) in enumerate([(y0s, y0r), (y1s, y1r), (y2s, y2r)])
    ]

    pair = pl.ds(2 * (1 - lo), 2)
    groups_of = [(1 - row, slice(None)), (row, pair)]

    def out_at(which):
        def at(half, xx, yy, part):
            xs_ = slice(None) if xx is None else xx
            ys_ = slice(None) if yy is None else yy
            cols = pl.ds(half * 256, 256) if part is None else pl.ds(half * 256 + part * HEAD, HEAD)
            return w_all.at[(*groups_of[which], xs_, ys_, k, slice(None), cols)]

        return at

    def out_bulk(which):
        def bulk(phase, count):
            xs_, ys_ = (count // 2, 4) if phase else (1, count // 2)
            return w_all.at[0, pl.ds(0, 4 - 2 * which), pl.ds(0, xs_), pl.ds(0, ys_), 0]

        return bulk

    out_spreads = [Spread(out_at(0), out_bulk(0), y3s, y3r), Spread(out_at(1), out_bulk(1), y4s, y4r)]
    out_pieces = [
        remote(
            w_out.at[px, py, kk], w_all.at[row, col, px, py, kk],
            os_.at[2 * dz + kk], or_.at[me], on_ring((z + dz) % 4, kk),
        )
        for dz in (1, 3, 2)
        for kk in range(2)
    ]
    keep_out = pltpu.make_async_copy(w_out, w_all.at[row, col], loc_s.at[3])
    give_out = remote(w_out, w_all.at[row, col], os_.at[0], or_.at[me], peer)

    def out_arrived(j):
        dst = w_all.at[j // 4, j % 4, px, py, k]
        return remote(dst, dst, os_.at[0], or_.at[j], peer)

    def out_share(which, core):
        ref = w_all.at[(*groups_of[which], slice(None), slice(None), core)]
        return remote(ref, ref, ts.at[7 + which], tr.at[7 + which], peer)

    def hand(o):
        there = (me + o) % 8
        rows = pl.ds(pl.multiple_of(there * OWN, OWN), OWN)
        device = {"row": there // 4, "col": there % 4}
        return remote(att.at[:, rows], heard.at[me], ts.at[o - 1], tr.at[o - 1], device)

    def handed(o):
        dst = heard.at[(me + 8 - o) % 8]
        return remote(dst, dst, ts.at[o - 1], tr.at[o - 1], peer)

    for kk in range(2):
        crossing(0, kk).start()
    for copy in out_pieces:
        copy.start()
    x_gather = Gather(tile_at(x), xs, xr, tok)
    x_gather.start()
    for copy in gain_copies:
        copy.start()
    keep_x = pltpu.make_async_copy(tok, tile_at(x)(me), loc_s.at[4])
    keep_x.start()
    keep_g = pltpu.make_async_copy(og, tile_at(g)(me), loc_s.at[5])
    keep_g.start()
    keep_out.start()
    give_out.start()
    raws[2].wait()

    @pl.loop(0, 16)
    def _(i):
        rows = pl.ds(pl.multiple_of(i * 32, 32), 32)
        for kk in range(2):
            q_cut[kk, i // 4, i % 4] = jnp.where(lo == 0, q_raw[rows, kk, :], q_raw[rows, 2 + kk, :])

    beside(0)[0].start()
    beside(0)[1].start()
    for kk in range(2):
        crossed(0, kk).wait_recv()
    spreads[0].start(0)
    for dz in (1, 3, 2):
        for kk in range(2):
            out_arrived(2 * ((z + dz) % 4) + kk).wait_recv()
    for spread in out_spreads:
        spread.start(0)
    for a in (1, 3):
        raws[a].wait()
    slot = (
        lax.broadcasted_iota(jnp.int32, (8, HEAD), 0) * HEAD + lax.broadcasted_iota(jnp.int32, (8, HEAD), 1)
    ).astype(F32)

    def one_sequence(i, begun):
        first = starts[i].astype(F32)
        last = first + jnp.where(groups[i] == p, lengths[i], 0).astype(F32)
        return jnp.where((slot >= first) & (slot < last), first, begun)

    begun = lax.fori_loop(0, lengths.shape[0], one_sequence, jnp.zeros((8, HEAD), F32))
    for i in range(8):
        rows = slice(i * HEAD, (i + 1) * HEAD)
        begin = jnp.broadcast_to(begun[i : i + 1], (HEAD, HEAD)).T
        there = lax.broadcasted_iota(jnp.int32, (HEAD, HEAD), 0).astype(F32) + float(i * HEAD)
        angle = (there - begin) * freq[...]
        start[rows] = begin.astype(jnp.int32)
        cosine[rows] = jnp.cos(angle)
        lane = lax.broadcasted_iota(jnp.int32, (HEAD, HEAD), 1)
        sine[rows] = jnp.where(lane < HEAD // 2, -1.0, 1.0) * jnp.sin(angle)
    spreads[0].pass_on(0)
    for spread in out_spreads:
        spread.pass_on(0)
    for u in range(3):
        for half in range(2):
            into = slice(u * 512 + half * 256, u * 512 + half * 256 + 256)
            for kk in range(2):
                cols = slice(kk * UNITS + u * 256, kk * UNITS + u * 256 + 256)
                g_part[kk, :, into] = g_raw_part[:, half, cols]
    spreads[0].wait(0)
    spreads[0].start(1)
    x_gather.forward()
    spreads[0].pass_on(1)
    for spread in out_spreads:
        spread.wait(0)
        spread.start(1)
    for c in range(4):

        @pl.when(c != col)
        def _():
            remote(gain.at[c], gain.at[c], ns.at[0], nr.at[c], peer).wait_recv()

    keep_x.wait()
    x_gather.finish([4, 5, 6])

    def gain_row(which):
        return jnp.concatenate([gain[c, which : which + 1] for c in range(4)], axis=1)

    gain_one = gain_row(0)

    def norm_one(half):
        @pl.loop(0, TILE // 64)
        def _(i):
            rows = pl.ds(pl.multiple_of(half * TILE + i * 64, 64), 64)
            value = x[rows].astype(F32)
            h1[rows] = (value * head_norm(value) * gain_one).astype(BF)

    def heads(half):
        @pl.loop(0, TILE // 256)
        def _(i):
            rows = pl.ds(pl.multiple_of(half * TILE + i * 256, 256), 256)
            mixed = mm(h1[rows], wq[...].reshape(WIDTH, 4 * HEAD)).astype(BF)
            raw[rows] = mixed
            cos_rows, sin_rows = cosine[rows], sine[rows]
            for piece in range(3):
                value = mixed[:, piece * HEAD : (piece + 1) * HEAD].astype(F32)
                by = q_gain[...] if piece < 2 else k_gain[...]
                turned = turn(value * head_norm(value) * by, cos_rows, sin_rows).astype(BF)
                if piece < 2:
                    qs[piece, rows] = turned
                else:
                    ks[rows] = turned

    norm_one(row)
    keep, _, take = beside(0)
    keep.wait()
    take.wait_recv()
    spreads[0].wait(1)
    heads(row)
    x_gather.share()
    for a in (1, 2):
        for kk in range(2):
            crossing(a, kk).start()
    g_gather = Gather(tile_at(g), gs, gr, og)
    g_gather.start()
    x_gather.finish([7, 8])
    beside(2)[0].start()
    beside(2)[1].start()
    norm_one(1 - row)
    heads(1 - row)
    for spread in out_spreads:
        spread.pass_on(1)
    mine = pl.ds(pl.multiple_of(me * OWN, OWN), OWN)
    saves = [
        pltpu.make_async_copy(src, dst, out_s.at[i])
        for i, (src, dst) in enumerate(
            [
                (wq, wq_o), (raw, raw_o), (qs, q_o), (ks, k_o), (gain, gain_o), (x.at[mine], x_o),
                (start, start_o), (cosine, cos_o), (sine, sin_o),
                (att, att_o), (lse, lse_o), (h1t, h1t_o), (g, g_o), (mid, mid_o),
                (w_all.at[row, :, pl.ds(col, 1)], wo_o),
            ]
        )
    ]
    for i in range(9):
        saves[i].start()

    for block in range(GROUP // QROWS):
        first, keys = block * QROWS, (block + 1) * QROWS
        rows = pl.ds(first, QROWS)
        allowed = allowed_keys(start[rows, :1], first, keys)

        @pl.loop(0, 2)
        def _(h):
            score = mm_t(qs[h, rows], ks[:keys]) * (SCALE * LOG2)
            score = jnp.where(allowed, score, -1e30)
            peak = jnp.max(score, axis=1, keepdims=True)
            weight = jnp.exp2(score - peak)
            total = jnp.sum(weight, axis=1, keepdims=True)
            out = mm(weight.astype(BF), raw[:keys, 3 * HEAD :]) / total
            att[h, rows] = out.astype(BF)
            lse[h, rows] = jnp.broadcast_to(peak + jnp.log2(total), (QROWS, HEAD))

        if block == 1:
            for a in (1, 2):
                for kk in range(2):
                    crossed(a, kk).wait_recv()
                spreads[a].start(0)

    for which, spread in enumerate(out_spreads):
        spread.wait(1)
        out_share(which, k).start()
    for o in range(1, 8):
        hand(o).start()
    for h in range(2):
        heard[me, h] = att[h, mine]
    saves[9].start()
    saves[10].start()
    for a in (1, 2):
        spreads[a].pass_on(0)
    for a in (1, 2):
        spreads[a].wait(0)
        spreads[a].start(1)
    def cut(i):
        rows = pl.ds(pl.multiple_of(i * 32, 32), 32)
        for u in range(3):
            for half in range(2):
                into = slice(u * 512 + half * 256, u * 512 + half * 256 + 256)
                for kk in range(2):
                    cols = slice(kk * UNITS + u * 256, kk * UNITS + u * 256 + 256)
                    g_cut[kk, i // 4, i % 4, :, into] = g_raw[rows, half, cols]

    pl.loop(0, 8)(cut)
    g_gather.forward()
    pl.loop(8, 16)(cut)
    beside(1)[0].start()
    beside(1)[1].start()
    keep_out.wait()
    out_arrived_peer = w_all.at[row, beside_col]
    remote(out_arrived_peer, out_arrived_peer, os_.at[0], or_.at[2 * z + 1 - k], peer).wait_recv()
    for which in range(2):
        out_share(which, 1 - k).wait_recv()
    saves[14].start()
    for o in range(1, 8):
        handed(o).wait_recv()
    left = [
        jnp.concatenate([heard[4 * half + c, h] for c in range(4) for h in range(2)], axis=1) for half in range(2)
    ]
    for c in range(4):
        mid[:, c * TILE : (c + 1) * TILE] = mm(left[0], w_all[0, c].reshape(2 * TILE, TILE)) + mm(
            left[1], w_all[1, c].reshape(2 * TILE, TILE)
        )
    gain_two = gain_row(1)

    @pl.loop(0, OWN // 16)
    def _(i):
        first = pl.multiple_of(i * 16, 16)
        there = pl.ds(pl.multiple_of(me * OWN + first, 16), 16)
        value = x[there].astype(F32) + mid[pl.ds(first, 16)]
        mid[pl.ds(first, 16)] = value
        h2[there] = (value * head_norm(value) * gain_two).astype(BF)

    h2_gather = Gather(rows_at(h2), hs, hr)
    h2_gather.start()
    saves[13].start()

    @pl.loop(0, 8)
    def _(i):
        cols = pl.ds(pl.multiple_of(i * 256, 256), 256)
        h1t[cols] = h1[:, cols].T

    saves[11].start()
    g_gather.share()
    for a in (1, 2):
        spreads[a].pass_on(1)
    x_gather.drain()
    saves[5].wait()
    row_saves = []

    def feed(d):
        rows = pl.ds(pl.multiple_of((z + d) % 4 * 256, 256), 256)

        @pl.loop(0, 3)
        def _(u):
            wide = pl.ds(pl.multiple_of(u * 512, 512), 512)
            gate_cols = pl.ds(pl.multiple_of(u * 512, 256), 256)
            up_cols = pl.ds(pl.multiple_of(u * 512 + 256, 256), 256)
            pair_ = mm(h2[rows], wg[:, :, :, :, wide].reshape(WIDTH, 512))
            back = mm_t(g[rows, :TILE], wd[0, u].reshape(256, TILE))
            for c in range(1, 4):
                back += mm_t(g[rows, c * TILE : (c + 1) * TILE], wd[c, u].reshape(256, TILE))
            gate, up = pair_[:, :256], pair_[:, 256:]
            sig = 1.0 / (1.0 + jnp.exp(-gate))
            silu = gate * sig
            h1[rows, pl.ds(pl.multiple_of(u * 256, 256), 256)] = (silu * up).astype(BF)
            x[rows, gate_cols] = (back * up * sig * (1.0 + gate * (1.0 - sig))).astype(BF)
            x[rows, up_cols] = (back * silu).astype(BF)

        for i, (src, dst) in enumerate(
            [
                (h2.at[rows], h2_o.at[rows]),
                (x.at[rows, pl.ds(0, 2 * UNITS)], ggu_o.at[rows]),
                (h1.at[rows, pl.ds(0, UNITS)], hid_o.at[rows]),
            ]
        ):
            copy = pltpu.make_async_copy(src, dst, row_s.at[d, i])
            copy.start()
            row_saves.append(copy)

    for a in (1, 2):
        keep, _, take = beside(a)
        keep.wait()
        take.wait_recv()
        spreads[a].wait(1)
    g_gather.finish()
    keep_g.wait()
    saves[12].start()
    h2_gather.finish([4])
    feed(0)
    h2_gather.forward()
    h2_gather.finish([5, 6])
    feed(1)
    weight_saves = [pltpu.make_async_copy(weights[a], (wg_o, wd_o)[a - 1], loc_s.at[a + 5]) for a in (1, 2)]
    for copy in weight_saves:
        copy.start()
    h2_gather.share()
    feed(3)
    h2_gather.finish([7, 8])
    feed(2)
    for copy in gain_copies + out_pieces + [give_out]:
        copy.wait_send()
    for a in range(3):
        beside(a)[1].wait_send()
        for kk in range(2):
            crossing(a, kk).wait_send()
    for o in range(1, 8):
        hand(o).wait_send()
    for which in range(2):
        out_share(which, k).wait_send()
    for spread in spreads + out_spreads:
        spread.drain()
    g_gather.drain()
    h2_gather.drain()
    for i, copy in enumerate(saves):
        if i != 5:
            copy.wait()
    for copy in weight_saves + row_saves:
        copy.wait()


def forward_call(*args):
    hbm = pl.BlockSpec(memory_space=pl.ANY)
    vmem = pl.BlockSpec(memory_space=pltpu.VMEM)
    smem = pl.BlockSpec(memory_space=pltpu.SMEM)
    dma = pltpu.SemaphoreType.DMA

    def out(shape, dtype=BF):
        return jax.ShapeDtypeStruct(shape, dtype)

    wide = (GROUP, WIDTH)
    return pl.pallas_call(
        forward_kernel,
        out_shape=[
            out(wide), out(wide), out((4, 4, 4, 32, 512)), out((4, 1, 4, 2, 32, TILE)), out((4, 4, 4, 32, 2 * UNITS)),
            out((4, 3, 4, 4, 16, TILE)), out((WIDTH, GROUP)), out((GROUP, 512)), out((2, GROUP, HEAD)), out((GROUP, HEAD)),
            out((2, GROUP, HEAD)), out((2, GROUP, HEAD), F32), out((OWN, WIDTH), F32), out((4, 8, TILE), F32),
            out((OWN, WIDTH)), out((GROUP, HEAD), jnp.int32), out((GROUP, HEAD), F32), out((GROUP, HEAD), F32),
            out((GROUP, 2 * UNITS)), out((GROUP, UNITS)),
        ],
        in_specs=[hbm] * 2 + [vmem] * 5 + [smem] * 3 + [hbm] * 4,
        out_specs=[hbm] * 20,
        scratch_shapes=[
            pltpu.VMEM(wide, BF), pltpu.VMEM(wide, BF), pltpu.VMEM((WIDTH, GROUP), BF), pltpu.VMEM(wide, BF),
            pltpu.VMEM(wide, BF), pltpu.VMEM((4, 4, 4, 32, 512), BF), pltpu.VMEM((4, 4, 4, 32, 2 * UNITS), BF),
            pltpu.VMEM((4, 3, 4, 4, 16, TILE), BF), pltpu.VMEM((2, 4, 4, 4, 2, 32, TILE), BF),
            pltpu.VMEM((GROUP, 512), BF), pltpu.VMEM((2, GROUP, HEAD), BF), pltpu.VMEM((GROUP, HEAD), BF),
            pltpu.VMEM((2, GROUP, HEAD), BF), pltpu.VMEM((8, 2, OWN, HEAD), BF), pltpu.VMEM((2, GROUP, HEAD), F32),
            pltpu.VMEM((OWN, WIDTH), F32), pltpu.VMEM((4, 8, TILE), F32), pltpu.VMEM((8, TILE), F32),
            pltpu.VMEM((GROUP, HEAD), jnp.int32), pltpu.VMEM((GROUP, HEAD), F32), pltpu.VMEM((GROUP, HEAD), F32),
            pltpu.VMEM((TILE, 4, 512), BF), pltpu.VMEM((2, 4, 4, 32, 512), BF), pltpu.VMEM((32, 4, 512), BF),
            pltpu.VMEM((2, 32, 512), BF), pltpu.VMEM((TILE, 2, 2 * UNITS), BF), pltpu.VMEM((2, 4, 4, 32, 2 * UNITS), BF),
            pltpu.VMEM((32, 2, 2 * UNITS), BF), pltpu.VMEM((2, 32, 2 * UNITS), BF),
        ]
        + GATHER_SEMS * 3
        + [
            dma((3, 2)), dma((3, 2)), dma((3,)), dma((3,)), dma((3,)), dma((4,)), dma((8,)), dma((15,)), dma((4,)),
            dma((4, 3)), dma((8,)), dma((8,)), dma((9,)), dma((9,)),
        ]
        + SPREAD_SEMS * 5,
        compiler_params=pltpu.CompilerParams(
            collective_id=1, has_side_effects=True, vmem_limit_bytes=VMEM_LIMIT
        ),
        cost_estimate=pl.CostEstimate(flops=14_000_000_000, bytes_accessed=60_000_000, transcendentals=2_000_000),
        name="forward",
    )(*args)


class Collapse:
    def __init__(self, which, data, near, full, done, send, recv):
        here = dp_place()
        self.which, self.data, self.near, self.full, self.done, self.here = which, data, near, full, done, here
        self.copies, self.send, self.recv = {}, send, recv
        for half in range(2):
            for phase in range(2):
                axis = half ^ phase

                def copy(slot, src, dst, o):
                    return remote(src, dst, send.at[which, phase], recv.at[which, phase, slot // 2], along(axis, o))

                self.copies[half, phase] = [
                    copy(0, self.block(half, phase, 2, 0), near[phase].at[half, 0], 1),
                    copy(1, self.block(half, phase, 2, 1), near[phase].at[half, 1], 3),
                    copy(2, self.block(half, phase, 1), full[phase].at[half, 0], 1),
                    copy(3, self.block(half, phase, 3), full[phase].at[half, 1], 3),
                ]

    def at(self, half, phase, o):
        there = (self.here[half ^ phase] + o) % 4
        if phase == 0:
            return (there, slice(None)) if half == 0 else (slice(None), there)
        return (self.here[0], there) if half == 0 else (there, self.here[1])

    def block(self, half, phase, o, part=None):
        which = pl.ds(2 * half, 2) if part is None else 2 * half + part
        return self.data.at[(*self.at(half, phase, o), which)]

    def cell(self, half, phase, o, a, c):
        x, y = self.at(half, phase, o)
        x, y = (a if isinstance(x, slice) else x), (a if isinstance(y, slice) else y)
        return (x, y, 2 * half + c)

    def arrived(self, phase, step):
        ref = (self.near, self.full)[step][phase]
        sems = (self.send.at[self.which, phase], self.recv.at[self.which, phase, step])
        remote(ref, ref, *sems, along(0, 1)).wait_recv()

    def start(self, phase=0):
        for half in range(2):
            for slot in range(2):
                self.copies[half, phase][slot].start()

    def mid(self, phase=0):
        self.arrived(phase, 0)
        for half in range(2):
            for slot in range(2):

                def add(a):
                    index = self.cell(half, phase, (1, 3)[slot], a, slot)
                    here = (half, slot, a) if phase == 0 else (half, slot)
                    self.data[index] = (
                        self.data[index].astype(F32) + self.near[phase][here].astype(F32)
                    ).astype(BF)

                if phase == 0:
                    pl.loop(0, 4)(add)
                else:
                    add(0)
                self.copies[half, phase][2 + slot].start()

    def first(self):
        self.arrived(0, 1)
        for half in range(2):

            @pl.loop(0, 4)
            def _(a):
                for c in range(2):
                    index = self.cell(half, 0, 0, a, c)
                    total = self.data[index].astype(F32)
                    for slot in range(2):
                        total += self.full[0][half, slot, a, c].astype(F32)
                    self.data[index] = total.astype(BF)

        self.start(1)

    def second(self):
        self.arrived(1, 1)
        for half in range(2):
            for c in range(2):
                total = self.data[self.cell(half, 1, 0, 0, c)].astype(F32)
                for slot in range(2):
                    total += self.full[1][half, slot, c].astype(F32)
                self.done[self.which, 2 * half + c] = total.astype(BF)

    def drain(self):
        for phase in range(2):
            ref = self.data.at[0, pl.ds(0, 3)] if phase else self.data.at[pl.ds(0, 3)]
            sems = (self.send.at[self.which, phase], self.recv.at[self.which, phase, 0])
            remote(ref, ref, *sems, along(0, 1)).wait_send()


CHUNKS, BUFFERS = 4, 3


def collapse_scratch():
    dma = pltpu.SemaphoreType.DMA
    return (
        [pltpu.VMEM((4, 4, 4, 48, 512), BF)] * BUFFERS
        + [pltpu.VMEM((2, 2, 4, 48, 512), BF)] * BUFFERS
        + [pltpu.VMEM((2, 2, 48, 512), BF)] * BUFFERS
        + [pltpu.VMEM((2, 2, 4, 2, 48, 512), BF)] * BUFFERS
        + [pltpu.VMEM((2, 2, 2, 48, 512), BF)] * BUFFERS
        + [pltpu.VMEM((CHUNKS, 4, 48, 512), BF), dma((CHUNKS, 2)), dma((CHUNKS, 2, 2))]
        + [dma((CHUNKS, 3)), dma((CHUNKS, 4)), dma((CHUNKS, 2)), dma((CHUNKS, 2, 2))]
    )


class Trade:
    def __init__(self, block, slot, send, recv, which=()):
        _, row, col, z, k = place()
        self.col, self.peer = col, on_ring(z, 1 - k)
        self.recv, self.send, self.slot, self.which = recv, send, slot, which
        self.copies = [
            remote(block((col + o) % 4), slot(col), send.at[(*which, o - 1)], recv.at[(*which, o - 1)], {"col": (col + o) % 4})
            for o in range(1, 4)
        ]
        self.keep = pltpu.make_async_copy(block(col), slot(col), recv.at[(*which, 3)])

    def start(self):
        for copy in self.copies:
            copy.start()
        self.keep.start()

    def finish(self):
        for o in range(1, 4):
            dst = self.slot((self.col - o + 4) % 4)
            sems = (self.send.at[(*self.which, o - 1)], self.recv.at[(*self.which, o - 1)])
            remote(dst, dst, *sems, self.peer).wait_recv()
        self.keep.wait()

    def drain(self):
        for copy in self.copies:
            copy.wait_send()


def norm_back(grad, value, gain):
    scale = head_norm(value)
    weighted = grad * gain
    inner = jnp.mean(weighted * value, axis=1, keepdims=True)
    return scale * weighted - value * (scale * scale * scale * inner), grad * value * scale


def norm_back(grad, value, gain):
    scale = head_norm(value)
    weighted = grad * gain
    inner = jnp.mean(weighted * value, axis=1, keepdims=True)
    return scale * weighted - value * (scale * scale * scale * inner), grad * value * scale


def backward_kernel(
    h2_i, ggu_i, hid_i, g_i, wg_i, wd_i, wo_i, wq_i, h1t_i, raw_i, q_i, k_i, att_i, lse_i, mid_i, gain_i, x_i,
    start_i, cos_i, sin_i, q_gain, k_gain,
    result_o, stream_o, grads_o, sums_o,
    m, gm, dqkv, mid, gain, x_own, g_own, acc, head_acc, tile_f, tile_b, totals, heard,
    ms, mr,
    parts, theirs, psums, near, full, rs_s, rs_r,
    data0, data1, data2, near0, near1, near2, next0, next1, next2, full0, full1, full2, last0, last1, last2,
    done, c_s, c_r, t_s, t_r, a_s, a_r,
    fs, fr, ls, lr, as_, ar, in_s, free,
):
    p, row, col, z, k = place()
    px, py = dp_place()
    me = 2 * z + k
    up, down, peer = on_ring((z + 1) % 4, k), on_ring((z + 3) % 4, k), on_ring(z, 1 - k)
    far = on_ring((z + 2) % 4, k)
    loads = []

    def load(src, dst, now=True):
        copy = pltpu.make_async_copy(src, dst, in_s.at[len(loads)])
        if now:
            copy.start()
        loads.append(copy)
        return copy

    def wait(copies):
        for copy in copies:
            copy.wait()

    collapses, trades, spreads = [], [], []
    datas, nears, nexts = (data0, data1, data2), (near0, near1, near2), (next0, next1, next2)
    fulls, lasts = (full0, full1, full2), (last0, last1, last2)

    def chunk(i):
        def at(half, x, y, part):
            xs = slice(None) if x is None else x
            ys = slice(None) if y is None else y
            which = pl.ds(2 * half, 2) if part is None else 2 * half + part
            return grads_o.at[i, xs, ys, which]

        b = i % BUFFERS
        collapses.append(Collapse(i, datas[b], (nears[b], nexts[b]), (fulls[b], lasts[b]), done, c_s, c_r))
        trades.append(
            Trade(lambda c: done.at[i, c], lambda c: grads_o.at[i, px, py, c], t_s, t_r, (i,))
        )
        def bulk(phase, count):
            xs_, ys_ = (count // 2, 4) if phase else (1, count // 2)
            return grads_o.at[i, pl.ds(0, xs_), pl.ds(0, ys_)]

        spreads.append(Spread(at, bulk, a_s, a_r, (i,)))

    for i in range(CHUNKS):
        chunk(i)
    scatter = Scatter(parts, theirs, psums, near, full, rs_s, rs_r)
    stream_trade = Trade(
        lambda c: tile_f.at[:, pl.ds(pl.multiple_of(c * TILE, TILE), TILE)],
        lambda c: stream_o.at[pl.ds(pl.multiple_of(c * OWN, OWN), OWN)], fs, fr,
    )
    result_trade = Trade(
        lambda c: tile_b.at[:, pl.ds(pl.multiple_of(c * TILE, TILE), TILE)],
        lambda c: result_o.at[pl.ds(pl.multiple_of(c * OWN, OWN), OWN)], ls, lr,
    )

    def release():
        scatter.drain()
        for device in (up, down, peer):
            pl.semaphore_signal(free, inc=1, device_id=device, device_id_type=MESH)

    def project(d, product):
        rows = pl.ds(pl.multiple_of((z + d) % 4 * 256, 256), 256)

        @pl.loop(0, 4)
        def _(c):
            cols = pl.ds(pl.multiple_of(c * TILE, TILE), TILE)
            parts[d, :, cols] = product(rows, c, cols).astype(BF)

        scatter.put(d)

    def weight_grads(i, first, second):
        data = datas[i % BUFFERS]
        for c in range(4):
            cols = slice(c * TILE, (c + 1) * TILE)
            data[:, :, c, :32] = first(cols).astype(BF).reshape(4, 4, 32, 512)
            data[:, :, c, 32:] = second(cols).astype(BF).reshape(4, 4, 16, 512)
        collapses[i].start()

    def gain_row(which):
        return jnp.concatenate([gain[c, which : which + 1] for c in range(4)], axis=1)

    own_rows = pl.ds(pl.multiple_of(me * OWN, OWN), OWN)

    def stage_one(h2, g, ggu, hid, wg):
        first_loads = [load(ggu_i, ggu)]
        wg_loads = [load(wg_i.at[c], wg.at[c]) for c in range(4)]
        more_loads = [load(hid_i, hid), load(h2_i, h2), load(g_i, g)]
        for copy in early:
            copy.start()
        meet(ring_friends() + [far] + xy_friends())
        def grads(u):
            weight_grads(
                u,
                lambda cols: t_mm(h2[:, cols], ggu[:, u * 512 : (u + 1) * 512]),
                lambda cols: t_mm(hid[:, u * 256 : (u + 1) * 256], g[:, cols]),
            )

        def product(rows, c, cols):
            return mm_t(ggu[rows], wg[c])

        wait(first_loads)
        far_rows = pl.ds(pl.multiple_of((z + 2) % 4 * 256, 256), 256)
        for c in range(4):
            wg_loads[c].wait()
            parts[2, :, c * TILE : (c + 1) * TILE] = mm_t(ggu[far_rows], wg[c]).astype(BF)
        scatter.put(2)
        wait(more_loads)
        grads(0)
        scatter.across()
        project(1, product)
        project(3, product)
        collapses[0].mid()
        scatter.beside(0)
        scatter.beside(1)
        grads(1)
        project(0, product)
        grads(2)

    early = [
        load(src, dst, False)
        for src, dst in [(mid_i, mid), (gain_i, gain), (x_i, x_own), (g_i.at[own_rows], g_own)]
    ]
    pl.run_scoped(
        stage_one,
        pltpu.VMEM((GROUP, WIDTH), BF), pltpu.VMEM((GROUP, WIDTH), BF), pltpu.VMEM((GROUP, 2 * UNITS), BF),
        pltpu.VMEM((GROUP, UNITS), BF), pltpu.VMEM((4, TILE, 2 * UNITS), BF),
    )

    def stage_two(wo, att, qs, ks, raw, lse, ga, dk, dv, h1t, wq, att_t, start, cosine, sine):
        l_wo, l_att = load(wo_i, wo), load(att_i, att)
        l_heads = [
            load(q_i, qs), load(k_i, ks), load(raw_i, raw), load(lse_i, lse),
            load(start_i, start), load(cos_i, cosine), load(sin_i, sine),
        ]
        l_last = [load(h1t_i, h1t), load(wq_i, wq)]
        wait(early)
        acc[...] = jnp.zeros_like(acc)
        head_acc[...] = jnp.zeros_like(head_acc)
        dk[...] = jnp.zeros_like(dk)
        dv[...] = jnp.zeros_like(dv)
        totals[0] = jnp.zeros((8, TILE + HEAD), F32)
        gain_two = gain_row(1)
        scatter.arrive()

        @pl.loop(0, OWN // 16)
        def _(i):
            rows = pl.ds(pl.multiple_of(i * 16, 16), 16)
            back, gained = norm_back(scatter.total(pl.multiple_of(i * 16, 16), 16), mid[rows], gain_two)
            acc[1] += gained
            back = back + g_own[rows].astype(F32)
            gm[rows] = back
            m[pl.ds(pl.multiple_of(me * OWN + i * 16, 16), 16)] = back.astype(BF)

        m_gather = Gather(rows_at(m), ms, mr)
        m_gather.start()
        release()
        collapses[0].first()
        collapses[1].mid()
        collapses[0].mid(1)
        l_att.wait()
        for h in range(2):
            att_t[h * HEAD : (h + 1) * HEAD] = att[h].T
        l_wo.wait()
        wait(l_heads)

        def attend(d):
            block = (z + d) % 4
            first = pl.multiple_of(block * QROWS, QROWS)
            rows = pl.ds(first, QROWS)
            back = mm_t(m[rows, :TILE], wo[0])
            for c in range(1, 4):
                back += mm_t(m[rows, c * TILE : (c + 1) * TILE], wo[c])
            for h in range(2):
                ga[h, rows] = back[:, h * HEAD : (h + 1) * HEAD].astype(BF)

            def over(keys):
                allowed = allowed_keys(start[rows, :1], first, keys)

                @pl.loop(0, 2)
                def _(h):
                    cols = pl.ds(pl.multiple_of(h * HEAD, HEAD), HEAD)
                    score = mm_t(qs[h, rows], ks[:keys]) * (SCALE * LOG2)
                    prob = jnp.exp2(jnp.where(allowed, score, -1e30) - lse[h, rows, :1])
                    grad = ga[h, rows]
                    delta = jnp.sum(grad.astype(F32) * att[h, rows].astype(F32), axis=1, keepdims=True)
                    prob_grad = mm_t(grad, raw[:keys, 3 * HEAD :])
                    score_grad = (prob * (prob_grad - delta)).astype(BF)
                    dk[:keys] += t_mm(score_grad, qs[h, rows])
                    dv[:keys] += t_mm(prob.astype(BF), grad)
                    back = turn_back(mm(score_grad, ks[:keys]) * SCALE, cosine[rows], sine[rows])
                    back, gained = norm_back(back, raw[rows, cols].astype(F32), q_gain[...])
                    dqkv[rows, cols] = back.astype(BF)
                    head_acc[0:1] += jnp.sum(gained, axis=0, keepdims=True)

            @pl.when(block < 2)
            def _():
                over(2 * QROWS)

            @pl.when(block >= 2)
            def _():
                over(4 * QROWS)

        m_gather.finish([4])
        attend(0)
        collapses[1].first()
        collapses[2].mid()
        m_gather.forward()
        collapses[1].mid(1)
        collapses[0].second()
        trades[0].start()
        m_gather.finish([5, 6])
        attend(1)
        m_gather.share()
        attend(3)
        collapses[2].first()
        m_gather.finish([7, 8])
        attend(2)
        trades[0].finish()
        spreads[0].start(0)

        @pl.loop(0, 4)
        def _(i):
            rows = pl.ds(pl.multiple_of(i * 256, 256), 256)
            back = turn_back(dk[rows] * SCALE, cosine[rows], sine[rows])
            back, gained = norm_back(back, raw[rows, 2 * HEAD : 3 * HEAD].astype(F32), k_gain[...])
            dqkv[rows, 2 * HEAD : 3 * HEAD] = back.astype(BF)
            dqkv[rows, 3 * HEAD :] = dv[rows].astype(BF)
            head_acc[1:2] += jnp.sum(gained, axis=0, keepdims=True)

        collapses[2].mid(1)
        wait(l_last)
        collapses[0].drain()
        weight_grads(3, lambda cols: mm(h1t[cols], dqkv[...]), lambda cols: mm(att_t[...], m[:, cols]))
        collapses[1].second()
        trades[1].start()
        spreads[0].pass_on(0)
        collapses[2].second()
        trades[2].start()
        pl.semaphore_wait(free, 3)

        def product(rows, c, cols):
            return mm_t(dqkv[rows], wq[c])

        project(2, product)
        project(1, product)
        collapses[3].mid()
        trades[1].finish()
        spreads[1].start(0)
        scatter.across()
        trades[2].finish()
        spreads[2].start(0)
        project(3, product)
        spreads[0].wait(0)
        spreads[0].start(1)
        spreads[1].pass_on(0)
        project(0, product)
        collapses[3].first()
        scatter.beside(0)
        scatter.beside(1)
        m_gather.drain()

    pl.run_scoped(
        stage_two,
        pltpu.VMEM((4, 256, TILE), BF), pltpu.VMEM((2, GROUP, HEAD), BF), pltpu.VMEM((2, GROUP, HEAD), BF),
        pltpu.VMEM((GROUP, HEAD), BF), pltpu.VMEM((GROUP, 512), BF), pltpu.VMEM((2, GROUP, HEAD), F32),
        pltpu.VMEM((2, GROUP, HEAD), BF), pltpu.VMEM((GROUP, HEAD), F32), pltpu.VMEM((GROUP, HEAD), F32),
        pltpu.VMEM((WIDTH, GROUP), BF), pltpu.VMEM((4, TILE, 512), BF), pltpu.VMEM((2 * HEAD, GROUP), BF),
        pltpu.VMEM((GROUP, HEAD), jnp.int32), pltpu.VMEM((GROUP, HEAD), F32), pltpu.VMEM((GROUP, HEAD), F32),
    )

    def stage_three(hid, wd):
        last = [load(hid_i, hid), load(wd_i, wd)]
        gain_one = gain_row(0)
        collapses[3].mid(1)
        spreads[1].wait(0)
        spreads[1].start(1)
        spreads[2].pass_on(0)
        collapses[3].second()
        trades[3].start()
        scatter.arrive()

        @pl.loop(0, OWN // 16)
        def _(i):
            rows = pl.ds(pl.multiple_of(i * 16, 16), 16)
            back, gained = norm_back(
                scatter.total(pl.multiple_of(i * 16, 16), 16), x_own[rows].astype(F32), gain_one
            )
            acc[0] += gained
            tile_f[rows] = gm[rows] + back

        stream_trade.start()
        release()
        for c in range(4):
            for which in range(2):
                part = jnp.sum(acc[which, :, c * TILE : (c + 1) * TILE], axis=0, keepdims=True)
                totals[0, 4 * which + c : 4 * which + c + 1, :TILE] = part
        totals[0, 0:2, TILE:] = head_acc[0:2]
        sent = []

        def tell(phase, devices, slots):
            for device, slot in zip(devices, slots):
                copy = remote(totals.at[phase], heard.at[slot], as_.at[slot], ar.at[slot], device)
                copy.start()
                sent.append(copy)

        def listen(phase, slots):
            total = totals[phase]
            for slot in slots:
                remote(heard.at[slot], heard.at[slot], as_.at[slot], ar.at[slot], peer).wait_recv()
                total += heard[slot]
            totals[phase + 1] = total

        tell(0, [peer], [0])
        spreads[0].pass_on(1)
        wait(last)
        pl.semaphore_wait(free, 3)

        def product(rows, c, cols):
            return mm(hid[rows], wd[c])

        project(2, product)
        project(1, product)
        listen(0, [0])
        tell(1, [up, down, far], [1, 2, 3])
        project(3, product)
        trades[3].finish()
        spreads[3].start(0)
        scatter.across()
        spreads[1].pass_on(1)
        spreads[3].pass_on(0)
        listen(1, [1, 2, 3])
        tell(2, [along(0, o) for o in range(1, 4)], [4, 5, 6])
        spreads[2].wait(0)
        spreads[2].start(1)
        project(0, product)
        scatter.beside(0)
        scatter.beside(1)
        spreads[3].wait(0)
        spreads[3].start(1)
        spreads[2].pass_on(1)
        listen(2, [4, 5, 6])
        tell(3, [along(1, o) for o in range(1, 4)], [7, 8, 9])
        scatter.arrive()

        @pl.loop(0, OWN // 16)
        def _(i):
            rows = pl.ds(pl.multiple_of(i * 16, 16), 16)
            tile_b[rows] = (mid[rows] + scatter.total(pl.multiple_of(i * 16, 16), 16)).astype(BF)

        result_trade.start()
        spreads[3].pass_on(1)
        listen(3, [7, 8, 9])
        sums_o[...] = totals[4]
        stream_trade.finish()
        result_trade.finish()
        for spread in spreads:
            spread.wait(1)
        scatter.drain()
        for thing in collapses[1:] + trades + spreads + [stream_trade, result_trade]:
            thing.drain()
        for copy in sent:
            copy.wait_send()

    pl.run_scoped(stage_three, pltpu.VMEM((GROUP, UNITS), BF), pltpu.VMEM((4, UNITS, TILE), BF))


def backward_call(*args):
    hbm = pl.BlockSpec(memory_space=pl.ANY)
    vmem = pl.BlockSpec(memory_space=pltpu.VMEM)
    dma = pltpu.SemaphoreType.DMA
    out = jax.ShapeDtypeStruct
    grads = out((CHUNKS, 4, 4, 4, 48, 512), BF)
    return pl.pallas_call(
        backward_kernel,
        out_shape=[out((TILE, TILE), BF), out((TILE, TILE), F32), grads, out((8, TILE + HEAD), F32)],
        in_specs=[hbm] * 20 + [vmem] * 2,
        out_specs=[hbm] * 3 + [vmem],
        scratch_shapes=[
            pltpu.VMEM((GROUP, WIDTH), BF), pltpu.VMEM((OWN, WIDTH), F32), pltpu.VMEM((GROUP, 512), BF),
            pltpu.VMEM((OWN, WIDTH), F32), pltpu.VMEM((4, 8, TILE), F32),
            pltpu.VMEM((OWN, WIDTH), BF), pltpu.VMEM((OWN, WIDTH), BF), pltpu.VMEM((2, 16, WIDTH), F32),
            pltpu.VMEM((8, HEAD), F32), pltpu.VMEM((OWN, WIDTH), F32), pltpu.VMEM((OWN, WIDTH), BF),
            pltpu.VMEM((5, 8, TILE + HEAD), F32), pltpu.VMEM((10, 8, TILE + HEAD), F32),
        ]
        + GATHER_SEMS
        + scatter_scratch()
        + collapse_scratch()
        + [
            dma((3,)), dma((4,)), dma((3,)), dma((4,)), dma((10,)), dma((10,)), dma((28,)), pltpu.SemaphoreType.REGULAR,
        ],
        compiler_params=pltpu.CompilerParams(
            collective_id=2, has_side_effects=True, vmem_limit_bytes=VMEM_LIMIT
        ),
        cost_estimate=pl.CostEstimate(flops=25_000_000_000, bytes_accessed=100_000_000, transcendentals=2_000_000),
        name="backward",
    )(*args)


PLACE = 4


def place_kernel(grads, result, stream, totals, gate_up, down, qkv, out, result_o, stream_o, one, two, q_o, k_o):
    for c in range(4):
        for u in range(3):
            t = c * 3 + u
            value = grads[u, :, c, :32].reshape(PLACE * 32, 512).astype(F32)
            for g in range(2):
                gate_up[:, g, t * 256 : (t + 1) * 256] = value[:, g * 256 : (g + 1) * 256]
            down[t] = grads[u, :, c, 32:].astype(F32)
        qkv[:, c, :] = grads[3, :, c, :32].reshape(PLACE * 32, 512).astype(F32)
        out[c] = grads[3, :, c, 32:].astype(F32)
    result_o[...] = result[...]
    stream_o[...] = stream[...]
    for c in range(4):
        one[:, c * TILE : (c + 1) * TILE] = totals[c : c + 1, :TILE]
        two[:, c * TILE : (c + 1) * TILE] = totals[4 + c : 5 + c, :TILE]
    q_o[...] = totals[0:1, TILE:]
    k_o[...] = totals[1:2, TILE:]


def place_grads(grads, result, stream, totals):
    tile = pl.BlockSpec((32 * PLACE, TILE), lambda p: (p, 0))

    def whole(*shape):
        return pl.BlockSpec(shape, lambda p: (0,) * len(shape))

    return pl.pallas_call(
        place_kernel,
        grid=(DP // PLACE,),
        in_specs=[
            pl.BlockSpec((CHUNKS, PLACE, 4, 48, 512), lambda p: (0, p, 0, 0, 0)), tile, tile, whole(8, TILE + HEAD),
        ],
        out_specs=[
            pl.BlockSpec((32 * PLACE, 2, 4 * UNITS), lambda p: (p, 0, 0)),
            pl.BlockSpec((12, PLACE, 16, TILE), lambda p: (0, p, 0, 0)),
            pl.BlockSpec((32 * PLACE, 4, 512), lambda p: (p, 0, 0)),
            pl.BlockSpec((4, PLACE, 16, TILE), lambda p: (0, p, 0, 0)),
            tile, tile, whole(1, WIDTH), whole(1, WIDTH), whole(1, HEAD), whole(1, HEAD),
        ],
        out_shape=[
            jax.ShapeDtypeStruct((TILE, 2, 4 * UNITS), F32),
            jax.ShapeDtypeStruct((12, DP, 16, TILE), F32),
            jax.ShapeDtypeStruct((TILE, 4, 512), F32),
            jax.ShapeDtypeStruct((4, DP, 16, TILE), F32),
            jax.ShapeDtypeStruct((TILE, TILE), BF),
            jax.ShapeDtypeStruct((TILE, TILE), F32),
            jax.ShapeDtypeStruct((1, WIDTH), F32),
            jax.ShapeDtypeStruct((1, WIDTH), F32),
            jax.ShapeDtypeStruct((1, HEAD), F32),
            jax.ShapeDtypeStruct((1, HEAD), F32),
        ],
        compiler_params=pltpu.CompilerParams(vmem_limit_bytes=VMEM_LIMIT),
        cost_estimate=pl.CostEstimate(flops=0, bytes_accessed=41_000_000, transcendentals=0),
        name="place",
    )(grads, result, stream, totals)


def body(
    tokens, norm1_gain, w_qkv, q_gain, k_gain, w_out, norm2_gain, w_gate_up, w_down, out_grad,
    seq_lengths, seq_group, seq_start,
):
    (h2, g, wq, wo, wg, wd, h1t, raw, qs, ks, att, lse, middle, gain, x_own, start, cosine, sine, ggu, hid) = forward_call(
        tokens, out_grad, norm1_gain[None], norm2_gain[None], q_gain[None], k_gain[None], jnp.asarray(FREQ),
        seq_lengths, seq_group, seq_start, w_qkv, w_gate_up,
        w_out.reshape(4, 4, 2, 32, TILE), w_down.reshape(4, 3, 4, 4, 16, TILE),
    )
    wg = wg.reshape(4, TILE, 2 * UNITS)
    wd = wd.reshape(4, UNITS, TILE)
    result, stream, grads, totals = backward_call(
        h2, ggu, hid, g, wg, wd, wo.reshape(4, 256, TILE), wq.reshape(4, TILE, 512), h1t, raw, qs, ks, att, lse,
        middle, gain, x_own, start, cosine, sine, q_gain[None], k_gain[None],
    )
    grads = grads.reshape(CHUNKS, DP, 4, 48, 512)
    g_gate_up, g_down, g_qkv, g_out, result, stream, one, two, q_grad, k_grad = place_grads(grads, result, stream, totals)
    return (
        result,
        stream,
        one.reshape(WIDTH),
        g_qkv,
        q_grad.reshape(HEAD),
        k_grad.reshape(HEAD),
        g_out.reshape(w_out.shape),
        two.reshape(WIDTH),
        g_gate_up,
        g_down.reshape(w_down.shape),
    )


def solution(mesh):
    in_specs = (
        P(("dp", "row"), "col"),
        P("col"),
        P("col", "row", None),
        P(),
        P(),
        P("row", "col"),
        P("col"),
        P("col", None, "row"),
        P("row", "col"),
        P(("dp", "row"), "col"),
        P(),
        P(),
        P(),
    )
    out_specs = (
        P(("dp", "row"), "col"),
        P(("dp", "row"), "col"),
        P(),
        P("col", "row", None),
        P(),
        P(),
        P("row", "col"),
        P(),
        P("col", None, "row"),
        P("row", "col"),
    )
    return jax.shard_map(body, mesh=mesh, in_specs=in_specs, out_specs=out_specs, check_vma=False)
```
